32 devices in a mesh: expert: 4 (over z), shard: 8 (over y, x, core).
Axes of the slice: x: 2, y: 2, z: 4, core: 2. Of those that a mesh axis runs over, the one named last changes fastest.
Arguments:
- hidden_in: bfloat16 [26624, 768], P(('expert', 'shard')), may hold values from -6 to 6
- prior_logits: float32 [26624, 8], P(('expert', 'shard')), may hold values from -3 to 3
- project_weight: bfloat16 [2, 3, 768, 768], P(None, None, 'shard'), may hold values from -0.21875 to 0.21875
- output_weight: bfloat16 [2, 768, 768], P(None, 'shard'), may hold values from -1.75 to 1.75
- norm_gain: bfloat16 [2, 2, 768], P(None, None, 'shard'), may hold values from 0.5 to 1.5
- router_weight: bfloat16 [2, 768, 8], P(None, 'shard'), may hold values from -0.15625 to 0.15625
- mixing_weight: float32 [2, 8, 8], replicated, may hold values from -1.5 to 1.5
- const_vector: bfloat16 [2, 2, 768], P(None, None, 'shard'), may hold values from -6 to 6
- const_weight: bfloat16 [2, 2, 768, 2], P(None, None, 'shard'), may hold values from -0.21875 to 0.21875
- gate_weight: bfloat16 [2, 4, 768, 2048], P(None, 'expert', 'shard'), may hold values from -0.21875 to 0.21875
- up_weight: bfloat16 [2, 4, 768, 2048], P(None, 'expert', 'shard'), may hold values from -0.21875 to 0.21875
- down_weight: bfloat16 [2, 4, 2048, 768], P(None, 'expert', 'shard'), may hold values from -0.75 to 0.75
- routes: int32 [2, 26624, 2], P(None, ('expert', 'shard')), may hold values from 0 to 7, all different within a row
- priority: int32 [32, 832], P(('expert', 'shard')), may hold values from 0 to 831, each once within a row
- leaf_parent: int32 [32, 8], P(('expert', 'shard')), may hold values from 0 to 3
- cotangent: bfloat16 [26624, 768], P(('expert', 'shard')), may hold values from -6 to 6
Outputs:
- hidden_out: bfloat16 [26624, 768], P(('expert', 'shard'))
- hidden_grad: float32 [26624, 768], P(('expert', 'shard'))
- prior_grad: float32 [26624, 8], P(('expert', 'shard'))
- project_grad: float32 [2, 3, 768, 768], P(None, None, 'shard')
- output_grad: float32 [2, 768, 768], P(None, 'shard')
- gain_grad: float32 [2, 2, 768], P(None, None, 'shard')
- router_grad: float32 [2, 768, 8], P(None, 'shard')
- mixing_grad: float32 [2, 8, 8], replicated
- vector_grad: float32 [2, 2, 768], P(None, None, 'shard')
- const_grad: float32 [2, 2, 768, 2], P(None, None, 'shard')
- gate_grad: float32 [2, 4, 768, 2048], P(None, 'expert', 'shard')
- up_grad: float32 [2, 4, 768, 2048], P(None, 'expert', 'shard')
- down_grad: float32 [2, 4, 2048, 768], P(None, 'expert', 'shard')
The draws below stay inside these ranges and needn't reach their ends.
Inputs may be any that keep to these rules, and one draw needn't show every extreme that they name: A token's 2 routes in a block name different experts. `priority`: each device's row is a permutation.
All inputs are finite; a program needn't handle non-finite values.
Results may differ from the reference program's by a relative error of at most 0.023.
Values may be sent and summed in bfloat16 or wider, within the bound.
A program may use at most 256 MiB of HBM per device.

```python
import jax
import jax.numpy as jnp
from jax import lax

D = 768
H = 12
HD = 64
FF = 2048
TOP = 2
LAYERS = 2
TRUNK = 320
BRANCH = 64
LEAF = 32
TREE = 832
TOK_DEV = 832
TREES = 32
TOKENS = 26624
FFN = 4
NE = 8
CAP = 234
N_EXPERT = 4
N_SHARD = 8


def place_ends(values, own_key, smallest, largest):
    longest = values.shape.index(max(values.shape))
    spots = []
    for shift in (0, 1):
        where = [jax.random.randint(jax.random.fold_in(own_key, axis), (), 0, length) for axis, length in enumerate(values.shape)]
        where[longest] = (where[longest] + shift) % values.shape[longest]
        spots.append(tuple(where))
    return values.at[spots[0]].set(smallest).at[spots[1]].set(largest)


def steps_of(rng, shape, shards, smallest, high):
    loudness = 1.0
    for dim, blocks in shards:
        heights = jax.random.uniform(jax.random.fold_in(jax.random.fold_in(rng, 6), dim), (blocks,), jnp.float32, smallest / len(shards), high / len(shards))
        loudness = loudness * jnp.repeat(jnp.exp(heights), shape[dim] // blocks).reshape((-1,) + (1,) * (len(shape) - 1 - dim))
    return loudness


def different_ones(key, rows, number_of, top, lift):
    sequence = jax.random.permutation(jax.random.fold_in(key, 1), number_of)
    boost = sequence
    for power in range(3):
        boost = boost * boost // number_of
    boost = boost * lift // number_of
    chance = jax.random.randint(jax.random.fold_in(key, 2), (rows, number_of), 0, 4096) + boost
    sure = jax.random.permutation(jax.random.fold_in(key, 3), rows)[jnp.arange(number_of) % rows]
    chance = jnp.where(jnp.arange(rows)[:, None] == sure[None, :], 1 << 14, chance)
    merit = chance * number_of + jnp.arange(number_of)
    return lax.top_k(merit.astype(jnp.int32), top)[1].astype(jnp.int32)


def scatter_about(own_key, extent, spread, bound, shards=(), kind=jnp.bfloat16):
    loudness = steps_of(own_key, extent, shards, -0.22, 0.18) if shards else 1.0
    entries = jax.random.normal(own_key, extent, jnp.float32) * spread * loudness
    return jnp.minimum(jnp.maximum(entries, -bound), bound).astype(kind)


def setup_inputs(seed: int = 0) -> dict:
    key_list = jax.random.split(jax.random.key(seed), 17)
    return {
        "hidden_in": scatter_about(key_list[0], (TOKENS, D), 1.0, 6.0, ((0, 32),)),
        "prior_logits": scatter_about(key_list[1], (TOKENS, NE), 0.5, 3.0, ((0, 32),), jnp.float32),
        "project_weight": scatter_about(key_list[2], (LAYERS, 3, D, D), D ** -0.5, 0.21875, ((2, 8),)),
        "output_weight": scatter_about(key_list[3], (LAYERS, D, D), (D // 64) ** -0.5, 1.75, ((1, 8),)),
        "norm_gain": jnp.clip(1.0 + 0.1 * jax.random.normal(key_list[4], (LAYERS, 2, D), jnp.float32), 0.5, 1.5).astype(jnp.bfloat16),
        "router_weight": scatter_about(key_list[5], (LAYERS, D, NE), (2 * D) ** -0.5, 0.15625, ((1, 8),)),
        "mixing_weight": scatter_about(key_list[6], (LAYERS, NE, NE), (2 * NE) ** -0.5, 1.5, (), jnp.float32),
        "const_vector": scatter_about(key_list[7], (LAYERS, 2, D), 1.0, 6.0, ((2, 8),)),
        "const_weight": scatter_about(key_list[8], (LAYERS, 2, D, 2), D ** -0.5, 0.21875, ((2, 8),)),
        "gate_weight": scatter_about(key_list[9], (LAYERS, FFN, D, FF), D ** -0.5, 0.21875, ((1, 4), (2, 8))),
        "up_weight": scatter_about(key_list[10], (LAYERS, FFN, D, FF), D ** -0.5, 0.21875, ((1, 4), (2, 8))),
        "down_weight": scatter_about(key_list[11], (LAYERS, FFN, FF, D), (FF // 32) ** -0.5, 0.75, ((1, 4), (2, 8))),
        "routes": different_ones(key_list[12], LAYERS * TOKENS, NE, TOP, 2048).reshape((LAYERS, TOKENS, TOP)),
        "priority": jax.vmap(lambda own: jax.random.permutation(own, TOK_DEV))(jax.random.split(key_list[13], (N_EXPERT * N_SHARD))).reshape((N_EXPERT * N_SHARD, TOK_DEV)).astype(jnp.int32),
        "leaf_parent": place_ends(jax.random.randint(key_list[14], (TREES, 8), 0, 4), jax.random.fold_in(key_list[14], 1), 0, 3).astype(jnp.int32),
        "cotangent": scatter_about(key_list[15], (TOKENS, D), 1.0, 6.0, ((0, 32),)),
    }


@jax.custom_vjp
def low(v):
    return lax.optimization_barrier(v.astype(jnp.bfloat16)).astype(jnp.float32)

@jax.custom_vjp
def low_back(v):
    return v

def low_keep(v):
    return (low(v), None)

def low_pass(kept, grad):
    return (grad,)

def back_keep(v):
    return (v, None)

def back_low(kept, grad):
    return (low(grad),)
low.defvjp(low_keep, low_pass)
low_back.defvjp(back_keep, back_low)
epsilon = 1e-06
highest = lax.Precision.HIGHEST
masked_fill = -1e+30

def rounded_both(values):
    return low(low_back(values))

def rmsnorm(values, gain):
    return values * lax.rsqrt(lax.optimization_barrier(jnp.mean(values * values, axis=-1, keepdims=True)) + epsilon) * gain

def softmax_rows(logits):
    peak_value = lax.optimization_barrier(jnp.max(logits, axis=-1, keepdims=True))
    exponent = jnp.exp(logits - peak_value)
    return exponent / lax.optimization_barrier(jnp.sum(exponent, axis=-1, keepdims=True))

def tree_visible(parents):
    position = jnp.arange(TREE, dtype=jnp.int32)
    offset = position - TRUNK
    segment = jnp.where(position < TRUNK, 0, jnp.where(offset < 4 * BRANCH, 1 + offset // BRANCH, 5 + (offset - 4 * BRANCH) // LEAF))
    leaf_hits = (segment[:, None] - 5 == jnp.arange(8, dtype=jnp.int32)[None, :]).astype(jnp.int32)
    upper = jnp.where(segment >= 5, 1 + lax.optimization_barrier(jnp.sum(leaf_hits * parents[None, :], axis=1)), 0)
    key_segment = segment[None, :]
    causal = position[None, :] <= position[:, None]
    return causal & ((key_segment == segment[:, None]) | (key_segment == 0) | (key_segment == upper[:, None]))

def side_experts(normed, gate_values, chosen, vectors, constants, experts_ffn):
    copy_share = lax.optimization_barrier(jnp.sum(gate_values * (chosen == experts_ffn + 1).astype(jnp.float32), axis=1))
    result = copy_share[:, None] * normed
    for const_index in range(2):
        share_const = lax.optimization_barrier(jnp.sum(gate_values * (chosen == experts_ffn + 2 + const_index).astype(jnp.float32), axis=1))
        mixture = softmax_rows(jnp.dot(normed, constants[const_index], precision=highest))
        result = result + share_const[:, None] * (mixture[:, 0:1] * normed + mixture[:, 1:2] * vectors[const_index][None, :])
    return result

def attend_tree(packed):
    queries, keys_tree, values_tree, parents = packed
    visible = tree_visible(parents)
    head_queries = queries.reshape(TREE, H, HD)
    head_keys = keys_tree.reshape(TREE, H, HD)
    head_values = values_tree.reshape(TREE, H, HD)
    raw_scores = jnp.einsum('ihd,jhd->hij', head_queries, head_keys, precision=highest) * HD ** (-0.5)
    scores = low_back(raw_scores)
    attention = softmax_rows(jnp.where(visible[None], scores, masked_fill))
    mixed = jnp.einsum('hij,jhd->ihd', low(attention), head_values, precision=highest)
    return mixed.reshape(TREE, D)

def expert_sum(normed, weights_ffn, gate_layer, up_layer, down_layer):

    def expert_step(running, packed):
        gate_one, up_one, down_one, weight_one = packed
        inputs = low_back(normed)
        gate_value = low_back(jnp.dot(inputs, gate_one, precision=highest))
        up_value = low_back(jnp.dot(inputs, up_one, precision=highest))
        hidden_act = low(jax.nn.silu(gate_value) * up_value)
        produced = rounded_both(jnp.dot(hidden_act, down_one, precision=highest))
        return (running + weight_one[:, None] * produced, None)
    total_out, unused_part = lax.scan(jax.checkpoint(expert_step), jnp.zeros_like(normed), (gate_layer, up_layer, down_layer, weights_ffn.T))
    return total_out

def device_kept(packed):
    chosen, ranking = packed
    labels = jnp.arange(FFN, dtype=jnp.int32)
    loaded = lax.optimization_barrier(jnp.sum((chosen[:, :, None] == labels[None, None, :]).astype(jnp.int32), axis=1))
    earlier = (ranking[None, :] < ranking[:, None]).astype(jnp.int32)
    ranked = jnp.dot(earlier, loaded)
    return (loaded * (ranked < CAP).astype(jnp.int32)).astype(jnp.float32)

def forward(hidden, prior, project, output, gains, router, mixing, vectors, constants, gate_all, up_all, down_all, routes, kept_all, leaf_parent):
    logits = prior
    labels = jnp.arange(NE, dtype=jnp.int32)
    for layer_index in range(LAYERS):
        normed = low(rmsnorm(hidden, gains[layer_index, 0]))
        projected = rounded_both(jnp.einsum('td,cde->cte', normed, project[layer_index], precision=highest))
        trees = projected.reshape(3, TREES, TREE, D)
        mixed = lax.map(jax.checkpoint(attend_tree), (trees[0], trees[1], trees[2], leaf_parent))
        attended = rounded_both(mixed.reshape(TOKENS, D))
        middle = hidden + low_back(jnp.dot(attended, output[layer_index], precision=highest))
        normed_mid = low(rmsnorm(middle, gains[layer_index, 1]))
        logits = jnp.dot(normed_mid, router[layer_index], precision=highest) + jnp.dot(logits, mixing[layer_index], precision=highest)
        chances = softmax_rows(logits)
        chosen = routes[layer_index]
        choose = (chosen[:, :, None] == labels[None, None, :]).astype(jnp.float32)
        gate_values = lax.optimization_barrier(jnp.sum(choose * chances[:, None, :], axis=2))
        weights_ffn = lax.optimization_barrier(jnp.sum(gate_values[:, :, None] * choose[:, :, :FFN], axis=1)) * kept_all[layer_index]
        routed = expert_sum(normed_mid, weights_ffn, gate_all[layer_index], up_all[layer_index], down_all[layer_index])
        hidden = middle + (routed + side_experts(normed_mid, gate_values, chosen, vectors[layer_index], constants[layer_index], FFN))
    return hidden

def reference(hidden_in, prior_logits, project_weight, output_weight, norm_gain, router_weight, mixing_weight, const_vector, const_weight, gate_weight, up_weight, down_weight, routes, priority, leaf_parent, cotangent):
    kept_list = []
    for layer_index in range(LAYERS):
        per_device = routes[layer_index].reshape(N_EXPERT * N_SHARD, TOK_DEV, TOP)
        kept_list.append(lax.map(device_kept, (per_device, priority)).reshape(TOKENS, FFN))
    kept_all = jnp.stack(kept_list)

    def run(hidden, prior, project, output, gains, router, mixing, vectors, constants, gate_all, up_all, down_all):
        return forward(hidden, prior, project, output, gains, router, mixing, vectors, constants, gate_all, up_all, down_all, routes, kept_all, leaf_parent)
    result, pullback = jax.vjp(run, hidden_in.astype(jnp.float32), prior_logits, project_weight.astype(jnp.float32), output_weight.astype(jnp.float32), norm_gain.astype(jnp.float32), router_weight.astype(jnp.float32), mixing_weight, const_vector.astype(jnp.float32), const_weight.astype(jnp.float32), gate_weight.astype(jnp.float32), up_weight.astype(jnp.float32), down_weight.astype(jnp.float32))
    grads = pullback(cotangent.astype(jnp.float32))
    return (result.astype(jnp.bfloat16), grads[0], grads[1], grads[2], grads[3], grads[4], grads[5], grads[6], grads[7], grads[8], grads[9], grads[10], grads[11])
```

```python
import functools

import jax
import jax.numpy as jnp
from jax import lax
from jax.experimental import pallas as pl
from jax.experimental.pallas import tpu as pltpu
from jax.sharding import PartitionSpec as P

D = 768
H = 12
HD = 64
TOP = 2
LAYERS = 2
TRUNK = 320
BRANCH = 64
LEAF = 32
TREE = 832

W_OUT = 3 * D
W_SMALL = 4 * D
W_ALL = 4 * D + 128
S_CONST = 16
S_GAIN = 24
S_VEC = 26

epsilon = 1e-06
masked_fill = -1e30
f32 = jnp.float32
bf16 = jnp.bfloat16
BLOCKS = 4
VMEM = 56 << 20


def dot(a, b):
    return jnp.dot(a, b, preferred_element_type=f32)


def dot_nt(a, b):
    return lax.dot_general(a, b, (((1,), (1,)), ((), ())), preferred_element_type=f32)


def dot_tn(a, b):
    return lax.dot_general(a, b, (((0,), (0,)), ((), ())), preferred_element_type=f32)


def split_bf16(v):
    high = v.astype(bf16)
    return high, (v - high.astype(f32)).astype(bf16)


def inv_rms(v):
    return lax.rsqrt(jnp.mean(v * v, axis=1, keepdims=True) + epsilon)


def tree_visible(parents):
    position = jnp.arange(TREE, dtype=jnp.int32)
    offset = position - TRUNK
    segment = jnp.where(
        position < TRUNK,
        0,
        jnp.where(offset < 4 * BRANCH, 1 + offset // BRANCH, 5 + (offset - 4 * BRANCH) // LEAF),
    )
    leaf_hits = (segment[:, None] - 5 == jnp.arange(8, dtype=jnp.int32)[None, :]).astype(jnp.int32)
    upper = jnp.where(segment >= 5, 1 + jnp.sum(leaf_hits * parents[None, :], axis=1), 0)
    key_segment = segment[None, :]
    causal = position[None, :] <= position[:, None]
    return causal & (
        (key_segment == segment[:, None]) | (key_segment == 0) | (key_segment == upper[:, None])
    )


def one_hot(slot_row, e, slots):
    row = lax.broadcasted_iota(jnp.int32, (slots, slot_row.shape[1]), 0).astype(f32)
    return jnp.where(row == slot_row[e : e + 1, :], 1.0, 0.0).astype(bf16)


def one_hot_col(slot_col, e, slots, scale=None):
    lane = lax.broadcasted_iota(jnp.int32, (slot_col.shape[0], slots), 1).astype(f32)
    value = 1.0 if scale is None else scale
    return jnp.where(lane == slot_col[:, e : e + 1], value, 0.0).astype(bf16)


def combine_rows(rows, middle_ref, n2_ref, y_ref, gcol_ref, slotc_ref, vectors, experts, slots):
    gcol = gcol_ref[rows, :]
    slot = slotc_ref[rows, :]
    total = middle_ref[rows, :] + gcol[:, 16:17] * n2_ref[rows, :].astype(f32)
    for c in range(2):
        total = total + gcol[:, 17 + c : 18 + c] * vectors[c : c + 1, :]
    for e in range(experts):
        weight = one_hot_col(slot, e, slots, gcol[:, e : e + 1])
        total = total + dot(weight, y_ref[e * slots : (e + 1) * slots, :])
    return total


def send_grads(slot_row, gx, gpack, gxs_ref, gy_ref, experts, slots):
    for e in range(experts):
        hot = one_hot(slot_row, e, slots)
        rows = slice(e * slots, (e + 1) * slots)
        got = dot(hot, gx)
        gates = dot(hot, gpack)
        gxs_ref[rows, :] = got.astype(bf16)
        gy_ref[rows, :] = (got * (gates[:, e : e + 1] + gates[:, 64 + e : 65 + e])).astype(bf16)


def row_blocks(tokens):
    size = tokens // BLOCKS
    return size, lambda i: pl.ds(pl.multiple_of(i * size, 16), size)


def causal_spans(tokens):
    edges = [0, 384, 640, tokens]
    return list(zip(edges[:-1], edges[1:]))


def forward_kernel(first, last, experts, slots, *refs):
    refs = list(refs)
    if first:
        x_in = refs.pop(0)
    else:
        mid_prev, n2_prev, y_ref, gcol_prev, slotc_prev, w_prev = [refs.pop(0) for _ in range(6)]
    w_ref, bias_ref, z_ref, mixt_ref, chosen_ref, slotr_ref = [refs.pop(0) for _ in range(6)]
    if last:
        cot_ref = refs.pop(0)
    if not first:
        x_out = refs.pop(0)
    n1_ref, qkv_ref, att_ref, lse_ref, mid_ref, n2_ref, info_ref, gcol_ref, gpack_ref, send_ref = [
        refs.pop(0) for _ in range(10)
    ]
    if last:
        gxs_ref, gy_ref = refs.pop(0), refs.pop(0)
    lse_cols, turn = refs
    tokens = n1_ref.shape[0]
    size, block = row_blocks(tokens)
    small = w_ref[:, W_SMALL:].astype(f32).T
    gain0 = small[S_GAIN : S_GAIN + 1, :]
    gain1 = small[S_GAIN + 1 : S_GAIN + 2, :]
    if not first:
        vectors_prev = w_prev[...].astype(f32).T[S_VEC : S_VEC + 2, :]

    def project(i, carry):
        rows = block(i)
        if first:
            x = x_in[rows, :].astype(f32)
        else:
            x = combine_rows(
                rows, mid_prev, n2_prev, y_ref, gcol_prev, slotc_prev, vectors_prev, experts, slots
            )
            x_out[rows, :] = x
        n1 = (x * inv_rms(x) * gain0).astype(bf16)
        n1_ref[rows, :] = n1
        for c in range(3):
            qkv_ref[rows, c * D : (c + 1) * D] = dot(n1, w_ref[:, c * D : (c + 1) * D]).astype(bf16)
        return carry

    lax.fori_loop(0, BLOCKS, project, 0)
    lane = lax.broadcasted_iota(jnp.int32, (1, 128), 1)
    low_f = jnp.where(lane < HD, 1.0, 0.0)
    low = low_f.astype(bf16)
    high = (1.0 - low_f).astype(bf16)
    lse_cols[...] = jnp.zeros_like(lse_cols)

    def pair(p, carry):
        k = qkv_ref[:, pl.ds(pl.multiple_of(D + p * 128, 128), 128)]
        v = qkv_ref[:, pl.ds(pl.multiple_of(2 * D + p * 128, 128), 128)]
        va = v * low + high
        vb = v * high + low
        here = pl.ds(pl.multiple_of(p * 128, 128), 128)
        for start, stop in causal_spans(tokens):
            q = qkv_ref[start:stop, here] * bf16(HD**-0.5)
            outs = []
            for mask, value in ((low, va), (high, vb)):
                s = dot_nt(q * mask, k[:stop]) + bias_ref[start:stop, :stop]
                peak = jnp.max(s, axis=1, keepdims=True)
                expo = jnp.exp(s - peak).astype(bf16)
                outs.append((dot(expo, value[:stop]), peak))
            (oa, ma), (ob, mb) = outs
            numer = jnp.where(lane < HD, oa, ob)
            denom = pltpu.roll(jnp.where(lane < HD, ob, oa), HD, 1)
            att_ref[start:stop, here] = (numer / denom).astype(bf16)
            la = ma + jnp.log(oa[:, HD : HD + 1])
            lb = mb + jnp.log(ob[:, 0:1])
            old = lse_cols[start:stop, :]
            lse_cols[start:stop, :] = jnp.where(
                lane == 2 * p, la, jnp.where(lane == 2 * p + 1, lb, old)
            )
        return carry

    lax.fori_loop(0, H // 2, pair, 0)
    lse_ref[...] = lse_cols[...].T[0:16, :]

    def finish(i, carry):
        rows = block(i)
        if first:
            x = x_in[rows, :].astype(f32)
        else:
            x = x_out[rows, :]
        middle = x + dot(att_ref[rows, :], w_ref[:, W_OUT:W_SMALL])
        mid_ref[rows, :] = middle
        n2_ref[rows, :] = (middle * inv_rms(middle) * gain1).astype(bf16)
        return carry

    lax.fori_loop(0, BLOCKS, finish, 0)
    n2 = n2_ref[...]
    scores = dot_nt(small[0:32, :].astype(bf16), n2)
    logits = scores[0:16, :]
    z = z_ref[...]
    mixt = mixt_ref[...]
    for i in range(experts + 4):
        logits = logits + mixt[:, i : i + 1] * z[i : i + 1, :]
    row = lax.broadcasted_iota(jnp.int32, (16, tokens), 0)
    valid = row < experts + 4
    peak = jnp.max(jnp.where(valid, logits, masked_fill), axis=0, keepdims=True)
    expo = jnp.where(valid, jnp.exp(jnp.minimum(logits - peak, 0.0)), 0.0)
    prob = expo / jnp.sum(expo, axis=0, keepdims=True)
    gates = prob * chosen_ref[...]
    info_ref[0:16, :] = logits
    info_ref[16:32, :] = prob
    turn[...] = jnp.zeros_like(turn)
    turn[0:16, 0:tokens] = gates
    own = gates[experts + 1 : experts + 2, :]
    alphas = []
    for c in range(2):
        l0 = scores[S_CONST + 2 * c : S_CONST + 2 * c + 1, :]
        l1 = scores[S_CONST + 2 * c + 1 : S_CONST + 2 * c + 2, :]
        a0 = jax.nn.sigmoid(l0 - l1)
        a1 = jax.nn.sigmoid(l1 - l0)
        alphas += [a0, a1]
        share = gates[experts + 2 + c : experts + 3 + c, :]
        own = own + share * a0
        turn[17 + c : 18 + c, 0:tokens] = share * a1
    turn[16:17, 0:tokens] = own
    zero_row = jnp.zeros((4, tokens), f32)
    info_ref[32:40, :] = jnp.concatenate(alphas + [zero_row], axis=0)
    gcol = turn[...].T[0:tokens, :]
    gcol_ref[...] = gcol
    upper, lower = split_bf16(jnp.where(lane < 16, gcol, 0.0))
    gpack = upper + pltpu.roll(lower.astype(f32), 64, 1).astype(bf16)
    gpack_ref[...] = gpack
    slot_row = slotr_ref[...]
    for e in range(experts):
        hot = one_hot(slot_row, e, slots)
        rows = slice(e * slots, (e + 1) * slots)
        send_ref[rows, :] = dot(hot, n2).astype(bf16)
    if last:
        send_grads(slot_row, cot_ref[...], gpack, gxs_ref, gy_ref, experts, slots)


def shape(dims, dtype=f32):
    return jax.ShapeDtypeStruct(tuple(dims), dtype)


def whole_call(body, name, outs, scratch, args, flops):
    moved = sum(a.size * a.dtype.itemsize for a in args) + sum(
        o.size * o.dtype.itemsize for o in outs
    )
    return pl.pallas_call(
        body,
        out_shape=outs,
        in_specs=[pl.BlockSpec(memory_space=pltpu.VMEM)] * len(args),
        out_specs=[pl.BlockSpec(memory_space=pltpu.VMEM)] * len(outs),
        scratch_shapes=scratch,
        compiler_params=pltpu.CompilerParams(vmem_limit_bytes=VMEM),
        cost_estimate=pl.CostEstimate(flops=flops, bytes_accessed=moved, transcendentals=0),
        name=name,
    )(*args)


def forward_call(first, last, experts, slots, args):
    tokens = TREE
    sent = experts * slots
    outs = [] if first else [shape((tokens, D))]
    outs += [
        shape((tokens, D), bf16),
        shape((tokens, 3 * D), bf16),
        shape((tokens, D), bf16),
        shape((16, tokens)),
        shape((tokens, D)),
        shape((tokens, D), bf16),
        shape((40, tokens)),
        shape((tokens, 128)),
        shape((tokens, 128), bf16),
        shape((sent, D), bf16),
    ]
    if last:
        outs += [shape((sent, D), bf16), shape((sent, D), bf16)]
    padded = -(-tokens // 128) * 128
    scratch = [pltpu.VMEM((tokens, 128), f32), pltpu.VMEM((128, padded), f32)]
    body = functools.partial(forward_kernel, first, last, experts, slots)
    return whole_call(body, "block_forward", outs, scratch, args, 20 * 10**9)


def gating_kernel(last, experts, slots, *refs):
    refs = list(refs)
    gx_ref, n2_ref, y_ref, gxs_ref, slotr_ref, info_ref, chosen_ref, gcol_ref, small_ref = [
        refs.pop(0) for _ in range(9)
    ]
    z_ref, mix_ref = refs.pop(0), refs.pop(0)
    if last:
        mid_ref, slotc_ref = refs.pop(0), refs.pop(0)
    else:
        gz_ref = refs.pop(0)
    gn2_ref, gsm_ref, gmix_ref, gprev_ref = [refs.pop(0) for _ in range(4)]
    if last:
        out_ref = refs.pop(0)
    tokens = n2_ref.shape[0]
    size, block = row_blocks(tokens)
    small = small_ref[...].astype(f32).T
    small_half = small[0:32, :].astype(bf16)
    vectors = small[S_VEC : S_VEC + 2, :]
    slot_row = slotr_ref[...]
    ones = jnp.ones((16, D), bf16)
    row = lax.broadcasted_iota(jnp.int32, (16, slots), 0)
    scattered = jnp.zeros((16, tokens), f32)
    for e in range(experts):
        rows = slice(e * slots, (e + 1) * slots)
        inner = y_ref[rows, :].astype(f32) * gxs_ref[rows, :].astype(f32)
        upper, lower = split_bf16(inner)
        sums = dot_nt(ones, upper) + dot_nt(ones, lower)
        upper, lower = split_bf16(sums)
        lhs = jnp.where(row == e, upper.astype(f32), 0.0) + jnp.where(
            row == 8 + e, lower.astype(f32), 0.0
        )
        scattered = scattered + dot(lhs.astype(bf16), one_hot(slot_row, e, slots))
    gx = gx_ref[...].astype(f32)
    gx_half = gx.astype(bf16)
    n2 = n2_ref[...]
    upper, lower = split_bf16(gx * n2.astype(f32))
    gx_n2 = (dot_nt(ones, upper) + dot_nt(ones, lower))[0:1, :]
    gx_small = dot_nt(small_half, gx_half)
    prob = info_ref[16:32, :]
    chosen = chosen_ref[...]
    gates = prob * chosen
    trow = lax.broadcasted_iota(jnp.int32, (16, tokens), 0)
    gp = jnp.concatenate([scattered[0:8, :] + scattered[8:16, :], jnp.zeros((8, tokens), f32)], 0)
    gp = jnp.where(trow == experts + 1, gx_n2, jnp.where(trow < experts, gp, 0.0))
    crow = lax.broadcasted_iota(jnp.int32, (8, tokens), 0)
    glog = jnp.zeros((8, tokens), f32)
    coefs = jnp.zeros((8, tokens), f32)
    for c in range(2):
        a0 = info_ref[32 + 2 * c : 33 + 2 * c, :]
        a1 = info_ref[33 + 2 * c : 34 + 2 * c, :]
        gx_v = gx_small[S_VEC + c : S_VEC + c + 1, :]
        share = gates[experts + 2 + c : experts + 3 + c, :]
        gp = jnp.where(trow == experts + 2 + c, a0 * gx_n2 + a1 * gx_v, gp)
        gl = share * (gx_n2 - gx_v) * a0 * a1
        glog = jnp.where(crow == 2 * c, gl, jnp.where(crow == 2 * c + 1, -gl, glog))
        coefs = jnp.where(crow == c, share * a1, coefs)
    gp = gp * chosen
    gz = prob * (gp - jnp.sum(prob * gp, axis=0, keepdims=True))
    if not last:
        gz = gz + gz_ref[...]
    z = z_ref[...]
    gmix_ref[...] = lax.dot_general(
        z, gz, (((1,), (1,)), ((), ())), precision=lax.Precision.HIGHEST, preferred_element_type=f32
    )
    mix = mix_ref[...]
    gprev = jnp.zeros((16, tokens), f32)
    for o in range(experts + 4):
        gprev = gprev + mix[:, o : o + 1] * gz[o : o + 1, :]
    gprev_ref[...] = gprev
    allg = jnp.concatenate([gz, glog, jnp.zeros((8, tokens), f32)], axis=0)
    upper, lower = split_bf16(allg)
    gsm = dot(upper, n2) + dot(lower, n2)
    cu, cl = split_bf16(jnp.concatenate([coefs, jnp.zeros((8, tokens), f32)], axis=0))
    gvec = dot(cu, gx_half) + dot(cl, gx_half)
    gsm_ref[0:24, :] = gsm[0:24, :]
    gsm_ref[24:32, :] = jnp.concatenate(
        [jnp.zeros((2, D), f32), gvec[0:2, :], jnp.zeros((4, D), f32)], axis=0
    )
    both = jnp.concatenate([upper, lower], axis=0)
    twice = jnp.concatenate([small_half, small_half], axis=0)
    gn2_ref[...] = dot_tn(both, twice)

    def add(i, carry):
        rows = block(i)
        gn2_ref[rows, :] = gn2_ref[rows, :] + gcol_ref[rows, 16:17] * gx_ref[rows, :].astype(f32)
        if last:
            out_ref[rows, :] = combine_rows(
                rows, mid_ref, n2_ref, y_ref, gcol_ref, slotc_ref, vectors, experts, slots
            ).astype(bf16)
        return carry

    lax.fori_loop(0, BLOCKS, add, 0)


def gating_call(last, experts, slots, args):
    tokens = TREE
    outs = [shape((tokens, D)), shape((32, D)), shape((16, 16)), shape((16, tokens))]
    if last:
        outs += [shape((tokens, D), bf16)]
    body = functools.partial(gating_kernel, last, experts, slots)
    return whole_call(body, "gating_backward", outs, [], args, 5 * 10**9)


def backward_kernel(first, experts, slots, *refs):
    refs = list(refs)
    gx_ref, gn2p_ref, gn2e_ref, slotc_ref, mid_ref, att_ref, w_ref, qkv_ref, n1_ref, x_ref = [
        refs.pop(0) for _ in range(10)
    ]
    biast_ref, lse_ref, gsm_ref = [refs.pop(0) for _ in range(3)]
    if not first:
        slotr_ref, gpack_ref = refs.pop(0), refs.pop(0)
    gout_ref, dw_ref = refs.pop(0), refs.pop(0)
    if not first:
        gxs_ref, gy_ref = refs.pop(0), refs.pop(0)
    gatt, go, gqkv, turn = refs
    tokens = n1_ref.shape[0]
    size, block = row_blocks(tokens)
    small = w_ref[:, W_SMALL:].astype(f32).T
    gain0 = small[S_GAIN : S_GAIN + 1, :]
    gain1 = small[S_GAIN + 1 : S_GAIN + 2, :]

    def enter(i, total):
        rows = block(i)
        gn2 = gn2p_ref[rows, :]
        slot = slotc_ref[rows, :]
        for e in range(experts):
            gn2 = gn2 + dot(one_hot_col(slot, e, slots), gn2e_ref[e * slots : (e + 1) * slots, :])
        middle = mid_ref[rows, :]
        r = inv_rms(middle)
        scaled = gain1 * gn2
        inner = jnp.mean(middle * scaled, axis=1, keepdims=True)
        gmid = gx_ref[rows, :].astype(f32) + r * scaled - middle * (r * r * r * inner)
        gout_ref[rows, :] = gmid
        half = gmid.astype(bf16)
        gatt[rows, :] = half
        go[rows, :] = dot_nt(half, w_ref[:, W_OUT:W_SMALL]).astype(bf16)
        return total + jnp.sum(gn2 * middle * r, axis=0, keepdims=True)

    ggain1 = lax.fori_loop(0, BLOCKS, enter, jnp.zeros((1, D), f32))
    lane = lax.broadcasted_iota(jnp.int32, (1, 128), 1)
    low_f = jnp.where(lane < HD, 1.0, 0.0)
    low = low_f.astype(bf16)
    high = (1.0 - low_f).astype(bf16)
    scale = HD**-0.5

    def out_grad(p, carry):
        here = pl.ds(pl.multiple_of(p * 128, 128), 128)
        dw_ref[here, W_OUT:W_SMALL] = dot_tn(att_ref[:, here], gatt[...]).astype(bf16)
        return carry

    lax.fori_loop(0, D // 128, out_grad, 0)
    spans = causal_spans(tokens)

    def pair(p, carry):
        here = pl.ds(pl.multiple_of(p * 128, 128), 128)
        lanes_k = pl.ds(pl.multiple_of(D + p * 128, 128), 128)
        lanes_v = pl.ds(pl.multiple_of(2 * D + p * 128, 128), 128)
        q = qkv_ref[:, here] * bf16(scale)
        k = qkv_ref[:, lanes_k]
        v = qkv_ref[:, lanes_v]
        g = go[:, here]
        turn[0:tokens, :] = g.astype(f32) * att_ref[:, here].astype(f32)
        inner = turn[...].T[:, 0:tokens]
        turn[0:tokens, :] = k.astype(f32)
        kt = turn[...].T[:, 0:tokens].astype(bf16)
        gq_t = []
        gk = [0.0] * len(spans)
        gv = [0.0] * len(spans)
        for h, mask in ((0, low), (1, high)):
            qh = q * mask
            gh = g * mask
            dsum = jnp.sum(inner[h * HD : (h + 1) * HD, :], axis=0, keepdims=True)
            lse = lse_ref[pl.ds(2 * p + h, 1), :]
            gq_h = []
            for n, (start, stop) in enumerate(spans):
                st = dot_nt(k[start:stop], qh[start:]) + biast_ref[start:stop, start:]
                pt = jnp.exp(st - lse[:, start:])
                gpt = dot_nt(v[start:stop], gh[start:])
                gst = (pt * (gpt - dsum[:, start:])).astype(bf16)
                gv[n] = gv[n] + dot(pt.astype(bf16), gh[start:])
                gk[n] = gk[n] + dot(gst, qh[start:])
                part = dot(kt[h * HD : (h + 1) * HD, start:stop], gst)
                gq_h.append(part)
            cols = []
            for n, (start, stop) in enumerate(spans):
                piece = 0.0
                for m in range(n + 1):
                    origin = spans[m][0]
                    piece = piece + gq_h[m][:, start - origin : stop - origin]
                cols.append(piece)
            gq_t.append(jnp.concatenate(cols, axis=1))
        turn_t = jnp.concatenate(gq_t, axis=0) * scale
        pad = turn.shape[0] - tokens
        turn_t = jnp.concatenate([turn_t, jnp.zeros((128, pad), f32)], axis=1)
        gqkv[:, here] = turn_t.T[0:tokens, :].astype(bf16)
        for n, (start, stop) in enumerate(spans):
            gqkv[start:stop, lanes_k] = gk[n].astype(bf16)
            gqkv[start:stop, lanes_v] = gv[n].astype(bf16)
        return carry

    turn[...] = jnp.zeros_like(turn)
    lax.fori_loop(0, H // 2, pair, 0)

    def in_grad(p, carry):
        here = pl.ds(pl.multiple_of(p * 128, 128), 128)
        dw_ref[here, 0:W_OUT] = dot_tn(n1_ref[:, here], gqkv[...]).astype(bf16)
        return carry

    lax.fori_loop(0, D // 128, in_grad, 0)

    def leave(i, total):
        rows = block(i)
        gn1 = dot_nt(gqkv[rows, :], w_ref[:, 0:W_OUT])
        x = x_ref[rows, :].astype(f32)
        r = inv_rms(x)
        scaled = gain0 * gn1
        inner = jnp.mean(x * scaled, axis=1, keepdims=True)
        gx = gout_ref[rows, :] + r * scaled - x * (r * r * r * inner)
        gout_ref[rows, :] = gx
        gatt[rows, :] = gx.astype(bf16)
        return total + jnp.sum(gn1 * x * r, axis=0, keepdims=True)

    ggain0 = lax.fori_loop(0, BLOCKS, leave, jnp.zeros((1, D), f32))
    rows = jnp.concatenate(
        [gsm_ref[0:24, :], ggain0, ggain1, gsm_ref[26:32, :], jnp.zeros((96, D), f32)], axis=0
    )
    dw_ref[:, W_SMALL:] = rows.T.astype(bf16)
    if not first:
        send_grads(slotr_ref[...], gatt[...], gpack_ref[...], gxs_ref, gy_ref, experts, slots)


def backward_call(first, experts, slots, args):
    tokens = TREE
    sent = experts * slots
    outs = [shape((tokens, D)), shape((D, W_ALL), bf16)]
    if not first:
        outs += [shape((sent, D), bf16), shape((sent, D), bf16)]
    padded = -(-tokens // 128) * 128
    scratch = [
        pltpu.VMEM((tokens, D), bf16),
        pltpu.VMEM((tokens, D), bf16),
        pltpu.VMEM((tokens, 3 * D), bf16),
        pltpu.VMEM((padded, 128), f32),
    ]
    body = functools.partial(backward_kernel, first, experts, slots)
    return whole_call(body, "block_backward", outs, scratch, args, 40 * 10**9)


class Packing:
    def __init__(self, shards, part, ff):
        self.shards, self.part, self.ff = shards, part, ff
        self.padded = -(-part // 16) * 16
        self.chunks = ff // 256
        self.own = ff // shards
        self.down = 2 * self.chunks * self.padded
        self.rows = self.down + (D // 256) * self.own
        self.group = 2 * 256 // self.own

    def pack(self, gate, up, down):
        pieces = []
        for wide in (gate, up):
            cut = wide.reshape(self.part, self.chunks, 256).transpose(1, 0, 2)
            cut = jnp.pad(cut, [(0, 0), (0, self.padded - self.part), (0, 0)])
            pieces.append(cut.reshape(self.chunks * self.padded, 256))
        pieces.append(
            down.reshape(self.own, D // 256, 256).transpose(1, 0, 2).reshape(-1, 256)
        )
        return jnp.concatenate(pieces, axis=0)

    def unpack(self, packed):
        wide = []
        for n in range(2):
            cut = packed[n * self.chunks * self.padded : (n + 1) * self.chunks * self.padded]
            cut = cut.reshape(self.chunks, self.padded, 256)[:, : self.part]
            wide.append(cut.transpose(1, 0, 2).reshape(self.part, self.ff))
        down = packed[self.down :].reshape(D // 256, self.own, 256)
        return wide[0], wide[1], down.transpose(1, 0, 2).reshape(self.own, D)

    def specs(self):
        two = self.shards, 2 * self.padded, 256
        steps = self.chunks // 2
        wide = [pl.BlockSpec(two, lambda j, n=n: (0, n * steps + j, 0)) for n in range(2)]
        base = self.down // self.own
        tall = [
            pl.BlockSpec((self.group, self.own, 256), lambda j, c=c: (j, base + c, 0))
            for c in range(D // 256)
        ]
        return wide + tall

    def wide_part(self, ref, i):
        at = i * self.padded
        return ref[:, at : at + self.part, :].reshape(D, 256)

    def tall_part(self, refs):
        return jnp.concatenate([ref[...].reshape(512, 256) for ref in refs], axis=1)


def accumulate(total, part, out_ref):
    j = pl.program_id(0)

    @pl.when(j == 0)
    def _():
        total[...] = part

    @pl.when(j > 0)
    def _():
        total[...] = total[...] + part

    @pl.when(j == pl.num_programs(0) - 1)
    def _():
        out_ref[...] = total[...].astype(bf16)


def ffn_forward_kernel(pack, r_ref, g_w, u_w, d0, d1, d2, y_ref, gu_ref, uv_ref, total):
    r = r_ref[...]
    hids = []
    for i in range(2):
        lanes = slice(i * 256, (i + 1) * 256)
        gate = dot(r, pack.wide_part(g_w, i))
        up = dot(r, pack.wide_part(u_w, i))
        gu_ref[:, lanes] = gate.astype(bf16)
        uv_ref[:, lanes] = up.astype(bf16)
        hids.append((gate * jax.nn.sigmoid(gate) * up).astype(bf16))
    hid = jnp.concatenate(hids, axis=1)
    accumulate(total, dot(hid, pack.tall_part((d0, d1, d2))), y_ref)


def ffn_call(body, name, pack, count, flat, wide, with_weights, outs, out_specs, scratch, args):
    ff = pack.ff
    in_specs = [pl.BlockSpec((count, D), lambda j: (0, 0))] * flat
    in_specs += [pl.BlockSpec((count, 512), lambda j: (0, j))] * wide
    if with_weights:
        in_specs += pack.specs()
        args = list(args) + [args[-1]] * 4
    return pl.pallas_call(
        functools.partial(body, pack),
        grid=(ff // 512,),
        out_shape=outs,
        in_specs=in_specs,
        out_specs=out_specs,
        scratch_shapes=scratch,
        compiler_params=pltpu.CompilerParams(vmem_limit_bytes=VMEM),
        cost_estimate=pl.CostEstimate(
            flops=6 * count * D * ff, bytes_accessed=6 * D * ff + 8 * count * ff, transcendentals=0
        ),
        name=name,
    )(*args)


def ffn_forward(pack, rows, weights):
    count, ff = rows.shape[0], pack.ff
    flat = pl.BlockSpec((count, D), lambda j: (0, 0))
    wide = pl.BlockSpec((count, 512), lambda j: (0, j))
    outs = [shape((count, D), bf16), shape((count, ff), bf16), shape((count, ff), bf16)]
    scratch = [pltpu.VMEM((count, D), f32)]
    return ffn_call(
        ffn_forward_kernel, "ffn_forward", pack, count, 1, 0, True, outs, [flat, wide, wide],
        scratch, [rows, weights],
    )


def ffn_input_kernel(
    pack, gy_ref, gu_ref, uv_ref, g_w, u_w, d0, d1, d2, gin_ref, hid_ref, ggu_ref, guv_ref, total
):
    ghid_all = dot_nt(gy_ref[...], pack.tall_part((d0, d1, d2)))
    part = 0.0
    for i in range(2):
        lanes = slice(i * 256, (i + 1) * 256)
        ghid = ghid_all[:, lanes]
        gate = gu_ref[:, lanes].astype(f32)
        up = uv_ref[:, lanes].astype(f32)
        s = jax.nn.sigmoid(gate)
        act = gate * s
        hid_ref[:, lanes] = (act * up).astype(bf16)
        guv = (ghid * act).astype(bf16)
        ggu = (ghid * up * (s * (1.0 + gate * (1.0 - s)))).astype(bf16)
        ggu_ref[:, lanes] = ggu
        guv_ref[:, lanes] = guv
        part = part + dot_nt(ggu, pack.wide_part(g_w, i)) + dot_nt(guv, pack.wide_part(u_w, i))
    accumulate(total, part, gin_ref)


def ffn_input_grad(pack, gy, gate, up, weights):
    count, ff = gy.shape[0], pack.ff
    flat = pl.BlockSpec((count, D), lambda j: (0, 0))
    wide = pl.BlockSpec((count, 512), lambda j: (0, j))
    outs = [shape((count, D), bf16)] + [shape((count, ff), bf16)] * 3
    scratch = [pltpu.VMEM((count, D), f32)]
    return ffn_call(
        ffn_input_kernel, "ffn_input_grad", pack, count, 1, 2, True, outs,
        [flat, wide, wide, wide], scratch, [gy, gate, up, weights],
    )


def ffn_weight_kernel(pack, r_ref, gy_ref, hid_ref, ggu_ref, guv_ref, out_ref, rt):
    j = pl.program_id(0)

    @pl.when(j == 0)
    def _():
        rt[...] = r_ref[...].T
        if pack.padded != pack.part:
            out_ref[...] = jnp.zeros_like(out_ref)

    for n, ref in enumerate((ggu_ref, guv_ref)):
        for i in range(2):
            grad = dot(rt[...], ref[:, i * 256 : (i + 1) * 256]).astype(bf16)
            at = (n * pack.chunks + i) * pack.padded + j * (2 * pack.padded)
            at = pl.multiple_of(at, 16)
            out_ref[:, pl.ds(at, pack.part), :] = grad.reshape(pack.shards, pack.part, 256)
    grad = dot_tn(hid_ref[...], gy_ref[...]).astype(bf16)
    for c in range(D // 256):
        at = pack.down + c * pack.own
        out_ref[pl.ds(j * pack.group, pack.group), at : at + pack.own, :] = grad[
            :, c * 256 : (c + 1) * 256
        ].reshape(pack.group, pack.own, 256)


def ffn_weight_grad(pack, rows, gy, hid, ggu, guv):
    count = rows.shape[0]
    outs = shape((pack.shards, pack.rows, 256), bf16)
    spec = pl.BlockSpec(outs.shape, lambda j: (0, 0, 0))
    return ffn_call(
        ffn_weight_kernel, "ffn_weight_grad", pack, count, 2, 3, False, outs, spec,
        [pltpu.VMEM((D, count), bf16)], [rows, gy, hid, ggu, guv],
    )


def to_owner(rows, owners):
    slots = rows.shape[0] // owners
    return lax.all_to_all(
        rows.reshape(owners, slots, D), "expert", split_axis=0, concat_axis=0, tiled=True
    ).reshape(owners * slots, D)


def on_device(
    hidden_in,
    prior_logits,
    project_weight,
    output_weight,
    norm_gain,
    router_weight,
    mixing_weight,
    const_vector,
    const_weight,
    gate_weight,
    up_weight,
    down_weight,
    routes,
    priority,
    leaf_parent,
    cotangent,
):
    experts = lax.axis_size("expert")
    total_experts = experts + 4
    tokens = hidden_in.shape[0]
    capacity = 9 * tokens * TOP // (8 * total_experts)
    slots = -(-capacity // 16) * 16
    part = project_weight.shape[2]

    def pad_cols(a, width):
        return jnp.pad(a, [(0, 0)] * (a.ndim - 1) + [(0, width - a.shape[-1])])

    dense = []
    experts_w = []
    pack = Packing(lax.axis_size("shard"), part, gate_weight.shape[3])
    for l in range(LAYERS):
        small = jnp.concatenate(
            [
                pad_cols(router_weight[l], S_CONST),
                const_weight[l, 0],
                const_weight[l, 1],
                jnp.zeros((part, S_GAIN - S_CONST - 4), bf16),
                norm_gain[l].T,
                const_vector[l].T,
            ],
            axis=1,
        )
        packed = jnp.concatenate(
            [project_weight[l, c] for c in range(3)] + [output_weight[l], pad_cols(small, 128)],
            axis=1,
        )
        dense.append(lax.all_gather(packed, "shard", axis=0, tiled=True))
        mine = pack.pack(gate_weight[l, 0], up_weight[l, 0], down_weight[l, 0])
        experts_w.append(lax.all_gather(mine, "shard", axis=0, tiled=False))

    ranking = priority[0]
    earlier = (ranking[None, :] < ranking[:, None]).astype(bf16)
    labels = jnp.arange(total_experts, dtype=jnp.int32)
    hits = jnp.sum((routes[:, :, :, None] == labels).astype(f32), axis=2)
    chosen_rows = [jnp.pad(hits[l].T, [(0, 16 - total_experts), (0, 0)]) for l in range(LAYERS)]
    loaded = jnp.concatenate([hits[l, :, :experts] for l in range(LAYERS)], axis=1)
    loaded_half = loaded.astype(bf16)
    rank_col = dot(earlier, loaded_half)
    rank_row = lax.dot_general(
        loaded_half, earlier, (((0,), (1,)), ((), ())), preferred_element_type=f32
    )
    slot_col_all = jnp.where((loaded > 0) & (rank_col < capacity), rank_col, -1.0)
    slot_row_all = jnp.where((loaded.T > 0) & (rank_row < capacity), rank_row, -1.0)
    slot_col = [slot_col_all[:, l * experts : (l + 1) * experts] for l in range(LAYERS)]
    slot_row = [
        jnp.pad(
            slot_row_all[l * experts : (l + 1) * experts],
            [(0, 8 - experts), (0, 0)],
            constant_values=-1.0,
        )
        for l in range(LAYERS)
    ]
    visible = tree_visible(leaf_parent[0])
    bias = jnp.where(visible, 0.0, masked_fill)
    bias_t = jnp.where(visible.T, 0.0, masked_fill)
    mixes = [
        jnp.pad(mixing_weight[l], [(0, 16 - total_experts), (0, 16 - total_experts)])
        for l in range(LAYERS)
    ]
    z_rows = jnp.pad(prior_logits.T, [(0, 16 - total_experts), (0, 0)])

    saved = []
    front = [hidden_in]
    x_now = hidden_in
    for l in range(LAYERS):
        last = l == LAYERS - 1
        args = front + [dense[l], bias, z_rows, mixes[l].T, chosen_rows[l], slot_row[l]]
        if last:
            args.append(cotangent)
        outs = list(forward_call(l == 0, last, experts, slots, args))
        if l > 0:
            x_now = outs.pop(0)
        n1, qkv, att, lse, middle, n2, info, gcol, gpack, send = outs[:10]
        received = to_owner(send, experts)
        keep = dict(
            x=x_now, n1=n1, qkv=qkv, att=att, lse=lse, middle=middle, n2=n2, info=info,
            gcol=gcol, gpack=gpack, received=received, z=z_rows,
        )
        if last:
            keep["gxs"] = outs[10]
            keep["gy"] = to_owner(outs[11], experts)
        produced, keep["gate"], keep["up"] = ffn_forward(pack, received, experts_w[l])
        keep["y"] = to_owner(produced, experts)
        front = [middle, n2, keep["y"], gcol, slot_col[l], dense[l][:, W_SMALL:]]
        z_rows = info[0:16]
        saved.append(keep)

    gx = cotangent
    gz = None
    dense_grads = [None] * LAYERS
    expert_grads = [None] * LAYERS
    mix_grads = [None] * LAYERS
    hidden_out = None
    for l in range(LAYERS - 1, -1, -1):
        last = l == LAYERS - 1
        keep = saved[l]
        gin, hid, ggu, guv = ffn_input_grad(
            pack, keep["gy"], keep["gate"], keep["up"], experts_w[l]
        )
        gin_back = to_owner(gin, experts)
        d_experts = ffn_weight_grad(pack, keep["received"], keep["gy"], hid, ggu, guv)
        d_experts, keep["n2"] = lax.optimization_barrier((d_experts, keep["n2"]))
        expert_grads[l] = lax.psum_scatter(d_experts, "shard", scatter_dimension=0, tiled=False)
        args = [
            gx, keep["n2"], keep["y"], keep["gxs"], slot_row[l], keep["info"], chosen_rows[l],
            keep["gcol"], dense[l][:, W_SMALL:], keep["z"], mixes[l],
        ]
        args += [keep["middle"], slot_col[l]] if last else [gz]
        outs = gating_call(last, experts, slots, args)
        gn2, gsm, mix_grads[l], gz = outs[:4]
        if last:
            hidden_out = outs[4]
        args = [
            gx, gn2, gin_back, slot_col[l], keep["middle"], keep["att"], dense[l], keep["qkv"],
            keep["n1"], keep["x"], bias_t, keep["lse"], gsm,
        ]
        if l > 0:
            args += [slot_row[l - 1], saved[l - 1]["gpack"]]
        outs = backward_call(l == 0, experts, slots, args)
        gx, d_dense = outs[:2]
        if l > 0:
            saved[l - 1]["gxs"] = outs[2]
            saved[l - 1]["gy"] = to_owner(outs[3], experts)
        if not last:
            d_dense, dense_grads[l + 1] = lax.optimization_barrier((d_dense, dense_grads[l + 1]))
        mine = lax.psum_scatter(d_dense, "shard", scatter_dimension=0, tiled=True)
        dense_grads[l] = lax.psum(mine, "expert").astype(f32)

    mixing_total = lax.psum(jnp.stack(mix_grads), ("expert", "shard"))
    grads = jnp.stack(dense_grads)
    small = grads[:, :, W_SMALL:]
    project_grad = jnp.stack([grads[:, :, c * D : (c + 1) * D] for c in range(3)], axis=1)
    const_grad = jnp.stack(
        [small[:, :, S_CONST + 2 * c : S_CONST + 2 * c + 2] for c in range(2)], axis=1
    )
    unpacked = [pack.unpack(expert_grads[l].astype(f32)) for l in range(LAYERS)]
    return (
        hidden_out,
        gx,
        gz[0:total_experts].T,
        project_grad,
        grads[:, :, W_OUT:W_SMALL],
        small[:, :, S_GAIN : S_GAIN + 2].transpose(0, 2, 1),
        small[:, :, 0:total_experts],
        mixing_total[:, 0:total_experts, 0:total_experts],
        small[:, :, S_VEC : S_VEC + 2].transpose(0, 2, 1),
        const_grad,
        *[jnp.stack([unpacked[l][n] for l in range(LAYERS)])[:, None] for n in range(3)],
    )


def solution(mesh):
    both = ("expert", "shard")
    in_specs = (
        P(both, None),
        P(both, None),
        P(None, None, "shard", None),
        P(None, "shard", None),
        P(None, None, "shard"),
        P(None, "shard", None),
        P(),
        P(None, None, "shard"),
        P(None, None, "shard", None),
        P(None, "expert", "shard", None),
        P(None, "expert", "shard", None),
        P(None, "expert", "shard", None),
        P(None, both, None),
        P(both, None),
        P(both, None),
        P(both, None),
    )
    out_specs = (
        P(both, None),
        P(both, None),
        P(both, None),
        P(None, None, "shard", None),
        P(None, "shard", None),
        P(None, None, "shard"),
        P(None, "shard", None),
        P(),
        P(None, None, "shard"),
        P(None, None, "shard", None),
        P(None, "expert", "shard", None),
        P(None, "expert", "shard", None),
        P(None, "expert", "shard", None),
    )
    return jax.shard_map(
        on_device, mesh=mesh, in_specs=in_specs, out_specs=out_specs, check_vma=False
    )
```

```python
import functools

import jax
import jax.numpy as jnp
from jax import lax
from jax.experimental import pallas as pl
from jax.experimental.pallas import tpu as pltpu
from jax.sharding import PartitionSpec as P

D = 768
H = 12
HD = 64
TOP = 2
LAYERS = 2
TRUNK = 320
BRANCH = 64
LEAF = 32
TREE = 832

W_OUT = 3 * D
W_SMALL = 4 * D
W_ALL = 4 * D + 128
S_CONST = 16
S_GAIN = 24
S_VEC = 26

epsilon = 1e-06
masked_fill = -1e30
f32 = jnp.float32
bf16 = jnp.bfloat16
BLOCKS = 4
VMEM = 56 << 20


def dot(a, b):
    return jnp.dot(a, b, preferred_element_type=f32)


def dot_nt(a, b):
    return lax.dot_general(a, b, (((1,), (1,)), ((), ())), preferred_element_type=f32)


def dot_tn(a, b):
    return lax.dot_general(a, b, (((0,), (0,)), ((), ())), preferred_element_type=f32)


def split_bf16(v):
    high = v.astype(bf16)
    return high, (v - high.astype(f32)).astype(bf16)


def inv_rms(v):
    return lax.rsqrt(jnp.mean(v * v, axis=1, keepdims=True) + epsilon)


def tree_visible(parents):
    position = jnp.arange(TREE, dtype=jnp.int32)
    offset = position - TRUNK
    segment = jnp.where(
        position < TRUNK,
        0,
        jnp.where(offset < 4 * BRANCH, 1 + offset // BRANCH, 5 + (offset - 4 * BRANCH) // LEAF),
    )
    leaf_hits = (segment[:, None] - 5 == jnp.arange(8, dtype=jnp.int32)[None, :]).astype(jnp.int32)
    upper = jnp.where(segment >= 5, 1 + jnp.sum(leaf_hits * parents[None, :], axis=1), 0)
    key_segment = segment[None, :]
    causal = position[None, :] <= position[:, None]
    return causal & (
        (key_segment == segment[:, None]) | (key_segment == 0) | (key_segment == upper[:, None])
    )


def one_hot(slot_row, e, slots):
    row = lax.broadcasted_iota(jnp.int32, (slots, slot_row.shape[1]), 0).astype(f32)
    return jnp.where(row == slot_row[e : e + 1, :], 1.0, 0.0).astype(bf16)


def one_hot_col(slot_col, e, slots, scale=None):
    lane = lax.broadcasted_iota(jnp.int32, (slot_col.shape[0], slots), 1).astype(f32)
    value = 1.0 if scale is None else scale
    return jnp.where(lane == slot_col[:, e : e + 1], value, 0.0).astype(bf16)


def combine_rows(rows, middle_ref, n2_ref, y_ref, gcol_ref, slotc_ref, vectors, experts, slots):
    gcol = gcol_ref[rows, :]
    slot = slotc_ref[rows, :]
    total = middle_ref[rows, :] + gcol[:, 16:17] * n2_ref[rows, :].astype(f32)
    for c in range(2):
        total = total + gcol[:, 17 + c : 18 + c] * vectors[c : c + 1, :]
    for e in range(experts):
        weight = one_hot_col(slot, e, slots, gcol[:, e : e + 1])
        total = total + dot(weight, y_ref[e * slots : (e + 1) * slots, :])
    return total


def send_grads(slot_row, gx, gpack, gxs_ref, gy_ref, experts, slots):
    for e in range(experts):
        hot = one_hot(slot_row, e, slots)
        rows = slice(e * slots, (e + 1) * slots)
        got = dot(hot, gx)
        gates = dot(hot, gpack)
        gxs_ref[rows, :] = got.astype(bf16)
        gy_ref[rows, :] = (got * (gates[:, e : e + 1] + gates[:, 64 + e : 65 + e])).astype(bf16)


def row_blocks(tokens):
    size = tokens // BLOCKS
    return size, lambda i: pl.ds(pl.multiple_of(i * size, 16), size)


def causal_spans(tokens):
    edges = [0, 384, 640, tokens]
    return list(zip(edges[:-1], edges[1:]))


def forward_kernel(first, last, experts, slots, *refs):
    refs = list(refs)
    if first:
        x_in = refs.pop(0)
    else:
        mid_prev, n2_prev, y_ref, gcol_prev, slotc_prev, w_prev = [refs.pop(0) for _ in range(6)]
    w_ref, bias_ref, z_ref, mixt_ref, chosen_ref, slotr_ref = [refs.pop(0) for _ in range(6)]
    if last:
        cot_ref = refs.pop(0)
    if not first:
        x_out = refs.pop(0)
    n1_ref, qkv_ref, att_ref, lse_ref, mid_ref, n2_ref, info_ref, gcol_ref, gpack_ref, send_ref = [
        refs.pop(0) for _ in range(10)
    ]
    if last:
        gxs_ref, gy_ref = refs.pop(0), refs.pop(0)
    lse_cols, turn = refs
    tokens = n1_ref.shape[0]
    size, block = row_blocks(tokens)
    small = w_ref[:, W_SMALL:].astype(f32).T
    gain0 = small[S_GAIN : S_GAIN + 1, :]
    gain1 = small[S_GAIN + 1 : S_GAIN + 2, :]
    if not first:
        vectors_prev = w_prev[...].astype(f32).T[S_VEC : S_VEC + 2, :]

    def project(i, carry):
        rows = block(i)
        if first:
            x = x_in[rows, :].astype(f32)
        else:
            x = combine_rows(
                rows, mid_prev, n2_prev, y_ref, gcol_prev, slotc_prev, vectors_prev, experts, slots
            )
            x_out[rows, :] = x
        n1 = (x * inv_rms(x) * gain0).astype(bf16)
        n1_ref[rows, :] = n1
        for c in range(3):
            qkv_ref[rows, c * D : (c + 1) * D] = dot(n1, w_ref[:, c * D : (c + 1) * D]).astype(bf16)
        return carry

    lax.fori_loop(0, BLOCKS, project, 0)
    lane = lax.broadcasted_iota(jnp.int32, (1, 128), 1)
    low_f = jnp.where(lane < HD, 1.0, 0.0)
    low = low_f.astype(bf16)
    high = (1.0 - low_f).astype(bf16)
    lse_cols[...] = jnp.zeros_like(lse_cols)

    def pair(p, carry):
        k = qkv_ref[:, pl.ds(pl.multiple_of(D + p * 128, 128), 128)]
        v = qkv_ref[:, pl.ds(pl.multiple_of(2 * D + p * 128, 128), 128)]
        va = v * low + high
        vb = v * high + low
        here = pl.ds(pl.multiple_of(p * 128, 128), 128)
        for start, stop in causal_spans(tokens):
            q = qkv_ref[start:stop, here] * bf16(HD**-0.5)
            outs = []
            for mask, value in ((low, va), (high, vb)):
                s = dot_nt(q * mask, k[:stop]) + bias_ref[start:stop, :stop]
                peak = jnp.max(s, axis=1, keepdims=True)
                expo = jnp.exp(s - peak).astype(bf16)
                outs.append((dot(expo, value[:stop]), peak))
            (oa, ma), (ob, mb) = outs
            numer = jnp.where(lane < HD, oa, ob)
            denom = pltpu.roll(jnp.where(lane < HD, ob, oa), HD, 1)
            att_ref[start:stop, here] = (numer / denom).astype(bf16)
            la = ma + jnp.log(oa[:, HD : HD + 1])
            lb = mb + jnp.log(ob[:, 0:1])
            old = lse_cols[start:stop, :]
            lse_cols[start:stop, :] = jnp.where(
                lane == 2 * p, la, jnp.where(lane == 2 * p + 1, lb, old)
            )
        return carry

    lax.fori_loop(0, H // 2, pair, 0)
    lse_ref[...] = lse_cols[...].T[0:16, :]

    def finish(i, carry):
        rows = block(i)
        if first:
            x = x_in[rows, :].astype(f32)
        else:
            x = x_out[rows, :]
        middle = x + dot(att_ref[rows, :], w_ref[:, W_OUT:W_SMALL])
        mid_ref[rows, :] = middle
        n2_ref[rows, :] = (middle * inv_rms(middle) * gain1).astype(bf16)
        return carry

    lax.fori_loop(0, BLOCKS, finish, 0)
    n2 = n2_ref[...]
    scores = dot_nt(small[0:32, :].astype(bf16), n2)
    logits = scores[0:16, :]
    z = z_ref[...]
    mixt = mixt_ref[...]
    for i in range(experts + 4):
        logits = logits + mixt[:, i : i + 1] * z[i : i + 1, :]
    row = lax.broadcasted_iota(jnp.int32, (16, tokens), 0)
    valid = row < experts + 4
    peak = jnp.max(jnp.where(valid, logits, masked_fill), axis=0, keepdims=True)
    expo = jnp.where(valid, jnp.exp(jnp.minimum(logits - peak, 0.0)), 0.0)
    prob = expo / jnp.sum(expo, axis=0, keepdims=True)
    gates = prob * chosen_ref[...]
    info_ref[0:16, :] = logits
    info_ref[16:32, :] = prob
    turn[...] = jnp.zeros_like(turn)
    turn[0:16, 0:tokens] = gates
    own = gates[experts + 1 : experts + 2, :]
    alphas = []
    for c in range(2):
        l0 = scores[S_CONST + 2 * c : S_CONST + 2 * c + 1, :]
        l1 = scores[S_CONST + 2 * c + 1 : S_CONST + 2 * c + 2, :]
        a0 = jax.nn.sigmoid(l0 - l1)
        a1 = jax.nn.sigmoid(l1 - l0)
        alphas += [a0, a1]
        share = gates[experts + 2 + c : experts + 3 + c, :]
        own = own + share * a0
        turn[17 + c : 18 + c, 0:tokens] = share * a1
    turn[16:17, 0:tokens] = own
    zero_row = jnp.zeros((4, tokens), f32)
    info_ref[32:40, :] = jnp.concatenate(alphas + [zero_row], axis=0)
    gcol = turn[...].T[0:tokens, :]
    gcol_ref[...] = gcol
    upper, lower = split_bf16(jnp.where(lane < 16, gcol, 0.0))
    gpack = upper + pltpu.roll(lower.astype(f32), 64, 1).astype(bf16)
    gpack_ref[...] = gpack
    slot_row = slotr_ref[...]
    for e in range(experts):
        hot = one_hot(slot_row, e, slots)
        rows = slice(e * slots, (e + 1) * slots)
        send_ref[rows, :] = dot(hot, n2).astype(bf16)
    if last:
        send_grads(slot_row, cot_ref[...], gpack, gxs_ref, gy_ref, experts, slots)


def shape(dims, dtype=f32):
    return jax.ShapeDtypeStruct(tuple(dims), dtype)


def whole_call(body, name, outs, scratch, args, flops):
    moved = sum(a.size * a.dtype.itemsize for a in args) + sum(
        o.size * o.dtype.itemsize for o in outs
    )
    return pl.pallas_call(
        body,
        out_shape=outs,
        in_specs=[pl.BlockSpec(memory_space=pltpu.VMEM)] * len(args),
        out_specs=[pl.BlockSpec(memory_space=pltpu.VMEM)] * len(outs),
        scratch_shapes=scratch,
        compiler_params=pltpu.CompilerParams(vmem_limit_bytes=VMEM),
        cost_estimate=pl.CostEstimate(flops=flops, bytes_accessed=moved, transcendentals=0),
        name=name,
    )(*args)


def forward_call(first, last, experts, slots, args):
    tokens = TREE
    sent = experts * slots
    outs = [] if first else [shape((tokens, D))]
    outs += [
        shape((tokens, D), bf16),
        shape((tokens, 3 * D), bf16),
        shape((tokens, D), bf16),
        shape((16, tokens)),
        shape((tokens, D)),
        shape((tokens, D), bf16),
        shape((40, tokens)),
        shape((tokens, 128)),
        shape((tokens, 128), bf16),
        shape((sent, D), bf16),
    ]
    if last:
        outs += [shape((sent, D), bf16), shape((sent, D), bf16)]
    padded = -(-tokens // 128) * 128
    scratch = [pltpu.VMEM((tokens, 128), f32), pltpu.VMEM((128, padded), f32)]
    body = functools.partial(forward_kernel, first, last, experts, slots)
    return whole_call(body, "block_forward", outs, scratch, args, 20 * 10**9)


def gating_kernel(last, experts, slots, *refs):
    refs = list(refs)
    gx_ref, n2_ref, y_ref, gxs_ref, slotr_ref, info_ref, chosen_ref, gcol_ref, small_ref = [
        refs.pop(0) for _ in range(9)
    ]
    z_ref, mix_ref = refs.pop(0), refs.pop(0)
    if last:
        mid_ref, slotc_ref = refs.pop(0), refs.pop(0)
    else:
        gz_ref = refs.pop(0)
    gn2_ref, gsm_ref, gmix_ref, gprev_ref = [refs.pop(0) for _ in range(4)]
    if last:
        out_ref = refs.pop(0)
    tokens = n2_ref.shape[0]
    size, block = row_blocks(tokens)
    small = small_ref[...].astype(f32).T
    small_half = small[0:32, :].astype(bf16)
    vectors = small[S_VEC : S_VEC + 2, :]
    slot_row = slotr_ref[...]
    ones = jnp.ones((16, D), bf16)
    row = lax.broadcasted_iota(jnp.int32, (16, slots), 0)
    scattered = jnp.zeros((16, tokens), f32)
    for e in range(experts):
        rows = slice(e * slots, (e + 1) * slots)
        inner = y_ref[rows, :].astype(f32) * gxs_ref[rows, :].astype(f32)
        upper, lower = split_bf16(inner)
        sums = dot_nt(ones, upper) + dot_nt(ones, lower)
        upper, lower = split_bf16(sums)
        lhs = jnp.where(row == e, upper.astype(f32), 0.0) + jnp.where(
            row == 8 + e, lower.astype(f32), 0.0
        )
        scattered = scattered + dot(lhs.astype(bf16), one_hot(slot_row, e, slots))
    gx = gx_ref[...].astype(f32)
    gx_half = gx.astype(bf16)
    n2 = n2_ref[...]
    upper, lower = split_bf16(gx * n2.astype(f32))
    gx_n2 = (dot_nt(ones, upper) + dot_nt(ones, lower))[0:1, :]
    gx_small = dot_nt(small_half, gx_half)
    prob = info_ref[16:32, :]
    chosen = chosen_ref[...]
    gates = prob * chosen
    trow = lax.broadcasted_iota(jnp.int32, (16, tokens), 0)
    gp = jnp.concatenate([scattered[0:8, :] + scattered[8:16, :], jnp.zeros((8, tokens), f32)], 0)
    gp = jnp.where(trow == experts + 1, gx_n2, jnp.where(trow < experts, gp, 0.0))
    crow = lax.broadcasted_iota(jnp.int32, (8, tokens), 0)
    glog = jnp.zeros((8, tokens), f32)
    coefs = jnp.zeros((8, tokens), f32)
    for c in range(2):
        a0 = info_ref[32 + 2 * c : 33 + 2 * c, :]
        a1 = info_ref[33 + 2 * c : 34 + 2 * c, :]
        gx_v = gx_small[S_VEC + c : S_VEC + c + 1, :]
        share = gates[experts + 2 + c : experts + 3 + c, :]
        gp = jnp.where(trow == experts + 2 + c, a0 * gx_n2 + a1 * gx_v, gp)
        gl = share * (gx_n2 - gx_v) * a0 * a1
        glog = jnp.where(crow == 2 * c, gl, jnp.where(crow == 2 * c + 1, -gl, glog))
        coefs = jnp.where(crow == c, share * a1, coefs)
    gp = gp * chosen
    gz = prob * (gp - jnp.sum(prob * gp, axis=0, keepdims=True))
    if not last:
        gz = gz + gz_ref[...]
    z = z_ref[...]
    gmix_ref[...] = lax.dot_general(
        z, gz, (((1,), (1,)), ((), ())), precision=lax.Precision.HIGHEST, preferred_element_type=f32
    )
    mix = mix_ref[...]
    gprev = jnp.zeros((16, tokens), f32)
    for o in range(experts + 4):
        gprev = gprev + mix[:, o : o + 1] * gz[o : o + 1, :]
    gprev_ref[...] = gprev
    allg = jnp.concatenate([gz, glog, jnp.zeros((8, tokens), f32)], axis=0)
    upper, lower = split_bf16(allg)
    gsm = dot(upper, n2) + dot(lower, n2)
    cu, cl = split_bf16(jnp.concatenate([coefs, jnp.zeros((8, tokens), f32)], axis=0))
    gvec = dot(cu, gx_half) + dot(cl, gx_half)
    gsm_ref[0:24, :] = gsm[0:24, :]
    gsm_ref[24:32, :] = jnp.concatenate(
        [jnp.zeros((2, D), f32), gvec[0:2, :], jnp.zeros((4, D), f32)], axis=0
    )
    both = jnp.concatenate([upper, lower], axis=0)
    twice = jnp.concatenate([small_half, small_half], axis=0)
    gn2_ref[...] = dot_tn(both, twice)

    def add(i, carry):
        rows = block(i)
        gn2_ref[rows, :] = gn2_ref[rows, :] + gcol_ref[rows, 16:17] * gx_ref[rows, :].astype(f32)
        if last:
            out_ref[rows, :] = combine_rows(
                rows, mid_ref, n2_ref, y_ref, gcol_ref, slotc_ref, vectors, experts, slots
            ).astype(bf16)
        return carry

    lax.fori_loop(0, BLOCKS, add, 0)


def gating_call(last, experts, slots, args):
    tokens = TREE
    outs = [shape((tokens, D)), shape((32, D)), shape((16, 16)), shape((16, tokens))]
    if last:
        outs += [shape((tokens, D), bf16)]
    body = functools.partial(gating_kernel, last, experts, slots)
    return whole_call(body, "gating_backward", outs, [], args, 5 * 10**9)


def backward_kernel(first, experts, slots, *refs):
    refs = list(refs)
    gx_ref, gn2p_ref, gn2e_ref, slotc_ref, mid_ref, att_ref, w_ref, qkv_ref, n1_ref, x_ref = [
        refs.pop(0) for _ in range(10)
    ]
    biast_ref, lse_ref, gsm_ref = [refs.pop(0) for _ in range(3)]
    if not first:
        slotr_ref, gpack_ref = refs.pop(0), refs.pop(0)
    gout_ref, dw_ref = refs.pop(0), refs.pop(0)
    if not first:
        gxs_ref, gy_ref = refs.pop(0), refs.pop(0)
    gatt, go, gqkv, turn = refs
    tokens = n1_ref.shape[0]
    size, block = row_blocks(tokens)
    small = w_ref[:, W_SMALL:].astype(f32).T
    gain0 = small[S_GAIN : S_GAIN + 1, :]
    gain1 = small[S_GAIN + 1 : S_GAIN + 2, :]

    def enter(i, total):
        rows = block(i)
        gn2 = gn2p_ref[rows, :]
        slot = slotc_ref[rows, :]
        for e in range(experts):
            gn2 = gn2 + dot(one_hot_col(slot, e, slots), gn2e_ref[e * slots : (e + 1) * slots, :])
        middle = mid_ref[rows, :]
        r = inv_rms(middle)
        scaled = gain1 * gn2
        inner = jnp.mean(middle * scaled, axis=1, keepdims=True)
        gmid = gx_ref[rows, :].astype(f32) + r * scaled - middle * (r * r * r * inner)
        gout_ref[rows, :] = gmid
        half = gmid.astype(bf16)
        gatt[rows, :] = half
        go[rows, :] = dot_nt(half, w_ref[:, W_OUT:W_SMALL]).astype(bf16)
        return total + jnp.sum(gn2 * middle * r, axis=0, keepdims=True)

    ggain1 = lax.fori_loop(0, BLOCKS, enter, jnp.zeros((1, D), f32))
    lane = lax.broadcasted_iota(jnp.int32, (1, 128), 1)
    low_f = jnp.where(lane < HD, 1.0, 0.0)
    low = low_f.astype(bf16)
    high = (1.0 - low_f).astype(bf16)
    scale = HD**-0.5

    def out_grad(p, carry):
        here = pl.ds(pl.multiple_of(p * 128, 128), 128)
        dw_ref[here, W_OUT:W_SMALL] = dot_tn(att_ref[:, here], gatt[...]).astype(bf16)
        return carry

    lax.fori_loop(0, D // 128, out_grad, 0)
    spans = causal_spans(tokens)

    def pair(p, carry):
        here = pl.ds(pl.multiple_of(p * 128, 128), 128)
        lanes_k = pl.ds(pl.multiple_of(D + p * 128, 128), 128)
        lanes_v = pl.ds(pl.multiple_of(2 * D + p * 128, 128), 128)
        q = qkv_ref[:, here] * bf16(scale)
        k = qkv_ref[:, lanes_k]
        v = qkv_ref[:, lanes_v]
        g = go[:, here]
        turn[0:tokens, :] = g.astype(f32) * att_ref[:, here].astype(f32)
        inner = turn[...].T[:, 0:tokens]
        turn[0:tokens, :] = k.astype(f32)
        kt = turn[...].T[:, 0:tokens].astype(bf16)
        gq_t = []
        gk = [0.0] * len(spans)
        gv = [0.0] * len(spans)
        for h, mask in ((0, low), (1, high)):
            qh = q * mask
            gh = g * mask
            dsum = jnp.sum(inner[h * HD : (h + 1) * HD, :], axis=0, keepdims=True)
            lse = lse_ref[pl.ds(2 * p + h, 1), :]
            gq_h = []
            for n, (start, stop) in enumerate(spans):
                st = dot_nt(k[start:stop], qh[start:]) + biast_ref[start:stop, start:]
                pt = jnp.exp(st - lse[:, start:])
                gpt = dot_nt(v[start:stop], gh[start:])
                gst = (pt * (gpt - dsum[:, start:])).astype(bf16)
                gv[n] = gv[n] + dot(pt.astype(bf16), gh[start:])
                gk[n] = gk[n] + dot(gst, qh[start:])
                part = dot(kt[h * HD : (h + 1) * HD, start:stop], gst)
                gq_h.append(part)
            cols = []
            for n, (start, stop) in enumerate(spans):
                piece = 0.0
                for m in range(n + 1):
                    origin = spans[m][0]
                    piece = piece + gq_h[m][:, start - origin : stop - origin]
                cols.append(piece)
            gq_t.append(jnp.concatenate(cols, axis=1))
        turn_t = jnp.concatenate(gq_t, axis=0) * scale
        pad = turn.shape[0] - tokens
        turn_t = jnp.concatenate([turn_t, jnp.zeros((128, pad), f32)], axis=1)
        gqkv[:, here] = turn_t.T[0:tokens, :].astype(bf16)
        for n, (start, stop) in enumerate(spans):
            gqkv[start:stop, lanes_k] = gk[n].astype(bf16)
            gqkv[start:stop, lanes_v] = gv[n].astype(bf16)
        return carry

    turn[...] = jnp.zeros_like(turn)
    lax.fori_loop(0, H // 2, pair, 0)

    def in_grad(p, carry):
        here = pl.ds(pl.multiple_of(p * 128, 128), 128)
        dw_ref[here, 0:W_OUT] = dot_tn(n1_ref[:, here], gqkv[...]).astype(bf16)
        return carry

    lax.fori_loop(0, D // 128, in_grad, 0)

    def leave(i, total):
        rows = block(i)
        gn1 = dot_nt(gqkv[rows, :], w_ref[:, 0:W_OUT])
        x = x_ref[rows, :].astype(f32)
        r = inv_rms(x)
        scaled = gain0 * gn1
        inner = jnp.mean(x * scaled, axis=1, keepdims=True)
        gx = gout_ref[rows, :] + r * scaled - x * (r * r * r * inner)
        gout_ref[rows, :] = gx
        gatt[rows, :] = gx.astype(bf16)
        return total + jnp.sum(gn1 * x * r, axis=0, keepdims=True)

    ggain0 = lax.fori_loop(0, BLOCKS, leave, jnp.zeros((1, D), f32))
    rows = jnp.concatenate(
        [gsm_ref[0:24, :], ggain0, ggain1, gsm_ref[26:32, :], jnp.zeros((96, D), f32)], axis=0
    )
    dw_ref[:, W_SMALL:] = rows.T.astype(bf16)
    if not first:
        send_grads(slotr_ref[...], gatt[...], gpack_ref[...], gxs_ref, gy_ref, experts, slots)


def backward_call(first, experts, slots, args):
    tokens = TREE
    sent = experts * slots
    outs = [shape((tokens, D)), shape((D, W_ALL), bf16)]
    if not first:
        outs += [shape((sent, D), bf16), shape((sent, D), bf16)]
    padded = -(-tokens // 128) * 128
    scratch = [
        pltpu.VMEM((tokens, D), bf16),
        pltpu.VMEM((tokens, D), bf16),
        pltpu.VMEM((tokens, 3 * D), bf16),
        pltpu.VMEM((padded, 128), f32),
    ]
    body = functools.partial(backward_kernel, first, experts, slots)
    return whole_call(body, "block_backward", outs, scratch, args, 40 * 10**9)


class Packing:
    def __init__(self, shards, part, ff):
        self.shards, self.part, self.ff = shards, part, ff
        self.padded = -(-part // 16) * 16
        self.chunks = ff // 256
        self.own = ff // shards
        self.down = 2 * self.chunks * self.padded
        self.rows = self.down + (D // 256) * self.own
        self.group = 2 * 256 // self.own

    def pack(self, gate, up, down):
        pieces = []
        for wide in (gate, up):
            cut = wide.reshape(self.part, self.chunks, 256).transpose(1, 0, 2)
            cut = jnp.pad(cut, [(0, 0), (0, self.padded - self.part), (0, 0)])
            pieces.append(cut.reshape(self.chunks * self.padded, 256))
        pieces.append(
            down.reshape(self.own, D // 256, 256).transpose(1, 0, 2).reshape(-1, 256)
        )
        return jnp.concatenate(pieces, axis=0)

    def specs(self):
        two = self.shards, 2 * self.padded, 256
        steps = self.chunks // 2
        wide = [pl.BlockSpec(two, lambda j, n=n: (0, n * steps + j, 0)) for n in range(2)]
        base = self.down // self.own
        tall = [
            pl.BlockSpec((self.group, self.own, 256), lambda j, c=c: (j, base + c, 0))
            for c in range(D // 256)
        ]
        return wide + tall

    def wide_part(self, ref, i):
        at = i * self.padded
        return ref[:, at : at + self.part, :].reshape(D, 256)

    def tall_part(self, refs):
        return jnp.concatenate([ref[...].reshape(512, 256) for ref in refs], axis=1)


def accumulate(total, part, out_ref):
    j = pl.program_id(0)

    @pl.when(j == 0)
    def _():
        total[...] = part

    @pl.when(j > 0)
    def _():
        total[...] = total[...] + part

    @pl.when(j == pl.num_programs(0) - 1)
    def _():
        out_ref[...] = total[...].astype(bf16)


def ffn_forward_kernel(pack, r_ref, g_w, u_w, d0, d1, d2, y_ref, gu_ref, uv_ref, total):
    r = r_ref[...]
    hids = []
    for i in range(2):
        lanes = slice(i * 256, (i + 1) * 256)
        gate = dot(r, pack.wide_part(g_w, i))
        up = dot(r, pack.wide_part(u_w, i))
        gu_ref[:, lanes] = gate.astype(bf16)
        uv_ref[:, lanes] = up.astype(bf16)
        hids.append((gate * jax.nn.sigmoid(gate) * up).astype(bf16))
    hid = jnp.concatenate(hids, axis=1)
    accumulate(total, dot(hid, pack.tall_part((d0, d1, d2))), y_ref)


def ffn_call(body, name, pack, count, flat, wide, with_weights, outs, out_specs, scratch, args):
    ff = pack.ff
    in_specs = [pl.BlockSpec((count, D), lambda j: (0, 0))] * flat
    in_specs += [pl.BlockSpec((count, 512), lambda j: (0, j))] * wide
    if with_weights:
        in_specs += pack.specs()
        args = list(args) + [args[-1]] * 4
    return pl.pallas_call(
        functools.partial(body, pack),
        grid=(ff // 512,),
        out_shape=outs,
        in_specs=in_specs,
        out_specs=out_specs,
        scratch_shapes=scratch,
        compiler_params=pltpu.CompilerParams(vmem_limit_bytes=VMEM),
        cost_estimate=pl.CostEstimate(
            flops=6 * count * D * ff, bytes_accessed=6 * D * ff + 8 * count * ff, transcendentals=0
        ),
        name=name,
    )(*args)


def ffn_forward(pack, rows, weights):
    count, ff = rows.shape[0], pack.ff
    flat = pl.BlockSpec((count, D), lambda j: (0, 0))
    wide = pl.BlockSpec((count, 512), lambda j: (0, j))
    outs = [shape((count, D), bf16), shape((count, ff), bf16), shape((count, ff), bf16)]
    scratch = [pltpu.VMEM((count, D), f32)]
    return ffn_call(
        ffn_forward_kernel, "ffn_forward", pack, count, 1, 0, True, outs, [flat, wide, wide],
        scratch, [rows, weights],
    )


def ffn_input_kernel(
    pack, gy_ref, gu_ref, uv_ref, g_w, u_w, d0, d1, d2, gin_ref, hid_ref, ggu_ref, guv_ref, total
):
    ghid_all = dot_nt(gy_ref[...], pack.tall_part((d0, d1, d2)))
    part = 0.0
    for i in range(2):
        lanes = slice(i * 256, (i + 1) * 256)
        ghid = ghid_all[:, lanes]
        gate = gu_ref[:, lanes].astype(f32)
        up = uv_ref[:, lanes].astype(f32)
        s = jax.nn.sigmoid(gate)
        act = gate * s
        hid_ref[:, lanes] = (act * up).astype(bf16)
        guv = (ghid * act).astype(bf16)
        ggu = (ghid * up * (s * (1.0 + gate * (1.0 - s)))).astype(bf16)
        ggu_ref[:, lanes] = ggu
        guv_ref[:, lanes] = guv
        part = part + dot_nt(ggu, pack.wide_part(g_w, i)) + dot_nt(guv, pack.wide_part(u_w, i))
    accumulate(total, part, gin_ref)


def ffn_input_grad(pack, gy, gate, up, weights):
    count, ff = gy.shape[0], pack.ff
    flat = pl.BlockSpec((count, D), lambda j: (0, 0))
    wide = pl.BlockSpec((count, 512), lambda j: (0, j))
    outs = [shape((count, D), bf16)] + [shape((count, ff), bf16)] * 3
    scratch = [pltpu.VMEM((count, D), f32)]
    return ffn_call(
        ffn_input_kernel, "ffn_input_grad", pack, count, 1, 2, True, outs,
        [flat, wide, wide, wide], scratch, [gy, gate, up, weights],
    )


def ffn_weight_kernel(pack, r_ref, gy_ref, hid_ref, ggu_ref, guv_ref, out_ref, rt):
    j = pl.program_id(0)

    @pl.when(j == 0)
    def _():
        rt[...] = r_ref[...].T
        if pack.padded != pack.part:
            out_ref[...] = jnp.zeros_like(out_ref)

    for n, ref in enumerate((ggu_ref, guv_ref)):
        for i in range(2):
            grad = dot(rt[...], ref[:, i * 256 : (i + 1) * 256]).astype(bf16)
            at = (n * pack.chunks + i) * pack.padded + j * (2 * pack.padded)
            at = pl.multiple_of(at, 16)
            out_ref[:, pl.ds(at, pack.part), :] = grad.reshape(pack.shards, pack.part, 256)
    grad = dot_tn(hid_ref[...], gy_ref[...]).astype(bf16)
    for c in range(D // 256):
        at = pack.down + c * pack.own
        out_ref[pl.ds(j * pack.group, pack.group), at : at + pack.own, :] = grad[
            :, c * 256 : (c + 1) * 256
        ].reshape(pack.group, pack.own, 256)


def ffn_weight_grad(pack, rows, gy, hid, ggu, guv):
    count = rows.shape[0]
    outs = shape((pack.shards, pack.rows, 256), bf16)
    spec = pl.BlockSpec(outs.shape, lambda j: (0, 0, 0))
    return ffn_call(
        ffn_weight_kernel, "ffn_weight_grad", pack, count, 2, 3, False, outs, spec,
        [pltpu.VMEM((D, count), bf16)], [rows, gy, hid, ggu, guv],
    )


def expert_outputs_kernel(pack, first_ref, second_ref, gate_ref, up_ref, down_ref):
    for l, ref in enumerate((first_ref, second_ref)):
        for n, out in enumerate((gate_ref, up_ref)):
            for j in range(pack.chunks):
                at = (n * pack.chunks + j) * pack.padded
                out[l, :, j * 256 : (j + 1) * 256] = ref[at : at + pack.part, :].astype(f32)
        for c in range(D // 256):
            at = pack.down + c * pack.own
            down_ref[l, :, c * 256 : (c + 1) * 256] = ref[at : at + pack.own, :].astype(f32)


def expert_outputs(pack, grads):
    wide = shape((LAYERS, pack.part, pack.ff))
    outs = [wide, wide, shape((LAYERS, pack.own, D))]
    body = functools.partial(expert_outputs_kernel, pack)
    return whole_call(body, "expert_outputs", outs, [], grads, 10**6)


def dense_outputs_kernel(
    part, labels, first_ref, second_ref, proj_ref, out_ref, gain_ref, router_ref, vec_ref, const_ref,
    turn,
):
    for l, ref in enumerate((first_ref, second_ref)):
        for c in range(3):
            proj_ref[l, c] = ref[:, c * D : (c + 1) * D].astype(f32)
        out_ref[l] = ref[:, W_OUT:W_SMALL].astype(f32)
        small = ref[:, W_SMALL:].astype(f32)
        router_ref[l] = small[:, 0:labels]
        for c in range(2):
            const_ref[l, c] = small[:, S_CONST + 2 * c : S_CONST + 2 * c + 2]
        turn[0:part, :] = small
        rows = turn[...].T
        gain_ref[l] = rows[S_GAIN : S_GAIN + 2, 0:part]
        vec_ref[l] = rows[S_VEC : S_VEC + 2, 0:part]


def dense_outputs(part, labels, grads):
    outs = [
        shape((LAYERS, 3, part, D)),
        shape((LAYERS, part, D)),
        shape((LAYERS, 2, part)),
        shape((LAYERS, part, labels)),
        shape((LAYERS, 2, part)),
        shape((LAYERS, 2, part, 2)),
    ]
    body = functools.partial(dense_outputs_kernel, part, labels)
    return whole_call(body, "dense_outputs", outs, [pltpu.VMEM((128, 128), f32)], grads, 10**6)


def to_owner(rows, owners):
    slots = rows.shape[0] // owners
    return lax.all_to_all(
        rows.reshape(owners, slots, D), "expert", split_axis=0, concat_axis=0, tiled=True
    ).reshape(owners * slots, D)


def on_device(
    hidden_in,
    prior_logits,
    project_weight,
    output_weight,
    norm_gain,
    router_weight,
    mixing_weight,
    const_vector,
    const_weight,
    gate_weight,
    up_weight,
    down_weight,
    routes,
    priority,
    leaf_parent,
    cotangent,
):
    experts = lax.axis_size("expert")
    total_experts = experts + 4
    tokens = hidden_in.shape[0]
    capacity = 9 * tokens * TOP // (8 * total_experts)
    slots = -(-capacity // 16) * 16
    part = project_weight.shape[2]

    def pad_cols(a, width):
        return jnp.pad(a, [(0, 0)] * (a.ndim - 1) + [(0, width - a.shape[-1])])

    dense = []
    experts_w = []
    pack = Packing(lax.axis_size("shard"), part, gate_weight.shape[3])
    for l in range(LAYERS):
        small = jnp.concatenate(
            [
                pad_cols(router_weight[l], S_CONST),
                const_weight[l, 0],
                const_weight[l, 1],
                jnp.zeros((part, S_GAIN - S_CONST - 4), bf16),
                norm_gain[l].T,
                const_vector[l].T,
            ],
            axis=1,
        )
        packed = jnp.concatenate(
            [project_weight[l, c] for c in range(3)] + [output_weight[l], pad_cols(small, 128)],
            axis=1,
        )
        dense.append(lax.all_gather(packed, "shard", axis=0, tiled=True))
        mine = pack.pack(gate_weight[l, 0], up_weight[l, 0], down_weight[l, 0])
        experts_w.append(lax.all_gather(mine, "shard", axis=0, tiled=False))

    ranking = priority[0]
    earlier = (ranking[None, :] < ranking[:, None]).astype(bf16)
    labels = jnp.arange(total_experts, dtype=jnp.int32)
    hits = jnp.sum((routes[:, :, :, None] == labels).astype(f32), axis=2)
    chosen_rows = [jnp.pad(hits[l].T, [(0, 16 - total_experts), (0, 0)]) for l in range(LAYERS)]
    loaded = jnp.concatenate([hits[l, :, :experts] for l in range(LAYERS)], axis=1)
    loaded_half = loaded.astype(bf16)
    rank_col = dot(earlier, loaded_half)
    rank_row = lax.dot_general(
        loaded_half, earlier, (((0,), (1,)), ((), ())), preferred_element_type=f32
    )
    slot_col_all = jnp.where((loaded > 0) & (rank_col < capacity), rank_col, -1.0)
    slot_row_all = jnp.where((loaded.T > 0) & (rank_row < capacity), rank_row, -1.0)
    slot_col = [slot_col_all[:, l * experts : (l + 1) * experts] for l in range(LAYERS)]
    slot_row = [
        jnp.pad(
            slot_row_all[l * experts : (l + 1) * experts],
            [(0, 8 - experts), (0, 0)],
            constant_values=-1.0,
        )
        for l in range(LAYERS)
    ]
    visible = tree_visible(leaf_parent[0])
    bias = jnp.where(visible, 0.0, masked_fill)
    bias_t = jnp.where(visible.T, 0.0, masked_fill)
    mixes = [
        jnp.pad(mixing_weight[l], [(0, 16 - total_experts), (0, 16 - total_experts)])
        for l in range(LAYERS)
    ]
    z_rows = jnp.pad(prior_logits.T, [(0, 16 - total_experts), (0, 0)])

    saved = []
    front = [hidden_in]
    x_now = hidden_in
    for l in range(LAYERS):
        last = l == LAYERS - 1
        args = front + [dense[l], bias, z_rows, mixes[l].T, chosen_rows[l], slot_row[l]]
        if last:
            args.append(cotangent)
        outs = list(forward_call(l == 0, last, experts, slots, args))
        if l > 0:
            x_now = outs.pop(0)
        n1, qkv, att, lse, middle, n2, info, gcol, gpack, send = outs[:10]
        received = to_owner(send, experts)
        keep = dict(
            x=x_now, n1=n1, qkv=qkv, att=att, lse=lse, middle=middle, n2=n2, info=info,
            gcol=gcol, gpack=gpack, received=received, z=z_rows,
        )
        if last:
            keep["gxs"] = outs[10]
            keep["gy"] = to_owner(outs[11], experts)
        produced, keep["gate"], keep["up"] = ffn_forward(pack, received, experts_w[l])
        keep["y"] = to_owner(produced, experts)
        front = [middle, n2, keep["y"], gcol, slot_col[l], dense[l][:, W_SMALL:]]
        z_rows = info[0:16]
        saved.append(keep)

    gx = cotangent
    gz = None
    dense_grads = [None] * LAYERS
    mix_grads = [None] * LAYERS
    expert_grads = [None] * LAYERS
    hidden_out = None
    for l in range(LAYERS - 1, -1, -1):
        last = l == LAYERS - 1
        keep = saved[l]
        if not last:
            keep["info"], mine = lax.optimization_barrier((keep["info"], mine))
            dense_grads[l + 1] = lax.psum(mine, "expert")
        gin, hid, ggu, guv = ffn_input_grad(
            pack, keep["gy"], keep["gate"], keep["up"], experts_w[l]
        )
        gin_back = to_owner(gin, experts)
        d_experts = ffn_weight_grad(pack, keep["received"], keep["gy"], hid, ggu, guv)
        d_experts, keep["n2"] = lax.optimization_barrier((d_experts, keep["n2"]))
        expert_grads[l] = lax.psum_scatter(d_experts, "shard", scatter_dimension=0, tiled=False)
        args = [
            gx, keep["n2"], keep["y"], keep["gxs"], slot_row[l], keep["info"], chosen_rows[l],
            keep["gcol"], dense[l][:, W_SMALL:], keep["z"], mixes[l],
        ]
        args += [keep["middle"], slot_col[l]] if last else [gz]
        outs = gating_call(last, experts, slots, args)
        gn2, gsm, mix_grads[l], gz = outs[:4]
        if last:
            hidden_out = outs[4]
        args = [
            gx, gn2, gin_back, slot_col[l], keep["middle"], keep["att"], dense[l], keep["qkv"],
            keep["n1"], keep["x"], bias_t, keep["lse"], gsm,
        ]
        if l > 0:
            args += [slot_row[l - 1], saved[l - 1]["gpack"]]
        outs = backward_call(l == 0, experts, slots, args)
        gx, d_dense = outs[:2]
        d_dense, expert_grads[l] = lax.optimization_barrier((d_dense, expert_grads[l]))
        if l > 0:
            saved[l - 1]["gxs"] = outs[2]
            gy, d_dense = lax.optimization_barrier((outs[3], d_dense))
            saved[l - 1]["gy"] = to_owner(gy, experts)
        if not last:
            d_dense, dense_grads[l + 1] = lax.optimization_barrier((d_dense, dense_grads[l + 1]))
        if l == 0:
            mix_grads[0], d_dense = lax.optimization_barrier((mix_grads[0], d_dense))
        mine = lax.psum_scatter(d_dense, "shard", scatter_dimension=0, tiled=True)

    dense_grads[0] = lax.psum(mine, "expert")
    mixing_total = lax.psum(jnp.stack(mix_grads), ("expert", "shard"))
    gate_grad, up_grad, down_grad = expert_outputs(pack, expert_grads)
    project_grad, output_grad, gain_grad, router_grad, vector_grad, const_grad = dense_outputs(
        part, total_experts, dense_grads
    )
    return (
        hidden_out,
        gx,
        gz[0:total_experts].T,
        project_grad,
        output_grad,
        gain_grad,
        router_grad,
        mixing_total[:, 0:total_experts, 0:total_experts],
        vector_grad,
        const_grad,
        gate_grad[:, None],
        up_grad[:, None],
        down_grad[:, None],
    )


def solution(mesh):
    both = ("expert", "shard")
    in_specs = (
        P(both, None),
        P(both, None),
        P(None, None, "shard", None),
        P(None, "shard", None),
        P(None, None, "shard"),
        P(None, "shard", None),
        P(),
        P(None, None, "shard"),
        P(None, None, "shard", None),
        P(None, "expert", "shard", None),
        P(None, "expert", "shard", None),
        P(None, "expert", "shard", None),
        P(None, both, None),
        P(both, None),
        P(both, None),
        P(both, None),
    )
    out_specs = (
        P(both, None),
        P(both, None),
        P(both, None),
        P(None, None, "shard", None),
        P(None, "shard", None),
        P(None, None, "shard"),
        P(None, "shard", None),
        P(),
        P(None, None, "shard"),
        P(None, None, "shard", None),
        P(None, "expert", "shard", None),
        P(None, "expert", "shard", None),
        P(None, "expert", "shard", None),
    )
    return jax.shard_map(
        on_device, mesh=mesh, in_specs=in_specs, out_specs=out_specs, check_vma=False
    )
```

```python
import functools

import jax
import jax.numpy as jnp
from jax import lax
from jax.experimental import pallas as pl
from jax.experimental.pallas import tpu as pltpu
from jax.sharding import PartitionSpec as P

D = 768
H = 12
HD = 64
TOP = 2
LAYERS = 2
TRUNK = 320
BRANCH = 64
LEAF = 32
TREE = 832

W_OUT = 3 * D
W_SMALL = 4 * D
W_ALL = 4 * D + 128
S_CONST = 16
S_GAIN = 24
S_VEC = 26

epsilon = 1e-06
masked_fill = -1e30
f32 = jnp.float32
bf16 = jnp.bfloat16
BLOCKS = 4
VMEM = 56 << 20


def dot(a, b):
    return jnp.dot(a, b, preferred_element_type=f32)


def dot_nt(a, b):
    return lax.dot_general(a, b, (((1,), (1,)), ((), ())), preferred_element_type=f32)


def dot_tn(a, b):
    return lax.dot_general(a, b, (((0,), (0,)), ((), ())), preferred_element_type=f32)


def split_bf16(v):
    high = v.astype(bf16)
    return high, (v - high.astype(f32)).astype(bf16)


def inv_rms(v):
    return lax.rsqrt(jnp.mean(v * v, axis=1, keepdims=True) + epsilon)


def tree_visible(parents):
    position = jnp.arange(TREE, dtype=jnp.int32)
    offset = position - TRUNK
    segment = jnp.where(
        position < TRUNK,
        0,
        jnp.where(offset < 4 * BRANCH, 1 + offset // BRANCH, 5 + (offset - 4 * BRANCH) // LEAF),
    )
    leaf_hits = (segment[:, None] - 5 == jnp.arange(8, dtype=jnp.int32)[None, :]).astype(jnp.int32)
    upper = jnp.where(segment >= 5, 1 + jnp.sum(leaf_hits * parents[None, :], axis=1), 0)
    key_segment = segment[None, :]
    causal = position[None, :] <= position[:, None]
    return causal & (
        (key_segment == segment[:, None]) | (key_segment == 0) | (key_segment == upper[:, None])
    )


def one_hot(slot_row, e, slots):
    row = lax.broadcasted_iota(jnp.int32, (slots, slot_row.shape[1]), 0).astype(f32)
    return jnp.where(row == slot_row[e : e + 1, :], 1.0, 0.0).astype(bf16)


def one_hot_col(slot_col, e, slots, scale=None):
    lane = lax.broadcasted_iota(jnp.int32, (slot_col.shape[0], slots), 1).astype(f32)
    value = 1.0 if scale is None else scale
    return jnp.where(lane == slot_col[:, e : e + 1], value, 0.0).astype(bf16)


def combine_rows(rows, middle_ref, n2_ref, y_ref, gcol_ref, slotc_ref, vectors, experts, slots):
    gcol = gcol_ref[rows, :]
    slot = slotc_ref[rows, :]
    total = middle_ref[rows, :] + gcol[:, 16:17] * n2_ref[rows, :].astype(f32)
    for c in range(2):
        total = total + gcol[:, 17 + c : 18 + c] * vectors[c : c + 1, :]
    for e in range(experts):
        weight = one_hot_col(slot, e, slots, gcol[:, e : e + 1])
        total = total + dot(weight, y_ref[e * slots : (e + 1) * slots, :])
    return total


def send_grads(slot_row, gx, gpack, gxs_ref, gy_ref, experts, slots):
    for e in range(experts):
        hot = one_hot(slot_row, e, slots)
        rows = slice(e * slots, (e + 1) * slots)
        got = dot(hot, gx)
        gates = dot(hot, gpack)
        gxs_ref[rows, :] = got.astype(bf16)
        gy_ref[rows, :] = (got * (gates[:, e : e + 1] + gates[:, 64 + e : 65 + e])).astype(bf16)


def row_blocks(tokens):
    size = tokens // BLOCKS
    return size, lambda i: pl.ds(pl.multiple_of(i * size, 16), size)


def causal_spans(tokens):
    edges = [0, 384, 640, tokens]
    return list(zip(edges[:-1], edges[1:]))


def forward_kernel(first, last, experts, slots, *refs):
    refs = list(refs)
    if first:
        x_in = refs.pop(0)
    else:
        mid_prev, n2_prev, y_ref, gcol_prev, slotc_prev, w_prev = [refs.pop(0) for _ in range(6)]
    w_ref, bias_ref, z_ref, mixt_ref, chosen_ref, slotr_ref = [refs.pop(0) for _ in range(6)]
    if last:
        cot_ref = refs.pop(0)
    if not first:
        x_out = refs.pop(0)
    n1_ref, qkv_ref, att_ref, lse_ref, mid_ref, n2_ref, info_ref, gcol_ref, gpack_ref, send_ref = [
        refs.pop(0) for _ in range(10)
    ]
    small_out = refs.pop(0)
    small_out[...] = w_ref[:, W_SMALL:]
    if last:
        gxs_ref, gy_ref = refs.pop(0), refs.pop(0)
    lse_cols, turn = refs
    tokens = n1_ref.shape[0]
    size, block = row_blocks(tokens)
    small = w_ref[:, W_SMALL:].astype(f32).T
    gain0 = small[S_GAIN : S_GAIN + 1, :]
    gain1 = small[S_GAIN + 1 : S_GAIN + 2, :]
    if not first:
        vectors_prev = w_prev[...].astype(f32).T[S_VEC : S_VEC + 2, :]

    def project(i, carry):
        rows = block(i)
        if first:
            x = x_in[rows, :].astype(f32)
        else:
            x = combine_rows(
                rows, mid_prev, n2_prev, y_ref, gcol_prev, slotc_prev, vectors_prev, experts, slots
            )
            x_out[rows, :] = x
        n1 = (x * inv_rms(x) * gain0).astype(bf16)
        n1_ref[rows, :] = n1
        for c in range(3):
            qkv_ref[rows, c * D : (c + 1) * D] = dot(n1, w_ref[:, c * D : (c + 1) * D]).astype(bf16)
        return carry

    lax.fori_loop(0, BLOCKS, project, 0)
    lane = lax.broadcasted_iota(jnp.int32, (1, 128), 1)
    low_f = jnp.where(lane < HD, 1.0, 0.0)
    low = low_f.astype(bf16)
    high = (1.0 - low_f).astype(bf16)
    lse_cols[...] = jnp.zeros_like(lse_cols)

    def pair(p, carry):
        k = qkv_ref[:, pl.ds(pl.multiple_of(D + p * 128, 128), 128)]
        v = qkv_ref[:, pl.ds(pl.multiple_of(2 * D + p * 128, 128), 128)]
        va = v * low + high
        vb = v * high + low
        here = pl.ds(pl.multiple_of(p * 128, 128), 128)
        for start, stop in causal_spans(tokens):
            q = qkv_ref[start:stop, here] * bf16(HD**-0.5)
            outs = []
            for mask, value in ((low, va), (high, vb)):
                s = dot_nt(q * mask, k[:stop]) + bias_ref[start:stop, :stop]
                peak = jnp.max(s, axis=1, keepdims=True)
                expo = jnp.exp(s - peak).astype(bf16)
                outs.append((dot(expo, value[:stop]), peak))
            (oa, ma), (ob, mb) = outs
            numer = jnp.where(lane < HD, oa, ob)
            denom = pltpu.roll(jnp.where(lane < HD, ob, oa), HD, 1)
            att_ref[start:stop, here] = (numer / denom).astype(bf16)
            la = ma + jnp.log(oa[:, HD : HD + 1])
            lb = mb + jnp.log(ob[:, 0:1])
            old = lse_cols[start:stop, :]
            lse_cols[start:stop, :] = jnp.where(
                lane == 2 * p, la, jnp.where(lane == 2 * p + 1, lb, old)
            )
        return carry

    lax.fori_loop(0, H // 2, pair, 0)
    lse_ref[...] = lse_cols[...].T[0:16, :]

    def finish(i, carry):
        rows = block(i)
        if first:
            x = x_in[rows, :].astype(f32)
        else:
            x = x_out[rows, :]
        middle = x + dot(att_ref[rows, :], w_ref[:, W_OUT:W_SMALL])
        mid_ref[rows, :] = middle
        n2_ref[rows, :] = (middle * inv_rms(middle) * gain1).astype(bf16)
        return carry

    lax.fori_loop(0, BLOCKS, finish, 0)
    n2 = n2_ref[...]
    scores = dot_nt(small[0:32, :].astype(bf16), n2)
    logits = scores[0:16, :]
    z = z_ref[...]
    mixt = mixt_ref[...]
    for i in range(experts + 4):
        logits = logits + mixt[:, i : i + 1] * z[i : i + 1, :]
    row = lax.broadcasted_iota(jnp.int32, (16, tokens), 0)
    valid = row < experts + 4
    peak = jnp.max(jnp.where(valid, logits, masked_fill), axis=0, keepdims=True)
    expo = jnp.where(valid, jnp.exp(jnp.minimum(logits - peak, 0.0)), 0.0)
    prob = expo / jnp.sum(expo, axis=0, keepdims=True)
    gates = prob * chosen_ref[...]
    info_ref[0:16, :] = logits
    info_ref[16:32, :] = prob
    turn[...] = jnp.zeros_like(turn)
    turn[0:16, 0:tokens] = gates
    own = gates[experts + 1 : experts + 2, :]
    alphas = []
    for c in range(2):
        l0 = scores[S_CONST + 2 * c : S_CONST + 2 * c + 1, :]
        l1 = scores[S_CONST + 2 * c + 1 : S_CONST + 2 * c + 2, :]
        a0 = jax.nn.sigmoid(l0 - l1)
        a1 = jax.nn.sigmoid(l1 - l0)
        alphas += [a0, a1]
        share = gates[experts + 2 + c : experts + 3 + c, :]
        own = own + share * a0
        turn[17 + c : 18 + c, 0:tokens] = share * a1
    turn[16:17, 0:tokens] = own
    zero_row = jnp.zeros((4, tokens), f32)
    info_ref[32:40, :] = jnp.concatenate(alphas + [zero_row], axis=0)
    gcol = turn[...].T[0:tokens, :]
    gcol_ref[...] = gcol
    upper, lower = split_bf16(jnp.where(lane < 16, gcol, 0.0))
    gpack = upper + pltpu.roll(lower.astype(f32), 64, 1).astype(bf16)
    gpack_ref[...] = gpack
    slot_row = slotr_ref[...]
    for e in range(experts):
        hot = one_hot(slot_row, e, slots)
        rows = slice(e * slots, (e + 1) * slots)
        send_ref[rows, :] = dot(hot, n2).astype(bf16)
    if last:
        send_grads(slot_row, cot_ref[...], gpack, gxs_ref, gy_ref, experts, slots)


def shape(dims, dtype=f32):
    return jax.ShapeDtypeStruct(tuple(dims), dtype)


def whole_call(body, name, outs, scratch, args, flops):
    moved = sum(a.size * a.dtype.itemsize for a in args) + sum(
        o.size * o.dtype.itemsize for o in outs
    )
    return pl.pallas_call(
        body,
        out_shape=outs,
        in_specs=[pl.BlockSpec(memory_space=pltpu.VMEM)] * len(args),
        out_specs=[pl.BlockSpec(memory_space=pltpu.VMEM)] * len(outs),
        scratch_shapes=scratch,
        compiler_params=pltpu.CompilerParams(vmem_limit_bytes=VMEM),
        cost_estimate=pl.CostEstimate(flops=flops, bytes_accessed=moved, transcendentals=0),
        name=name,
    )(*args)


def forward_call(first, last, experts, slots, args):
    tokens = TREE
    sent = experts * slots
    outs = [] if first else [shape((tokens, D))]
    outs += [
        shape((tokens, D), bf16),
        shape((tokens, 3 * D), bf16),
        shape((tokens, D), bf16),
        shape((16, tokens)),
        shape((tokens, D)),
        shape((tokens, D), bf16),
        shape((40, tokens)),
        shape((tokens, 128)),
        shape((tokens, 128), bf16),
        shape((sent, D), bf16),
        shape((D, 128), bf16),
    ]
    if last:
        outs += [shape((sent, D), bf16), shape((sent, D), bf16)]
    padded = -(-tokens // 128) * 128
    scratch = [pltpu.VMEM((tokens, 128), f32), pltpu.VMEM((128, padded), f32)]
    body = functools.partial(forward_kernel, first, last, experts, slots)
    return whole_call(body, "block_forward", outs, scratch, args, 20 * 10**9)


def gating_kernel(last, experts, slots, *refs):
    refs = list(refs)
    gx_ref, n2_ref, y_ref, gxs_ref, slotr_ref, info_ref, chosen_ref, gcol_ref, small_ref = [
        refs.pop(0) for _ in range(9)
    ]
    z_ref, mix_ref = refs.pop(0), refs.pop(0)
    if last:
        mid_ref, slotc_ref = refs.pop(0), refs.pop(0)
    else:
        gz_ref = refs.pop(0)
    gn2_ref, gsm_ref, gmix_ref, gprev_ref = [refs.pop(0) for _ in range(4)]
    if last:
        out_ref = refs.pop(0)
    tokens = n2_ref.shape[0]
    size, block = row_blocks(tokens)
    small = small_ref[...].astype(f32).T
    small_half = small[0:32, :].astype(bf16)
    vectors = small[S_VEC : S_VEC + 2, :]
    slot_row = slotr_ref[...]
    ones = jnp.ones((16, D), bf16)
    row = lax.broadcasted_iota(jnp.int32, (16, slots), 0)
    scattered = jnp.zeros((16, tokens), f32)
    for e in range(experts):
        rows = slice(e * slots, (e + 1) * slots)
        inner = y_ref[rows, :].astype(f32) * gxs_ref[rows, :].astype(f32)
        upper, lower = split_bf16(inner)
        sums = dot_nt(ones, upper) + dot_nt(ones, lower)
        upper, lower = split_bf16(sums)
        lhs = jnp.where(row == e, upper.astype(f32), 0.0) + jnp.where(
            row == 8 + e, lower.astype(f32), 0.0
        )
        scattered = scattered + dot(lhs.astype(bf16), one_hot(slot_row, e, slots))
    gx = gx_ref[...].astype(f32)
    gx_half = gx.astype(bf16)
    n2 = n2_ref[...]
    upper, lower = split_bf16(gx * n2.astype(f32))
    gx_n2 = (dot_nt(ones, upper) + dot_nt(ones, lower))[0:1, :]
    gx_small = dot_nt(small_half, gx_half)
    prob = info_ref[16:32, :]
    chosen = chosen_ref[...]
    gates = prob * chosen
    trow = lax.broadcasted_iota(jnp.int32, (16, tokens), 0)
    gp = jnp.concatenate([scattered[0:8, :] + scattered[8:16, :], jnp.zeros((8, tokens), f32)], 0)
    gp = jnp.where(trow == experts + 1, gx_n2, jnp.where(trow < experts, gp, 0.0))
    crow = lax.broadcasted_iota(jnp.int32, (8, tokens), 0)
    glog = jnp.zeros((8, tokens), f32)
    coefs = jnp.zeros((8, tokens), f32)
    for c in range(2):
        a0 = info_ref[32 + 2 * c : 33 + 2 * c, :]
        a1 = info_ref[33 + 2 * c : 34 + 2 * c, :]
        gx_v = gx_small[S_VEC + c : S_VEC + c + 1, :]
        share = gates[experts + 2 + c : experts + 3 + c, :]
        gp = jnp.where(trow == experts + 2 + c, a0 * gx_n2 + a1 * gx_v, gp)
        gl = share * (gx_n2 - gx_v) * a0 * a1
        glog = jnp.where(crow == 2 * c, gl, jnp.where(crow == 2 * c + 1, -gl, glog))
        coefs = jnp.where(crow == c, share * a1, coefs)
    gp = gp * chosen
    gz = prob * (gp - jnp.sum(prob * gp, axis=0, keepdims=True))
    if not last:
        gz = gz + gz_ref[...]
    z = z_ref[...]
    gmix_ref[...] = lax.dot_general(
        z, gz, (((1,), (1,)), ((), ())), precision=lax.Precision.HIGHEST, preferred_element_type=f32
    )
    mix = mix_ref[...]
    gprev = jnp.zeros((16, tokens), f32)
    for o in range(experts + 4):
        gprev = gprev + mix[:, o : o + 1] * gz[o : o + 1, :]
    gprev_ref[...] = gprev
    allg = jnp.concatenate([gz, glog, jnp.zeros((8, tokens), f32)], axis=0)
    upper, lower = split_bf16(allg)
    gsm = dot(upper, n2) + dot(lower, n2)
    cu, cl = split_bf16(jnp.concatenate([coefs, jnp.zeros((8, tokens), f32)], axis=0))
    gvec = dot(cu, gx_half) + dot(cl, gx_half)
    gsm_ref[0:24, :] = gsm[0:24, :]
    gsm_ref[24:32, :] = jnp.concatenate(
        [jnp.zeros((2, D), f32), gvec[0:2, :], jnp.zeros((4, D), f32)], axis=0
    )
    both = jnp.concatenate([upper, lower], axis=0)
    twice = jnp.concatenate([small_half, small_half], axis=0)
    gn2_ref[...] = dot_tn(both, twice)

    def add(i, carry):
        rows = block(i)
        gn2_ref[rows, :] = gn2_ref[rows, :] + gcol_ref[rows, 16:17] * gx_ref[rows, :].astype(f32)
        if last:
            out_ref[rows, :] = combine_rows(
                rows, mid_ref, n2_ref, y_ref, gcol_ref, slotc_ref, vectors, experts, slots
            ).astype(bf16)
        return carry

    lax.fori_loop(0, BLOCKS, add, 0)


def gating_call(last, experts, slots, args):
    tokens = TREE
    outs = [shape((tokens, D)), shape((32, D)), shape((16, 16)), shape((16, tokens))]
    if last:
        outs += [shape((tokens, D), bf16)]
    body = functools.partial(gating_kernel, last, experts, slots)
    return whole_call(body, "gating_backward", outs, [], args, 5 * 10**9)


def backward_kernel(first, experts, slots, *refs):
    refs = list(refs)
    gx_ref, gn2p_ref, gn2e_ref, slotc_ref, mid_ref, att_ref, w_ref, qkv_ref, n1_ref, x_ref = [
        refs.pop(0) for _ in range(10)
    ]
    biast_ref, lse_ref, gsm_ref = [refs.pop(0) for _ in range(3)]
    if not first:
        slotr_ref, gpack_ref = refs.pop(0), refs.pop(0)
    gout_ref, dw_ref = refs.pop(0), refs.pop(0)
    if not first:
        gxs_ref, gy_ref = refs.pop(0), refs.pop(0)
    gatt, go, gqkv, turn = refs
    tokens = n1_ref.shape[0]
    size, block = row_blocks(tokens)
    small = w_ref[:, W_SMALL:].astype(f32).T
    gain0 = small[S_GAIN : S_GAIN + 1, :]
    gain1 = small[S_GAIN + 1 : S_GAIN + 2, :]

    def enter(i, total):
        rows = block(i)
        gn2 = gn2p_ref[rows, :]
        slot = slotc_ref[rows, :]
        for e in range(experts):
            gn2 = gn2 + dot(one_hot_col(slot, e, slots), gn2e_ref[e * slots : (e + 1) * slots, :])
        middle = mid_ref[rows, :]
        r = inv_rms(middle)
        scaled = gain1 * gn2
        inner = jnp.mean(middle * scaled, axis=1, keepdims=True)
        gmid = gx_ref[rows, :].astype(f32) + r * scaled - middle * (r * r * r * inner)
        gout_ref[rows, :] = gmid
        half = gmid.astype(bf16)
        gatt[rows, :] = half
        go[rows, :] = dot_nt(half, w_ref[:, W_OUT:W_SMALL]).astype(bf16)
        return total + jnp.sum(gn2 * middle * r, axis=0, keepdims=True)

    ggain1 = lax.fori_loop(0, BLOCKS, enter, jnp.zeros((1, D), f32))
    lane = lax.broadcasted_iota(jnp.int32, (1, 128), 1)
    low_f = jnp.where(lane < HD, 1.0, 0.0)
    low = low_f.astype(bf16)
    high = (1.0 - low_f).astype(bf16)
    scale = HD**-0.5

    def out_grad(p, carry):
        here = pl.ds(pl.multiple_of(p * 128, 128), 128)
        dw_ref[here, W_OUT:W_SMALL] = dot_tn(att_ref[:, here], gatt[...]).astype(bf16)
        return carry

    lax.fori_loop(0, D // 128, out_grad, 0)
    spans = causal_spans(tokens)

    def pair(p, carry):
        here = pl.ds(pl.multiple_of(p * 128, 128), 128)
        lanes_k = pl.ds(pl.multiple_of(D + p * 128, 128), 128)
        lanes_v = pl.ds(pl.multiple_of(2 * D + p * 128, 128), 128)
        q = qkv_ref[:, here] * bf16(scale)
        k = qkv_ref[:, lanes_k]
        v = qkv_ref[:, lanes_v]
        g = go[:, here]
        turn[0:tokens, :] = g.astype(f32) * att_ref[:, here].astype(f32)
        inner = turn[...].T[:, 0:tokens]
        turn[0:tokens, :] = k.astype(f32)
        kt = turn[...].T[:, 0:tokens].astype(bf16)
        gq_t = []
        gk = [0.0] * len(spans)
        gv = [0.0] * len(spans)
        for h, mask in ((0, low), (1, high)):
            qh = q * mask
            gh = g * mask
            dsum = jnp.sum(inner[h * HD : (h + 1) * HD, :], axis=0, keepdims=True)
            lse = lse_ref[pl.ds(2 * p + h, 1), :]
            gq_h = []
            for n, (start, stop) in enumerate(spans):
                st = dot_nt(k[start:stop], qh[start:]) + biast_ref[start:stop, start:]
                pt = jnp.exp(st - lse[:, start:])
                gpt = dot_nt(v[start:stop], gh[start:])
                gst = (pt * (gpt - dsum[:, start:])).astype(bf16)
                gv[n] = gv[n] + dot(pt.astype(bf16), gh[start:])
                gk[n] = gk[n] + dot(gst, qh[start:])
                part = dot(kt[h * HD : (h + 1) * HD, start:stop], gst)
                gq_h.append(part)
            cols = []
            for n, (start, stop) in enumerate(spans):
                piece = 0.0
                for m in range(n + 1):
                    origin = spans[m][0]
                    piece = piece + gq_h[m][:, start - origin : stop - origin]
                cols.append(piece)
            gq_t.append(jnp.concatenate(cols, axis=1))
        turn_t = jnp.concatenate(gq_t, axis=0) * scale
        pad = turn.shape[0] - tokens
        turn_t = jnp.concatenate([turn_t, jnp.zeros((128, pad), f32)], axis=1)
        gqkv[:, here] = turn_t.T[0:tokens, :].astype(bf16)
        for n, (start, stop) in enumerate(spans):
            gqkv[start:stop, lanes_k] = gk[n].astype(bf16)
            gqkv[start:stop, lanes_v] = gv[n].astype(bf16)
        return carry

    turn[...] = jnp.zeros_like(turn)
    lax.fori_loop(0, H // 2, pair, 0)

    def in_grad(p, carry):
        here = pl.ds(pl.multiple_of(p * 128, 128), 128)
        dw_ref[here, 0:W_OUT] = dot_tn(n1_ref[:, here], gqkv[...]).astype(bf16)
        return carry

    lax.fori_loop(0, D // 128, in_grad, 0)

    def leave(i, total):
        rows = block(i)
        gn1 = dot_nt(gqkv[rows, :], w_ref[:, 0:W_OUT])
        x = x_ref[rows, :].astype(f32)
        r = inv_rms(x)
        scaled = gain0 * gn1
        inner = jnp.mean(x * scaled, axis=1, keepdims=True)
        gx = gout_ref[rows, :] + r * scaled - x * (r * r * r * inner)
        gout_ref[rows, :] = gx
        gatt[rows, :] = gx.astype(bf16)
        return total + jnp.sum(gn1 * x * r, axis=0, keepdims=True)

    ggain0 = lax.fori_loop(0, BLOCKS, leave, jnp.zeros((1, D), f32))
    rows = jnp.concatenate(
        [gsm_ref[0:24, :], ggain0, ggain1, gsm_ref[26:32, :], jnp.zeros((96, D), f32)], axis=0
    )
    dw_ref[:, W_SMALL:] = rows.T.astype(bf16)
    if not first:
        send_grads(slotr_ref[...], gatt[...], gpack_ref[...], gxs_ref, gy_ref, experts, slots)


def backward_call(first, experts, slots, args):
    tokens = TREE
    sent = experts * slots
    outs = [shape((tokens, D)), shape((D, W_ALL), bf16)]
    if not first:
        outs += [shape((sent, D), bf16), shape((sent, D), bf16)]
    padded = -(-tokens // 128) * 128
    scratch = [
        pltpu.VMEM((tokens, D), bf16),
        pltpu.VMEM((tokens, D), bf16),
        pltpu.VMEM((tokens, 3 * D), bf16),
        pltpu.VMEM((padded, 128), f32),
    ]
    body = functools.partial(backward_kernel, first, experts, slots)
    return whole_call(body, "block_backward", outs, scratch, args, 40 * 10**9)


class Packing:
    def __init__(self, shards, part, ff):
        self.shards, self.part, self.ff = shards, part, ff
        self.padded = -(-part // 16) * 16
        self.chunks = ff // 256
        self.own = ff // shards
        self.down = 2 * self.chunks * self.padded
        self.rows = self.down + (D // 256) * self.own

    def pack(self, gate, up, down):
        pieces = []
        for wide in (gate, up):
            cut = wide.reshape(self.part, self.chunks, 256).transpose(1, 0, 2)
            cut = jnp.pad(cut, [(0, 0), (0, self.padded - self.part), (0, 0)])
            pieces.append(cut.reshape(self.chunks * self.padded, 256))
        pieces.append(
            down.reshape(self.own, D // 256, 256).transpose(1, 0, 2).reshape(-1, 256)
        )
        return jnp.concatenate(pieces, axis=0)

    def wide_part(self, ref, n, j):
        at = pl.multiple_of((n * self.chunks + j) * self.padded, 16)
        return ref[:, pl.ds(at, self.padded), :][:, : self.part, :].reshape(D, 256)

    def tall_part(self, ref, j):
        group = 256 // self.own
        here = pl.ds(j * group, group)
        pieces = []
        for c in range(D // 256):
            at = self.down + c * self.own
            pieces.append(ref[here, at : at + self.own, :].reshape(256, 256))
        return jnp.concatenate(pieces, axis=1)

    def put_wide(self, ref, n, j, grad):
        at = pl.multiple_of((n * self.chunks + j) * self.padded, 16)
        ref[:, pl.ds(at, self.part), :] = grad.reshape(self.shards, self.part, 256)

    def put_tall(self, ref, j, grad):
        group = 256 // self.own
        for c in range(D // 256):
            at = self.down + c * self.own
            ref[pl.ds(j * group, group), at : at + self.own, :] = grad[
                :, c * 256 : (c + 1) * 256
            ].reshape(group, self.own, 256)


class Exchange:
    def __init__(self, experts, slots):
        self.experts, self.slots = experts, slots
        first = -(-slots // 32) * 16
        self.waves = ((0, first), (first, slots - first))
        self.ranges = [(0, slots)]
        for _, size in self.waves:
            start = self.ranges[-1][0] + self.ranges[-1][1]
            self.ranges.append((start, (experts - 1) * size))
        self.total = experts * slots

    def held(self, wave, d):
        size = self.waves[wave][1]
        return pl.ds(self.ranges[1 + wave][0] + (d - 1) * size, size)

    def slot(self, device, wave):
        offset, size = self.waves[wave]
        return pl.ds(pl.multiple_of(device * self.slots + offset, 16), size)


def exchange_kernel(mode, pack, ex, *refs):
    refs = list(refs)
    forward, backward = mode in ("forward", "both"), mode in ("backward", "both")
    if forward:
        send_n = refs.pop(0)
    if backward:
        send_g = refs.pop(0)
    w_hbm = refs.pop(0)
    if mode == "backward":
        gate_hbm, up_hbm, rows_hbm = refs.pop(0), refs.pop(0), refs.pop(0)
    if mode == "forward":
        recv_n, back_y, gates, ups = [refs.pop(0) for _ in range(4)]
    elif mode == "both":
        back_y, back_g, dw = [refs.pop(0) for _ in range(3)]
        recv_n = refs.pop(0)
    else:
        back_g, dw = refs.pop(0), refs.pop(0)
        recv_n = refs.pop(0)
    if forward:
        out_y = refs.pop(0)
    if backward:
        recv_g, out_g, hids, gates, ups, rows_t, acc_g = [refs.pop(0) for _ in range(7)]
    if forward:
        acc_y = refs.pop(0)
    w, sends, recvs, backs, gots, local = refs

    experts, slots = ex.experts, ex.slots
    me = lax.axis_index("expert")
    peers = range(1, experts)

    def ahead(d):
        return lax.rem(me + d, experts)

    def behind(d):
        return lax.rem(me + experts - d, experts)

    loads = [pltpu.make_async_copy(w_hbm, w, local.at[0])]
    if mode == "backward":
        loads.append(pltpu.make_async_copy(gate_hbm, gates, local.at[1]))
        loads.append(pltpu.make_async_copy(up_hbm, ups, local.at[2]))
        loads.append(pltpu.make_async_copy(rows_hbm, recv_n, local.at[3]))
    for copy in loads:
        copy.start()
    barrier = pltpu.get_barrier_semaphore()
    for d in peers:
        pl.semaphore_signal(
            barrier, inc=1, device_id={"expert": ahead(d)}, device_id_type=pl.DeviceIdType.MESH
        )
    pl.semaphore_wait(barrier, experts - 1)

    kinds = []
    if forward:
        kinds.append((send_n, recv_n))
    if backward:
        kinds.append((send_g, recv_g))
    returns = []
    if forward:
        returns.append((out_y, back_y))
    if backward:
        returns.append((out_g, back_g))

    def out_copies(wave):
        copies = []
        for d in peers:
            for n, (src, dst) in enumerate(kinds):
                copies.append(
                    pltpu.make_async_remote_copy(
                        src_ref=src.at[ex.slot(ahead(d), wave)],
                        dst_ref=dst.at[ex.held(wave, d)],
                        send_sem=sends.at[n, wave, d - 1],
                        recv_sem=recvs.at[n, wave, d - 1],
                        device_id={"expert": ahead(d)},
                        device_id_type=pl.DeviceIdType.MESH,
                    )
                )
        return copies

    def back_copies(wave):
        copies = []
        for n, (src, dst) in enumerate(returns):
            for d in peers:
                copies.append(
                    pltpu.make_async_remote_copy(
                        src_ref=src.at[ex.held(wave, d)],
                        dst_ref=dst.at[ex.slot(me, wave)],
                        send_sem=backs.at[n, wave, d - 1],
                        recv_sem=gots.at[n, wave, d - 1],
                        device_id={"expert": behind(d)},
                        device_id_type=pl.DeviceIdType.MESH,
                    )
                )
        return copies

    def work(start, size):
        rows = slice(start, start + size)
        part = slice(0, size)
        if forward:
            acc_y[part, :] = jnp.zeros((size, D), f32)
        if backward:
            acc_g[part, :] = jnp.zeros((size, D), f32)

        def chunk(j, carry):
            lanes = pl.ds(pl.multiple_of(j * 256, 256), 256)
            gate_w, up_w = pack.wide_part(w, 0, j), pack.wide_part(w, 1, j)
            down_w = pack.tall_part(w, j)
            if forward:
                r = recv_n[rows, :]
                gate, up = dot(r, gate_w), dot(r, up_w)
                if mode == "forward":
                    gates[rows, lanes] = gate.astype(bf16)
                    ups[rows, lanes] = up.astype(bf16)
            else:
                gate, up = gates[rows, lanes].astype(f32), ups[rows, lanes].astype(f32)
            s = jax.nn.sigmoid(gate)
            act = gate * s
            hid = (act * up).astype(bf16)
            if forward:
                acc_y[part, :] = acc_y[part, :] + dot(hid, down_w)
            if backward:
                hids[rows, lanes] = hid
                ghid = dot_nt(recv_g[rows, :], down_w)
                guv = (ghid * act).astype(bf16)
                ggu = (ghid * up * (s * (1.0 + gate * (1.0 - s)))).astype(bf16)
                gates[rows, lanes] = ggu
                ups[rows, lanes] = guv
                acc_g[part, :] = acc_g[part, :] + dot_nt(ggu, gate_w) + dot_nt(guv, up_w)
            return carry

        lax.fori_loop(0, pack.chunks, chunk, 0)
        if forward:
            out_y[rows, :] = acc_y[part, :].astype(bf16)
        if backward:
            out_g[rows, :] = acc_g[part, :].astype(bf16)

    waves = [out_copies(0), out_copies(1)]
    for copy in waves[0]:
        copy.start()
    mine = pl.ds(pl.multiple_of(me * slots, 16), slots)
    for copy in loads:
        copy.wait()
    for src, dst in kinds:
        dst[0:slots, :] = src[mine, :]
    work(*ex.ranges[0])
    for src, dst in returns:
        dst[mine, :] = src[0:slots, :]
    for copy in waves[0]:
        copy.wait_send()
    for copy in waves[1]:
        copy.start()
    for copy in waves[0]:
        copy.wait_recv()
    work(*ex.ranges[1])
    first = back_copies(0)
    for copy in first:
        copy.start()
    for copy in waves[1]:
        copy.wait()
    work(*ex.ranges[2])
    second = back_copies(1)
    for copy in second:
        copy.start()
    if backward:
        rows_t[...] = recv_n[...].T
        if pack.padded != pack.part:
            dw[...] = jnp.zeros_like(dw)

        def weights(j, carry):
            lanes = pl.ds(pl.multiple_of(j * 256, 256), 256)
            pack.put_wide(dw, 0, j, dot(rows_t[...], gates[:, lanes]).astype(bf16))
            pack.put_wide(dw, 1, j, dot(rows_t[...], ups[:, lanes]).astype(bf16))
            pack.put_tall(dw, j, dot_tn(hids[:, lanes], recv_g[...]).astype(bf16))
            return carry

        lax.fori_loop(0, pack.chunks, weights, 0)
    for copy in first + second:
        copy.wait()


EXCHANGE_IDS = {"forward": 0, "both": 1, "backward": 2}


def exchange_call(mode, pack, experts, slots, args):
    ex = Exchange(experts, slots)
    rows, ff = ex.total, pack.ff
    forward, backward = mode in ("forward", "both"), mode in ("backward", "both")
    flat, wide = shape((rows, D), bf16), shape((rows, ff), bf16)
    packed = (pack.shards, pack.rows, 256)
    most = max(size for _, size in ex.ranges)
    vmem = pl.BlockSpec(memory_space=pltpu.VMEM)
    far = pl.BlockSpec(memory_space=pl.ANY)
    in_specs = [vmem] * (2 if mode == "both" else 1) + [far]
    scratch = []
    if mode == "forward":
        outs = [flat, flat, wide, wide]
    elif mode == "both":
        outs = [flat, flat, shape(packed, bf16)]
        scratch.append(pltpu.VMEM((rows, D), bf16))
    else:
        in_specs += [far] * 3
        outs = [flat, shape(packed, bf16)]
        scratch.append(pltpu.VMEM((rows, D), bf16))
    if forward:
        scratch.append(pltpu.VMEM((rows, D), bf16))
    if backward:
        scratch += [pltpu.VMEM((rows, D), bf16)] * 2
        scratch += [pltpu.VMEM((rows, ff), bf16)] * 3
        scratch += [pltpu.VMEM((D, rows), bf16), pltpu.VMEM((most, D), f32)]
    if forward:
        scratch.append(pltpu.VMEM((most, D), f32))
    kinds = 2 if mode == "both" else 1
    scratch.append(pltpu.VMEM(packed, bf16))
    scratch += [pltpu.SemaphoreType.DMA((kinds, 2, experts - 1))] * 4
    scratch.append(pltpu.SemaphoreType.DMA((4,)))
    work = 6 * rows * D * ff * (1 if mode == "forward" else 2 if mode == "backward" else 3)
    return pl.pallas_call(
        functools.partial(exchange_kernel, mode, pack, ex),
        out_shape=outs,
        in_specs=in_specs,
        out_specs=[vmem] * len(outs),
        scratch_shapes=scratch,
        compiler_params=pltpu.CompilerParams(
            vmem_limit_bytes=60 << 20, collective_id=EXCHANGE_IDS[mode], has_side_effects=True
        ),
        cost_estimate=pl.CostEstimate(
            flops=work + 40 * 10**9, bytes_accessed=6 * D * ff, transcendentals=0
        ),
        name="experts_" + mode,
    )(*args)


def expert_outputs_kernel(pack, first_ref, second_ref, gate_ref, up_ref, down_ref):
    for l, ref in enumerate((first_ref, second_ref)):
        for n, out in enumerate((gate_ref, up_ref)):
            for j in range(pack.chunks):
                at = (n * pack.chunks + j) * pack.padded
                out[l, :, j * 256 : (j + 1) * 256] = ref[at : at + pack.part, :].astype(f32)
        for c in range(D // 256):
            at = pack.down + c * pack.own
            down_ref[l, :, c * 256 : (c + 1) * 256] = ref[at : at + pack.own, :].astype(f32)


def expert_outputs(pack, grads):
    wide = shape((LAYERS, pack.part, pack.ff))
    outs = [wide, wide, shape((LAYERS, pack.own, D))]
    body = functools.partial(expert_outputs_kernel, pack)
    return whole_call(body, "expert_outputs", outs, [], grads, 10**6)


def dense_outputs_kernel(
    part, labels, first_ref, second_ref, proj_ref, out_ref, gain_ref, router_ref, vec_ref, const_ref,
    turn,
):
    for l, ref in enumerate((first_ref, second_ref)):
        for c in range(3):
            proj_ref[l, c] = ref[:, c * D : (c + 1) * D].astype(f32)
        out_ref[l] = ref[:, W_OUT:W_SMALL].astype(f32)
        small = ref[:, W_SMALL:].astype(f32)
        router_ref[l] = small[:, 0:labels]
        for c in range(2):
            const_ref[l, c] = small[:, S_CONST + 2 * c : S_CONST + 2 * c + 2]
        turn[0:part, :] = small
        rows = turn[...].T
        gain_ref[l] = rows[S_GAIN : S_GAIN + 2, 0:part]
        vec_ref[l] = rows[S_VEC : S_VEC + 2, 0:part]


def dense_outputs(part, labels, grads):
    outs = [
        shape((LAYERS, 3, part, D)),
        shape((LAYERS, part, D)),
        shape((LAYERS, 2, part)),
        shape((LAYERS, part, labels)),
        shape((LAYERS, 2, part)),
        shape((LAYERS, 2, part, 2)),
    ]
    body = functools.partial(dense_outputs_kernel, part, labels)
    return whole_call(body, "dense_outputs", outs, [pltpu.VMEM((128, 128), f32)], grads, 10**6)


def on_device(
    hidden_in,
    prior_logits,
    project_weight,
    output_weight,
    norm_gain,
    router_weight,
    mixing_weight,
    const_vector,
    const_weight,
    gate_weight,
    up_weight,
    down_weight,
    routes,
    priority,
    leaf_parent,
    cotangent,
):
    experts = lax.axis_size("expert")
    total_experts = experts + 4
    tokens = hidden_in.shape[0]
    capacity = 9 * tokens * TOP // (8 * total_experts)
    slots = -(-capacity // 16) * 16
    part = project_weight.shape[2]

    def pad_cols(a, width):
        return jnp.pad(a, [(0, 0)] * (a.ndim - 1) + [(0, width - a.shape[-1])])

    dense = []
    experts_w = []
    pack = Packing(lax.axis_size("shard"), part, gate_weight.shape[3])
    for l in range(LAYERS):
        small = jnp.concatenate(
            [
                pad_cols(router_weight[l], S_CONST),
                const_weight[l, 0],
                const_weight[l, 1],
                jnp.zeros((part, S_GAIN - S_CONST - 4), bf16),
                norm_gain[l].T,
                const_vector[l].T,
            ],
            axis=1,
        )
        packed = jnp.concatenate(
            [project_weight[l, c] for c in range(3)] + [output_weight[l], pad_cols(small, 128)],
            axis=1,
        )
        dense.append(lax.all_gather(packed, "shard", axis=0, tiled=True))
        mine = pack.pack(gate_weight[l, 0], up_weight[l, 0], down_weight[l, 0])
        experts_w.append(lax.all_gather(mine, "shard", axis=0, tiled=False))

    ranking = priority[0]
    earlier = (ranking[None, :] < ranking[:, None]).astype(bf16)
    labels = jnp.arange(total_experts, dtype=jnp.int32)
    hits = jnp.sum((routes[:, :, :, None] == labels).astype(f32), axis=2)
    chosen_rows = [jnp.pad(hits[l].T, [(0, 16 - total_experts), (0, 0)]) for l in range(LAYERS)]
    loaded = jnp.concatenate([hits[l, :, :experts] for l in range(LAYERS)], axis=1)
    loaded_half = loaded.astype(bf16)
    rank_col = dot(earlier, loaded_half)
    rank_row = lax.dot_general(
        loaded_half, earlier, (((0,), (1,)), ((), ())), preferred_element_type=f32
    )
    slot_col_all = jnp.where((loaded > 0) & (rank_col < capacity), rank_col, -1.0)
    slot_row_all = jnp.where((loaded.T > 0) & (rank_row < capacity), rank_row, -1.0)
    slot_col = [slot_col_all[:, l * experts : (l + 1) * experts] for l in range(LAYERS)]
    slot_row = [
        jnp.pad(
            slot_row_all[l * experts : (l + 1) * experts],
            [(0, 8 - experts), (0, 0)],
            constant_values=-1.0,
        )
        for l in range(LAYERS)
    ]
    visible = tree_visible(leaf_parent[0])
    bias = jnp.where(visible, 0.0, masked_fill)
    bias_t = jnp.where(visible.T, 0.0, masked_fill)
    mixes = [
        jnp.pad(mixing_weight[l], [(0, 16 - total_experts), (0, 16 - total_experts)])
        for l in range(LAYERS)
    ]
    z_rows = jnp.pad(prior_logits.T, [(0, 16 - total_experts), (0, 0)])

    saved = []
    front = [hidden_in]
    x_now = hidden_in
    for l in range(LAYERS):
        last = l == LAYERS - 1
        args = front + [dense[l], bias, z_rows, mixes[l].T, chosen_rows[l], slot_row[l]]
        if last:
            args.append(cotangent)
        outs = list(forward_call(l == 0, last, experts, slots, args))
        if l > 0:
            x_now = outs.pop(0)
        n1, qkv, att, lse, middle, n2, info, gcol, gpack, send, small = outs[:11]
        keep = dict(
            x=x_now, n1=n1, qkv=qkv, att=att, lse=lse, middle=middle, n2=n2, info=info,
            gcol=gcol, gpack=gpack, z=z_rows, small=small,
        )
        if last:
            keep["gxs"] = outs[11]
            keep["y"], keep["gin"], keep["dw"] = exchange_call(
                "both", pack, experts, slots, [send, outs[12], experts_w[l]]
            )
        else:
            keep["received"], keep["y"], keep["gate"], keep["up"] = exchange_call(
                "forward", pack, experts, slots, [send, experts_w[l]]
            )
        front = [middle, n2, keep["y"], gcol, slot_col[l], small]
        z_rows = info[0:16]
        saved.append(keep)

    gx = cotangent
    gz = None
    dense_grads = [None] * LAYERS
    mix_grads = [None] * LAYERS
    expert_grads = [None] * LAYERS
    hidden_out = None
    for l in range(LAYERS - 1, -1, -1):
        last = l == LAYERS - 1
        keep = saved[l]
        if not last:
            keep["info"], mine = lax.optimization_barrier((keep["info"], mine))
            dense_grads[l + 1] = lax.psum(mine, "expert")
        if not last:
            keep["gin"], keep["dw"] = exchange_call(
                "backward", pack, experts, slots,
                [keep["gy"], experts_w[l], keep["gate"], keep["up"], keep["received"]],
            )
        d_experts, keep["n2"] = lax.optimization_barrier((keep["dw"], keep["n2"]))
        expert_grads[l] = lax.psum_scatter(d_experts, "shard", scatter_dimension=0, tiled=False)
        args = [
            gx, keep["n2"], keep["y"], keep["gxs"], slot_row[l], keep["info"], chosen_rows[l],
            keep["gcol"], keep["small"], keep["z"], mixes[l],
        ]
        args += [keep["middle"], slot_col[l]] if last else [gz]
        outs = gating_call(last, experts, slots, args)
        gn2, gsm, mix_grads[l], gz = outs[:4]
        if last:
            hidden_out = outs[4]
        args = [
            gx, gn2, keep["gin"], slot_col[l], keep["middle"], keep["att"], dense[l], keep["qkv"],
            keep["n1"], keep["x"], bias_t, keep["lse"], gsm,
        ]
        if l > 0:
            args += [slot_row[l - 1], saved[l - 1]["gpack"]]
        outs = backward_call(l == 0, experts, slots, args)
        gx, d_dense = outs[:2]
        d_dense, expert_grads[l] = lax.optimization_barrier((d_dense, expert_grads[l]))
        if l > 0:
            saved[l - 1]["gxs"] = outs[2]
            gy, d_dense = lax.optimization_barrier((outs[3], d_dense))
            saved[l - 1]["gy"] = gy
        if not last:
            d_dense, dense_grads[l + 1] = lax.optimization_barrier((d_dense, dense_grads[l + 1]))
        if l == 0:
            mix_grads[0], d_dense = lax.optimization_barrier((mix_grads[0], d_dense))
        mine = lax.psum_scatter(d_dense, "shard", scatter_dimension=0, tiled=True)

    dense_grads[0] = lax.psum(mine, "expert")
    mixing_total = lax.psum(jnp.stack(mix_grads), ("expert", "shard"))
    gate_grad, up_grad, down_grad = expert_outputs(pack, expert_grads)
    project_grad, output_grad, gain_grad, router_grad, vector_grad, const_grad = dense_outputs(
        part, total_experts, dense_grads
    )
    return (
        hidden_out,
        gx,
        gz[0:total_experts].T,
        project_grad,
        output_grad,
        gain_grad,
        router_grad,
        mixing_total[:, 0:total_experts, 0:total_experts],
        vector_grad,
        const_grad,
        gate_grad[:, None],
        up_grad[:, None],
        down_grad[:, None],
    )


def solution(mesh):
    both = ("expert", "shard")
    in_specs = (
        P(both, None),
        P(both, None),
        P(None, None, "shard", None),
        P(None, "shard", None),
        P(None, None, "shard"),
        P(None, "shard", None),
        P(),
        P(None, None, "shard"),
        P(None, None, "shard", None),
        P(None, "expert", "shard", None),
        P(None, "expert", "shard", None),
        P(None, "expert", "shard", None),
        P(None, both, None),
        P(both, None),
        P(both, None),
        P(both, None),
    )
    out_specs = (
        P(both, None),
        P(both, None),
        P(both, None),
        P(None, None, "shard", None),
        P(None, "shard", None),
        P(None, None, "shard"),
        P(None, "shard", None),
        P(),
        P(None, None, "shard"),
        P(None, None, "shard", None),
        P(None, "expert", "shard", None),
        P(None, "expert", "shard", None),
        P(None, "expert", "shard", None),
    )
    return jax.shard_map(
        on_device, mesh=mesh, in_specs=in_specs, out_specs=out_specs, check_vma=False
    )
```

```python
import functools

import jax
import jax.numpy as jnp
from jax import lax
from jax.experimental import pallas as pl
from jax.experimental.pallas import tpu as pltpu
from jax.sharding import PartitionSpec as P

D = 768
H = 12
HD = 64
TOP = 2
LAYERS = 2
TRUNK = 320
BRANCH = 64
LEAF = 32
TREE = 832

W_OUT = 3 * D
W_SMALL = 4 * D
W_ALL = 4 * D + 128
S_CONST = 16
S_GAIN = 24
S_VEC = 26

epsilon = 1e-06
masked_fill = -1e30
f32 = jnp.float32
bf16 = jnp.bfloat16
BLOCKS = 4
VMEM = 56 << 20


def dot(a, b):
    return jnp.dot(a, b, preferred_element_type=f32)


def dot_nt(a, b):
    return lax.dot_general(a, b, (((1,), (1,)), ((), ())), preferred_element_type=f32)


def dot_tn(a, b):
    return lax.dot_general(a, b, (((0,), (0,)), ((), ())), preferred_element_type=f32)


def split_bf16(v):
    high = v.astype(bf16)
    return high, (v - high.astype(f32)).astype(bf16)


def inv_rms(v):
    return lax.rsqrt(jnp.mean(v * v, axis=1, keepdims=True) + epsilon)


def tree_visible(parents):
    position = jnp.arange(TREE, dtype=jnp.int32)
    offset = position - TRUNK
    segment = jnp.where(
        position < TRUNK,
        0,
        jnp.where(offset < 4 * BRANCH, 1 + offset // BRANCH, 5 + (offset - 4 * BRANCH) // LEAF),
    )
    leaf_hits = (segment[:, None] - 5 == jnp.arange(8, dtype=jnp.int32)[None, :]).astype(jnp.int32)
    upper = jnp.where(segment >= 5, 1 + jnp.sum(leaf_hits * parents[None, :], axis=1), 0)
    key_segment = segment[None, :]
    causal = position[None, :] <= position[:, None]
    return causal & (
        (key_segment == segment[:, None]) | (key_segment == 0) | (key_segment == upper[:, None])
    )


def one_hot(slot_row, e, slots):
    row = lax.broadcasted_iota(jnp.int32, (slots, slot_row.shape[1]), 0).astype(f32)
    return jnp.where(row == slot_row[e : e + 1, :], 1.0, 0.0).astype(bf16)


def one_hot_col(slot_col, e, slots, scale=None):
    lane = lax.broadcasted_iota(jnp.int32, (slot_col.shape[0], slots), 1).astype(f32)
    value = 1.0 if scale is None else scale
    return jnp.where(lane == slot_col[:, e : e + 1], value, 0.0).astype(bf16)


def combine_rows(rows, middle_ref, n2_ref, y_ref, gcol_ref, slotc_ref, vectors, experts, slots):
    gcol = gcol_ref[rows, :]
    slot = slotc_ref[rows, :]
    total = middle_ref[rows, :] + gcol[:, 16:17] * n2_ref[rows, :].astype(f32)
    for c in range(2):
        total = total + gcol[:, 17 + c : 18 + c] * vectors[c : c + 1, :]
    for e in range(experts):
        weight = one_hot_col(slot, e, slots, gcol[:, e : e + 1])
        total = total + dot(weight, y_ref[e * slots : (e + 1) * slots, :])
    return total


def send_grads(slot_row, gx, gpack, gxs_ref, gy_ref, experts, slots):
    for e in range(experts):
        hot = one_hot(slot_row, e, slots)
        rows = slice(e * slots, (e + 1) * slots)
        got = dot(hot, gx)
        gates = dot(hot, gpack)
        gxs_ref[rows, :] = got.astype(bf16)
        gy_ref[rows, :] = (got * (gates[:, e : e + 1] + gates[:, 64 + e : 65 + e])).astype(bf16)


def row_blocks(tokens):
    size = tokens // BLOCKS
    return size, lambda i: pl.ds(pl.multiple_of(i * size, 16), size)


def causal_spans(tokens):
    edges = [0, 384, 640, tokens]
    return list(zip(edges[:-1], edges[1:]))


def forward_kernel(first, last, experts, slots, *refs):
    refs = list(refs)
    if first:
        x_in = refs.pop(0)
    else:
        mid_prev, n2_prev, y_ref, gcol_prev, slotc_prev, w_prev = [refs.pop(0) for _ in range(6)]
    w_ref, bias_ref, z_ref, mixt_ref, chosen_ref, slotr_ref = [refs.pop(0) for _ in range(6)]
    if last:
        cot_ref = refs.pop(0)
    if not first:
        x_out = refs.pop(0)
    n1_ref, qkv_ref, att_ref, lse_ref, mid_ref, n2_ref, info_ref, gcol_ref, gpack_ref, send_ref = [
        refs.pop(0) for _ in range(10)
    ]
    small_out = refs.pop(0)
    small_out[...] = w_ref[:, W_SMALL:]
    if last:
        gxs_ref, gy_ref = refs.pop(0), refs.pop(0)
    lse_cols, turn = refs
    tokens = n1_ref.shape[0]
    size, block = row_blocks(tokens)
    small = w_ref[:, W_SMALL:].astype(f32).T
    gain0 = small[S_GAIN : S_GAIN + 1, :]
    gain1 = small[S_GAIN + 1 : S_GAIN + 2, :]
    if not first:
        vectors_prev = w_prev[...].astype(f32).T[S_VEC : S_VEC + 2, :]

    def project(i, carry):
        rows = block(i)
        if first:
            x = x_in[rows, :].astype(f32)
        else:
            x = combine_rows(
                rows, mid_prev, n2_prev, y_ref, gcol_prev, slotc_prev, vectors_prev, experts, slots
            )
            x_out[rows, :] = x
        n1 = (x * inv_rms(x) * gain0).astype(bf16)
        n1_ref[rows, :] = n1
        for c in range(3):
            qkv_ref[rows, c * D : (c + 1) * D] = dot(n1, w_ref[:, c * D : (c + 1) * D]).astype(bf16)
        return carry

    lax.fori_loop(0, BLOCKS, project, 0)
    lane = lax.broadcasted_iota(jnp.int32, (1, 128), 1)
    low_f = jnp.where(lane < HD, 1.0, 0.0)
    low = low_f.astype(bf16)
    high = (1.0 - low_f).astype(bf16)
    lse_cols[...] = jnp.zeros_like(lse_cols)

    def pair(p, carry):
        k = qkv_ref[:, pl.ds(pl.multiple_of(D + p * 128, 128), 128)]
        v = qkv_ref[:, pl.ds(pl.multiple_of(2 * D + p * 128, 128), 128)]
        va = v * low + high
        vb = v * high + low
        here = pl.ds(pl.multiple_of(p * 128, 128), 128)
        for start, stop in causal_spans(tokens):
            q = qkv_ref[start:stop, here] * bf16(HD**-0.5)
            outs = []
            for mask, value in ((low, va), (high, vb)):
                s = dot_nt(q * mask, k[:stop]) + bias_ref[start:stop, :stop]
                peak = jnp.max(s, axis=1, keepdims=True)
                expo = jnp.exp(s - peak).astype(bf16)
                outs.append((dot(expo, value[:stop]), peak))
            (oa, ma), (ob, mb) = outs
            numer = jnp.where(lane < HD, oa, ob)
            denom = pltpu.roll(jnp.where(lane < HD, ob, oa), HD, 1)
            att_ref[start:stop, here] = (numer / denom).astype(bf16)
            la = ma + jnp.log(oa[:, HD : HD + 1])
            lb = mb + jnp.log(ob[:, 0:1])
            old = lse_cols[start:stop, :]
            lse_cols[start:stop, :] = jnp.where(
                lane == 2 * p, la, jnp.where(lane == 2 * p + 1, lb, old)
            )
        return carry

    lax.fori_loop(0, H // 2, pair, 0)
    lse_ref[...] = lse_cols[...].T[0:16, :]

    def finish(i, carry):
        rows = block(i)
        if first:
            x = x_in[rows, :].astype(f32)
        else:
            x = x_out[rows, :]
        middle = x + dot(att_ref[rows, :], w_ref[:, W_OUT:W_SMALL])
        mid_ref[rows, :] = middle
        n2_ref[rows, :] = (middle * inv_rms(middle) * gain1).astype(bf16)
        return carry

    lax.fori_loop(0, BLOCKS, finish, 0)
    n2 = n2_ref[...]
    scores = dot_nt(small[0:32, :].astype(bf16), n2)
    logits = scores[0:16, :]
    z = z_ref[...]
    mixt = mixt_ref[...]
    for i in range(experts + 4):
        logits = logits + mixt[:, i : i + 1] * z[i : i + 1, :]
    row = lax.broadcasted_iota(jnp.int32, (16, tokens), 0)
    valid = row < experts + 4
    peak = jnp.max(jnp.where(valid, logits, masked_fill), axis=0, keepdims=True)
    expo = jnp.where(valid, jnp.exp(jnp.minimum(logits - peak, 0.0)), 0.0)
    prob = expo / jnp.sum(expo, axis=0, keepdims=True)
    gates = prob * chosen_ref[...]
    info_ref[0:16, :] = logits
    info_ref[16:32, :] = prob
    turn[...] = jnp.zeros_like(turn)
    turn[0:16, 0:tokens] = gates
    own = gates[experts + 1 : experts + 2, :]
    alphas = []
    for c in range(2):
        l0 = scores[S_CONST + 2 * c : S_CONST + 2 * c + 1, :]
        l1 = scores[S_CONST + 2 * c + 1 : S_CONST + 2 * c + 2, :]
        a0 = jax.nn.sigmoid(l0 - l1)
        a1 = jax.nn.sigmoid(l1 - l0)
        alphas += [a0, a1]
        share = gates[experts + 2 + c : experts + 3 + c, :]
        own = own + share * a0
        turn[17 + c : 18 + c, 0:tokens] = share * a1
    turn[16:17, 0:tokens] = own
    zero_row = jnp.zeros((4, tokens), f32)
    info_ref[32:40, :] = jnp.concatenate(alphas + [zero_row], axis=0)
    gcol = turn[...].T[0:tokens, :]
    gcol_ref[...] = gcol
    upper, lower = split_bf16(jnp.where(lane < 16, gcol, 0.0))
    gpack = upper + pltpu.roll(lower.astype(f32), 64, 1).astype(bf16)
    gpack_ref[...] = gpack
    slot_row = slotr_ref[...]
    for e in range(experts):
        hot = one_hot(slot_row, e, slots)
        rows = slice(e * slots, (e + 1) * slots)
        send_ref[rows, :] = dot(hot, n2).astype(bf16)
    if last:
        send_grads(slot_row, cot_ref[...], gpack, gxs_ref, gy_ref, experts, slots)


def shape(dims, dtype=f32):
    return jax.ShapeDtypeStruct(tuple(dims), dtype)


def whole_call(body, name, outs, scratch, args, flops):
    moved = sum(a.size * a.dtype.itemsize for a in args) + sum(
        o.size * o.dtype.itemsize for o in outs
    )
    return pl.pallas_call(
        body,
        out_shape=outs,
        in_specs=[pl.BlockSpec(memory_space=pltpu.VMEM)] * len(args),
        out_specs=[pl.BlockSpec(memory_space=pltpu.VMEM)] * len(outs),
        scratch_shapes=scratch,
        compiler_params=pltpu.CompilerParams(vmem_limit_bytes=VMEM),
        cost_estimate=pl.CostEstimate(flops=flops, bytes_accessed=moved, transcendentals=0),
        name=name,
    )(*args)


def forward_call(first, last, experts, slots, args):
    tokens = TREE
    sent = experts * slots
    outs = [] if first else [shape((tokens, D))]
    outs += [
        shape((tokens, D), bf16),
        shape((tokens, 3 * D), bf16),
        shape((tokens, D), bf16),
        shape((16, tokens)),
        shape((tokens, D)),
        shape((tokens, D), bf16),
        shape((40, tokens)),
        shape((tokens, 128)),
        shape((tokens, 128), bf16),
        shape((sent, D), bf16),
        shape((D, 128), bf16),
    ]
    if last:
        outs += [shape((sent, D), bf16), shape((sent, D), bf16)]
    padded = -(-tokens // 128) * 128
    scratch = [pltpu.VMEM((tokens, 128), f32), pltpu.VMEM((128, padded), f32)]
    body = functools.partial(forward_kernel, first, last, experts, slots)
    return whole_call(body, "block_forward", outs, scratch, args, 20 * 10**9)


def gating_kernel(last, experts, slots, *refs):
    refs = list(refs)
    gx_ref, n2_ref, y_ref, gxs_ref, slotr_ref, info_ref, chosen_ref, gcol_ref, small_ref = [
        refs.pop(0) for _ in range(9)
    ]
    z_ref, mix_ref = refs.pop(0), refs.pop(0)
    if last:
        mid_ref, slotc_ref = refs.pop(0), refs.pop(0)
    else:
        gz_ref = refs.pop(0)
    gn2_ref, gsm_ref, gmix_ref, gprev_ref = [refs.pop(0) for _ in range(4)]
    if last:
        out_ref = refs.pop(0)
    tokens = n2_ref.shape[0]
    size, block = row_blocks(tokens)
    small = small_ref[...].astype(f32).T
    small_half = small[0:32, :].astype(bf16)
    vectors = small[S_VEC : S_VEC + 2, :]
    slot_row = slotr_ref[...]
    ones = jnp.ones((16, D), bf16)
    row = lax.broadcasted_iota(jnp.int32, (16, slots), 0)
    scattered = jnp.zeros((16, tokens), f32)
    for e in range(experts):
        rows = slice(e * slots, (e + 1) * slots)
        inner = y_ref[rows, :].astype(f32) * gxs_ref[rows, :].astype(f32)
        upper, lower = split_bf16(inner)
        sums = dot_nt(ones, upper) + dot_nt(ones, lower)
        upper, lower = split_bf16(sums)
        lhs = jnp.where(row == e, upper.astype(f32), 0.0) + jnp.where(
            row == 8 + e, lower.astype(f32), 0.0
        )
        scattered = scattered + dot(lhs.astype(bf16), one_hot(slot_row, e, slots))
    gx = gx_ref[...].astype(f32)
    gx_half = gx.astype(bf16)
    n2 = n2_ref[...]
    upper, lower = split_bf16(gx * n2.astype(f32))
    gx_n2 = (dot_nt(ones, upper) + dot_nt(ones, lower))[0:1, :]
    gx_small = dot_nt(small_half, gx_half)
    prob = info_ref[16:32, :]
    chosen = chosen_ref[...]
    gates = prob * chosen
    trow = lax.broadcasted_iota(jnp.int32, (16, tokens), 0)
    gp = jnp.concatenate([scattered[0:8, :] + scattered[8:16, :], jnp.zeros((8, tokens), f32)], 0)
    gp = jnp.where(trow == experts + 1, gx_n2, jnp.where(trow < experts, gp, 0.0))
    crow = lax.broadcasted_iota(jnp.int32, (8, tokens), 0)
    glog = jnp.zeros((8, tokens), f32)
    coefs = jnp.zeros((8, tokens), f32)
    for c in range(2):
        a0 = info_ref[32 + 2 * c : 33 + 2 * c, :]
        a1 = info_ref[33 + 2 * c : 34 + 2 * c, :]
        gx_v = gx_small[S_VEC + c : S_VEC + c + 1, :]
        share = gates[experts + 2 + c : experts + 3 + c, :]
        gp = jnp.where(trow == experts + 2 + c, a0 * gx_n2 + a1 * gx_v, gp)
        gl = share * (gx_n2 - gx_v) * a0 * a1
        glog = jnp.where(crow == 2 * c, gl, jnp.where(crow == 2 * c + 1, -gl, glog))
        coefs = jnp.where(crow == c, share * a1, coefs)
    gp = gp * chosen
    gz = prob * (gp - jnp.sum(prob * gp, axis=0, keepdims=True))
    if not last:
        gz = gz + gz_ref[...]
    z = z_ref[...]
    gmix_ref[...] = lax.dot_general(
        z, gz, (((1,), (1,)), ((), ())), precision=lax.Precision.HIGHEST, preferred_element_type=f32
    )
    mix = mix_ref[...]
    gprev = jnp.zeros((16, tokens), f32)
    for o in range(experts + 4):
        gprev = gprev + mix[:, o : o + 1] * gz[o : o + 1, :]
    gprev_ref[...] = gprev
    allg = jnp.concatenate([gz, glog, jnp.zeros((8, tokens), f32)], axis=0)
    upper, lower = split_bf16(allg)
    gsm = dot(upper, n2) + dot(lower, n2)
    cu, cl = split_bf16(jnp.concatenate([coefs, jnp.zeros((8, tokens), f32)], axis=0))
    gvec = dot(cu, gx_half) + dot(cl, gx_half)
    gsm_ref[0:24, :] = gsm[0:24, :]
    gsm_ref[24:32, :] = jnp.concatenate(
        [jnp.zeros((2, D), f32), gvec[0:2, :], jnp.zeros((4, D), f32)], axis=0
    )
    both = jnp.concatenate([upper, lower], axis=0)
    twice = jnp.concatenate([small_half, small_half], axis=0)
    gn2_ref[...] = dot_tn(both, twice)

    def add(i, carry):
        rows = block(i)
        gn2_ref[rows, :] = gn2_ref[rows, :] + gcol_ref[rows, 16:17] * gx_ref[rows, :].astype(f32)
        if last:
            out_ref[rows, :] = combine_rows(
                rows, mid_ref, n2_ref, y_ref, gcol_ref, slotc_ref, vectors, experts, slots
            ).astype(bf16)
        return carry

    lax.fori_loop(0, BLOCKS, add, 0)


def gating_outputs(last):
    tokens = TREE
    outs = [shape((tokens, D)), shape((32, D)), shape((16, 16)), shape((16, tokens))]
    if last:
        outs += [shape((tokens, D), bf16)]
    return outs


def backward_kernel(first, experts, slots, *refs):
    refs = list(refs)
    gx_ref, gn2p_ref, gn2e_ref, slotc_ref, mid_ref, att_ref, w_ref, qkv_ref, n1_ref, x_ref = [
        refs.pop(0) for _ in range(10)
    ]
    biast_ref, lse_ref, gsm_ref = [refs.pop(0) for _ in range(3)]
    if not first:
        slotr_ref, gpack_ref = refs.pop(0), refs.pop(0)
    gout_ref, dw_ref = refs.pop(0), refs.pop(0)
    if not first:
        gxs_ref, gy_ref = refs.pop(0), refs.pop(0)
    gatt, go, gqkv, turn = refs
    tokens = n1_ref.shape[0]
    size, block = row_blocks(tokens)
    small = w_ref[:, W_SMALL:].astype(f32).T
    gain0 = small[S_GAIN : S_GAIN + 1, :]
    gain1 = small[S_GAIN + 1 : S_GAIN + 2, :]

    def enter(i, total):
        rows = block(i)
        gn2 = gn2p_ref[rows, :]
        slot = slotc_ref[rows, :]
        for e in range(experts):
            gn2 = gn2 + dot(one_hot_col(slot, e, slots), gn2e_ref[e * slots : (e + 1) * slots, :])
        middle = mid_ref[rows, :]
        r = inv_rms(middle)
        scaled = gain1 * gn2
        inner = jnp.mean(middle * scaled, axis=1, keepdims=True)
        gmid = gx_ref[rows, :].astype(f32) + r * scaled - middle * (r * r * r * inner)
        gout_ref[rows, :] = gmid
        half = gmid.astype(bf16)
        gatt[rows, :] = half
        go[rows, :] = dot_nt(half, w_ref[:, W_OUT:W_SMALL]).astype(bf16)
        return total + jnp.sum(gn2 * middle * r, axis=0, keepdims=True)

    ggain1 = lax.fori_loop(0, BLOCKS, enter, jnp.zeros((1, D), f32))
    lane = lax.broadcasted_iota(jnp.int32, (1, 128), 1)
    low_f = jnp.where(lane < HD, 1.0, 0.0)
    low = low_f.astype(bf16)
    high = (1.0 - low_f).astype(bf16)
    scale = HD**-0.5

    def out_grad(p, carry):
        here = pl.ds(pl.multiple_of(p * 128, 128), 128)
        dw_ref[here, W_OUT:W_SMALL] = dot_tn(att_ref[:, here], gatt[...]).astype(bf16)
        return carry

    lax.fori_loop(0, D // 128, out_grad, 0)
    spans = causal_spans(tokens)

    def pair(p, carry):
        here = pl.ds(pl.multiple_of(p * 128, 128), 128)
        lanes_k = pl.ds(pl.multiple_of(D + p * 128, 128), 128)
        lanes_v = pl.ds(pl.multiple_of(2 * D + p * 128, 128), 128)
        q = qkv_ref[:, here] * bf16(scale)
        k = qkv_ref[:, lanes_k]
        v = qkv_ref[:, lanes_v]
        g = go[:, here]
        turn[0:tokens, :] = g.astype(f32) * att_ref[:, here].astype(f32)
        inner = turn[...].T[:, 0:tokens]
        turn[0:tokens, :] = k.astype(f32)
        kt = turn[...].T[:, 0:tokens].astype(bf16)
        gq_t = []
        gk = [0.0] * len(spans)
        gv = [0.0] * len(spans)
        for h, mask in ((0, low), (1, high)):
            qh = q * mask
            gh = g * mask
            dsum = jnp.sum(inner[h * HD : (h + 1) * HD, :], axis=0, keepdims=True)
            lse = lse_ref[pl.ds(2 * p + h, 1), :]
            gq_h = []
            for n, (start, stop) in enumerate(spans):
                st = dot_nt(k[start:stop], qh[start:]) + biast_ref[start:stop, start:]
                pt = jnp.exp(st - lse[:, start:])
                gpt = dot_nt(v[start:stop], gh[start:])
                gst = (pt * (gpt - dsum[:, start:])).astype(bf16)
                gv[n] = gv[n] + dot(pt.astype(bf16), gh[start:])
                gk[n] = gk[n] + dot(gst, qh[start:])
                part = dot(kt[h * HD : (h + 1) * HD, start:stop], gst)
                gq_h.append(part)
            cols = []
            for n, (start, stop) in enumerate(spans):
                piece = 0.0
                for m in range(n + 1):
                    origin = spans[m][0]
                    piece = piece + gq_h[m][:, start - origin : stop - origin]
                cols.append(piece)
            gq_t.append(jnp.concatenate(cols, axis=1))
        turn_t = jnp.concatenate(gq_t, axis=0) * scale
        pad = turn.shape[0] - tokens
        turn_t = jnp.concatenate([turn_t, jnp.zeros((128, pad), f32)], axis=1)
        gqkv[:, here] = turn_t.T[0:tokens, :].astype(bf16)
        for n, (start, stop) in enumerate(spans):
            gqkv[start:stop, lanes_k] = gk[n].astype(bf16)
            gqkv[start:stop, lanes_v] = gv[n].astype(bf16)
        return carry

    turn[...] = jnp.zeros_like(turn)
    lax.fori_loop(0, H // 2, pair, 0)

    def in_grad(p, carry):
        here = pl.ds(pl.multiple_of(p * 128, 128), 128)
        dw_ref[here, 0:W_OUT] = dot_tn(n1_ref[:, here], gqkv[...]).astype(bf16)
        return carry

    lax.fori_loop(0, D // 128, in_grad, 0)

    def leave(i, total):
        rows = block(i)
        gn1 = dot_nt(gqkv[rows, :], w_ref[:, 0:W_OUT])
        x = x_ref[rows, :].astype(f32)
        r = inv_rms(x)
        scaled = gain0 * gn1
        inner = jnp.mean(x * scaled, axis=1, keepdims=True)
        gx = gout_ref[rows, :] + r * scaled - x * (r * r * r * inner)
        gout_ref[rows, :] = gx
        gatt[rows, :] = gx.astype(bf16)
        return total + jnp.sum(gn1 * x * r, axis=0, keepdims=True)

    ggain0 = lax.fori_loop(0, BLOCKS, leave, jnp.zeros((1, D), f32))
    rows = jnp.concatenate(
        [gsm_ref[0:24, :], ggain0, ggain1, gsm_ref[26:32, :], jnp.zeros((96, D), f32)], axis=0
    )
    dw_ref[:, W_SMALL:] = rows.T.astype(bf16)
    if not first:
        send_grads(slotr_ref[...], gatt[...], gpack_ref[...], gxs_ref, gy_ref, experts, slots)


def backward_call(first, experts, slots, args):
    tokens = TREE
    sent = experts * slots
    outs = [shape((tokens, D)), shape((D, W_ALL), bf16)]
    if not first:
        outs += [shape((sent, D), bf16), shape((sent, D), bf16)]
    padded = -(-tokens // 128) * 128
    scratch = [
        pltpu.VMEM((tokens, D), bf16),
        pltpu.VMEM((tokens, D), bf16),
        pltpu.VMEM((tokens, 3 * D), bf16),
        pltpu.VMEM((padded, 128), f32),
    ]
    body = functools.partial(backward_kernel, first, experts, slots)
    return whole_call(body, "block_backward", outs, scratch, args, 40 * 10**9)


class Packing:
    def __init__(self, shards, part, ff):
        self.shards, self.part, self.ff = shards, part, ff
        self.padded = -(-part // 16) * 16
        self.chunks = ff // 256
        self.own = ff // shards
        self.down = 2 * self.chunks * self.padded
        self.rows = self.down + (D // 256) * self.own

    def pack(self, gate, up, down):
        pieces = []
        for wide in (gate, up):
            cut = wide.reshape(self.part, self.chunks, 256).transpose(1, 0, 2)
            cut = jnp.pad(cut, [(0, 0), (0, self.padded - self.part), (0, 0)])
            pieces.append(cut.reshape(self.chunks * self.padded, 256))
        pieces.append(
            down.reshape(self.own, D // 256, 256).transpose(1, 0, 2).reshape(-1, 256)
        )
        return jnp.concatenate(pieces, axis=0)

    def wide_part(self, ref, n, j):
        at = pl.multiple_of((n * self.chunks + j) * self.padded, 16)
        return ref[:, pl.ds(at, self.padded), :][:, : self.part, :].reshape(D, 256)

    def tall_part(self, ref, j):
        group = 256 // self.own
        here = pl.ds(j * group, group)
        pieces = []
        for c in range(D // 256):
            at = self.down + c * self.own
            pieces.append(ref[here, at : at + self.own, :].reshape(256, 256))
        return jnp.concatenate(pieces, axis=1)

    def put_wide(self, ref, n, j, grad):
        at = pl.multiple_of((n * self.chunks + j) * self.padded, 16)
        ref[:, pl.ds(at, self.part), :] = grad.reshape(self.shards, self.part, 256)

    def put_tall(self, ref, j, grad):
        group = 256 // self.own
        for c in range(D // 256):
            at = self.down + c * self.own
            ref[pl.ds(j * group, group), at : at + self.own, :] = grad[
                :, c * 256 : (c + 1) * 256
            ].reshape(group, self.own, 256)


class Exchange:
    def __init__(self, experts, slots):
        self.experts, self.slots = experts, slots
        first = -(-slots // 32) * 16
        self.waves = ((0, first), (first, slots - first))
        self.ranges = [(0, slots)]
        for _, size in self.waves:
            start = self.ranges[-1][0] + self.ranges[-1][1]
            self.ranges.append((start, (experts - 1) * size))
        self.total = experts * slots

    def held(self, wave, d):
        size = self.waves[wave][1]
        return pl.ds(self.ranges[1 + wave][0] + (d - 1) * size, size)

    def slot(self, device, wave):
        offset, size = self.waves[wave]
        return pl.ds(pl.multiple_of(device * self.slots + offset, 16), size)


MESH = pl.DeviceIdType.MESH


def greet(experts):
    me = lax.axis_index("expert")
    barrier = pltpu.get_barrier_semaphore()
    for d in range(1, experts):
        pl.semaphore_signal(
            barrier, inc=1, device_id={"expert": lax.rem(me + d, experts)}, device_id_type=MESH
        )
    pl.semaphore_wait(barrier, experts - 1)


def out_copies(ex, wave, src, dst, sends, recvs):
    me = lax.axis_index("expert")
    copies = []
    for d in range(1, ex.experts):
        to = lax.rem(me + d, ex.experts)
        copies.append(
            pltpu.make_async_remote_copy(
                src_ref=src.at[ex.slot(to, wave)],
                dst_ref=dst.at[ex.held(wave, d)],
                send_sem=sends.at[wave, d - 1],
                recv_sem=recvs.at[wave, d - 1],
                device_id={"expert": to},
                device_id_type=MESH,
            )
        )
    return copies


def back_copies(ex, wave, n, src, dst, sends, recvs):
    me = lax.axis_index("expert")
    copies = []
    for d in range(1, ex.experts):
        copies.append(
            pltpu.make_async_remote_copy(
                src_ref=src.at[ex.held(wave, d)],
                dst_ref=dst.at[ex.slot(me, wave)],
                send_sem=sends.at[n, wave, d - 1],
                recv_sem=recvs.at[n, wave, d - 1],
                device_id={"expert": lax.rem(me + ex.experts - d, ex.experts)},
                device_id_type=MESH,
            )
        )
    return copies


def own_slots(ex):
    me = lax.axis_index("expert")
    return pl.ds(pl.multiple_of(me * ex.slots, 16), ex.slots)


def dispatch_kernel(ex, send, recv, sends, recvs):
    greet(ex.experts)
    copies = out_copies(ex, 0, send, recv, sends, recvs)
    copies += out_copies(ex, 1, send, recv, sends, recvs)
    for copy in copies:
        copy.start()
    recv[0 : ex.slots, :] = send[own_slots(ex), :]
    for copy in copies:
        copy.wait()


def dispatch_call(ex, rows):
    vmem = pl.BlockSpec(memory_space=pltpu.VMEM)
    return pl.pallas_call(
        functools.partial(dispatch_kernel, ex),
        out_shape=shape((ex.total, D), bf16),
        in_specs=[vmem],
        out_specs=vmem,
        scratch_shapes=[pltpu.SemaphoreType.DMA((2, ex.experts - 1))] * 2,
        compiler_params=pltpu.CompilerParams(
            vmem_limit_bytes=8 << 20, collective_id=3, has_side_effects=True
        ),
        cost_estimate=pl.CostEstimate(flops=35 * 10**9, bytes_accessed=10**6, transcendentals=0),
        name="dispatch",
    )(rows)


def exchange_kernel(mode, pack, ex, *refs):
    refs = list(refs)
    forward, backward = mode in ("forward", "both"), mode in ("backward", "both")
    recv_n = refs.pop(0)
    w_hbm = refs.pop(0)
    gating = []
    if backward:
        send_g = refs.pop(0)
        if mode == "backward":
            gate_hbm, up_hbm = refs.pop(0), refs.pop(0)
        gating = [refs.pop(0) for _ in range(12)]
    if forward:
        back_y = refs.pop(0)
    if mode == "forward":
        gates, ups = refs.pop(0), refs.pop(0)
    else:
        back_g, dw = refs.pop(0), refs.pop(0)
        gating_outs = [refs.pop(0) for _ in range(5 if mode == "both" else 4)]
    if forward:
        out_y, acc_y = refs.pop(0), refs.pop(0)
    if backward:
        recv_g, out_g, hids, gates, ups, rows_t, acc_g = [refs.pop(0) for _ in range(7)]
        w = dw
    else:
        w = refs.pop(0)
    sends, recvs, backs, gots, local = refs

    loads = [pltpu.make_async_copy(w_hbm, w, local.at[0])]
    if mode == "backward":
        loads.append(pltpu.make_async_copy(gate_hbm, gates, local.at[1]))
        loads.append(pltpu.make_async_copy(up_hbm, ups, local.at[2]))
    for copy in loads:
        copy.start()
    greet(ex.experts)

    def work(start, size):
        rows = slice(start, start + size)
        part = slice(0, size)
        if forward:
            acc_y[part, :] = jnp.zeros((size, D), f32)
        if backward:
            acc_g[part, :] = jnp.zeros((size, D), f32)

        def chunk(j, carry):
            lanes = pl.ds(pl.multiple_of(j * 256, 256), 256)
            gate_w, up_w = pack.wide_part(w, 0, j), pack.wide_part(w, 1, j)
            down_w = pack.tall_part(w, j)
            if forward:
                r = recv_n[rows, :]
                gate, up = dot(r, gate_w), dot(r, up_w)
                if mode == "forward":
                    gates[rows, lanes] = gate.astype(bf16)
                    ups[rows, lanes] = up.astype(bf16)
            else:
                gate, up = gates[rows, lanes].astype(f32), ups[rows, lanes].astype(f32)
            s = jax.nn.sigmoid(gate)
            act = gate * s
            hid = (act * up).astype(bf16)
            if forward:
                acc_y[part, :] = acc_y[part, :] + dot(hid, down_w)
            if backward:
                hids[rows, lanes] = hid
                ghid = dot_nt(recv_g[rows, :], down_w)
                guv = (ghid * act).astype(bf16)
                ggu = (ghid * up * (s * (1.0 + gate * (1.0 - s)))).astype(bf16)
                gates[rows, lanes] = ggu
                ups[rows, lanes] = guv
                acc_g[part, :] = acc_g[part, :] + dot_nt(ggu, gate_w) + dot_nt(guv, up_w)
            return carry

        lax.fori_loop(0, pack.chunks, chunk, 0)
        if forward:
            out_y[rows, :] = acc_y[part, :].astype(bf16)
        if backward:
            out_g[rows, :] = acc_g[part, :].astype(bf16)

    def send_back(wave):
        ys = back_copies(ex, wave, 0, out_y, back_y, backs, gots) if forward else []
        gs = back_copies(ex, wave, 1, out_g, back_g, backs, gots) if backward else []
        for copy in ys + gs:
            copy.start()
        return ys, gs

    if backward:
        waves = [out_copies(ex, n, send_g, recv_g, sends, recvs) for n in range(2)]
        for copy in waves[0]:
            copy.start()
        recv_g[0 : ex.slots, :] = send_g[own_slots(ex), :]
        if mode == "backward":
            gating_kernel(False, ex.experts, ex.slots, *gating, *gating_outs)
    for copy in loads:
        copy.wait()
    if backward:
        work(*ex.ranges[0])
        for copy in waves[0]:
            copy.wait_send()
        for copy in waves[1]:
            copy.start()
        for copy in waves[0]:
            copy.wait_recv()
    work(*ex.ranges[1])
    ys, gs = send_back(0)
    if backward:
        for copy in waves[1]:
            copy.wait()
    work(*ex.ranges[2])
    more = send_back(1)
    ys, gs = ys + more[0], gs + more[1]
    if mode == "forward":
        work(*ex.ranges[0])
    if forward:
        back_y[own_slots(ex), :] = out_y[0 : ex.slots, :]
    if backward:
        back_g[own_slots(ex), :] = out_g[0 : ex.slots, :]
        rows_t[...] = recv_n[...].T
        if pack.padded != pack.part:
            dw[...] = jnp.zeros_like(dw)

        def weights(j, carry):
            lanes = pl.ds(pl.multiple_of(j * 256, 256), 256)
            pack.put_wide(dw, 0, j, dot(rows_t[...], gates[:, lanes]).astype(bf16))
            pack.put_wide(dw, 1, j, dot(rows_t[...], ups[:, lanes]).astype(bf16))
            pack.put_tall(dw, j, dot_tn(hids[:, lanes], recv_g[...]).astype(bf16))
            return carry

        lax.fori_loop(0, pack.chunks, weights, 0)
    for copy in ys:
        copy.wait()
    if mode == "both":
        gating_kernel(True, ex.experts, ex.slots, *gating[:2], back_y, *gating[2:], *gating_outs)
    for copy in gs:
        copy.wait()


EXCHANGE_IDS = {"forward": 0, "both": 1, "backward": 2}


def exchange_call(mode, pack, ex, args):
    rows, ff = ex.total, pack.ff
    forward, backward = mode in ("forward", "both"), mode in ("backward", "both")
    flat, wide = shape((rows, D), bf16), shape((rows, ff), bf16)
    packed = (pack.shards, pack.rows, 256)
    most = max(size for _, size in ex.ranges)
    vmem = pl.BlockSpec(memory_space=pltpu.VMEM)
    far = pl.BlockSpec(memory_space=pl.ANY)
    in_specs = [vmem] * len(args)
    in_specs[1] = far
    scratch = []
    if mode == "forward":
        outs = [flat, wide, wide]
    elif mode == "both":
        outs = [flat, flat, shape(packed, bf16)] + gating_outputs(True)
    else:
        in_specs[3] = in_specs[4] = far
        outs = [flat, shape(packed, bf16)] + gating_outputs(False)
    if forward:
        scratch += [pltpu.VMEM((rows, D), bf16), pltpu.VMEM((most, D), f32)]
    if backward:
        scratch += [pltpu.VMEM((rows, D), bf16)] * 2
        scratch += [pltpu.VMEM((rows, ff), bf16)] * 3
        scratch += [pltpu.VMEM((D, rows), bf16), pltpu.VMEM((most, D), f32)]
    else:
        scratch.append(pltpu.VMEM(packed, bf16))
    scratch += [pltpu.SemaphoreType.DMA((2, ex.experts - 1))] * 2
    scratch += [pltpu.SemaphoreType.DMA((2, 2, ex.experts - 1))] * 2
    scratch.append(pltpu.SemaphoreType.DMA((3,)))
    work = 6 * rows * D * ff * (1 if mode == "forward" else 2 if mode == "backward" else 3)
    return pl.pallas_call(
        functools.partial(exchange_kernel, mode, pack, ex),
        out_shape=outs,
        in_specs=in_specs,
        out_specs=[vmem] * len(outs),
        scratch_shapes=scratch,
        compiler_params=pltpu.CompilerParams(
            vmem_limit_bytes=62 << 20, collective_id=EXCHANGE_IDS[mode], has_side_effects=True
        ),
        cost_estimate=pl.CostEstimate(
            flops=work + 40 * 10**9, bytes_accessed=6 * D * ff, transcendentals=0
        ),
        name="experts_" + mode,
    )(*args)


def expert_outputs_kernel(pack, first_ref, second_ref, gate_ref, up_ref, down_ref):
    for l, ref in enumerate((first_ref, second_ref)):
        for n, out in enumerate((gate_ref, up_ref)):
            for j in range(pack.chunks):
                at = (n * pack.chunks + j) * pack.padded
                out[l, :, j * 256 : (j + 1) * 256] = ref[at : at + pack.part, :].astype(f32)
        for c in range(D // 256):
            at = pack.down + c * pack.own
            down_ref[l, :, c * 256 : (c + 1) * 256] = ref[at : at + pack.own, :].astype(f32)


def expert_outputs(pack, grads):
    wide = shape((LAYERS, pack.part, pack.ff))
    outs = [wide, wide, shape((LAYERS, pack.own, D))]
    body = functools.partial(expert_outputs_kernel, pack)
    return whole_call(body, "expert_outputs", outs, [], grads, 10**6)


def dense_outputs_kernel(
    part, labels, first_ref, second_ref, proj_ref, out_ref, gain_ref, router_ref, vec_ref, const_ref,
    turn,
):
    for l, ref in enumerate((first_ref, second_ref)):
        for c in range(3):
            proj_ref[l, c] = ref[:, c * D : (c + 1) * D].astype(f32)
        out_ref[l] = ref[:, W_OUT:W_SMALL].astype(f32)
        small = ref[:, W_SMALL:].astype(f32)
        router_ref[l] = small[:, 0:labels]
        for c in range(2):
            const_ref[l, c] = small[:, S_CONST + 2 * c : S_CONST + 2 * c + 2]
        turn[0:part, :] = small
        rows = turn[...].T
        gain_ref[l] = rows[S_GAIN : S_GAIN + 2, 0:part]
        vec_ref[l] = rows[S_VEC : S_VEC + 2, 0:part]


def dense_outputs(part, labels, grads):
    outs = [
        shape((LAYERS, 3, part, D)),
        shape((LAYERS, part, D)),
        shape((LAYERS, 2, part)),
        shape((LAYERS, part, labels)),
        shape((LAYERS, 2, part)),
        shape((LAYERS, 2, part, 2)),
    ]
    body = functools.partial(dense_outputs_kernel, part, labels)
    return whole_call(body, "dense_outputs", outs, [pltpu.VMEM((128, 128), f32)], grads, 10**6)


def on_device(
    hidden_in,
    prior_logits,
    project_weight,
    output_weight,
    norm_gain,
    router_weight,
    mixing_weight,
    const_vector,
    const_weight,
    gate_weight,
    up_weight,
    down_weight,
    routes,
    priority,
    leaf_parent,
    cotangent,
):
    experts = lax.axis_size("expert")
    total_experts = experts + 4
    tokens = hidden_in.shape[0]
    capacity = 9 * tokens * TOP // (8 * total_experts)
    slots = -(-capacity // 16) * 16
    part = project_weight.shape[2]

    def pad_cols(a, width):
        return jnp.pad(a, [(0, 0)] * (a.ndim - 1) + [(0, width - a.shape[-1])])

    dense = []
    experts_w = []
    pack = Packing(lax.axis_size("shard"), part, gate_weight.shape[3])
    for l in range(LAYERS):
        small = jnp.concatenate(
            [
                pad_cols(router_weight[l], S_CONST),
                const_weight[l, 0],
                const_weight[l, 1],
                jnp.zeros((part, S_GAIN - S_CONST - 4), bf16),
                norm_gain[l].T,
                const_vector[l].T,
            ],
            axis=1,
        )
        packed = jnp.concatenate(
            [project_weight[l, c] for c in range(3)] + [output_weight[l], pad_cols(small, 128)],
            axis=1,
        )
        dense.append(lax.all_gather(packed, "shard", axis=0, tiled=True))
        mine = pack.pack(gate_weight[l, 0], up_weight[l, 0], down_weight[l, 0])
        experts_w.append(lax.all_gather(mine, "shard", axis=0, tiled=False))

    ranking = priority[0]
    earlier = (ranking[None, :] < ranking[:, None]).astype(bf16)
    labels = jnp.arange(total_experts, dtype=jnp.int32)
    hits = jnp.sum((routes[:, :, :, None] == labels).astype(f32), axis=2)
    chosen_rows = [jnp.pad(hits[l].T, [(0, 16 - total_experts), (0, 0)]) for l in range(LAYERS)]
    loaded = jnp.concatenate([hits[l, :, :experts] for l in range(LAYERS)], axis=1)
    loaded_half = loaded.astype(bf16)
    rank_col = dot(earlier, loaded_half)
    rank_row = lax.dot_general(
        loaded_half, earlier, (((0,), (1,)), ((), ())), preferred_element_type=f32
    )
    slot_col_all = jnp.where((loaded > 0) & (rank_col < capacity), rank_col, -1.0)
    slot_row_all = jnp.where((loaded.T > 0) & (rank_row < capacity), rank_row, -1.0)
    slot_col = [slot_col_all[:, l * experts : (l + 1) * experts] for l in range(LAYERS)]
    slot_row = [
        jnp.pad(
            slot_row_all[l * experts : (l + 1) * experts],
            [(0, 8 - experts), (0, 0)],
            constant_values=-1.0,
        )
        for l in range(LAYERS)
    ]
    visible = tree_visible(leaf_parent[0])
    bias = jnp.where(visible, 0.0, masked_fill)
    bias_t = jnp.where(visible.T, 0.0, masked_fill)
    mixes = [
        jnp.pad(mixing_weight[l], [(0, 16 - total_experts), (0, 16 - total_experts)])
        for l in range(LAYERS)
    ]
    z_rows = jnp.pad(prior_logits.T, [(0, 16 - total_experts), (0, 0)])

    ex = Exchange(experts, slots)
    saved = []
    front = [hidden_in]
    x_now = hidden_in
    for l in range(LAYERS):
        last = l == LAYERS - 1
        args = front + [dense[l], bias, z_rows, mixes[l].T, chosen_rows[l], slot_row[l]]
        if last:
            args.append(cotangent)
        outs = list(forward_call(l == 0, last, experts, slots, args))
        if l > 0:
            x_now = outs.pop(0)
        n1, qkv, att, lse, middle, n2, info, gcol, gpack, send, small = outs[:11]
        keep = dict(
            x=x_now, n1=n1, qkv=qkv, att=att, lse=lse, middle=middle, n2=n2, info=info,
            gcol=gcol, gpack=gpack, z=z_rows, small=small,
        )
        keep["received"] = dispatch_call(ex, send)
        if last:
            gating = [
                cotangent, n2, outs[11], slot_row[l], info, chosen_rows[l], gcol, small, z_rows,
                mixes[l], middle, slot_col[l],
            ]
            done = exchange_call(
                "both", pack, ex, [keep["received"], experts_w[l], outs[12]] + gating
            )
            keep["y"], keep["gin"], keep["dw"] = done[:3]
            keep["gating"] = done[3:]
        else:
            keep["y"], keep["gate"], keep["up"] = exchange_call(
                "forward", pack, ex, [keep["received"], experts_w[l]]
            )
        front = [middle, n2, keep["y"], gcol, slot_col[l], small]
        z_rows = info[0:16]
        saved.append(keep)

    gx = cotangent
    gz = None
    dense_grads = [None] * LAYERS
    mix_grads = [None] * LAYERS
    expert_grads = [None] * LAYERS
    hidden_out = None
    for l in range(LAYERS - 1, -1, -1):
        last = l == LAYERS - 1
        keep = saved[l]
        if not last:
            gating = [
                gx, keep["n2"], keep["y"], keep["gxs"], slot_row[l], keep["info"], chosen_rows[l],
                keep["gcol"], keep["small"], keep["z"], mixes[l], gz,
            ]
            done = exchange_call(
                "backward", pack, ex,
                [keep["received"], experts_w[l], keep["gy"], keep["gate"], keep["up"]] + gating,
            )
            keep["gin"], keep["dw"] = done[:2]
            keep["gating"] = done[2:]
        gn2, gsm, mix_grads[l], gz = keep["gating"][:4]
        if last:
            hidden_out = keep["gating"][4]
        d_experts, gn2 = lax.optimization_barrier((keep["dw"], gn2))
        if not last:
            gn2, dense_grads[l + 1] = lax.optimization_barrier((gn2, dense_grads[l + 1]))
        expert_grads[l] = lax.psum_scatter(d_experts, "shard", scatter_dimension=0, tiled=False)
        args = [
            gx, gn2, keep["gin"], slot_col[l], keep["middle"], keep["att"], dense[l], keep["qkv"],
            keep["n1"], keep["x"], bias_t, keep["lse"], gsm,
        ]
        if l > 0:
            args += [slot_row[l - 1], saved[l - 1]["gpack"]]
        outs = backward_call(l == 0, experts, slots, args)
        gx, d_dense = outs[:2]
        d_dense, expert_grads[l] = lax.optimization_barrier((d_dense, expert_grads[l]))
        if l > 0:
            saved[l - 1]["gxs"] = outs[2]
            gy, d_dense = lax.optimization_barrier((outs[3], d_dense))
            saved[l - 1]["gy"] = gy
        if l == 0:
            mix_grads[0], d_dense = lax.optimization_barrier((mix_grads[0], d_dense))
        dense_grads[l] = lax.psum_scatter(d_dense, "shard", scatter_dimension=0, tiled=True)

    both_dense = lax.psum(jnp.stack(dense_grads), "expert")
    dense_grads = [both_dense[l] for l in range(LAYERS)]
    mixing_total = lax.psum(jnp.stack(mix_grads), ("expert", "shard"))
    gate_grad, up_grad, down_grad = expert_outputs(pack, expert_grads)
    project_grad, output_grad, gain_grad, router_grad, vector_grad, const_grad = dense_outputs(
        part, total_experts, dense_grads
    )
    return (
        hidden_out,
        gx,
        gz[0:total_experts].T,
        project_grad,
        output_grad,
        gain_grad,
        router_grad,
        mixing_total[:, 0:total_experts, 0:total_experts],
        vector_grad,
        const_grad,
        gate_grad[:, None],
        up_grad[:, None],
        down_grad[:, None],
    )


def solution(mesh):
    both = ("expert", "shard")
    in_specs = (
        P(both, None),
        P(both, None),
        P(None, None, "shard", None),
        P(None, "shard", None),
        P(None, None, "shard"),
        P(None, "shard", None),
        P(),
        P(None, None, "shard"),
        P(None, None, "shard", None),
        P(None, "expert", "shard", None),
        P(None, "expert", "shard", None),
        P(None, "expert", "shard", None),
        P(None, both, None),
        P(both, None),
        P(both, None),
        P(both, None),
    )
    out_specs = (
        P(both, None),
        P(both, None),
        P(both, None),
        P(None, None, "shard", None),
        P(None, "shard", None),
        P(None, None, "shard"),
        P(None, "shard", None),
        P(),
        P(None, None, "shard"),
        P(None, None, "shard", None),
        P(None, "expert", "shard", None),
        P(None, "expert", "shard", None),
        P(None, "expert", "shard", None),
    )
    return jax.shard_map(
        on_device, mesh=mesh, in_specs=in_specs, out_specs=out_specs, check_vma=False
    )
```

```python
import functools

import jax
import jax.numpy as jnp
from jax import lax
from jax.experimental import pallas as pl
from jax.experimental.pallas import tpu as pltpu
from jax.sharding import PartitionSpec as P

D = 768
H = 12
HD = 64
TOP = 2
LAYERS = 2
TRUNK = 320
BRANCH = 64
LEAF = 32
TREE = 832

W_OUT = 3 * D
W_SMALL = 4 * D
W_ALL = 4 * D + 128
S_CONST = 16
S_GAIN = 24
S_VEC = 26

epsilon = 1e-06
masked_fill = -1e30
f32 = jnp.float32
bf16 = jnp.bfloat16
BLOCKS = 4
VMEM = 56 << 20


def dot(a, b):
    return jnp.dot(a, b, preferred_element_type=f32)


def dot_nt(a, b):
    return lax.dot_general(a, b, (((1,), (1,)), ((), ())), preferred_element_type=f32)


def dot_tn(a, b):
    return lax.dot_general(a, b, (((0,), (0,)), ((), ())), preferred_element_type=f32)


def split_bf16(v):
    high = v.astype(bf16)
    return high, (v - high.astype(f32)).astype(bf16)


def inv_rms(v):
    return lax.rsqrt(jnp.mean(v * v, axis=1, keepdims=True) + epsilon)


def tree_visible(parents):
    position = jnp.arange(TREE, dtype=jnp.int32)
    offset = position - TRUNK
    segment = jnp.where(
        position < TRUNK,
        0,
        jnp.where(offset < 4 * BRANCH, 1 + offset // BRANCH, 5 + (offset - 4 * BRANCH) // LEAF),
    )
    leaf_hits = (segment[:, None] - 5 == jnp.arange(8, dtype=jnp.int32)[None, :]).astype(jnp.int32)
    upper = jnp.where(segment >= 5, 1 + jnp.sum(leaf_hits * parents[None, :], axis=1), 0)
    key_segment = segment[None, :]
    causal = position[None, :] <= position[:, None]
    return causal & (
        (key_segment == segment[:, None]) | (key_segment == 0) | (key_segment == upper[:, None])
    )


def one_hot(slot_row, e, slots):
    row = lax.broadcasted_iota(jnp.int32, (slots, slot_row.shape[1]), 0).astype(f32)
    return jnp.where(row == slot_row[e : e + 1, :], 1.0, 0.0).astype(bf16)


def one_hot_col(slot_col, e, slots, scale=None):
    lane = lax.broadcasted_iota(jnp.int32, (slot_col.shape[0], slots), 1).astype(f32)
    value = 1.0 if scale is None else scale
    return jnp.where(lane == slot_col[:, e : e + 1], value, 0.0).astype(bf16)


def combine_rows(rows, middle_ref, n2_ref, y_ref, gcol_ref, slotc_ref, vectors, experts, slots):
    gcol = gcol_ref[rows, :]
    slot = slotc_ref[rows, :]
    total = middle_ref[rows, :] + gcol[:, 16:17] * n2_ref[rows, :].astype(f32)
    for c in range(2):
        total = total + gcol[:, 17 + c : 18 + c] * vectors[c : c + 1, :]
    for e in range(experts):
        weight = one_hot_col(slot, e, slots, gcol[:, e : e + 1])
        total = total + dot(weight, y_ref[e * slots : (e + 1) * slots, :])
    return total


def send_grads(slot_row, gx, gpack, gxs_ref, gy_ref, experts, slots):
    for e in range(experts):
        hot = one_hot(slot_row, e, slots)
        rows = slice(e * slots, (e + 1) * slots)
        got = dot(hot, gx)
        gates = dot(hot, gpack)
        gxs_ref[rows, :] = got.astype(bf16)
        gy_ref[rows, :] = (got * (gates[:, e : e + 1] + gates[:, 64 + e : 65 + e])).astype(bf16)


def row_blocks(tokens):
    size = tokens // BLOCKS
    return size, lambda i: pl.ds(pl.multiple_of(i * size, 16), size)


def causal_spans(tokens):
    edges = [0, 384, 640, tokens]
    return list(zip(edges[:-1], edges[1:]))


def forward_kernel(first, last, experts, slots, *refs):
    refs = list(refs)
    if first:
        x_in = refs.pop(0)
    else:
        mid_prev, n2_prev, y_ref, gcol_prev, slotc_prev, w_prev = [refs.pop(0) for _ in range(6)]
    w_ref, bias_ref, z_ref, mixt_ref, chosen_ref, slotr_ref = [refs.pop(0) for _ in range(6)]
    if last:
        cot_ref = refs.pop(0)
    if not first:
        x_out = refs.pop(0)
    n1_ref, qkv_ref, att_ref, lse_ref, mid_ref, n2_ref, info_ref, gcol_ref, gpack_ref, send_ref = [
        refs.pop(0) for _ in range(10)
    ]
    small_out = refs.pop(0)
    small_out[...] = w_ref[:, W_SMALL:]
    if last:
        gxs_ref, gy_ref = refs.pop(0), refs.pop(0)
    lse_cols, turn = refs
    tokens = n1_ref.shape[0]
    size, block = row_blocks(tokens)
    small = w_ref[:, W_SMALL:].astype(f32).T
    gain0 = small[S_GAIN : S_GAIN + 1, :]
    gain1 = small[S_GAIN + 1 : S_GAIN + 2, :]
    if not first:
        vectors_prev = w_prev[...].astype(f32).T[S_VEC : S_VEC + 2, :]

    def project(i, carry):
        rows = block(i)
        if first:
            x = x_in[rows, :].astype(f32)
        else:
            x = combine_rows(
                rows, mid_prev, n2_prev, y_ref, gcol_prev, slotc_prev, vectors_prev, experts, slots
            )
            x_out[rows, :] = x
        n1 = (x * inv_rms(x) * gain0).astype(bf16)
        n1_ref[rows, :] = n1
        for c in range(3):
            qkv_ref[rows, c * D : (c + 1) * D] = dot(n1, w_ref[:, c * D : (c + 1) * D]).astype(bf16)
        return carry

    lax.fori_loop(0, BLOCKS, project, 0)
    lane = lax.broadcasted_iota(jnp.int32, (1, 128), 1)
    low_f = jnp.where(lane < HD, 1.0, 0.0)
    low = low_f.astype(bf16)
    high = (1.0 - low_f).astype(bf16)
    lse_cols[...] = jnp.zeros_like(lse_cols)

    def pair(p, carry):
        k = qkv_ref[:, pl.ds(pl.multiple_of(D + p * 128, 128), 128)]
        v = qkv_ref[:, pl.ds(pl.multiple_of(2 * D + p * 128, 128), 128)]
        va = v * low + high
        vb = v * high + low
        here = pl.ds(pl.multiple_of(p * 128, 128), 128)
        for start, stop in causal_spans(tokens):
            q = qkv_ref[start:stop, here] * bf16(HD**-0.5)
            outs = []
            for mask, value in ((low, va), (high, vb)):
                s = dot_nt(q * mask, k[:stop]) + bias_ref[start:stop, :stop]
                peak = jnp.max(s, axis=1, keepdims=True)
                expo = jnp.exp(s - peak).astype(bf16)
                outs.append((dot(expo, value[:stop]), peak))
            (oa, ma), (ob, mb) = outs
            numer = jnp.where(lane < HD, oa, ob)
            denom = pltpu.roll(jnp.where(lane < HD, ob, oa), HD, 1)
            att_ref[start:stop, here] = (numer / denom).astype(bf16)
            la = ma + jnp.log(oa[:, HD : HD + 1])
            lb = mb + jnp.log(ob[:, 0:1])
            old = lse_cols[start:stop, :]
            lse_cols[start:stop, :] = jnp.where(
                lane == 2 * p, la, jnp.where(lane == 2 * p + 1, lb, old)
            )
        return carry

    lax.fori_loop(0, H // 2, pair, 0)
    lse_ref[...] = lse_cols[...].T[0:16, :]

    def finish(i, carry):
        rows = block(i)
        if first:
            x = x_in[rows, :].astype(f32)
        else:
            x = x_out[rows, :]
        middle = x + dot(att_ref[rows, :], w_ref[:, W_OUT:W_SMALL])
        mid_ref[rows, :] = middle
        n2_ref[rows, :] = (middle * inv_rms(middle) * gain1).astype(bf16)
        return carry

    lax.fori_loop(0, BLOCKS, finish, 0)
    n2 = n2_ref[...]
    scores = dot_nt(small[0:32, :].astype(bf16), n2)
    logits = scores[0:16, :]
    z = z_ref[...]
    mixt = mixt_ref[...]
    for i in range(experts + 4):
        logits = logits + mixt[:, i : i + 1] * z[i : i + 1, :]
    row = lax.broadcasted_iota(jnp.int32, (16, tokens), 0)
    valid = row < experts + 4
    peak = jnp.max(jnp.where(valid, logits, masked_fill), axis=0, keepdims=True)
    expo = jnp.where(valid, jnp.exp(jnp.minimum(logits - peak, 0.0)), 0.0)
    prob = expo / jnp.sum(expo, axis=0, keepdims=True)
    gates = prob * chosen_ref[...]
    info_ref[0:16, :] = logits
    info_ref[16:32, :] = prob
    turn[...] = jnp.zeros_like(turn)
    turn[0:16, 0:tokens] = gates
    own = gates[experts + 1 : experts + 2, :]
    alphas = []
    for c in range(2):
        l0 = scores[S_CONST + 2 * c : S_CONST + 2 * c + 1, :]
        l1 = scores[S_CONST + 2 * c + 1 : S_CONST + 2 * c + 2, :]
        a0 = jax.nn.sigmoid(l0 - l1)
        a1 = jax.nn.sigmoid(l1 - l0)
        alphas += [a0, a1]
        share = gates[experts + 2 + c : experts + 3 + c, :]
        own = own + share * a0
        turn[17 + c : 18 + c, 0:tokens] = share * a1
    turn[16:17, 0:tokens] = own
    zero_row = jnp.zeros((4, tokens), f32)
    info_ref[32:40, :] = jnp.concatenate(alphas + [zero_row], axis=0)
    gcol = turn[...].T[0:tokens, :]
    gcol_ref[...] = gcol
    upper, lower = split_bf16(jnp.where(lane < 16, gcol, 0.0))
    gpack = upper + pltpu.roll(lower.astype(f32), 64, 1).astype(bf16)
    gpack_ref[...] = gpack
    slot_row = slotr_ref[...]
    for e in range(experts):
        hot = one_hot(slot_row, e, slots)
        rows = slice(e * slots, (e + 1) * slots)
        send_ref[rows, :] = dot(hot, n2).astype(bf16)
    if last:
        send_grads(slot_row, cot_ref[...], gpack, gxs_ref, gy_ref, experts, slots)


def shape(dims, dtype=f32):
    return jax.ShapeDtypeStruct(tuple(dims), dtype)


def whole_call(body, name, outs, scratch, args, flops):
    moved = sum(a.size * a.dtype.itemsize for a in args) + sum(
        o.size * o.dtype.itemsize for o in outs
    )
    return pl.pallas_call(
        body,
        out_shape=outs,
        in_specs=[pl.BlockSpec(memory_space=pltpu.VMEM)] * len(args),
        out_specs=[pl.BlockSpec(memory_space=pltpu.VMEM)] * len(outs),
        scratch_shapes=scratch,
        compiler_params=pltpu.CompilerParams(vmem_limit_bytes=VMEM),
        cost_estimate=pl.CostEstimate(flops=flops, bytes_accessed=moved, transcendentals=0),
        name=name,
    )(*args)


def forward_call(first, last, experts, slots, args):
    tokens = TREE
    sent = experts * slots
    outs = [] if first else [shape((tokens, D))]
    outs += [
        shape((tokens, D), bf16),
        shape((tokens, 3 * D), bf16),
        shape((tokens, D), bf16),
        shape((16, tokens)),
        shape((tokens, D)),
        shape((tokens, D), bf16),
        shape((40, tokens)),
        shape((tokens, 128)),
        shape((tokens, 128), bf16),
        shape((sent, D), bf16),
        shape((D, 128), bf16),
    ]
    if last:
        outs += [shape((sent, D), bf16), shape((sent, D), bf16)]
    padded = -(-tokens // 128) * 128
    scratch = [pltpu.VMEM((tokens, 128), f32), pltpu.VMEM((128, padded), f32)]
    body = functools.partial(forward_kernel, first, last, experts, slots)
    return whole_call(body, "block_forward", outs, scratch, args, 20 * 10**9)


def gating_kernel(last, experts, slots, *refs):
    refs = list(refs)
    gx_ref, n2_ref, y_ref, gxs_ref, slotr_ref, info_ref, chosen_ref, gcol_ref, small_ref = [
        refs.pop(0) for _ in range(9)
    ]
    z_ref, mix_ref = refs.pop(0), refs.pop(0)
    if last:
        mid_ref, slotc_ref = refs.pop(0), refs.pop(0)
    else:
        gz_ref = refs.pop(0)
    gn2_ref, gsm_ref, gmix_ref, gprev_ref = [refs.pop(0) for _ in range(4)]
    if last:
        out_ref = refs.pop(0)
    tokens = n2_ref.shape[0]
    size, block = row_blocks(tokens)
    small = small_ref[...].astype(f32).T
    small_half = small[0:32, :].astype(bf16)
    vectors = small[S_VEC : S_VEC + 2, :]
    slot_row = slotr_ref[...]
    ones = jnp.ones((16, D), bf16)
    row = lax.broadcasted_iota(jnp.int32, (16, slots), 0)
    scattered = jnp.zeros((16, tokens), f32)
    for e in range(experts):
        rows = slice(e * slots, (e + 1) * slots)
        inner = y_ref[rows, :].astype(f32) * gxs_ref[rows, :].astype(f32)
        upper, lower = split_bf16(inner)
        sums = dot_nt(ones, upper) + dot_nt(ones, lower)
        upper, lower = split_bf16(sums)
        lhs = jnp.where(row == e, upper.astype(f32), 0.0) + jnp.where(
            row == 8 + e, lower.astype(f32), 0.0
        )
        scattered = scattered + dot(lhs.astype(bf16), one_hot(slot_row, e, slots))
    gx = gx_ref[...].astype(f32)
    gx_half = gx.astype(bf16)
    n2 = n2_ref[...]
    upper, lower = split_bf16(gx * n2.astype(f32))
    gx_n2 = (dot_nt(ones, upper) + dot_nt(ones, lower))[0:1, :]
    gx_small = dot_nt(small_half, gx_half)
    prob = info_ref[16:32, :]
    chosen = chosen_ref[...]
    gates = prob * chosen
    trow = lax.broadcasted_iota(jnp.int32, (16, tokens), 0)
    gp = jnp.concatenate([scattered[0:8, :] + scattered[8:16, :], jnp.zeros((8, tokens), f32)], 0)
    gp = jnp.where(trow == experts + 1, gx_n2, jnp.where(trow < experts, gp, 0.0))
    crow = lax.broadcasted_iota(jnp.int32, (8, tokens), 0)
    glog = jnp.zeros((8, tokens), f32)
    coefs = jnp.zeros((8, tokens), f32)
    for c in range(2):
        a0 = info_ref[32 + 2 * c : 33 + 2 * c, :]
        a1 = info_ref[33 + 2 * c : 34 + 2 * c, :]
        gx_v = gx_small[S_VEC + c : S_VEC + c + 1, :]
        share = gates[experts + 2 + c : experts + 3 + c, :]
        gp = jnp.where(trow == experts + 2 + c, a0 * gx_n2 + a1 * gx_v, gp)
        gl = share * (gx_n2 - gx_v) * a0 * a1
        glog = jnp.where(crow == 2 * c, gl, jnp.where(crow == 2 * c + 1, -gl, glog))
        coefs = jnp.where(crow == c, share * a1, coefs)
    gp = gp * chosen
    gz = prob * (gp - jnp.sum(prob * gp, axis=0, keepdims=True))
    if not last:
        gz = gz + gz_ref[...]
    z = z_ref[...]
    gmix_ref[...] = lax.dot_general(
        z, gz, (((1,), (1,)), ((), ())), precision=lax.Precision.HIGHEST, preferred_element_type=f32
    )
    mix = mix_ref[...]
    gprev = jnp.zeros((16, tokens), f32)
    for o in range(experts + 4):
        gprev = gprev + mix[:, o : o + 1] * gz[o : o + 1, :]
    gprev_ref[...] = gprev
    allg = jnp.concatenate([gz, glog, jnp.zeros((8, tokens), f32)], axis=0)
    upper, lower = split_bf16(allg)
    gsm = dot(upper, n2) + dot(lower, n2)
    cu, cl = split_bf16(jnp.concatenate([coefs, jnp.zeros((8, tokens), f32)], axis=0))
    gvec = dot(cu, gx_half) + dot(cl, gx_half)
    gsm_ref[0:24, :] = gsm[0:24, :]
    gsm_ref[24:32, :] = jnp.concatenate(
        [jnp.zeros((2, D), f32), gvec[0:2, :], jnp.zeros((4, D), f32)], axis=0
    )
    both = jnp.concatenate([upper, lower], axis=0)
    twice = jnp.concatenate([small_half, small_half], axis=0)
    gn2_ref[...] = dot_tn(both, twice)

    def add(i, carry):
        rows = block(i)
        gn2_ref[rows, :] = gn2_ref[rows, :] + gcol_ref[rows, 16:17] * gx_ref[rows, :].astype(f32)
        if last:
            out_ref[rows, :] = combine_rows(
                rows, mid_ref, n2_ref, y_ref, gcol_ref, slotc_ref, vectors, experts, slots
            ).astype(bf16)
        return carry

    lax.fori_loop(0, BLOCKS, add, 0)


def gating_outputs(last):
    tokens = TREE
    outs = [shape((tokens, D)), shape((32, D)), shape((16, 16)), shape((16, tokens))]
    if last:
        outs += [shape((tokens, D), bf16)]
    return outs


def backward_kernel(first, experts, slots, *refs):
    refs = list(refs)
    gx_ref, gn2p_ref, gn2e_ref, slotc_ref, mid_ref, att_ref, w_ref, qkv_ref, n1_ref, x_ref = [
        refs.pop(0) for _ in range(10)
    ]
    biast_ref, lse_ref, gsm_ref = [refs.pop(0) for _ in range(3)]
    if not first:
        slotr_ref, gpack_ref = refs.pop(0), refs.pop(0)
    gout_ref, dw_ref = refs.pop(0), refs.pop(0)
    if not first:
        gxs_ref, gy_ref = refs.pop(0), refs.pop(0)
    gatt, go, gqkv, turn = refs
    tokens = n1_ref.shape[0]
    size, block = row_blocks(tokens)
    small = w_ref[:, W_SMALL:].astype(f32).T
    gain0 = small[S_GAIN : S_GAIN + 1, :]
    gain1 = small[S_GAIN + 1 : S_GAIN + 2, :]

    def enter(i, total):
        rows = block(i)
        gn2 = gn2p_ref[rows, :]
        slot = slotc_ref[rows, :]
        for e in range(experts):
            gn2 = gn2 + dot(one_hot_col(slot, e, slots), gn2e_ref[e * slots : (e + 1) * slots, :])
        middle = mid_ref[rows, :]
        r = inv_rms(middle)
        scaled = gain1 * gn2
        inner = jnp.mean(middle * scaled, axis=1, keepdims=True)
        gmid = gx_ref[rows, :].astype(f32) + r * scaled - middle * (r * r * r * inner)
        gout_ref[rows, :] = gmid
        half = gmid.astype(bf16)
        gatt[rows, :] = half
        go[rows, :] = dot_nt(half, w_ref[:, W_OUT:W_SMALL]).astype(bf16)
        return total + jnp.sum(gn2 * middle * r, axis=0, keepdims=True)

    ggain1 = lax.fori_loop(0, BLOCKS, enter, jnp.zeros((1, D), f32))
    lane = lax.broadcasted_iota(jnp.int32, (1, 128), 1)
    low_f = jnp.where(lane < HD, 1.0, 0.0)
    low = low_f.astype(bf16)
    high = (1.0 - low_f).astype(bf16)
    scale = HD**-0.5

    def out_grad(p, carry):
        here = pl.ds(pl.multiple_of(p * 128, 128), 128)
        dw_ref[here, W_OUT:W_SMALL] = dot_tn(att_ref[:, here], gatt[...]).astype(bf16)
        return carry

    lax.fori_loop(0, D // 128, out_grad, 0)
    spans = causal_spans(tokens)

    def pair(p, carry):
        here = pl.ds(pl.multiple_of(p * 128, 128), 128)
        lanes_k = pl.ds(pl.multiple_of(D + p * 128, 128), 128)
        lanes_v = pl.ds(pl.multiple_of(2 * D + p * 128, 128), 128)
        q = qkv_ref[:, here] * bf16(scale)
        k = qkv_ref[:, lanes_k]
        v = qkv_ref[:, lanes_v]
        g = go[:, here]
        turn[0:tokens, :] = g.astype(f32) * att_ref[:, here].astype(f32)
        inner = turn[...].T[:, 0:tokens]
        turn[0:tokens, :] = k.astype(f32)
        kt = turn[...].T[:, 0:tokens].astype(bf16)
        gq_t = []
        gk = [0.0] * len(spans)
        gv = [0.0] * len(spans)
        for h, mask in ((0, low), (1, high)):
            qh = q * mask
            gh = g * mask
            dsum = jnp.sum(inner[h * HD : (h + 1) * HD, :], axis=0, keepdims=True)
            lse = lse_ref[pl.ds(2 * p + h, 1), :]
            gq_h = []
            for n, (start, stop) in enumerate(spans):
                st = dot_nt(k[start:stop], qh[start:]) + biast_ref[start:stop, start:]
                pt = jnp.exp(st - lse[:, start:])
                gpt = dot_nt(v[start:stop], gh[start:])
                gst = (pt * (gpt - dsum[:, start:])).astype(bf16)
                gv[n] = gv[n] + dot(pt.astype(bf16), gh[start:])
                gk[n] = gk[n] + dot(gst, qh[start:])
                part = dot(kt[h * HD : (h + 1) * HD, start:stop], gst)
                gq_h.append(part)
            cols = []
            for n, (start, stop) in enumerate(spans):
                piece = 0.0
                for m in range(n + 1):
                    origin = spans[m][0]
                    piece = piece + gq_h[m][:, start - origin : stop - origin]
                cols.append(piece)
            gq_t.append(jnp.concatenate(cols, axis=1))
        turn_t = jnp.concatenate(gq_t, axis=0) * scale
        pad = turn.shape[0] - tokens
        turn_t = jnp.concatenate([turn_t, jnp.zeros((128, pad), f32)], axis=1)
        gqkv[:, here] = turn_t.T[0:tokens, :].astype(bf16)
        for n, (start, stop) in enumerate(spans):
            gqkv[start:stop, lanes_k] = gk[n].astype(bf16)
            gqkv[start:stop, lanes_v] = gv[n].astype(bf16)
        return carry

    turn[...] = jnp.zeros_like(turn)
    lax.fori_loop(0, H // 2, pair, 0)

    def in_grad(p, carry):
        here = pl.ds(pl.multiple_of(p * 128, 128), 128)
        dw_ref[here, 0:W_OUT] = dot_tn(n1_ref[:, here], gqkv[...]).astype(bf16)
        return carry

    lax.fori_loop(0, D // 128, in_grad, 0)

    def leave(i, total):
        rows = block(i)
        gn1 = dot_nt(gqkv[rows, :], w_ref[:, 0:W_OUT])
        x = x_ref[rows, :].astype(f32)
        r = inv_rms(x)
        scaled = gain0 * gn1
        inner = jnp.mean(x * scaled, axis=1, keepdims=True)
        gx = gout_ref[rows, :] + r * scaled - x * (r * r * r * inner)
        gout_ref[rows, :] = gx
        gatt[rows, :] = gx.astype(bf16)
        return total + jnp.sum(gn1 * x * r, axis=0, keepdims=True)

    ggain0 = lax.fori_loop(0, BLOCKS, leave, jnp.zeros((1, D), f32))
    rows = jnp.concatenate(
        [gsm_ref[0:24, :], ggain0, ggain1, gsm_ref[26:32, :], jnp.zeros((96, D), f32)], axis=0
    )
    dw_ref[:, W_SMALL:] = rows.T.astype(bf16)
    if not first:
        send_grads(slotr_ref[...], gatt[...], gpack_ref[...], gxs_ref, gy_ref, experts, slots)


def backward_call(first, experts, slots, args):
    tokens = TREE
    sent = experts * slots
    outs = [shape((tokens, D)), shape((D, W_ALL), bf16)]
    if not first:
        outs += [shape((sent, D), bf16), shape((sent, D), bf16)]
    padded = -(-tokens // 128) * 128
    scratch = [
        pltpu.VMEM((tokens, D), bf16),
        pltpu.VMEM((tokens, D), bf16),
        pltpu.VMEM((tokens, 3 * D), bf16),
        pltpu.VMEM((padded, 128), f32),
    ]
    body = functools.partial(backward_kernel, first, experts, slots)
    return whole_call(body, "block_backward", outs, scratch, args, 40 * 10**9)


class Packing:
    def __init__(self, shards, part, ff):
        self.shards, self.part, self.ff = shards, part, ff
        self.padded = -(-part // 16) * 16
        self.chunks = ff // 256
        self.own = ff // shards
        self.down = 2 * self.chunks * self.padded
        self.rows = self.down + (D // 256) * self.own

    def pack(self, gate, up, down):
        pieces = []
        for wide in (gate, up):
            cut = wide.reshape(self.part, self.chunks, 256).transpose(1, 0, 2)
            cut = jnp.pad(cut, [(0, 0), (0, self.padded - self.part), (0, 0)])
            pieces.append(cut.reshape(self.chunks * self.padded, 256))
        pieces.append(
            down.reshape(self.own, D // 256, 256).transpose(1, 0, 2).reshape(-1, 256)
        )
        return jnp.concatenate(pieces, axis=0)

    def wide_part(self, ref, n, j):
        at = pl.multiple_of((n * self.chunks + j) * self.padded, 16)
        return ref[:, pl.ds(at, self.padded), :][:, : self.part, :].reshape(D, 256)

    def tall_part(self, ref, j):
        group = 256 // self.own
        here = pl.ds(j * group, group)
        pieces = []
        for c in range(D // 256):
            at = self.down + c * self.own
            pieces.append(ref[here, at : at + self.own, :].reshape(256, 256))
        return jnp.concatenate(pieces, axis=1)

    def put_wide(self, ref, n, j, grad):
        at = pl.multiple_of((n * self.chunks + j) * self.padded, 16)
        ref[:, pl.ds(at, self.part), :] = grad.reshape(self.shards, self.part, 256)

    def put_tall(self, ref, j, grad):
        group = 256 // self.own
        for c in range(D // 256):
            at = self.down + c * self.own
            ref[pl.ds(j * group, group), at : at + self.own, :] = grad[
                :, c * 256 : (c + 1) * 256
            ].reshape(group, self.own, 256)


class Exchange:
    def __init__(self, experts, slots):
        self.experts, self.slots = experts, slots
        first = -(-slots // 32) * 16
        self.waves = ((0, first), (first, slots - first))
        self.ranges = [(0, slots)]
        for _, size in self.waves:
            start = self.ranges[-1][0] + self.ranges[-1][1]
            self.ranges.append((start, (experts - 1) * size))
        self.total = experts * slots

    def held(self, wave, d):
        size = self.waves[wave][1]
        return pl.ds(self.ranges[1 + wave][0] + (d - 1) * size, size)

    def slot(self, device, wave):
        offset, size = self.waves[wave]
        return pl.ds(pl.multiple_of(device * self.slots + offset, 16), size)


MESH = pl.DeviceIdType.MESH


def greet(experts):
    me = lax.axis_index("expert")
    barrier = pltpu.get_barrier_semaphore()
    for d in range(1, experts):
        pl.semaphore_signal(
            barrier, inc=1, device_id={"expert": lax.rem(me + d, experts)}, device_id_type=MESH
        )
    pl.semaphore_wait(barrier, experts - 1)


def out_copies(ex, wave, src, dst, sends, recvs):
    me = lax.axis_index("expert")
    copies = []
    for d in range(1, ex.experts):
        to = lax.rem(me + d, ex.experts)
        copies.append(
            pltpu.make_async_remote_copy(
                src_ref=src.at[ex.slot(to, wave)],
                dst_ref=dst.at[ex.held(wave, d)],
                send_sem=sends.at[wave, d - 1],
                recv_sem=recvs.at[wave, d - 1],
                device_id={"expert": to},
                device_id_type=MESH,
            )
        )
    return copies


def back_copies(ex, wave, n, src, dst, sends, recvs):
    me = lax.axis_index("expert")
    copies = []
    for d in range(1, ex.experts):
        copies.append(
            pltpu.make_async_remote_copy(
                src_ref=src.at[ex.held(wave, d)],
                dst_ref=dst.at[ex.slot(me, wave)],
                send_sem=sends.at[n, wave, d - 1],
                recv_sem=recvs.at[n, wave, d - 1],
                device_id={"expert": lax.rem(me + ex.experts - d, ex.experts)},
                device_id_type=MESH,
            )
        )
    return copies


def own_slots(ex):
    me = lax.axis_index("expert")
    return pl.ds(pl.multiple_of(me * ex.slots, 16), ex.slots)


def dispatch_kernel(ex, send, recv, sends, recvs):
    greet(ex.experts)
    copies = out_copies(ex, 0, send, recv, sends, recvs)
    copies += out_copies(ex, 1, send, recv, sends, recvs)
    for copy in copies:
        copy.start()
    recv[0 : ex.slots, :] = send[own_slots(ex), :]
    for copy in copies:
        copy.wait()


def dispatch_call(ex, rows):
    vmem = pl.BlockSpec(memory_space=pltpu.VMEM)
    return pl.pallas_call(
        functools.partial(dispatch_kernel, ex),
        out_shape=shape((ex.total, D), bf16),
        in_specs=[vmem],
        out_specs=vmem,
        scratch_shapes=[pltpu.SemaphoreType.DMA((2, ex.experts - 1))] * 2,
        compiler_params=pltpu.CompilerParams(
            vmem_limit_bytes=8 << 20, collective_id=3, has_side_effects=True
        ),
        cost_estimate=pl.CostEstimate(flops=35 * 10**9, bytes_accessed=10**6, transcendentals=0),
        name="dispatch",
    )(rows)


def exchange_kernel(mode, pack, ex, *refs):
    refs = list(refs)
    forward, backward = mode in ("forward", "both"), mode in ("backward", "both")
    recv_n = refs.pop(0)
    w_hbm = refs.pop(0)
    gating = []
    if backward:
        send_g = refs.pop(0)
        if mode == "backward":
            gate_hbm, up_hbm = refs.pop(0), refs.pop(0)
        gating = [refs.pop(0) for _ in range(12)]
    if forward:
        back_y = refs.pop(0)
    if mode == "forward":
        gates, ups = refs.pop(0), refs.pop(0)
    else:
        back_g, dw = refs.pop(0), refs.pop(0)
        gating_outs = [refs.pop(0) for _ in range(5 if mode == "both" else 4)]
    if forward:
        out_y, acc_y = refs.pop(0), refs.pop(0)
    if backward:
        recv_g, out_g, hids, gates, ups, rows_t, acc_g = [refs.pop(0) for _ in range(7)]
        w = dw
    else:
        w = refs.pop(0)
    sends, recvs, backs, gots, local = refs

    loads = [pltpu.make_async_copy(w_hbm, w, local.at[0])]
    if mode == "backward":
        loads.append(pltpu.make_async_copy(gate_hbm, gates, local.at[1]))
        loads.append(pltpu.make_async_copy(up_hbm, ups, local.at[2]))
    for copy in loads:
        copy.start()
    greet(ex.experts)

    def work(start, size):
        rows = slice(start, start + size)
        part = slice(0, size)
        if forward:
            acc_y[part, :] = jnp.zeros((size, D), f32)
        if backward:
            acc_g[part, :] = jnp.zeros((size, D), f32)

        def chunk(j, carry):
            lanes = pl.ds(pl.multiple_of(j * 256, 256), 256)
            gate_w, up_w = pack.wide_part(w, 0, j), pack.wide_part(w, 1, j)
            down_w = pack.tall_part(w, j)
            if forward:
                r = recv_n[rows, :]
                gate, up = dot(r, gate_w), dot(r, up_w)
                if mode == "forward":
                    gates[rows, lanes] = gate.astype(bf16)
                    ups[rows, lanes] = up.astype(bf16)
            else:
                gate, up = gates[rows, lanes].astype(f32), ups[rows, lanes].astype(f32)
            s = jax.nn.sigmoid(gate)
            act = gate * s
            hid = (act * up).astype(bf16)
            if forward:
                acc_y[part, :] = acc_y[part, :] + dot(hid, down_w)
            if backward:
                hids[rows, lanes] = hid
                ghid = dot_nt(recv_g[rows, :], down_w)
                guv = (ghid * act).astype(bf16)
                ggu = (ghid * up * (s * (1.0 + gate * (1.0 - s)))).astype(bf16)
                gates[rows, lanes] = ggu
                ups[rows, lanes] = guv
                acc_g[part, :] = acc_g[part, :] + dot_nt(ggu, gate_w) + dot_nt(guv, up_w)
            return carry

        lax.fori_loop(0, pack.chunks, chunk, 0)
        if forward:
            out_y[rows, :] = acc_y[part, :].astype(bf16)
        if backward:
            out_g[rows, :] = acc_g[part, :].astype(bf16)

    def send_back(wave):
        ys = back_copies(ex, wave, 0, out_y, back_y, backs, gots) if forward else []
        gs = back_copies(ex, wave, 1, out_g, back_g, backs, gots) if backward else []
        for copy in ys + gs:
            copy.start()
        return ys, gs

    if backward:
        waves = [out_copies(ex, n, send_g, recv_g, sends, recvs) for n in range(2)]
        for copy in waves[0]:
            copy.start()
        recv_g[0 : ex.slots, :] = send_g[own_slots(ex), :]
        if mode == "backward":
            gating_kernel(False, ex.experts, ex.slots, *gating, *gating_outs)
    for copy in loads:
        copy.wait()
    if backward:
        work(*ex.ranges[0])
        for copy in waves[0]:
            copy.wait_send()
        for copy in waves[1]:
            copy.start()
        for copy in waves[0]:
            copy.wait_recv()
    work(*ex.ranges[1])
    ys, gs = send_back(0)
    if backward:
        for copy in waves[1]:
            copy.wait()
    work(*ex.ranges[2])
    more = send_back(1)
    ys, gs = ys + more[0], gs + more[1]
    if mode == "forward":
        work(*ex.ranges[0])
    if forward:
        back_y[own_slots(ex), :] = out_y[0 : ex.slots, :]
    if backward:
        back_g[own_slots(ex), :] = out_g[0 : ex.slots, :]
        rows_t[...] = recv_n[...].T
        if pack.padded != pack.part:
            dw[...] = jnp.zeros_like(dw)

        def weights(j, carry):
            lanes = pl.ds(pl.multiple_of(j * 256, 256), 256)
            pack.put_wide(dw, 0, j, dot(rows_t[...], gates[:, lanes]).astype(bf16))
            pack.put_wide(dw, 1, j, dot(rows_t[...], ups[:, lanes]).astype(bf16))
            pack.put_tall(dw, j, dot_tn(hids[:, lanes], recv_g[...]).astype(bf16))
            return carry

        lax.fori_loop(0, pack.chunks, weights, 0)
    for copy in ys:
        copy.wait()
    if mode == "both":
        gating_kernel(True, ex.experts, ex.slots, *gating[:2], back_y, *gating[2:], *gating_outs)
    for copy in gs:
        copy.wait()


SPLIT = 13 * 128


def cube_kernel(part, g_ref, out_ref, got_c, sums, got_a, got_b, half_a, half_b, end_a, end_b, send, recv):
    me = lax.axis_index("shard")
    core, x, y = lax.rem(me, 2), lax.rem(me // 2, 2), me // 4
    near, over_x, over_y = (
        me + 1 - 2 * core,
        me + 2 - 4 * x,
        me + 4 - 8 * y,
    )
    barrier = pltpu.get_barrier_semaphore()
    for other in (near, over_x, over_y):
        pl.semaphore_signal(barrier, inc=1, device_id={"shard": other}, device_id_type=MESH)
    pl.semaphore_wait(barrier, 3)
    cols_a, cols_b = slice(0, SPLIT), slice(SPLIT, W_ALL)

    def rows(shard):
        return pl.ds(pl.multiple_of(shard * part, 16), part)

    def copy(n, src, dst, to):
        made = pltpu.make_async_remote_copy(
            src_ref=src,
            dst_ref=dst,
            send_sem=send.at[n],
            recv_sem=recv.at[n],
            device_id={"shard": to},
            device_id_type=MESH,
        )
        made.start()
        return made

    chips = [2 * (1 - y) + 1 - x, 2 * y + 1 - x, 2 * (1 - y) + x, 2 * y + x]
    first = [
        copy(n, g_ref.at[rows(2 * chip + 1 - core)], got_c.at[chip], near)
        for n, chip in enumerate(chips)
    ]

    def merge(n):
        chip = chips[n]
        first[n].wait_recv()
        own = g_ref[rows(2 * chip + core), :].astype(f32)
        sums[chip] = (own + got_c[chip].astype(f32)).astype(bf16)

    def total(chip, cols, got):
        return sums[chip, :, cols].astype(f32) + got[...].astype(f32)

    merge(0)
    a0 = copy(4, sums.at[chips[0], :, cols_a], got_a.at[1 - y], over_x)
    b0 = copy(5, sums.at[chips[0], :, cols_b], got_b.at[1 - x], over_y)
    merge(1)
    a1 = copy(6, sums.at[chips[1], :, cols_a], got_a.at[y], over_x)
    merge(2)
    b1 = copy(7, sums.at[chips[2], :, cols_b], got_b.at[x], over_y)
    merge(3)
    a0.wait_recv()
    half_a[...] = total(chips[2], cols_a, got_a.at[1 - y]).astype(bf16)
    a2 = copy(8, half_a, end_a, over_y)
    b0.wait_recv()
    half_b[...] = total(chips[1], cols_b, got_b.at[1 - x]).astype(bf16)
    b2 = copy(9, half_b, end_b, over_x)
    a1.wait_recv()
    keep_a = total(chips[3], cols_a, got_a.at[y])
    a2.wait_recv()
    out_ref[:, cols_a] = (keep_a + end_a[...].astype(f32)).astype(bf16)
    b1.wait_recv()
    keep_b = total(chips[3], cols_b, got_b.at[x])
    b2.wait_recv()
    out_ref[:, cols_b] = (keep_b + end_b[...].astype(f32)).astype(bf16)
    for made in first + [a0, b0, a1, b1, a2, b2]:
        made.wait_send()


def scatter_sum(grads, part):
    if lax.axis_size("shard") != 8:
        return lax.psum_scatter(grads, "shard", scatter_dimension=0, tiled=True)
    vmem = pl.BlockSpec(memory_space=pltpu.VMEM)
    rest = W_ALL - SPLIT
    return pl.pallas_call(
        functools.partial(cube_kernel, part),
        out_shape=shape((part, W_ALL), bf16),
        in_specs=[vmem],
        out_specs=vmem,
        scratch_shapes=[
            pltpu.VMEM((4, part, W_ALL), bf16),
            pltpu.VMEM((4, part, W_ALL), bf16),
            pltpu.VMEM((2, part, SPLIT), bf16),
            pltpu.VMEM((2, part, rest), bf16),
            pltpu.VMEM((part, SPLIT), bf16),
            pltpu.VMEM((part, rest), bf16),
            pltpu.VMEM((part, SPLIT), bf16),
            pltpu.VMEM((part, rest), bf16),
            pltpu.SemaphoreType.DMA((10,)),
            pltpu.SemaphoreType.DMA((10,)),
        ],
        compiler_params=pltpu.CompilerParams(
            vmem_limit_bytes=32 << 20, collective_id=4, has_side_effects=True
        ),
        cost_estimate=pl.CostEstimate(flops=35 * 10**9, bytes_accessed=10**7, transcendentals=0),
        name="scatter_sum",
    )(grads)


EXCHANGE_IDS = {"forward": 0, "both": 1, "backward": 2}


def exchange_call(mode, pack, ex, args):
    rows, ff = ex.total, pack.ff
    forward, backward = mode in ("forward", "both"), mode in ("backward", "both")
    flat, wide = shape((rows, D), bf16), shape((rows, ff), bf16)
    packed = (pack.shards, pack.rows, 256)
    most = max(size for _, size in ex.ranges)
    vmem = pl.BlockSpec(memory_space=pltpu.VMEM)
    far = pl.BlockSpec(memory_space=pl.ANY)
    in_specs = [vmem] * len(args)
    in_specs[1] = far
    scratch = []
    if mode == "forward":
        outs = [flat, wide, wide]
    elif mode == "both":
        outs = [flat, flat, shape(packed, bf16)] + gating_outputs(True)
    else:
        in_specs[3] = in_specs[4] = far
        outs = [flat, shape(packed, bf16)] + gating_outputs(False)
    if forward:
        scratch += [pltpu.VMEM((rows, D), bf16), pltpu.VMEM((most, D), f32)]
    if backward:
        scratch += [pltpu.VMEM((rows, D), bf16)] * 2
        scratch += [pltpu.VMEM((rows, ff), bf16)] * 3
        scratch += [pltpu.VMEM((D, rows), bf16), pltpu.VMEM((most, D), f32)]
    else:
        scratch.append(pltpu.VMEM(packed, bf16))
    scratch += [pltpu.SemaphoreType.DMA((2, ex.experts - 1))] * 2
    scratch += [pltpu.SemaphoreType.DMA((2, 2, ex.experts - 1))] * 2
    scratch.append(pltpu.SemaphoreType.DMA((3,)))
    work = 6 * rows * D * ff * (1 if mode == "forward" else 2 if mode == "backward" else 3)
    return pl.pallas_call(
        functools.partial(exchange_kernel, mode, pack, ex),
        out_shape=outs,
        in_specs=in_specs,
        out_specs=[vmem] * len(outs),
        scratch_shapes=scratch,
        compiler_params=pltpu.CompilerParams(
            vmem_limit_bytes=62 << 20, collective_id=EXCHANGE_IDS[mode], has_side_effects=True
        ),
        cost_estimate=pl.CostEstimate(
            flops=10**9 if mode == "backward" else work + 40 * 10**9,
            bytes_accessed=6 * D * ff,
            transcendentals=0,
        ),
        name="experts_" + mode,
    )(*args)


def expert_outputs_kernel(pack, first_ref, second_ref, gate_ref, up_ref, down_ref):
    for l, ref in enumerate((first_ref, second_ref)):
        for n, out in enumerate((gate_ref, up_ref)):
            for j in range(pack.chunks):
                at = (n * pack.chunks + j) * pack.padded
                out[l, :, j * 256 : (j + 1) * 256] = ref[at : at + pack.part, :].astype(f32)
        for c in range(D // 256):
            at = pack.down + c * pack.own
            down_ref[l, :, c * 256 : (c + 1) * 256] = ref[at : at + pack.own, :].astype(f32)


def expert_outputs(pack, grads):
    wide = shape((LAYERS, pack.part, pack.ff))
    outs = [wide, wide, shape((LAYERS, pack.own, D))]
    body = functools.partial(expert_outputs_kernel, pack)
    return whole_call(body, "expert_outputs", outs, [], grads, 10**6)


def dense_outputs_kernel(
    part, labels, first_ref, second_ref, proj_ref, out_ref, gain_ref, router_ref, vec_ref, const_ref,
    turn,
):
    for l, ref in enumerate((first_ref, second_ref)):
        for c in range(3):
            proj_ref[l, c] = ref[:, c * D : (c + 1) * D].astype(f32)
        out_ref[l] = ref[:, W_OUT:W_SMALL].astype(f32)
        small = ref[:, W_SMALL:].astype(f32)
        router_ref[l] = small[:, 0:labels]
        for c in range(2):
            const_ref[l, c] = small[:, S_CONST + 2 * c : S_CONST + 2 * c + 2]
        turn[0:part, :] = small
        rows = turn[...].T
        gain_ref[l] = rows[S_GAIN : S_GAIN + 2, 0:part]
        vec_ref[l] = rows[S_VEC : S_VEC + 2, 0:part]


def dense_outputs(part, labels, grads):
    outs = [
        shape((LAYERS, 3, part, D)),
        shape((LAYERS, part, D)),
        shape((LAYERS, 2, part)),
        shape((LAYERS, part, labels)),
        shape((LAYERS, 2, part)),
        shape((LAYERS, 2, part, 2)),
    ]
    body = functools.partial(dense_outputs_kernel, part, labels)
    return whole_call(body, "dense_outputs", outs, [pltpu.VMEM((128, 128), f32)], grads, 10**6)


def on_device(
    hidden_in,
    prior_logits,
    project_weight,
    output_weight,
    norm_gain,
    router_weight,
    mixing_weight,
    const_vector,
    const_weight,
    gate_weight,
    up_weight,
    down_weight,
    routes,
    priority,
    leaf_parent,
    cotangent,
):
    experts = lax.axis_size("expert")
    total_experts = experts + 4
    tokens = hidden_in.shape[0]
    capacity = 9 * tokens * TOP // (8 * total_experts)
    slots = -(-capacity // 16) * 16
    part = project_weight.shape[2]

    def pad_cols(a, width):
        return jnp.pad(a, [(0, 0)] * (a.ndim - 1) + [(0, width - a.shape[-1])])

    dense = []
    experts_w = []
    pack = Packing(lax.axis_size("shard"), part, gate_weight.shape[3])
    for l in range(LAYERS):
        small = jnp.concatenate(
            [
                pad_cols(router_weight[l], S_CONST),
                const_weight[l, 0],
                const_weight[l, 1],
                jnp.zeros((part, S_GAIN - S_CONST - 4), bf16),
                norm_gain[l].T,
                const_vector[l].T,
            ],
            axis=1,
        )
        packed = jnp.concatenate(
            [project_weight[l, c] for c in range(3)] + [output_weight[l], pad_cols(small, 128)],
            axis=1,
        )
        dense.append(lax.all_gather(packed, "shard", axis=0, tiled=True))
        mine = pack.pack(gate_weight[l, 0], up_weight[l, 0], down_weight[l, 0])
        experts_w.append(lax.all_gather(mine, "shard", axis=0, tiled=False))

    ranking = priority[0]
    earlier = (ranking[None, :] < ranking[:, None]).astype(bf16)
    labels = jnp.arange(total_experts, dtype=jnp.int32)
    hits = jnp.sum((routes[:, :, :, None] == labels).astype(f32), axis=2)
    chosen_rows = [jnp.pad(hits[l].T, [(0, 16 - total_experts), (0, 0)]) for l in range(LAYERS)]
    loaded = jnp.concatenate([hits[l, :, :experts] for l in range(LAYERS)], axis=1)
    loaded_half = loaded.astype(bf16)
    rank_col = dot(earlier, loaded_half)
    rank_row = lax.dot_general(
        loaded_half, earlier, (((0,), (1,)), ((), ())), preferred_element_type=f32
    )
    slot_col_all = jnp.where((loaded > 0) & (rank_col < capacity), rank_col, -1.0)
    slot_row_all = jnp.where((loaded.T > 0) & (rank_row < capacity), rank_row, -1.0)
    slot_col = [slot_col_all[:, l * experts : (l + 1) * experts] for l in range(LAYERS)]
    slot_row = [
        jnp.pad(
            slot_row_all[l * experts : (l + 1) * experts],
            [(0, 8 - experts), (0, 0)],
            constant_values=-1.0,
        )
        for l in range(LAYERS)
    ]
    visible = tree_visible(leaf_parent[0])
    bias = jnp.where(visible, 0.0, masked_fill)
    bias_t = jnp.where(visible.T, 0.0, masked_fill)
    mixes = [
        jnp.pad(mixing_weight[l], [(0, 16 - total_experts), (0, 16 - total_experts)])
        for l in range(LAYERS)
    ]
    z_rows = jnp.pad(prior_logits.T, [(0, 16 - total_experts), (0, 0)])

    ex = Exchange(experts, slots)
    saved = []
    front = [hidden_in]
    x_now = hidden_in
    for l in range(LAYERS):
        last = l == LAYERS - 1
        args = front + [dense[l], bias, z_rows, mixes[l].T, chosen_rows[l], slot_row[l]]
        if last:
            args.append(cotangent)
        outs = list(forward_call(l == 0, last, experts, slots, args))
        if l > 0:
            x_now = outs.pop(0)
        n1, qkv, att, lse, middle, n2, info, gcol, gpack, send, small = outs[:11]
        keep = dict(
            x=x_now, n1=n1, qkv=qkv, att=att, lse=lse, middle=middle, n2=n2, info=info,
            gcol=gcol, gpack=gpack, z=z_rows, small=small,
        )
        keep["received"] = dispatch_call(ex, send)
        if last:
            gating = [
                cotangent, n2, outs[11], slot_row[l], info, chosen_rows[l], gcol, small, z_rows,
                mixes[l], middle, slot_col[l],
            ]
            done = exchange_call(
                "both", pack, ex, [keep["received"], experts_w[l], outs[12]] + gating
            )
            keep["y"], keep["gin"], keep["dw"] = done[:3]
            keep["gating"] = done[3:]
        else:
            keep["y"], keep["gate"], keep["up"] = exchange_call(
                "forward", pack, ex, [keep["received"], experts_w[l]]
            )
        front = [middle, n2, keep["y"], gcol, slot_col[l], small]
        z_rows = info[0:16]
        saved.append(keep)

    gx = cotangent
    gz = None
    dense_grads = [None] * LAYERS
    mix_grads = [None] * LAYERS
    expert_grads = [None] * LAYERS
    hidden_out = None
    for l in range(LAYERS - 1, -1, -1):
        last = l == LAYERS - 1
        keep = saved[l]
        if not last:
            gating = [
                gx, keep["n2"], keep["y"], keep["gxs"], slot_row[l], keep["info"], chosen_rows[l],
                keep["gcol"], keep["small"], keep["z"], mixes[l], gz,
            ]
            done = exchange_call(
                "backward", pack, ex,
                [keep["received"], experts_w[l], keep["gy"], keep["gate"], keep["up"]] + gating,
            )
            keep["gin"], keep["dw"] = done[:2]
            keep["gating"] = done[2:]
        gn2, gsm, mix_grads[l], gz = keep["gating"][:4]
        if last:
            hidden_out = keep["gating"][4]
        d_experts, gn2 = lax.optimization_barrier((keep["dw"], gn2))
        if not last:
            gn2, expert_grads[l + 1] = lax.optimization_barrier((gn2, expert_grads[l + 1]))
        expert_grads[l] = lax.psum_scatter(d_experts, "shard", scatter_dimension=0, tiled=False)
        args = [
            gx, gn2, keep["gin"], slot_col[l], keep["middle"], keep["att"], dense[l], keep["qkv"],
            keep["n1"], keep["x"], bias_t, keep["lse"], gsm,
        ]
        if l > 0:
            args += [slot_row[l - 1], saved[l - 1]["gpack"]]
        outs = backward_call(l == 0, experts, slots, args)
        gx, d_dense = outs[:2]
        if l > 0:
            saved[l - 1]["gxs"], saved[l - 1]["gy"] = outs[2:4]
        if l == 0:
            mix_grads[0], d_dense = lax.optimization_barrier((mix_grads[0], d_dense))
        if l == 0:
            dense_grads[l] = scatter_sum(d_dense, part)
        else:
            dense_grads[l] = lax.psum_scatter(d_dense, "shard", scatter_dimension=0, tiled=True)

    both_dense = lax.psum(jnp.stack(dense_grads), "expert")
    dense_grads = [both_dense[l] for l in range(LAYERS)]
    mixing_total = lax.psum(jnp.stack(mix_grads), ("expert", "shard"))
    gate_grad, up_grad, down_grad = expert_outputs(pack, expert_grads)
    project_grad, output_grad, gain_grad, router_grad, vector_grad, const_grad = dense_outputs(
        part, total_experts, dense_grads
    )
    return (
        hidden_out,
        gx,
        gz[0:total_experts].T,
        project_grad,
        output_grad,
        gain_grad,
        router_grad,
        mixing_total[:, 0:total_experts, 0:total_experts],
        vector_grad,
        const_grad,
        gate_grad[:, None],
        up_grad[:, None],
        down_grad[:, None],
    )


def solution(mesh):
    both = ("expert", "shard")
    in_specs = (
        P(both, None),
        P(both, None),
        P(None, None, "shard", None),
        P(None, "shard", None),
        P(None, None, "shard"),
        P(None, "shard", None),
        P(),
        P(None, None, "shard"),
        P(None, None, "shard", None),
        P(None, "expert", "shard", None),
        P(None, "expert", "shard", None),
        P(None, "expert", "shard", None),
        P(None, both, None),
        P(both, None),
        P(both, None),
        P(both, None),
    )
    out_specs = (
        P(both, None),
        P(both, None),
        P(both, None),
        P(None, None, "shard", None),
        P(None, "shard", None),
        P(None, None, "shard"),
        P(None, "shard", None),
        P(),
        P(None, None, "shard"),
        P(None, None, "shard", None),
        P(None, "expert", "shard", None),
        P(None, "expert", "shard", None),
        P(None, "expert", "shard", None),
    )
    return jax.shard_map(
        on_device, mesh=mesh, in_specs=in_specs, out_specs=out_specs, check_vma=False
    )
```

```python
import functools

import jax
import jax.numpy as jnp
from jax import lax
from jax.experimental import pallas as pl
from jax.experimental.pallas import tpu as pltpu
from jax.sharding import PartitionSpec as P

D = 768
H = 12
HD = 64
TOP = 2
LAYERS = 2
TRUNK = 320
BRANCH = 64
LEAF = 32
TREE = 832

W_OUT = 3 * D
W_SMALL = 4 * D
W_ALL = 4 * D + 128
S_CONST = 16
S_GAIN = 24
S_VEC = 26

epsilon = 1e-06
masked_fill = -1e30
f32 = jnp.float32
bf16 = jnp.bfloat16
BLOCKS = 2
VMEM = 56 << 20


def dot(a, b):
    return jnp.dot(a, b, preferred_element_type=f32)


def dot_nt(a, b):
    return lax.dot_general(a, b, (((1,), (1,)), ((), ())), preferred_element_type=f32)


def dot_tn(a, b):
    return lax.dot_general(a, b, (((0,), (0,)), ((), ())), preferred_element_type=f32)


def split_bf16(v):
    high = v.astype(bf16)
    return high, (v - high.astype(f32)).astype(bf16)


def inv_rms(v):
    return lax.rsqrt(jnp.mean(v * v, axis=1, keepdims=True) + epsilon)


def tree_visible(parents):
    position = jnp.arange(TREE, dtype=jnp.int32)
    offset = position - TRUNK
    segment = jnp.where(
        position < TRUNK,
        0,
        jnp.where(offset < 4 * BRANCH, 1 + offset // BRANCH, 5 + (offset - 4 * BRANCH) // LEAF),
    )
    leaf_hits = (segment[:, None] - 5 == jnp.arange(8, dtype=jnp.int32)[None, :]).astype(jnp.int32)
    upper = jnp.where(segment >= 5, 1 + jnp.sum(leaf_hits * parents[None, :], axis=1), 0)
    key_segment = segment[None, :]
    causal = position[None, :] <= position[:, None]
    return causal & (
        (key_segment == segment[:, None]) | (key_segment == 0) | (key_segment == upper[:, None])
    )


def one_hot(slot_row, e, slots):
    row = lax.broadcasted_iota(jnp.int32, (slots, slot_row.shape[1]), 0).astype(f32)
    return jnp.where(row == slot_row[e : e + 1, :], 1.0, 0.0).astype(bf16)


def one_hot_col(slot_col, e, slots, scale=None):
    lane = lax.broadcasted_iota(jnp.int32, (slot_col.shape[0], slots), 1).astype(f32)
    value = 1.0 if scale is None else scale
    return jnp.where(lane == slot_col[:, e : e + 1], value, 0.0).astype(bf16)


def combine_rows(rows, middle_ref, n2_ref, y_ref, gcol_ref, slotc_ref, vectors, experts, slots):
    gcol = gcol_ref[rows, :]
    slot = slotc_ref[rows, :]
    total = middle_ref[rows, :] + gcol[:, 16:17] * n2_ref[rows, :].astype(f32)
    for c in range(2):
        total = total + gcol[:, 17 + c : 18 + c] * vectors[c : c + 1, :]
    for e in range(experts):
        weight = one_hot_col(slot, e, slots, gcol[:, e : e + 1])
        total = total + dot(weight, y_ref[e * slots : (e + 1) * slots, :])
    return total


def all_one_hot(slot_row, experts, slots):
    return jnp.concatenate([one_hot(slot_row, e, slots) for e in range(experts)], axis=0)


def send_grads(hot, gx, gpack, gxs_ref, gy_ref, experts, slots):
    got = dot(hot, gx)
    gates = dot(hot, gpack)
    gxs_ref[...] = got.astype(bf16)
    for e in range(experts):
        rows = slice(e * slots, (e + 1) * slots)
        gate = gates[rows, e : e + 1] + gates[rows, 64 + e : 65 + e]
        gy_ref[rows, :] = (got[rows, :] * gate).astype(bf16)


def row_blocks(tokens):
    size = tokens // BLOCKS
    return size, lambda i: pl.ds(pl.multiple_of(i * size, 16), size)


def causal_spans(tokens):
    edges = [0, 384, 640, tokens]
    return list(zip(edges[:-1], edges[1:]))


def forward_kernel(first, last, experts, slots, traffic, *refs):
    refs = list(refs)
    if first:
        x_in = refs.pop(0)
    else:
        mid_prev, n2_prev, y_ref, gcol_prev, slotc_prev, w_prev = [refs.pop(0) for _ in range(6)]
    w_ref, bias_ref, z_ref, mixt_ref, chosen_ref, slotr_ref = [refs.pop(0) for _ in range(6)]
    if last:
        cot_ref = refs.pop(0)
    if not first:
        x_out = refs.pop(0)
    n1_ref, qkv_ref, att_ref, lse_ref, mid_ref, n2_ref, info_ref, gcol_ref, gpack_ref, send_ref = [
        refs.pop(0) for _ in range(10)
    ]
    small_out = refs.pop(0)
    small_out[...] = w_ref[:, W_SMALL:]
    if last:
        gxs_ref, gy_ref = refs.pop(0), refs.pop(0)
    lse_cols, turn = refs
    tokens = n1_ref.shape[0]
    size, block = row_blocks(tokens)
    small = w_ref[:, W_SMALL:].astype(f32).T
    gain0 = small[S_GAIN : S_GAIN + 1, :]
    gain1 = small[S_GAIN + 1 : S_GAIN + 2, :]
    if not first:
        vectors_prev = w_prev[...].astype(f32).T[S_VEC : S_VEC + 2, :]

    def project(i, carry):
        rows = block(i)
        if first:
            x = x_in[rows, :].astype(f32)
        else:
            x = combine_rows(
                rows, mid_prev, n2_prev, y_ref, gcol_prev, slotc_prev, vectors_prev, experts, slots
            )
            x_out[rows, :] = x
        n1 = (x * inv_rms(x) * gain0).astype(bf16)
        n1_ref[rows, :] = n1
        for c in range(3):
            qkv_ref[rows, c * D : (c + 1) * D] = dot(n1, w_ref[:, c * D : (c + 1) * D]).astype(bf16)
        return carry

    lax.fori_loop(0, BLOCKS, project, 0)
    if not first:
        traffic.flush(x_out)
    traffic.flush(n1_ref)
    traffic.flush(qkv_ref)
    traffic.need(bias_ref)
    lane = lax.broadcasted_iota(jnp.int32, (1, 128), 1)
    low_f = jnp.where(lane < HD, 1.0, 0.0)
    low = low_f.astype(bf16)
    high = (1.0 - low_f).astype(bf16)
    lse_cols[...] = jnp.zeros_like(lse_cols)

    def pair(p, carry):
        k = qkv_ref[:, pl.ds(pl.multiple_of(D + p * 128, 128), 128)]
        v = qkv_ref[:, pl.ds(pl.multiple_of(2 * D + p * 128, 128), 128)]
        va = v * low + high
        vb = v * high + low
        here = pl.ds(pl.multiple_of(p * 128, 128), 128)
        for start, stop in causal_spans(tokens):
            q = qkv_ref[start:stop, here] * bf16(HD**-0.5)
            outs = []
            for mask, value in ((low, va), (high, vb)):
                s = dot_nt(q * mask, k[:stop]) + bias_ref[start:stop, :stop]
                peak = jnp.max(s, axis=1, keepdims=True)
                expo = jnp.exp(s - peak).astype(bf16)
                outs.append((dot(expo, value[:stop]), peak))
            (oa, ma), (ob, mb) = outs
            numer = jnp.where(lane < HD, oa, ob)
            denom = pltpu.roll(jnp.where(lane < HD, ob, oa), HD, 1)
            att_ref[start:stop, here] = (numer / denom).astype(bf16)
            la = ma + jnp.log(oa[:, HD : HD + 1])
            lb = mb + jnp.log(ob[:, 0:1])
            old = lse_cols[start:stop, :]
            lse_cols[start:stop, :] = jnp.where(
                lane == 2 * p, la, jnp.where(lane == 2 * p + 1, lb, old)
            )
        return carry

    lax.fori_loop(0, H // 2, pair, 0)
    traffic.flush(att_ref)
    lse_ref[...] = lse_cols[...].T[0:16, :]

    def finish(i, carry):
        rows = block(i)
        if first:
            x = x_in[rows, :].astype(f32)
        else:
            x = x_out[rows, :]
        middle = x + dot(att_ref[rows, :], w_ref[:, W_OUT:W_SMALL])
        mid_ref[rows, :] = middle
        n2_ref[rows, :] = (middle * inv_rms(middle) * gain1).astype(bf16)
        return carry

    lax.fori_loop(0, BLOCKS, finish, 0)
    traffic.flush(mid_ref)
    traffic.flush(n2_ref)
    n2 = n2_ref[...]
    scores = dot_nt(small[0:32, :].astype(bf16), n2)
    logits = scores[0:16, :]
    z = z_ref[...]
    mixt = mixt_ref[...]
    for i in range(experts + 4):
        logits = logits + mixt[:, i : i + 1] * z[i : i + 1, :]
    row = lax.broadcasted_iota(jnp.int32, (16, tokens), 0)
    valid = row < experts + 4
    peak = jnp.max(jnp.where(valid, logits, masked_fill), axis=0, keepdims=True)
    expo = jnp.where(valid, jnp.exp(jnp.minimum(logits - peak, 0.0)), 0.0)
    prob = expo / jnp.sum(expo, axis=0, keepdims=True)
    gates = prob * chosen_ref[...]
    info_ref[0:16, :] = logits
    info_ref[16:32, :] = prob
    turn[...] = jnp.zeros_like(turn)
    turn[0:16, 0:tokens] = gates
    own = gates[experts + 1 : experts + 2, :]
    alphas = []
    for c in range(2):
        l0 = scores[S_CONST + 2 * c : S_CONST + 2 * c + 1, :]
        l1 = scores[S_CONST + 2 * c + 1 : S_CONST + 2 * c + 2, :]
        a0 = jax.nn.sigmoid(l0 - l1)
        a1 = jax.nn.sigmoid(l1 - l0)
        alphas += [a0, a1]
        share = gates[experts + 2 + c : experts + 3 + c, :]
        own = own + share * a0
        turn[17 + c : 18 + c, 0:tokens] = share * a1
    turn[16:17, 0:tokens] = own
    zero_row = jnp.zeros((4, tokens), f32)
    info_ref[32:40, :] = jnp.concatenate(alphas + [zero_row], axis=0)
    gcol = turn[...].T[0:tokens, :]
    gcol_ref[...] = gcol
    upper, lower = split_bf16(jnp.where(lane < 16, gcol, 0.0))
    gpack = upper + pltpu.roll(lower.astype(f32), 64, 1).astype(bf16)
    gpack_ref[...] = gpack
    hot = all_one_hot(slotr_ref[...], experts, slots)
    send_ref[...] = dot(hot, n2).astype(bf16)
    if last:
        traffic.need(cot_ref)
        send_grads(hot, cot_ref[...], gpack, gxs_ref, gy_ref, experts, slots)


def shape(dims, dtype=f32):
    return jax.ShapeDtypeStruct(tuple(dims), dtype)


class Traffic:
    def __init__(self):
        self.fetches, self.sinks, self.flushes = {}, {}, []

    def fetch(self, src, buffer, sem):
        copy = pltpu.make_async_copy(src, buffer, sem)
        copy.start()
        self.fetches[id(buffer)] = copy

    def need(self, *buffers):
        for buffer in buffers:
            copy = self.fetches.pop(id(buffer), None)
            if copy is not None:
                copy.wait()

    def sink(self, buffer, dst, sems):
        self.sinks[id(buffer)] = [dst, sems, 0]

    def flush(self, buffer, part=None):
        entry = self.sinks.get(id(buffer))
        if entry is None:
            return
        dst, sems, used = entry
        entry[2] += 1
        src, dst = (buffer, dst) if part is None else (buffer.at[part], dst.at[part])
        copy = pltpu.make_async_copy(src, dst, sems.at[used])
        copy.start()
        self.flushes.append(copy)

    def finish(self):
        for copy in self.flushes:
            copy.wait()


FLUSHES = 3


def whole_call(body, name, outs, scratch, args, flops, late=(), early=()):
    moved = sum(a.size * a.dtype.itemsize for a in args) + sum(
        o.size * o.dtype.itemsize for o in outs
    )
    late, early = sorted(late), sorted(early)

    def kernel(*refs):
        ins, rest = list(refs[: len(args)]), refs[len(args) :]
        results, rest = list(rest[: len(outs)]), rest[len(outs) :]
        own, rest = rest[: len(scratch)], rest[len(scratch) :]
        traffic = Traffic()
        fetch_sems, flush_sems = rest[len(late) + len(early) :]
        for n, at in enumerate(late):
            traffic.fetch(ins[at], rest[n], fetch_sems.at[n])
            ins[at] = rest[n]
        for n, at in enumerate(early):
            buffer = rest[len(late) + n]
            traffic.sink(buffer, results[at], flush_sems.at[n])
            results[at] = buffer
        body(traffic, *ins, *results, *own)
        traffic.finish()

    near, far = pl.BlockSpec(memory_space=pltpu.VMEM), pl.BlockSpec(memory_space=pl.ANY)
    buffers = [pltpu.VMEM(args[at].shape, args[at].dtype) for at in late]
    buffers += [pltpu.VMEM(outs[at].shape, outs[at].dtype) for at in early]
    buffers.append(pltpu.SemaphoreType.DMA((max(len(late), 1),)))
    buffers.append(pltpu.SemaphoreType.DMA((max(len(early), 1), FLUSHES)))
    return pl.pallas_call(
        kernel,
        out_shape=outs,
        in_specs=[far if n in late else near for n in range(len(args))],
        out_specs=[far if n in early else near for n in range(len(outs))],
        scratch_shapes=list(scratch) + buffers,
        compiler_params=pltpu.CompilerParams(vmem_limit_bytes=VMEM),
        cost_estimate=pl.CostEstimate(flops=flops, bytes_accessed=moved, transcendentals=0),
        name=name,
    )(*args)


def forward_call(first, last, experts, slots, args):
    tokens = TREE
    sent = experts * slots
    outs = [] if first else [shape((tokens, D))]
    outs += [
        shape((tokens, D), bf16),
        shape((tokens, 3 * D), bf16),
        shape((tokens, D), bf16),
        shape((16, tokens)),
        shape((tokens, D)),
        shape((tokens, D), bf16),
        shape((40, tokens)),
        shape((tokens, 128)),
        shape((tokens, 128), bf16),
        shape((sent, D), bf16),
        shape((D, 128), bf16),
    ]
    if last:
        outs += [shape((sent, D), bf16), shape((sent, D), bf16)]
    padded = -(-tokens // 128) * 128
    scratch = [pltpu.VMEM((tokens, 128), f32), pltpu.VMEM((128, padded), f32)]
    body = functools.partial(forward_kernel, first, last, experts, slots)
    inputs, results = (1, 0) if first else (6, 1)
    late = [inputs + 1] + ([inputs + 6] if last else [])
    early = ([] if first else [0]) + [results + n for n in (0, 1, 2, 4, 5)]
    return whole_call(body, "block_forward", outs, scratch, args, 20 * 10**9, late, early)


def gating_kernel(last, experts, slots, *refs):
    refs = list(refs)
    gx_ref, n2_ref, y_ref, gxs_ref, slotr_ref, info_ref, chosen_ref, gcol_ref, small_ref = [
        refs.pop(0) for _ in range(9)
    ]
    z_ref, mix_ref = refs.pop(0), refs.pop(0)
    if last:
        mid_ref, slotc_ref = refs.pop(0), refs.pop(0)
    else:
        gz_ref = refs.pop(0)
    gn2_ref, gsm_ref, gmix_ref, gprev_ref = [refs.pop(0) for _ in range(4)]
    if last:
        out_ref = refs.pop(0)
    tokens = n2_ref.shape[0]
    size, block = row_blocks(tokens)
    small = small_ref[...].astype(f32).T
    small_half = small[0:32, :].astype(bf16)
    vectors = small[S_VEC : S_VEC + 2, :]
    slot_row = slotr_ref[...]
    ones = jnp.ones((16, D), bf16)
    row = lax.broadcasted_iota(jnp.int32, (16, slots), 0)
    scattered = jnp.zeros((16, tokens), f32)
    for e in range(experts):
        rows = slice(e * slots, (e + 1) * slots)
        inner = y_ref[rows, :].astype(f32) * gxs_ref[rows, :].astype(f32)
        upper, lower = split_bf16(inner)
        sums = dot_nt(ones, upper) + dot_nt(ones, lower)
        upper, lower = split_bf16(sums)
        lhs = jnp.where(row == e, upper.astype(f32), 0.0) + jnp.where(
            row == 8 + e, lower.astype(f32), 0.0
        )
        scattered = scattered + dot(lhs.astype(bf16), one_hot(slot_row, e, slots))
    gx = gx_ref[...].astype(f32)
    gx_half = gx.astype(bf16)
    n2 = n2_ref[...]
    upper, lower = split_bf16(gx * n2.astype(f32))
    gx_n2 = (dot_nt(ones, upper) + dot_nt(ones, lower))[0:1, :]
    gx_small = dot_nt(small_half, gx_half)
    prob = info_ref[16:32, :]
    chosen = chosen_ref[...]
    gates = prob * chosen
    trow = lax.broadcasted_iota(jnp.int32, (16, tokens), 0)
    gp = jnp.concatenate([scattered[0:8, :] + scattered[8:16, :], jnp.zeros((8, tokens), f32)], 0)
    gp = jnp.where(trow == experts + 1, gx_n2, jnp.where(trow < experts, gp, 0.0))
    crow = lax.broadcasted_iota(jnp.int32, (8, tokens), 0)
    glog = jnp.zeros((8, tokens), f32)
    coefs = jnp.zeros((8, tokens), f32)
    for c in range(2):
        a0 = info_ref[32 + 2 * c : 33 + 2 * c, :]
        a1 = info_ref[33 + 2 * c : 34 + 2 * c, :]
        gx_v = gx_small[S_VEC + c : S_VEC + c + 1, :]
        share = gates[experts + 2 + c : experts + 3 + c, :]
        gp = jnp.where(trow == experts + 2 + c, a0 * gx_n2 + a1 * gx_v, gp)
        gl = share * (gx_n2 - gx_v) * a0 * a1
        glog = jnp.where(crow == 2 * c, gl, jnp.where(crow == 2 * c + 1, -gl, glog))
        coefs = jnp.where(crow == c, share * a1, coefs)
    gp = gp * chosen
    gz = prob * (gp - jnp.sum(prob * gp, axis=0, keepdims=True))
    if not last:
        gz = gz + gz_ref[...]
    z = z_ref[...]
    gmix_ref[...] = lax.dot_general(
        z, gz, (((1,), (1,)), ((), ())), precision=lax.Precision.HIGHEST, preferred_element_type=f32
    )
    mix = mix_ref[...]
    gprev = jnp.zeros((16, tokens), f32)
    for o in range(experts + 4):
        gprev = gprev + mix[:, o : o + 1] * gz[o : o + 1, :]
    gprev_ref[...] = gprev
    allg = jnp.concatenate([gz, glog, jnp.zeros((8, tokens), f32)], axis=0)
    upper, lower = split_bf16(allg)
    gsm = dot(upper, n2) + dot(lower, n2)
    cu, cl = split_bf16(jnp.concatenate([coefs, jnp.zeros((8, tokens), f32)], axis=0))
    gvec = dot(cu, gx_half) + dot(cl, gx_half)
    gsm_ref[0:24, :] = gsm[0:24, :]
    gsm_ref[24:32, :] = jnp.concatenate(
        [jnp.zeros((2, D), f32), gvec[0:2, :], jnp.zeros((4, D), f32)], axis=0
    )
    both = jnp.concatenate([upper, lower], axis=0)
    twice = jnp.concatenate([small_half, small_half], axis=0)
    gn2_ref[...] = dot_tn(both, twice)

    def add(i, carry):
        rows = block(i)
        gn2_ref[rows, :] = gn2_ref[rows, :] + gcol_ref[rows, 16:17] * gx_ref[rows, :].astype(f32)
        if last:
            out_ref[rows, :] = combine_rows(
                rows, mid_ref, n2_ref, y_ref, gcol_ref, slotc_ref, vectors, experts, slots
            ).astype(bf16)
        return carry

    lax.fori_loop(0, BLOCKS, add, 0)


def gating_outputs(last):
    tokens = TREE
    outs = [shape((tokens, D)), shape((32, D)), shape((16, 16)), shape((16, tokens))]
    if last:
        outs += [shape((tokens, D), bf16)]
    return outs


def backward_kernel(first, experts, slots, traffic, *refs):
    refs = list(refs)
    gx_ref, gn2p_ref, gn2e_ref, slotc_ref, mid_ref, att_ref, w_ref, qkv_ref, n1_ref, x_ref = [
        refs.pop(0) for _ in range(10)
    ]
    biast_ref, lse_ref, gsm_ref = [refs.pop(0) for _ in range(3)]
    if not first:
        slotr_ref, gpack_ref = refs.pop(0), refs.pop(0)
    gout_ref, dw_ref = refs.pop(0), refs.pop(0)
    if not first:
        gxs_ref, gy_ref = refs.pop(0), refs.pop(0)
    gatt, go, gqkv, turn = refs
    tokens = n1_ref.shape[0]
    size, block = row_blocks(tokens)
    small = w_ref[:, W_SMALL:].astype(f32).T
    gain0 = small[S_GAIN : S_GAIN + 1, :]
    gain1 = small[S_GAIN + 1 : S_GAIN + 2, :]

    def enter(i, total):
        rows = block(i)
        gn2 = gn2p_ref[rows, :]
        slot = slotc_ref[rows, :]
        for e in range(experts):
            gn2 = gn2 + dot(one_hot_col(slot, e, slots), gn2e_ref[e * slots : (e + 1) * slots, :])
        middle = mid_ref[rows, :]
        r = inv_rms(middle)
        scaled = gain1 * gn2
        inner = jnp.mean(middle * scaled, axis=1, keepdims=True)
        gmid = gx_ref[rows, :].astype(f32) + r * scaled - middle * (r * r * r * inner)
        gout_ref[rows, :] = gmid
        half = gmid.astype(bf16)
        gatt[rows, :] = half
        go[rows, :] = dot_nt(half, w_ref[:, W_OUT:W_SMALL]).astype(bf16)
        return total + jnp.sum(gn2 * middle * r, axis=0, keepdims=True)

    ggain1 = lax.fori_loop(0, BLOCKS, enter, jnp.zeros((1, D), f32))
    traffic.need(att_ref)
    lane = lax.broadcasted_iota(jnp.int32, (1, 128), 1)
    low_f = jnp.where(lane < HD, 1.0, 0.0)
    low = low_f.astype(bf16)
    high = (1.0 - low_f).astype(bf16)
    scale = HD**-0.5

    def out_grad(p, carry):
        here = pl.ds(pl.multiple_of(p * 128, 128), 128)
        dw_ref[here, W_OUT:W_SMALL] = dot_tn(att_ref[:, here], gatt[...]).astype(bf16)
        return carry

    lax.fori_loop(0, D // 128, out_grad, 0)
    traffic.flush(dw_ref, (slice(None), slice(W_OUT, W_SMALL)))
    traffic.need(qkv_ref, biast_ref, lse_ref)
    spans = causal_spans(tokens)

    def pair(p, carry):
        here = pl.ds(pl.multiple_of(p * 128, 128), 128)
        lanes_k = pl.ds(pl.multiple_of(D + p * 128, 128), 128)
        lanes_v = pl.ds(pl.multiple_of(2 * D + p * 128, 128), 128)
        q = qkv_ref[:, here] * bf16(scale)
        k = qkv_ref[:, lanes_k]
        v = qkv_ref[:, lanes_v]
        g = go[:, here]
        turn[0:tokens, :] = g.astype(f32) * att_ref[:, here].astype(f32)
        inner = turn[...].T[:, 0:tokens]
        turn[0:tokens, :] = k.astype(f32)
        kt = turn[...].T[:, 0:tokens].astype(bf16)
        gq_t = []
        gk = [0.0] * len(spans)
        gv = [0.0] * len(spans)
        for h, mask in ((0, low), (1, high)):
            qh = q * mask
            gh = g * mask
            dsum = jnp.sum(inner[h * HD : (h + 1) * HD, :], axis=0, keepdims=True)
            lse = lse_ref[pl.ds(2 * p + h, 1), :]
            gq_h = []
            for n, (start, stop) in enumerate(spans):
                st = dot_nt(k[start:stop], qh[start:]) + biast_ref[start:stop, start:]
                pt = jnp.exp(st - lse[:, start:])
                gpt = dot_nt(v[start:stop], gh[start:])
                gst = (pt * (gpt - dsum[:, start:])).astype(bf16)
                gv[n] = gv[n] + dot(pt.astype(bf16), gh[start:])
                gk[n] = gk[n] + dot(gst, qh[start:])
                part = dot(kt[h * HD : (h + 1) * HD, start:stop], gst)
                gq_h.append(part)
            cols = []
            for n, (start, stop) in enumerate(spans):
                piece = 0.0
                for m in range(n + 1):
                    origin = spans[m][0]
                    piece = piece + gq_h[m][:, start - origin : stop - origin]
                cols.append(piece)
            gq_t.append(jnp.concatenate(cols, axis=1))
        turn_t = jnp.concatenate(gq_t, axis=0) * scale
        pad = turn.shape[0] - tokens
        turn_t = jnp.concatenate([turn_t, jnp.zeros((128, pad), f32)], axis=1)
        gqkv[:, here] = turn_t.T[0:tokens, :].astype(bf16)
        for n, (start, stop) in enumerate(spans):
            gqkv[start:stop, lanes_k] = gk[n].astype(bf16)
            gqkv[start:stop, lanes_v] = gv[n].astype(bf16)
        return carry

    turn[...] = jnp.zeros_like(turn)
    lax.fori_loop(0, H // 2, pair, 0)
    traffic.need(n1_ref)

    def in_grad(p, carry):
        here = pl.ds(pl.multiple_of(p * 128, 128), 128)
        dw_ref[here, 0:W_OUT] = dot_tn(n1_ref[:, here], gqkv[...]).astype(bf16)
        return carry

    lax.fori_loop(0, D // 128, in_grad, 0)
    traffic.flush(dw_ref, (slice(None), slice(0, W_OUT)))
    traffic.need(x_ref)

    def leave(i, total):
        rows = block(i)
        gn1 = dot_nt(gqkv[rows, :], w_ref[:, 0:W_OUT])
        x = x_ref[rows, :].astype(f32)
        r = inv_rms(x)
        scaled = gain0 * gn1
        inner = jnp.mean(x * scaled, axis=1, keepdims=True)
        gx = gout_ref[rows, :] + r * scaled - x * (r * r * r * inner)
        gout_ref[rows, :] = gx
        gatt[rows, :] = gx.astype(bf16)
        return total + jnp.sum(gn1 * x * r, axis=0, keepdims=True)

    ggain0 = lax.fori_loop(0, BLOCKS, leave, jnp.zeros((1, D), f32))
    rows = jnp.concatenate(
        [gsm_ref[0:24, :], ggain0, ggain1, gsm_ref[26:32, :], jnp.zeros((96, D), f32)], axis=0
    )
    dw_ref[:, W_SMALL:] = rows.T.astype(bf16)
    traffic.flush(dw_ref, (slice(None), slice(W_SMALL, W_ALL)))
    traffic.flush(gout_ref)
    if not first:
        hot = all_one_hot(slotr_ref[...], experts, slots)
        send_grads(hot, gatt[...], gpack_ref[...], gxs_ref, gy_ref, experts, slots)


def backward_call(first, experts, slots, args):
    tokens = TREE
    sent = experts * slots
    outs = [shape((tokens, D)), shape((D, W_ALL), bf16)]
    if not first:
        outs += [shape((sent, D), bf16), shape((sent, D), bf16)]
    padded = -(-tokens // 128) * 128
    scratch = [
        pltpu.VMEM((tokens, D), bf16),
        pltpu.VMEM((tokens, D), bf16),
        pltpu.VMEM((tokens, 3 * D), bf16),
        pltpu.VMEM((padded, 128), f32),
    ]
    body = functools.partial(backward_kernel, first, experts, slots)
    return whole_call(
        body, "block_backward", outs, scratch, args, 40 * 10**9, (5, 7, 8, 9, 10, 11), (0, 1)
    )


class Packing:
    def __init__(self, shards, part, ff):
        self.shards, self.part, self.ff = shards, part, ff
        self.padded = -(-part // 16) * 16
        self.chunks = ff // 256
        self.own = ff // shards
        self.down = 2 * self.chunks * self.padded
        self.rows = self.down + (D // 256) * self.own

    def pack(self, gate, up, down):
        pieces = []
        for wide in (gate, up):
            cut = wide.reshape(self.part, self.chunks, 256).transpose(1, 0, 2)
            cut = jnp.pad(cut, [(0, 0), (0, self.padded - self.part), (0, 0)])
            pieces.append(cut.reshape(self.chunks * self.padded, 256))
        pieces.append(
            down.reshape(self.own, D // 256, 256).transpose(1, 0, 2).reshape(-1, 256)
        )
        return jnp.concatenate(pieces, axis=0)

    def wide_part(self, ref, n, j):
        at = pl.multiple_of((n * self.chunks + j) * self.padded, 16)
        return ref[:, pl.ds(at, self.padded), :][:, : self.part, :].reshape(D, 256)

    def tall_part(self, ref, j):
        group = 256 // self.own
        here = pl.ds(j * group, group)
        pieces = []
        for c in range(D // 256):
            at = self.down + c * self.own
            pieces.append(ref[here, at : at + self.own, :].reshape(256, 256))
        return jnp.concatenate(pieces, axis=1)

    def put_wide(self, ref, n, j, grad):
        at = pl.multiple_of((n * self.chunks + j) * self.padded, 16)
        ref[:, pl.ds(at, self.part), :] = grad.reshape(self.shards, self.part, 256)

    def put_tall(self, ref, j, grad):
        group = 256 // self.own
        for c in range(D // 256):
            at = self.down + c * self.own
            ref[pl.ds(j * group, group), at : at + self.own, :] = grad[
                :, c * 256 : (c + 1) * 256
            ].reshape(group, self.own, 256)


class Exchange:
    def __init__(self, experts, slots):
        self.experts, self.slots = experts, slots
        first = -(-slots // 32) * 16
        self.waves = ((0, first), (first, slots - first))
        self.ranges = [(0, slots)]
        for _, size in self.waves:
            start = self.ranges[-1][0] + self.ranges[-1][1]
            self.ranges.append((start, (experts - 1) * size))
        self.total = experts * slots

    def held(self, wave, d):
        size = self.waves[wave][1]
        return pl.ds(self.ranges[1 + wave][0] + (d - 1) * size, size)

    def slot(self, device, wave):
        offset, size = self.waves[wave]
        return pl.ds(pl.multiple_of(device * self.slots + offset, 16), size)


MESH = pl.DeviceIdType.MESH


def greet(experts):
    me = lax.axis_index("expert")
    barrier = pltpu.get_barrier_semaphore()
    for d in range(1, experts):
        pl.semaphore_signal(
            barrier, inc=1, device_id={"expert": lax.rem(me + d, experts)}, device_id_type=MESH
        )
    pl.semaphore_wait(barrier, experts - 1)


def out_copies(ex, wave, src, dst, sends, recvs):
    me = lax.axis_index("expert")
    copies = []
    for d in range(1, ex.experts):
        to = lax.rem(me + d, ex.experts)
        copies.append(
            pltpu.make_async_remote_copy(
                src_ref=src.at[ex.slot(to, wave)],
                dst_ref=dst.at[ex.held(wave, d)],
                send_sem=sends.at[wave, d - 1],
                recv_sem=recvs.at[wave, d - 1],
                device_id={"expert": to},
                device_id_type=MESH,
            )
        )
    return copies


def back_copies(ex, wave, n, src, dst, sends, recvs):
    me = lax.axis_index("expert")
    copies = []
    for d in range(1, ex.experts):
        copies.append(
            pltpu.make_async_remote_copy(
                src_ref=src.at[ex.held(wave, d)],
                dst_ref=dst.at[ex.slot(me, wave)],
                send_sem=sends.at[n, wave, d - 1],
                recv_sem=recvs.at[n, wave, d - 1],
                device_id={"expert": lax.rem(me + ex.experts - d, ex.experts)},
                device_id_type=MESH,
            )
        )
    return copies


def own_slots(ex):
    me = lax.axis_index("expert")
    return pl.ds(pl.multiple_of(me * ex.slots, 16), ex.slots)


def dispatch_kernel(ex, send, recv, sends, recvs):
    greet(ex.experts)
    copies = out_copies(ex, 0, send, recv, sends, recvs)
    copies += out_copies(ex, 1, send, recv, sends, recvs)
    for copy in copies:
        copy.start()
    recv[0 : ex.slots, :] = send[own_slots(ex), :]
    for copy in copies:
        copy.wait()


def dispatch_call(ex, rows):
    vmem = pl.BlockSpec(memory_space=pltpu.VMEM)
    return pl.pallas_call(
        functools.partial(dispatch_kernel, ex),
        out_shape=shape((ex.total, D), bf16),
        in_specs=[vmem],
        out_specs=vmem,
        scratch_shapes=[pltpu.SemaphoreType.DMA((2, ex.experts - 1))] * 2,
        compiler_params=pltpu.CompilerParams(
            vmem_limit_bytes=8 << 20, collective_id=3, has_side_effects=True
        ),
        cost_estimate=pl.CostEstimate(flops=35 * 10**9, bytes_accessed=10**6, transcendentals=0),
        name="dispatch",
    )(rows)


def exchange_kernel(mode, pack, ex, *refs):
    refs = list(refs)
    forward, backward = mode in ("forward", "both"), mode in ("backward", "both")
    recv_n = refs.pop(0)
    w_hbm = refs.pop(0)
    if backward:
        send_g = refs.pop(0)
        if mode == "backward":
            gate_hbm, up_hbm = refs.pop(0), refs.pop(0)
        gating_far = [refs.pop(0) for _ in range(12)]
    if forward:
        back_y = refs.pop(0)
    if mode == "forward":
        gates_far, ups_far, gates, ups = [refs.pop(0) for _ in range(4)]
    else:
        back_g, dw_far = refs.pop(0), refs.pop(0)
        gating_outs = [refs.pop(0) for _ in range(5 if mode == "both" else 4)]
    if forward:
        out_y, acc_y = refs.pop(0), refs.pop(0)
    if backward:
        recv_g, out_g, hids, gates, ups, rows_t, acc_g = [refs.pop(0) for _ in range(7)]
        gating = [refs.pop(0) for _ in range(12)]
    w = refs.pop(0)
    sends, recvs, backs, gots, local = refs
    traffic = Traffic()
    if mode == "forward":
        traffic.sink(gates, gates_far, local.at[4:7])
        traffic.sink(ups, ups_far, local.at[7:10])

    loads = [pltpu.make_async_copy(w_hbm, w, local.at[0])]
    if mode == "backward":
        loads.append(pltpu.make_async_copy(gate_hbm, gates, local.at[1]))
        loads.append(pltpu.make_async_copy(up_hbm, ups, local.at[2]))
    if mode == "backward":
        for n, (far, near) in enumerate(zip(gating_far, gating)):
            traffic.fetch(far, near, local.at[4 + n])
    for copy in loads:
        copy.start()
    if mode == "both":
        for n, (far, near) in enumerate(zip(gating_far, gating)):
            traffic.fetch(far, near, local.at[4 + n])
    greet(ex.experts)

    def work(start, size):
        rows = slice(start, start + size)
        part = slice(0, size)
        if forward:
            acc_y[part, :] = jnp.zeros((size, D), f32)
        if backward:
            acc_g[part, :] = jnp.zeros((size, D), f32)

        def chunk(j, carry):
            lanes = pl.ds(pl.multiple_of(j * 256, 256), 256)
            gate_w, up_w = pack.wide_part(w, 0, j), pack.wide_part(w, 1, j)
            down_w = pack.tall_part(w, j)
            if forward:
                r = recv_n[rows, :]
                gate, up = dot(r, gate_w), dot(r, up_w)
                if mode == "forward":
                    gates[rows, lanes] = gate.astype(bf16)
                    ups[rows, lanes] = up.astype(bf16)
            else:
                gate, up = gates[rows, lanes].astype(f32), ups[rows, lanes].astype(f32)
            s = jax.nn.sigmoid(gate)
            act = gate * s
            hid = (act * up).astype(bf16)
            if forward:
                acc_y[part, :] = acc_y[part, :] + dot(hid, down_w)
            if backward:
                hids[rows, lanes] = hid
                ghid = dot_nt(recv_g[rows, :], down_w)
                guv = (ghid * act).astype(bf16)
                ggu = (ghid * up * (s * (1.0 + gate * (1.0 - s)))).astype(bf16)
                gates[rows, lanes] = ggu
                ups[rows, lanes] = guv
                acc_g[part, :] = acc_g[part, :] + dot_nt(ggu, gate_w) + dot_nt(guv, up_w)
            return carry

        lax.fori_loop(0, pack.chunks, chunk, 0)
        if mode == "forward":
            here = pl.ds(start, size)
            traffic.flush(gates, here)
            traffic.flush(ups, here)
        if forward:
            out_y[rows, :] = acc_y[part, :].astype(bf16)
        if backward:
            out_g[rows, :] = acc_g[part, :].astype(bf16)

    def send_back(wave):
        ys = back_copies(ex, wave, 0, out_y, back_y, backs, gots) if forward else []
        gs = back_copies(ex, wave, 1, out_g, back_g, backs, gots) if backward else []
        for copy in ys + gs:
            copy.start()
        return ys, gs

    if backward:
        waves = [out_copies(ex, n, send_g, recv_g, sends, recvs) for n in range(2)]
        for copy in waves[0]:
            copy.start()
        recv_g[0 : ex.slots, :] = send_g[own_slots(ex), :]
        if mode == "backward":
            traffic.need(*gating)
            gating_kernel(False, ex.experts, ex.slots, *gating, *gating_outs)
    for copy in loads:
        copy.wait()
    if backward:
        work(*ex.ranges[0])
        for copy in waves[0]:
            copy.wait_send()
        for copy in waves[1]:
            copy.start()
        for copy in waves[0]:
            copy.wait_recv()
    work(*ex.ranges[1])
    ys, gs = send_back(0)
    if backward:
        for copy in waves[1]:
            copy.wait()
    work(*ex.ranges[2])
    more = send_back(1)
    ys, gs = ys + more[0], gs + more[1]
    if mode == "forward":
        work(*ex.ranges[0])
    if forward:
        back_y[own_slots(ex), :] = out_y[0 : ex.slots, :]
    if backward:
        back_g[own_slots(ex), :] = out_g[0 : ex.slots, :]
        rows_t[...] = recv_n[...].T
        dw = w
        if pack.padded != pack.part:
            dw[...] = jnp.zeros_like(dw)

        def weights(j, carry):
            lanes = pl.ds(pl.multiple_of(j * 256, 256), 256)
            pack.put_wide(dw, 0, j, dot(rows_t[...], gates[:, lanes]).astype(bf16))
            pack.put_wide(dw, 1, j, dot(rows_t[...], ups[:, lanes]).astype(bf16))
            pack.put_tall(dw, j, dot_tn(hids[:, lanes], recv_g[...]).astype(bf16))
            return carry

        lax.fori_loop(0, pack.chunks, weights, 0)
        leaving = pltpu.make_async_copy(dw, dw_far, local.at[3])
        leaving.start()
    for copy in ys:
        copy.wait()
    if mode == "both":
        traffic.need(*gating)
        gating_kernel(True, ex.experts, ex.slots, *gating[:2], back_y, *gating[2:], *gating_outs)
    for copy in gs:
        copy.wait()
    if backward:
        leaving.wait()
    traffic.finish()


SPLIT = 13 * 128


def cube_kernel(part, g_ref, out_ref, got_c, sums, got_a, got_b, half_a, half_b, end_a, end_b, send, recv):
    me = lax.axis_index("shard")
    core, x, y = lax.rem(me, 2), lax.rem(me // 2, 2), me // 4
    near, over_x, over_y = (
        me + 1 - 2 * core,
        me + 2 - 4 * x,
        me + 4 - 8 * y,
    )
    barrier = pltpu.get_barrier_semaphore()
    for other in (near, over_x, over_y):
        pl.semaphore_signal(barrier, inc=1, device_id={"shard": other}, device_id_type=MESH)
    pl.semaphore_wait(barrier, 3)
    cols_a, cols_b = slice(0, SPLIT), slice(SPLIT, W_ALL)

    def rows(shard):
        return pl.ds(pl.multiple_of(shard * part, 16), part)

    def copy(n, src, dst, to):
        made = pltpu.make_async_remote_copy(
            src_ref=src,
            dst_ref=dst,
            send_sem=send.at[n],
            recv_sem=recv.at[n],
            device_id={"shard": to},
            device_id_type=MESH,
        )
        made.start()
        return made

    chips = [2 * (1 - y) + 1 - x, 2 * y + 1 - x, 2 * (1 - y) + x, 2 * y + x]
    first = [
        copy(n, g_ref.at[rows(2 * chip + 1 - core)], got_c.at[chip], near)
        for n, chip in enumerate(chips)
    ]

    def merge(n):
        chip = chips[n]
        first[n].wait_recv()
        own = g_ref[rows(2 * chip + core), :].astype(f32)
        sums[chip] = (own + got_c[chip].astype(f32)).astype(bf16)

    def total(chip, cols, got):
        return sums[chip, :, cols].astype(f32) + got[...].astype(f32)

    merge(0)
    a0 = copy(4, sums.at[chips[0], :, cols_a], got_a.at[1 - y], over_x)
    b0 = copy(5, sums.at[chips[0], :, cols_b], got_b.at[1 - x], over_y)
    merge(1)
    a1 = copy(6, sums.at[chips[1], :, cols_a], got_a.at[y], over_x)
    merge(2)
    b1 = copy(7, sums.at[chips[2], :, cols_b], got_b.at[x], over_y)
    merge(3)
    a0.wait_recv()
    half_a[...] = total(chips[2], cols_a, got_a.at[1 - y]).astype(bf16)
    a2 = copy(8, half_a, end_a, over_y)
    b0.wait_recv()
    half_b[...] = total(chips[1], cols_b, got_b.at[1 - x]).astype(bf16)
    b2 = copy(9, half_b, end_b, over_x)
    a1.wait_recv()
    keep_a = total(chips[3], cols_a, got_a.at[y])
    a2.wait_recv()
    out_ref[:, cols_a] = (keep_a + end_a[...].astype(f32)).astype(bf16)
    b1.wait_recv()
    keep_b = total(chips[3], cols_b, got_b.at[x])
    b2.wait_recv()
    out_ref[:, cols_b] = (keep_b + end_b[...].astype(f32)).astype(bf16)
    for made in first + [a0, b0, a1, b1, a2, b2]:
        made.wait_send()


def scatter_sum(grads, part):
    if lax.axis_size("shard") != 8:
        return lax.psum_scatter(grads, "shard", scatter_dimension=0, tiled=True)
    vmem = pl.BlockSpec(memory_space=pltpu.VMEM)
    rest = W_ALL - SPLIT
    return pl.pallas_call(
        functools.partial(cube_kernel, part),
        out_shape=shape((part, W_ALL), bf16),
        in_specs=[vmem],
        out_specs=vmem,
        scratch_shapes=[
            pltpu.VMEM((4, part, W_ALL), bf16),
            pltpu.VMEM((4, part, W_ALL), bf16),
            pltpu.VMEM((2, part, SPLIT), bf16),
            pltpu.VMEM((2, part, rest), bf16),
            pltpu.VMEM((part, SPLIT), bf16),
            pltpu.VMEM((part, rest), bf16),
            pltpu.VMEM((part, SPLIT), bf16),
            pltpu.VMEM((part, rest), bf16),
            pltpu.SemaphoreType.DMA((10,)),
            pltpu.SemaphoreType.DMA((10,)),
        ],
        compiler_params=pltpu.CompilerParams(
            vmem_limit_bytes=32 << 20, collective_id=4, has_side_effects=True
        ),
        cost_estimate=pl.CostEstimate(flops=35 * 10**9, bytes_accessed=10**7, transcendentals=0),
        name="scatter_sum",
    )(grads)


EXCHANGE_IDS = {"forward": 0, "both": 1, "backward": 2}


def exchange_call(mode, pack, ex, args):
    rows, ff = ex.total, pack.ff
    forward, backward = mode in ("forward", "both"), mode in ("backward", "both")
    flat, wide = shape((rows, D), bf16), shape((rows, ff), bf16)
    packed = (pack.shards, pack.rows, 256)
    most = max(size for _, size in ex.ranges)
    vmem = pl.BlockSpec(memory_space=pltpu.VMEM)
    far = pl.BlockSpec(memory_space=pl.ANY)
    in_specs = [vmem] * len(args)
    in_specs[1] = far
    scratch = []
    if mode == "forward":
        outs = [flat, wide, wide]
    elif mode == "both":
        outs = [flat, flat, shape(packed, bf16)] + gating_outputs(True)
    else:
        in_specs[3] = in_specs[4] = far
        outs = [flat, shape(packed, bf16)] + gating_outputs(False)
    out_specs = [vmem] * len(outs)
    if mode == "forward":
        out_specs[1] = out_specs[2] = far
        scratch += [pltpu.VMEM((rows, ff), bf16)] * 2
    else:
        in_specs[-12:] = [far] * 12
        out_specs[2 if mode == "both" else 1] = far
    if forward:
        scratch += [pltpu.VMEM((rows, D), bf16), pltpu.VMEM((most, D), f32)]
    if backward:
        scratch += [pltpu.VMEM((rows, D), bf16)] * 2
        scratch += [pltpu.VMEM((rows, ff), bf16)] * 3
        scratch += [pltpu.VMEM((D, rows), bf16), pltpu.VMEM((most, D), f32)]
        scratch += [pltpu.VMEM(a.shape, a.dtype) for a in args[-12:]]
    scratch.append(pltpu.VMEM(packed, bf16))
    scratch += [pltpu.SemaphoreType.DMA((2, ex.experts - 1))] * 2
    scratch += [pltpu.SemaphoreType.DMA((2, 2, ex.experts - 1))] * 2
    scratch.append(pltpu.SemaphoreType.DMA((16,)))
    work = 6 * rows * D * ff * (1 if mode == "forward" else 2 if mode == "backward" else 3)
    return pl.pallas_call(
        functools.partial(exchange_kernel, mode, pack, ex),
        out_shape=outs,
        in_specs=in_specs,
        out_specs=out_specs,
        scratch_shapes=scratch,
        compiler_params=pltpu.CompilerParams(
            vmem_limit_bytes=62 << 20, collective_id=EXCHANGE_IDS[mode], has_side_effects=True
        ),
        cost_estimate=pl.CostEstimate(
            flops=10**9 if mode == "backward" else work + 40 * 10**9,
            bytes_accessed=6 * D * ff,
            transcendentals=0,
        ),
        name="experts_" + mode,
    )(*args)


def expert_outputs_kernel(pack, traffic, first_ref, second_ref, gate_ref, up_ref, down_ref):
    for l, ref in enumerate((first_ref, second_ref)):
        for n, out in enumerate((gate_ref, up_ref)):
            for j in range(pack.chunks):
                at = (n * pack.chunks + j) * pack.padded
                out[l, :, j * 256 : (j + 1) * 256] = ref[at : at + pack.part, :].astype(f32)
        for c in range(D // 256):
            at = pack.down + c * pack.own
            down_ref[l, :, c * 256 : (c + 1) * 256] = ref[at : at + pack.own, :].astype(f32)


def expert_outputs(pack, grads):
    wide = shape((LAYERS, pack.part, pack.ff))
    outs = [wide, wide, shape((LAYERS, pack.own, D))]
    body = functools.partial(expert_outputs_kernel, pack)
    return whole_call(body, "expert_outputs", outs, [], grads, 10**6)


def dense_outputs_kernel(
    part, labels, traffic, first_ref, second_ref, proj_ref, out_ref, gain_ref, router_ref, vec_ref, const_ref,
    turn,
):
    for l, ref in enumerate((first_ref, second_ref)):
        for c in range(3):
            proj_ref[l, c] = ref[:, c * D : (c + 1) * D].astype(f32)
        out_ref[l] = ref[:, W_OUT:W_SMALL].astype(f32)
        small = ref[:, W_SMALL:].astype(f32)
        router_ref[l] = small[:, 0:labels]
        for c in range(2):
            const_ref[l, c] = small[:, S_CONST + 2 * c : S_CONST + 2 * c + 2]
        turn[0:part, :] = small
        rows = turn[...].T
        gain_ref[l] = rows[S_GAIN : S_GAIN + 2, 0:part]
        vec_ref[l] = rows[S_VEC : S_VEC + 2, 0:part]


def dense_outputs(part, labels, grads):
    outs = [
        shape((LAYERS, 3, part, D)),
        shape((LAYERS, part, D)),
        shape((LAYERS, 2, part)),
        shape((LAYERS, part, labels)),
        shape((LAYERS, 2, part)),
        shape((LAYERS, 2, part, 2)),
    ]
    body = functools.partial(dense_outputs_kernel, part, labels)
    return whole_call(body, "dense_outputs", outs, [pltpu.VMEM((128, 128), f32)], grads, 10**6)


def on_device(
    hidden_in,
    prior_logits,
    project_weight,
    output_weight,
    norm_gain,
    router_weight,
    mixing_weight,
    const_vector,
    const_weight,
    gate_weight,
    up_weight,
    down_weight,
    routes,
    priority,
    leaf_parent,
    cotangent,
):
    experts = lax.axis_size("expert")
    total_experts = experts + 4
    tokens = hidden_in.shape[0]
    capacity = 9 * tokens * TOP // (8 * total_experts)
    slots = -(-capacity // 16) * 16
    part = project_weight.shape[2]

    def pad_cols(a, width):
        return jnp.pad(a, [(0, 0)] * (a.ndim - 1) + [(0, width - a.shape[-1])])

    dense = []
    experts_w = []
    pack = Packing(lax.axis_size("shard"), part, gate_weight.shape[3])
    for l in range(LAYERS):
        small = jnp.concatenate(
            [
                pad_cols(router_weight[l], S_CONST),
                const_weight[l, 0],
                const_weight[l, 1],
                jnp.zeros((part, S_GAIN - S_CONST - 4), bf16),
                norm_gain[l].T,
                const_vector[l].T,
            ],
            axis=1,
        )
        packed = jnp.concatenate(
            [project_weight[l, c] for c in range(3)] + [output_weight[l], pad_cols(small, 128)],
            axis=1,
        )
        dense.append(lax.all_gather(packed, "shard", axis=0, tiled=True))
        mine = pack.pack(gate_weight[l, 0], up_weight[l, 0], down_weight[l, 0])
        experts_w.append(lax.all_gather(mine, "shard", axis=0, tiled=False))

    ranking = priority[0]
    earlier = (ranking[None, :] < ranking[:, None]).astype(bf16)
    labels = jnp.arange(total_experts, dtype=jnp.int32)
    hits = jnp.sum((routes[:, :, :, None] == labels).astype(f32), axis=2)
    chosen_rows = [jnp.pad(hits[l].T, [(0, 16 - total_experts), (0, 0)]) for l in range(LAYERS)]
    loaded = jnp.concatenate([hits[l, :, :experts] for l in range(LAYERS)], axis=1)
    loaded_half = loaded.astype(bf16)
    rank_col = dot(earlier, loaded_half)
    rank_row = lax.dot_general(
        loaded_half, earlier, (((0,), (1,)), ((), ())), preferred_element_type=f32
    )
    slot_col_all = jnp.where((loaded > 0) & (rank_col < capacity), rank_col, -1.0)
    slot_row_all = jnp.where((loaded.T > 0) & (rank_row < capacity), rank_row, -1.0)
    slot_col = [slot_col_all[:, l * experts : (l + 1) * experts] for l in range(LAYERS)]
    slot_row = [
        jnp.pad(
            slot_row_all[l * experts : (l + 1) * experts],
            [(0, 8 - experts), (0, 0)],
            constant_values=-1.0,
        )
        for l in range(LAYERS)
    ]
    visible = tree_visible(leaf_parent[0])
    bias = jnp.where(visible, 0.0, masked_fill)
    bias_t = jnp.where(visible.T, 0.0, masked_fill)
    mixes = [
        jnp.pad(mixing_weight[l], [(0, 16 - total_experts), (0, 16 - total_experts)])
        for l in range(LAYERS)
    ]
    z_rows = jnp.pad(prior_logits.T, [(0, 16 - total_experts), (0, 0)])

    ex = Exchange(experts, slots)
    saved = []
    front = [hidden_in]
    x_now = hidden_in
    for l in range(LAYERS):
        last = l == LAYERS - 1
        args = front + [dense[l], bias, z_rows, mixes[l].T, chosen_rows[l], slot_row[l]]
        if last:
            args.append(cotangent)
        outs = list(forward_call(l == 0, last, experts, slots, args))
        if l > 0:
            x_now = outs.pop(0)
        n1, qkv, att, lse, middle, n2, info, gcol, gpack, send, small = outs[:11]
        keep = dict(
            x=x_now, n1=n1, qkv=qkv, att=att, lse=lse, middle=middle, n2=n2, info=info,
            gcol=gcol, gpack=gpack, z=z_rows, small=small,
        )
        keep["received"] = dispatch_call(ex, send)
        if last:
            gating = [
                cotangent, n2, outs[11], slot_row[l], info, chosen_rows[l], gcol, small, z_rows,
                mixes[l], middle, slot_col[l],
            ]
            done = exchange_call(
                "both", pack, ex, [keep["received"], experts_w[l], outs[12]] + gating
            )
            keep["y"], keep["gin"], keep["dw"] = done[:3]
            keep["gating"] = done[3:]
        else:
            keep["y"], keep["gate"], keep["up"] = exchange_call(
                "forward", pack, ex, [keep["received"], experts_w[l]]
            )
        front = [middle, n2, keep["y"], gcol, slot_col[l], small]
        z_rows = info[0:16]
        saved.append(keep)

    gx = cotangent
    gz = None
    dense_grads = [None] * LAYERS
    mix_grads = [None] * LAYERS
    expert_grads = [None] * LAYERS
    hidden_out = None
    for l in range(LAYERS - 1, -1, -1):
        last = l == LAYERS - 1
        keep = saved[l]
        if not last:
            gating = [
                gx, keep["n2"], keep["y"], keep["gxs"], slot_row[l], keep["info"], chosen_rows[l],
                keep["gcol"], keep["small"], keep["z"], mixes[l], gz,
            ]
            done = exchange_call(
                "backward", pack, ex,
                [keep["received"], experts_w[l], keep["gy"], keep["gate"], keep["up"]] + gating,
            )
            keep["gin"], keep["dw"] = done[:2]
            keep["gating"] = done[2:]
        gn2, gsm, mix_grads[l], gz = keep["gating"][:4]
        if last:
            hidden_out = keep["gating"][4]
        d_experts, gn2 = lax.optimization_barrier((keep["dw"], gn2))
        if not last:
            gn2, expert_grads[l + 1] = lax.optimization_barrier((gn2, expert_grads[l + 1]))
        expert_grads[l] = lax.psum_scatter(d_experts, "shard", scatter_dimension=0, tiled=False)
        args = [
            gx, gn2, keep["gin"], slot_col[l], keep["middle"], keep["att"], dense[l], keep["qkv"],
            keep["n1"], keep["x"], bias_t, keep["lse"], gsm,
        ]
        if l > 0:
            args += [slot_row[l - 1], saved[l - 1]["gpack"]]
        outs = backward_call(l == 0, experts, slots, args)
        gx, d_dense = outs[:2]
        if l > 0:
            saved[l - 1]["gxs"], saved[l - 1]["gy"] = outs[2:4]
        if l == 0:
            mix_grads[0], d_dense = lax.optimization_barrier((mix_grads[0], d_dense))
        if l == 0:
            dense_grads[l] = scatter_sum(d_dense, part)
        else:
            dense_grads[l] = lax.psum_scatter(d_dense, "shard", scatter_dimension=0, tiled=True)

    both_dense = lax.psum(jnp.stack(dense_grads), "expert")
    dense_grads = [both_dense[l] for l in range(LAYERS)]
    mixing_total = lax.psum(jnp.stack(mix_grads), ("expert", "shard"))
    gate_grad, up_grad, down_grad = expert_outputs(pack, expert_grads)
    project_grad, output_grad, gain_grad, router_grad, vector_grad, const_grad = dense_outputs(
        part, total_experts, dense_grads
    )
    return (
        hidden_out,
        gx,
        gz[0:total_experts].T,
        project_grad,
        output_grad,
        gain_grad,
        router_grad,
        mixing_total[:, 0:total_experts, 0:total_experts],
        vector_grad,
        const_grad,
        gate_grad[:, None],
        up_grad[:, None],
        down_grad[:, None],
    )


def solution(mesh):
    both = ("expert", "shard")
    in_specs = (
        P(both, None),
        P(both, None),
        P(None, None, "shard", None),
        P(None, "shard", None),
        P(None, None, "shard"),
        P(None, "shard", None),
        P(),
        P(None, None, "shard"),
        P(None, None, "shard", None),
        P(None, "expert", "shard", None),
        P(None, "expert", "shard", None),
        P(None, "expert", "shard", None),
        P(None, both, None),
        P(both, None),
        P(both, None),
        P(both, None),
    )
    out_specs = (
        P(both, None),
        P(both, None),
        P(both, None),
        P(None, None, "shard", None),
        P(None, "shard", None),
        P(None, None, "shard"),
        P(None, "shard", None),
        P(),
        P(None, None, "shard"),
        P(None, None, "shard", None),
        P(None, "expert", "shard", None),
        P(None, "expert", "shard", None),
        P(None, "expert", "shard", None),
    )
    return jax.shard_map(
        on_device, mesh=mesh, in_specs=in_specs, out_specs=out_specs, check_vma=False
    )
```

```python
import functools

import jax
import jax.numpy as jnp
from jax import lax
from jax.experimental import pallas as pl
from jax.experimental.pallas import tpu as pltpu
from jax.sharding import PartitionSpec as P

D = 768
H = 12
HD = 64
TOP = 2
LAYERS = 2
TRUNK = 320
BRANCH = 64
LEAF = 32
TREE = 832

W_OUT = 3 * D
W_SMALL = 4 * D
W_ALL = 4 * D + 128
S_CONST = 16
S_GAIN = 24
S_VEC = 26

epsilon = 1e-06
masked_fill = -1e30
f32 = jnp.float32
bf16 = jnp.bfloat16
BLOCKS = 2
VMEM = 56 << 20


def dot(a, b):
    return jnp.dot(a, b, preferred_element_type=f32)


def dot_nt(a, b):
    return lax.dot_general(a, b, (((1,), (1,)), ((), ())), preferred_element_type=f32)


def dot_tn(a, b):
    return lax.dot_general(a, b, (((0,), (0,)), ((), ())), preferred_element_type=f32)


def split_bf16(v):
    high = v.astype(bf16)
    return high, (v - high.astype(f32)).astype(bf16)


def inv_rms(v):
    return lax.rsqrt(jnp.mean(v * v, axis=1, keepdims=True) + epsilon)


def tree_visible(parents):
    position = jnp.arange(TREE, dtype=jnp.int32)
    offset = position - TRUNK
    segment = jnp.where(
        position < TRUNK,
        0,
        jnp.where(offset < 4 * BRANCH, 1 + offset // BRANCH, 5 + (offset - 4 * BRANCH) // LEAF),
    )
    leaf_hits = (segment[:, None] - 5 == jnp.arange(8, dtype=jnp.int32)[None, :]).astype(jnp.int32)
    upper = jnp.where(segment >= 5, 1 + jnp.sum(leaf_hits * parents[None, :], axis=1), 0)
    key_segment = segment[None, :]
    causal = position[None, :] <= position[:, None]
    return causal & (
        (key_segment == segment[:, None]) | (key_segment == 0) | (key_segment == upper[:, None])
    )


def one_hot(slot_row, e, slots):
    row = lax.broadcasted_iota(jnp.int32, (slots, slot_row.shape[1]), 0).astype(f32)
    return jnp.where(row == slot_row[e : e + 1, :], 1.0, 0.0).astype(bf16)


def one_hot_col(slot_col, e, slots, scale=None):
    lane = lax.broadcasted_iota(jnp.int32, (slot_col.shape[0], slots), 1).astype(f32)
    value = 1.0 if scale is None else scale
    return jnp.where(lane == slot_col[:, e : e + 1], value, 0.0).astype(bf16)


def combine_rows(rows, middle_ref, n2_ref, y_ref, gcol_ref, slotc_ref, vectors, experts, slots):
    gcol = gcol_ref[rows, :]
    slot = slotc_ref[rows, :]
    total = middle_ref[rows, :] + gcol[:, 16:17] * n2_ref[rows, :].astype(f32)
    for c in range(2):
        total = total + gcol[:, 17 + c : 18 + c] * vectors[c : c + 1, :]
    for e in range(experts):
        weight = one_hot_col(slot, e, slots, gcol[:, e : e + 1])
        total = total + dot(weight, y_ref[e * slots : (e + 1) * slots, :])
    return total


def all_one_hot(slot_row, experts, slots):
    return jnp.concatenate([one_hot(slot_row, e, slots) for e in range(experts)], axis=0)


def send_grads(hot, gx, gpack, gxs_ref, gy_ref, experts, slots):
    got = dot(hot, gx)
    gates = dot(hot, gpack)
    gxs_ref[...] = got.astype(bf16)
    for e in range(experts):
        rows = slice(e * slots, (e + 1) * slots)
        gate = gates[rows, e : e + 1] + gates[rows, 64 + e : 65 + e]
        gy_ref[rows, :] = (got[rows, :] * gate).astype(bf16)


def row_blocks(tokens):
    size = tokens // BLOCKS
    return size, lambda i: pl.ds(pl.multiple_of(i * size, 16), size)


def causal_spans(tokens):
    edges = [0, 384, 640, tokens]
    return list(zip(edges[:-1], edges[1:]))


def forward_kernel(first, last, experts, slots, traffic, *refs):
    refs = list(refs)
    if first:
        x_in = refs.pop(0)
    else:
        mid_prev, n2_prev, y_ref, gcol_prev, slotc_prev, w_prev = [refs.pop(0) for _ in range(6)]
    w_ref, bias_ref, z_ref, mixt_ref, chosen_ref, slotr_ref = [refs.pop(0) for _ in range(6)]
    if last:
        cot_ref = refs.pop(0)
    if not first:
        x_out = refs.pop(0)
    n1_ref, qkv_ref, att_ref, lse_ref, mid_ref, n2_ref, info_ref, gcol_ref, gpack_ref, send_ref = [
        refs.pop(0) for _ in range(10)
    ]
    small_out = refs.pop(0)
    small_out[...] = w_ref[:, W_SMALL:]
    if last:
        gxs_ref, gy_ref = refs.pop(0), refs.pop(0)
    lse_cols, turn = refs
    tokens = n1_ref.shape[0]
    size, block = row_blocks(tokens)
    small = w_ref[:, W_SMALL:].astype(f32).T
    gain0 = small[S_GAIN : S_GAIN + 1, :]
    gain1 = small[S_GAIN + 1 : S_GAIN + 2, :]
    if not first:
        vectors_prev = w_prev[...].astype(f32).T[S_VEC : S_VEC + 2, :]

    def project(i, carry):
        rows = block(i)
        if first:
            x = x_in[rows, :].astype(f32)
        else:
            x = combine_rows(
                rows, mid_prev, n2_prev, y_ref, gcol_prev, slotc_prev, vectors_prev, experts, slots
            )
            x_out[rows, :] = x
        n1 = (x * inv_rms(x) * gain0).astype(bf16)
        n1_ref[rows, :] = n1
        for c in range(3):
            qkv_ref[rows, c * D : (c + 1) * D] = dot(n1, w_ref[:, c * D : (c + 1) * D]).astype(bf16)
        return carry

    lax.fori_loop(0, BLOCKS, project, 0)
    if not first:
        traffic.flush(x_out)
    traffic.flush(n1_ref)
    traffic.flush(qkv_ref)
    traffic.need(bias_ref)
    lane = lax.broadcasted_iota(jnp.int32, (1, 128), 1)
    low_f = jnp.where(lane < HD, 1.0, 0.0)
    low = low_f.astype(bf16)
    high = (1.0 - low_f).astype(bf16)
    lse_cols[...] = jnp.zeros_like(lse_cols)

    def pair(p, carry):
        k = qkv_ref[:, pl.ds(pl.multiple_of(D + p * 128, 128), 128)]
        v = qkv_ref[:, pl.ds(pl.multiple_of(2 * D + p * 128, 128), 128)]
        va = v * low + high
        vb = v * high + low
        here = pl.ds(pl.multiple_of(p * 128, 128), 128)
        for start, stop in causal_spans(tokens):
            q = qkv_ref[start:stop, here] * bf16(HD**-0.5)
            outs = []
            for mask, value in ((low, va), (high, vb)):
                s = dot_nt(q * mask, k[:stop]) + bias_ref[start:stop, :stop]
                peak = jnp.max(s, axis=1, keepdims=True)
                expo = jnp.exp(s - peak).astype(bf16)
                outs.append((dot(expo, value[:stop]), peak))
            (oa, ma), (ob, mb) = outs
            numer = jnp.where(lane < HD, oa, ob)
            denom = pltpu.roll(jnp.where(lane < HD, ob, oa), HD, 1)
            att_ref[start:stop, here] = (numer / denom).astype(bf16)
            la = ma + jnp.log(oa[:, HD : HD + 1])
            lb = mb + jnp.log(ob[:, 0:1])
            old = lse_cols[start:stop, :]
            lse_cols[start:stop, :] = jnp.where(
                lane == 2 * p, la, jnp.where(lane == 2 * p + 1, lb, old)
            )
        return carry

    lax.fori_loop(0, H // 2, pair, 0)
    traffic.flush(att_ref)
    lse_ref[...] = lse_cols[...].T[0:16, :]

    def finish(i, carry):
        rows = block(i)
        if first:
            x = x_in[rows, :].astype(f32)
        else:
            x = x_out[rows, :]
        middle = x + dot(att_ref[rows, :], w_ref[:, W_OUT:W_SMALL])
        mid_ref[rows, :] = middle
        n2_ref[rows, :] = (middle * inv_rms(middle) * gain1).astype(bf16)
        return carry

    lax.fori_loop(0, BLOCKS, finish, 0)
    traffic.flush(mid_ref)
    traffic.flush(n2_ref)
    n2 = n2_ref[...]
    scores = dot_nt(small[0:32, :].astype(bf16), n2)
    logits = scores[0:16, :]
    z = z_ref[...]
    mixt = mixt_ref[...]
    for i in range(experts + 4):
        logits = logits + mixt[:, i : i + 1] * z[i : i + 1, :]
    row = lax.broadcasted_iota(jnp.int32, (16, tokens), 0)
    valid = row < experts + 4
    peak = jnp.max(jnp.where(valid, logits, masked_fill), axis=0, keepdims=True)
    expo = jnp.where(valid, jnp.exp(jnp.minimum(logits - peak, 0.0)), 0.0)
    prob = expo / jnp.sum(expo, axis=0, keepdims=True)
    gates = prob * chosen_ref[...]
    info_ref[0:16, :] = logits
    info_ref[16:32, :] = prob
    turn[...] = jnp.zeros_like(turn)
    turn[0:16, 0:tokens] = gates
    own = gates[experts + 1 : experts + 2, :]
    alphas = []
    for c in range(2):
        l0 = scores[S_CONST + 2 * c : S_CONST + 2 * c + 1, :]
        l1 = scores[S_CONST + 2 * c + 1 : S_CONST + 2 * c + 2, :]
        a0 = jax.nn.sigmoid(l0 - l1)
        a1 = jax.nn.sigmoid(l1 - l0)
        alphas += [a0, a1]
        share = gates[experts + 2 + c : experts + 3 + c, :]
        own = own + share * a0
        turn[17 + c : 18 + c, 0:tokens] = share * a1
    turn[16:17, 0:tokens] = own
    zero_row = jnp.zeros((4, tokens), f32)
    info_ref[32:40, :] = jnp.concatenate(alphas + [zero_row], axis=0)
    gcol = turn[...].T[0:tokens, :]
    gcol_ref[...] = gcol
    upper, lower = split_bf16(jnp.where(lane < 16, gcol, 0.0))
    gpack = upper + pltpu.roll(lower.astype(f32), 64, 1).astype(bf16)
    gpack_ref[...] = gpack
    hot = all_one_hot(slotr_ref[...], experts, slots)
    send_ref[...] = dot(hot, n2).astype(bf16)
    if last:
        traffic.need(cot_ref)
        send_grads(hot, cot_ref[...], gpack, gxs_ref, gy_ref, experts, slots)


def shape(dims, dtype=f32):
    return jax.ShapeDtypeStruct(tuple(dims), dtype)


class Traffic:
    def __init__(self):
        self.fetches, self.sinks, self.flushes = {}, {}, []

    def fetch(self, src, buffer, sem):
        copy = pltpu.make_async_copy(src, buffer, sem)
        copy.start()
        self.fetches[id(buffer)] = copy

    def need(self, *buffers):
        for buffer in buffers:
            copy = self.fetches.pop(id(buffer), None)
            if copy is not None:
                copy.wait()

    def sink(self, buffer, dst, sems):
        self.sinks[id(buffer)] = [dst, sems, 0]

    def flush(self, buffer, part=None):
        entry = self.sinks.get(id(buffer))
        if entry is None:
            return
        dst, sems, used = entry
        entry[2] += 1
        src, dst = (buffer, dst) if part is None else (buffer.at[part], dst.at[part])
        copy = pltpu.make_async_copy(src, dst, sems.at[used])
        copy.start()
        self.flushes.append(copy)

    def finish(self):
        for copy in self.flushes:
            copy.wait()


FLUSHES = 3


def whole_call(body, name, outs, scratch, args, flops, late=(), early=()):
    moved = sum(a.size * a.dtype.itemsize for a in args) + sum(
        o.size * o.dtype.itemsize for o in outs
    )
    late, early = sorted(late), sorted(early)

    def kernel(*refs):
        ins, rest = list(refs[: len(args)]), refs[len(args) :]
        results, rest = list(rest[: len(outs)]), rest[len(outs) :]
        own, rest = rest[: len(scratch)], rest[len(scratch) :]
        traffic = Traffic()
        fetch_sems, flush_sems = rest[len(late) + len(early) :]
        for n, at in enumerate(late):
            traffic.fetch(ins[at], rest[n], fetch_sems.at[n])
            ins[at] = rest[n]
        for n, at in enumerate(early):
            buffer = rest[len(late) + n]
            traffic.sink(buffer, results[at], flush_sems.at[n])
            results[at] = buffer
        body(traffic, *ins, *results, *own)
        traffic.finish()

    near, far = pl.BlockSpec(memory_space=pltpu.VMEM), pl.BlockSpec(memory_space=pl.ANY)
    buffers = [pltpu.VMEM(args[at].shape, args[at].dtype) for at in late]
    buffers += [pltpu.VMEM(outs[at].shape, outs[at].dtype) for at in early]
    buffers.append(pltpu.SemaphoreType.DMA((max(len(late), 1),)))
    buffers.append(pltpu.SemaphoreType.DMA((max(len(early), 1), FLUSHES)))
    return pl.pallas_call(
        kernel,
        out_shape=outs,
        in_specs=[far if n in late else near for n in range(len(args))],
        out_specs=[far if n in early else near for n in range(len(outs))],
        scratch_shapes=list(scratch) + buffers,
        compiler_params=pltpu.CompilerParams(vmem_limit_bytes=VMEM),
        cost_estimate=pl.CostEstimate(flops=flops, bytes_accessed=moved, transcendentals=0),
        name=name,
    )(*args)


def forward_call(first, last, experts, slots, args):
    tokens = TREE
    sent = experts * slots
    outs = [] if first else [shape((tokens, D))]
    outs += [
        shape((tokens, D), bf16),
        shape((tokens, 3 * D), bf16),
        shape((tokens, D), bf16),
        shape((16, tokens)),
        shape((tokens, D)),
        shape((tokens, D), bf16),
        shape((40, tokens)),
        shape((tokens, 128)),
        shape((tokens, 128), bf16),
        shape((sent, D), bf16),
        shape((D, 128), bf16),
    ]
    if last:
        outs += [shape((sent, D), bf16), shape((sent, D), bf16)]
    padded = -(-tokens // 128) * 128
    scratch = [pltpu.VMEM((tokens, 128), f32), pltpu.VMEM((128, padded), f32)]
    body = functools.partial(forward_kernel, first, last, experts, slots)
    inputs, results = (1, 0) if first else (6, 1)
    late = [inputs + 1] + ([inputs + 6] if last else [])
    early = ([] if first else [0]) + [results + n for n in (0, 1, 2, 4, 5)]
    return whole_call(body, "block_forward", outs, scratch, args, 20 * 10**9, late, early)


def gating_kernel(last, experts, slots, *refs):
    refs = list(refs)
    gx_ref, n2_ref, y_ref, gxs_ref, slotr_ref, info_ref, chosen_ref, gcol_ref, small_ref = [
        refs.pop(0) for _ in range(9)
    ]
    z_ref, mix_ref = refs.pop(0), refs.pop(0)
    if last:
        mid_ref, slotc_ref = refs.pop(0), refs.pop(0)
    else:
        gz_ref = refs.pop(0)
    gn2_ref, gsm_ref, gmix_ref, gprev_ref = [refs.pop(0) for _ in range(4)]
    if last:
        out_ref = refs.pop(0)
    tokens = n2_ref.shape[0]
    size, block = row_blocks(tokens)
    small = small_ref[...].astype(f32).T
    small_half = small[0:32, :].astype(bf16)
    vectors = small[S_VEC : S_VEC + 2, :]
    slot_row = slotr_ref[...]
    ones = jnp.ones((16, D), bf16)
    row = lax.broadcasted_iota(jnp.int32, (16, slots), 0)
    scattered = jnp.zeros((16, tokens), f32)
    for e in range(experts):
        rows = slice(e * slots, (e + 1) * slots)
        inner = y_ref[rows, :].astype(f32) * gxs_ref[rows, :].astype(f32)
        upper, lower = split_bf16(inner)
        sums = dot_nt(ones, upper) + dot_nt(ones, lower)
        upper, lower = split_bf16(sums)
        lhs = jnp.where(row == e, upper.astype(f32), 0.0) + jnp.where(
            row == 8 + e, lower.astype(f32), 0.0
        )
        scattered = scattered + dot(lhs.astype(bf16), one_hot(slot_row, e, slots))
    gx = gx_ref[...].astype(f32)
    gx_half = gx.astype(bf16)
    n2 = n2_ref[...]
    upper, lower = split_bf16(gx * n2.astype(f32))
    gx_n2 = (dot_nt(ones, upper) + dot_nt(ones, lower))[0:1, :]
    gx_small = dot_nt(small_half, gx_half)
    prob = info_ref[16:32, :]
    chosen = chosen_ref[...]
    gates = prob * chosen
    trow = lax.broadcasted_iota(jnp.int32, (16, tokens), 0)
    gp = jnp.concatenate([scattered[0:8, :] + scattered[8:16, :], jnp.zeros((8, tokens), f32)], 0)
    gp = jnp.where(trow == experts + 1, gx_n2, jnp.where(trow < experts, gp, 0.0))
    crow = lax.broadcasted_iota(jnp.int32, (8, tokens), 0)
    glog = jnp.zeros((8, tokens), f32)
    coefs = jnp.zeros((8, tokens), f32)
    for c in range(2):
        a0 = info_ref[32 + 2 * c : 33 + 2 * c, :]
        a1 = info_ref[33 + 2 * c : 34 + 2 * c, :]
        gx_v = gx_small[S_VEC + c : S_VEC + c + 1, :]
        share = gates[experts + 2 + c : experts + 3 + c, :]
        gp = jnp.where(trow == experts + 2 + c, a0 * gx_n2 + a1 * gx_v, gp)
        gl = share * (gx_n2 - gx_v) * a0 * a1
        glog = jnp.where(crow == 2 * c, gl, jnp.where(crow == 2 * c + 1, -gl, glog))
        coefs = jnp.where(crow == c, share * a1, coefs)
    gp = gp * chosen
    gz = prob * (gp - jnp.sum(prob * gp, axis=0, keepdims=True))
    if not last:
        gz = gz + gz_ref[...]
    z = z_ref[...]
    gmix_ref[...] = lax.dot_general(
        z, gz, (((1,), (1,)), ((), ())), precision=lax.Precision.HIGHEST, preferred_element_type=f32
    )
    mix = mix_ref[...]
    gprev = jnp.zeros((16, tokens), f32)
    for o in range(experts + 4):
        gprev = gprev + mix[:, o : o + 1] * gz[o : o + 1, :]
    gprev_ref[...] = gprev
    allg = jnp.concatenate([gz, glog, jnp.zeros((8, tokens), f32)], axis=0)
    upper, lower = split_bf16(allg)
    gsm = dot(upper, n2) + dot(lower, n2)
    cu, cl = split_bf16(jnp.concatenate([coefs, jnp.zeros((8, tokens), f32)], axis=0))
    gvec = dot(cu, gx_half) + dot(cl, gx_half)
    gsm_ref[0:24, :] = gsm[0:24, :]
    gsm_ref[24:32, :] = jnp.concatenate(
        [jnp.zeros((2, D), f32), gvec[0:2, :], jnp.zeros((4, D), f32)], axis=0
    )
    both = jnp.concatenate([upper, lower], axis=0)
    twice = jnp.concatenate([small_half, small_half], axis=0)
    gn2_ref[...] = dot_tn(both, twice)

    def add(i, carry):
        rows = block(i)
        gn2_ref[rows, :] = gn2_ref[rows, :] + gcol_ref[rows, 16:17] * gx_ref[rows, :].astype(f32)
        if last:
            out_ref[rows, :] = combine_rows(
                rows, mid_ref, n2_ref, y_ref, gcol_ref, slotc_ref, vectors, experts, slots
            ).astype(bf16)
        return carry

    lax.fori_loop(0, BLOCKS, add, 0)


def gating_outputs(last):
    tokens = TREE
    outs = [shape((tokens, D)), shape((32, D)), shape((16, 16)), shape((16, tokens))]
    if last:
        outs += [shape((tokens, D), bf16)]
    return outs


def backward_kernel(first, experts, slots, traffic, *refs):
    refs = list(refs)
    gx_ref, gn2p_ref, gn2e_ref, slotc_ref, mid_ref, att_ref, w_ref, qkv_ref, n1_ref, x_ref = [
        refs.pop(0) for _ in range(10)
    ]
    biast_ref, lse_ref, gsm_ref = [refs.pop(0) for _ in range(3)]
    if not first:
        slotr_ref, gpack_ref = refs.pop(0), refs.pop(0)
    gout_ref, dw_ref = refs.pop(0), refs.pop(0)
    if not first:
        gxs_ref, gy_ref = refs.pop(0), refs.pop(0)
    gatt, go, gqkv, turn = refs
    tokens = n1_ref.shape[0]
    size, block = row_blocks(tokens)
    small = w_ref[:, W_SMALL:].astype(f32).T
    gain0 = small[S_GAIN : S_GAIN + 1, :]
    gain1 = small[S_GAIN + 1 : S_GAIN + 2, :]

    def enter(i, total):
        rows = block(i)
        gn2 = gn2p_ref[rows, :]
        slot = slotc_ref[rows, :]
        for e in range(experts):
            gn2 = gn2 + dot(one_hot_col(slot, e, slots), gn2e_ref[e * slots : (e + 1) * slots, :])
        middle = mid_ref[rows, :]
        r = inv_rms(middle)
        scaled = gain1 * gn2
        inner = jnp.mean(middle * scaled, axis=1, keepdims=True)
        gmid = gx_ref[rows, :].astype(f32) + r * scaled - middle * (r * r * r * inner)
        gout_ref[rows, :] = gmid
        half = gmid.astype(bf16)
        gatt[rows, :] = half
        go[rows, :] = dot_nt(half, w_ref[:, W_OUT:W_SMALL]).astype(bf16)
        return total + jnp.sum(gn2 * middle * r, axis=0, keepdims=True)

    ggain1 = lax.fori_loop(0, BLOCKS, enter, jnp.zeros((1, D), f32))
    traffic.need(att_ref)
    lane = lax.broadcasted_iota(jnp.int32, (1, 128), 1)
    low_f = jnp.where(lane < HD, 1.0, 0.0)
    low = low_f.astype(bf16)
    high = (1.0 - low_f).astype(bf16)
    scale = HD**-0.5

    def out_grad(p, carry):
        here = pl.ds(pl.multiple_of(p * 128, 128), 128)
        dw_ref[here, W_OUT:W_SMALL] = dot_tn(att_ref[:, here], gatt[...]).astype(bf16)
        return carry

    lax.fori_loop(0, D // 128, out_grad, 0)
    traffic.flush(dw_ref, (slice(None), slice(W_OUT, W_SMALL)))
    traffic.need(qkv_ref, biast_ref, lse_ref)
    spans = causal_spans(tokens)

    def pair(p, carry):
        here = pl.ds(pl.multiple_of(p * 128, 128), 128)
        lanes_k = pl.ds(pl.multiple_of(D + p * 128, 128), 128)
        lanes_v = pl.ds(pl.multiple_of(2 * D + p * 128, 128), 128)
        q = qkv_ref[:, here] * bf16(scale)
        k = qkv_ref[:, lanes_k]
        v = qkv_ref[:, lanes_v]
        g = go[:, here]
        turn[0:tokens, :] = g.astype(f32) * att_ref[:, here].astype(f32)
        inner = turn[...].T[:, 0:tokens]
        turn[0:tokens, :] = k.astype(f32)
        kt = turn[...].T[:, 0:tokens].astype(bf16)
        gq_t = []
        gk = [0.0] * len(spans)
        gv = [0.0] * len(spans)
        for h, mask in ((0, low), (1, high)):
            qh = q * mask
            gh = g * mask
            dsum = jnp.sum(inner[h * HD : (h + 1) * HD, :], axis=0, keepdims=True)
            lse = lse_ref[pl.ds(2 * p + h, 1), :]
            gq_h = []
            for n, (start, stop) in enumerate(spans):
                st = dot_nt(k[start:stop], qh[start:]) + biast_ref[start:stop, start:]
                pt = jnp.exp(st - lse[:, start:])
                gpt = dot_nt(v[start:stop], gh[start:])
                gst = (pt * (gpt - dsum[:, start:])).astype(bf16)
                gv[n] = gv[n] + dot(pt.astype(bf16), gh[start:])
                gk[n] = gk[n] + dot(gst, qh[start:])
                part = dot(kt[h * HD : (h + 1) * HD, start:stop], gst)
                gq_h.append(part)
            cols = []
            for n, (start, stop) in enumerate(spans):
                piece = 0.0
                for m in range(n + 1):
                    origin = spans[m][0]
                    piece = piece + gq_h[m][:, start - origin : stop - origin]
                cols.append(piece)
            gq_t.append(jnp.concatenate(cols, axis=1))
        turn_t = jnp.concatenate(gq_t, axis=0) * scale
        pad = turn.shape[0] - tokens
        turn_t = jnp.concatenate([turn_t, jnp.zeros((128, pad), f32)], axis=1)
        gqkv[:, here] = turn_t.T[0:tokens, :].astype(bf16)
        for n, (start, stop) in enumerate(spans):
            gqkv[start:stop, lanes_k] = gk[n].astype(bf16)
            gqkv[start:stop, lanes_v] = gv[n].astype(bf16)
        return carry

    turn[...] = jnp.zeros_like(turn)
    lax.fori_loop(0, H // 2, pair, 0)
    traffic.need(n1_ref)

    def in_grad(p, carry):
        here = pl.ds(pl.multiple_of(p * 128, 128), 128)
        dw_ref[here, 0:W_OUT] = dot_tn(n1_ref[:, here], gqkv[...]).astype(bf16)
        return carry

    lax.fori_loop(0, D // 128, in_grad, 0)
    traffic.flush(dw_ref, (slice(None), slice(0, W_OUT)))
    traffic.need(x_ref)

    def leave(i, total):
        rows = block(i)
        gn1 = dot_nt(gqkv[rows, :], w_ref[:, 0:W_OUT])
        x = x_ref[rows, :].astype(f32)
        r = inv_rms(x)
        scaled = gain0 * gn1
        inner = jnp.mean(x * scaled, axis=1, keepdims=True)
        gx = gout_ref[rows, :] + r * scaled - x * (r * r * r * inner)
        gout_ref[rows, :] = gx
        gatt[rows, :] = gx.astype(bf16)
        return total + jnp.sum(gn1 * x * r, axis=0, keepdims=True)

    ggain0 = lax.fori_loop(0, BLOCKS, leave, jnp.zeros((1, D), f32))
    rows = jnp.concatenate(
        [gsm_ref[0:24, :], ggain0, ggain1, gsm_ref[26:32, :], jnp.zeros((96, D), f32)], axis=0
    )
    dw_ref[:, W_SMALL:] = rows.T.astype(bf16)
    traffic.flush(dw_ref, (slice(None), slice(W_SMALL, W_ALL)))
    traffic.flush(gout_ref)
    if not first:
        hot = all_one_hot(slotr_ref[...], experts, slots)
        send_grads(hot, gatt[...], gpack_ref[...], gxs_ref, gy_ref, experts, slots)


def backward_call(first, experts, slots, args):
    tokens = TREE
    sent = experts * slots
    outs = [shape((tokens, D)), shape((D, W_ALL), bf16)]
    if not first:
        outs += [shape((sent, D), bf16), shape((sent, D), bf16)]
    padded = -(-tokens // 128) * 128
    scratch = [
        pltpu.VMEM((tokens, D), bf16),
        pltpu.VMEM((tokens, D), bf16),
        pltpu.VMEM((tokens, 3 * D), bf16),
        pltpu.VMEM((padded, 128), f32),
    ]
    body = functools.partial(backward_kernel, first, experts, slots)
    return whole_call(
        body, "block_backward", outs, scratch, args, 40 * 10**9, (5, 7, 8, 9, 10, 11), (0, 1)
    )


class Packing:
    def __init__(self, shards, part, ff):
        self.shards, self.part, self.ff = shards, part, ff
        self.padded = -(-part // 16) * 16
        self.chunks = ff // 256
        self.own = ff // shards
        self.down = 2 * self.chunks * self.padded
        self.rows = self.down + (D // 256) * self.own

    def pack(self, gate, up, down):
        pieces = []
        for wide in (gate, up):
            cut = wide.reshape(self.part, self.chunks, 256).transpose(1, 0, 2)
            cut = jnp.pad(cut, [(0, 0), (0, self.padded - self.part), (0, 0)])
            pieces.append(cut.reshape(self.chunks * self.padded, 256))
        pieces.append(
            down.reshape(self.own, D // 256, 256).transpose(1, 0, 2).reshape(-1, 256)
        )
        return jnp.concatenate(pieces, axis=0)

    def wide_part(self, ref, n, j):
        at = pl.multiple_of((n * self.chunks + j) * self.padded, 16)
        return ref[:, pl.ds(at, self.padded), :][:, : self.part, :].reshape(D, 256)

    def tall_part(self, ref, j):
        group = 256 // self.own
        here = pl.ds(j * group, group)
        pieces = []
        for c in range(D // 256):
            at = self.down + c * self.own
            pieces.append(ref[here, at : at + self.own, :].reshape(256, 256))
        return jnp.concatenate(pieces, axis=1)

    def put_wide(self, ref, n, j, grad):
        at = pl.multiple_of((n * self.chunks + j) * self.padded, 16)
        ref[:, pl.ds(at, self.part), :] = grad.reshape(self.shards, self.part, 256)

    def put_tall(self, ref, j, grad):
        group = 256 // self.own
        for c in range(D // 256):
            at = self.down + c * self.own
            ref[pl.ds(j * group, group), at : at + self.own, :] = grad[
                :, c * 256 : (c + 1) * 256
            ].reshape(group, self.own, 256)


class Exchange:
    def __init__(self, experts, slots):
        self.experts, self.slots = experts, slots
        first = -(-slots // 32) * 16
        self.waves = ((0, first), (first, slots - first))
        self.ranges = [(0, slots)]
        for _, size in self.waves:
            start = self.ranges[-1][0] + self.ranges[-1][1]
            self.ranges.append((start, (experts - 1) * size))
        self.total = experts * slots

    def held(self, wave, d):
        size = self.waves[wave][1]
        return pl.ds(self.ranges[1 + wave][0] + (d - 1) * size, size)

    def slot(self, device, wave):
        offset, size = self.waves[wave]
        return pl.ds(pl.multiple_of(device * self.slots + offset, 16), size)


MESH = pl.DeviceIdType.MESH


def greet(experts):
    me = lax.axis_index("expert")
    barrier = pltpu.get_barrier_semaphore()
    for d in range(1, experts):
        pl.semaphore_signal(
            barrier, inc=1, device_id={"expert": lax.rem(me + d, experts)}, device_id_type=MESH
        )
    pl.semaphore_wait(barrier, experts - 1)


def out_copies(ex, wave, src, dst, sends, recvs):
    me = lax.axis_index("expert")
    copies = []
    for d in range(1, ex.experts):
        to = lax.rem(me + d, ex.experts)
        copies.append(
            pltpu.make_async_remote_copy(
                src_ref=src.at[ex.slot(to, wave)],
                dst_ref=dst.at[ex.held(wave, d)],
                send_sem=sends.at[wave, d - 1],
                recv_sem=recvs.at[wave, d - 1],
                device_id={"expert": to},
                device_id_type=MESH,
            )
        )
    return copies


def back_copies(ex, wave, n, src, dst, sends, recvs):
    me = lax.axis_index("expert")
    copies = []
    for d in range(1, ex.experts):
        copies.append(
            pltpu.make_async_remote_copy(
                src_ref=src.at[ex.held(wave, d)],
                dst_ref=dst.at[ex.slot(me, wave)],
                send_sem=sends.at[n, wave, d - 1],
                recv_sem=recvs.at[n, wave, d - 1],
                device_id={"expert": lax.rem(me + ex.experts - d, ex.experts)},
                device_id_type=MESH,
            )
        )
    return copies


def own_slots(ex):
    me = lax.axis_index("expert")
    return pl.ds(pl.multiple_of(me * ex.slots, 16), ex.slots)


def dispatch_kernel(ex, send, recv, sends, recvs):
    greet(ex.experts)
    copies = out_copies(ex, 0, send, recv, sends, recvs)
    copies += out_copies(ex, 1, send, recv, sends, recvs)
    for copy in copies:
        copy.start()
    recv[0 : ex.slots, :] = send[own_slots(ex), :]
    for copy in copies:
        copy.wait()


def dispatch_call(ex, rows):
    vmem = pl.BlockSpec(memory_space=pltpu.VMEM)
    return pl.pallas_call(
        functools.partial(dispatch_kernel, ex),
        out_shape=shape((ex.total, D), bf16),
        in_specs=[vmem],
        out_specs=vmem,
        scratch_shapes=[pltpu.SemaphoreType.DMA((2, ex.experts - 1))] * 2,
        compiler_params=pltpu.CompilerParams(
            vmem_limit_bytes=8 << 20, collective_id=3, has_side_effects=True
        ),
        cost_estimate=pl.CostEstimate(flops=35 * 10**9, bytes_accessed=10**6, transcendentals=0),
        name="dispatch",
    )(rows)


def exchange_kernel(mode, pack, ex, *refs):
    refs = list(refs)
    forward, backward = mode in ("forward", "both"), mode in ("backward", "both")
    recv_n = refs.pop(0)
    w_hbm = refs.pop(0)
    if backward:
        send_g = refs.pop(0)
        if mode == "backward":
            gate_hbm, up_hbm = refs.pop(0), refs.pop(0)
        gating_far = [refs.pop(0) for _ in range(12)]
    if forward:
        back_y = refs.pop(0)
    if mode == "forward":
        gates_far, ups_far, gates, ups = [refs.pop(0) for _ in range(4)]
    else:
        back_g, dw_far = refs.pop(0), refs.pop(0)
        gating_outs = [refs.pop(0) for _ in range(5 if mode == "both" else 4)]
    if forward:
        out_y, acc_y = refs.pop(0), refs.pop(0)
    if backward:
        recv_g, out_g, hids, gates, ups, rows_t, acc_g = [refs.pop(0) for _ in range(7)]
        gating = [refs.pop(0) for _ in range(12)]
    w = refs.pop(0)
    sends, recvs, backs, gots, local = refs
    traffic = Traffic()
    if mode == "forward":
        traffic.sink(gates, gates_far, local.at[4:7])
        traffic.sink(ups, ups_far, local.at[7:10])

    loads = [pltpu.make_async_copy(w_hbm, w, local.at[0])]
    if mode == "backward":
        loads.append(pltpu.make_async_copy(gate_hbm, gates, local.at[1]))
        loads.append(pltpu.make_async_copy(up_hbm, ups, local.at[2]))
    if mode == "backward":
        for n, (far, near) in enumerate(zip(gating_far, gating)):
            traffic.fetch(far, near, local.at[4 + n])
    for copy in loads:
        copy.start()
    if mode == "both":
        for n, (far, near) in enumerate(zip(gating_far, gating)):
            traffic.fetch(far, near, local.at[4 + n])
    greet(ex.experts)

    def work(start, size):
        rows = slice(start, start + size)
        part = slice(0, size)
        if forward:
            acc_y[part, :] = jnp.zeros((size, D), f32)
        if backward:
            acc_g[part, :] = jnp.zeros((size, D), f32)

        def chunk(j, carry):
            lanes = pl.ds(pl.multiple_of(j * 256, 256), 256)
            gate_w, up_w = pack.wide_part(w, 0, j), pack.wide_part(w, 1, j)
            down_w = pack.tall_part(w, j)
            if forward:
                r = recv_n[rows, :]
                gate, up = dot(r, gate_w), dot(r, up_w)
                if mode == "forward":
                    gates[rows, lanes] = gate.astype(bf16)
                    ups[rows, lanes] = up.astype(bf16)
            else:
                gate, up = gates[rows, lanes].astype(f32), ups[rows, lanes].astype(f32)
            s = jax.nn.sigmoid(gate)
            act = gate * s
            hid = (act * up).astype(bf16)
            if forward:
                acc_y[part, :] = acc_y[part, :] + dot(hid, down_w)
            if backward:
                hids[rows, lanes] = hid
                ghid = dot_nt(recv_g[rows, :], down_w)
                guv = (ghid * act).astype(bf16)
                ggu = (ghid * up * (s * (1.0 + gate * (1.0 - s)))).astype(bf16)
                gates[rows, lanes] = ggu
                ups[rows, lanes] = guv
                acc_g[part, :] = acc_g[part, :] + dot_nt(ggu, gate_w) + dot_nt(guv, up_w)
            return carry

        lax.fori_loop(0, pack.chunks, chunk, 0)
        if mode == "forward":
            here = pl.ds(start, size)
            traffic.flush(gates, here)
            traffic.flush(ups, here)
        if forward:
            out_y[rows, :] = acc_y[part, :].astype(bf16)
        if backward:
            out_g[rows, :] = acc_g[part, :].astype(bf16)

    def send_back(wave):
        ys = back_copies(ex, wave, 0, out_y, back_y, backs, gots) if forward else []
        gs = back_copies(ex, wave, 1, out_g, back_g, backs, gots) if backward else []
        for copy in ys + gs:
            copy.start()
        return ys, gs

    if backward:
        waves = [out_copies(ex, n, send_g, recv_g, sends, recvs) for n in range(2)]
        for copy in waves[0]:
            copy.start()
        recv_g[0 : ex.slots, :] = send_g[own_slots(ex), :]
        if mode == "backward":
            traffic.need(*gating)
            gating_kernel(False, ex.experts, ex.slots, *gating, *gating_outs)
    for copy in loads:
        copy.wait()
    if backward:
        work(*ex.ranges[0])
        for copy in waves[0]:
            copy.wait_send()
        for copy in waves[1]:
            copy.start()
        for copy in waves[0]:
            copy.wait_recv()
    work(*ex.ranges[1])
    ys, gs = send_back(0)
    if backward:
        for copy in waves[1]:
            copy.wait()
    work(*ex.ranges[2])
    more = send_back(1)
    ys, gs = ys + more[0], gs + more[1]
    if mode == "forward":
        work(*ex.ranges[0])
    if forward:
        back_y[own_slots(ex), :] = out_y[0 : ex.slots, :]
    if backward:
        back_g[own_slots(ex), :] = out_g[0 : ex.slots, :]
        rows_t[...] = recv_n[...].T
        dw = w
        if pack.padded != pack.part:
            dw[...] = jnp.zeros_like(dw)

        def weights(j, carry):
            lanes = pl.ds(pl.multiple_of(j * 256, 256), 256)
            pack.put_wide(dw, 0, j, dot(rows_t[...], gates[:, lanes]).astype(bf16))
            pack.put_wide(dw, 1, j, dot(rows_t[...], ups[:, lanes]).astype(bf16))
            pack.put_tall(dw, j, dot_tn(hids[:, lanes], recv_g[...]).astype(bf16))
            return carry

        lax.fori_loop(0, pack.chunks, weights, 0)
        leaving = pltpu.make_async_copy(dw, dw_far, local.at[3])
        leaving.start()
    for copy in ys:
        copy.wait()
    if mode == "both":
        traffic.need(*gating)
        gating_kernel(True, ex.experts, ex.slots, *gating[:2], back_y, *gating[2:], *gating_outs)
    for copy in gs:
        copy.wait()
    if backward:
        leaving.wait()
    traffic.finish()


SPLIT = 13 * 128


def cube_kernel(part, labels, g_ref, upper_ref, mix_ref, *refs):
    outs, refs = refs[:7], refs[7:]
    got_c, sums, got_a, got_b, half_a, half_b, end_a, end_b = refs[:8]
    mine, quarters, ready, mix_held, mix_got, turn, send, recv, z_send, z_recv, mix_send, mix_recv = refs[8:]
    mix_out = outs[6]
    me = lax.axis_index("shard")
    z = lax.axis_index("expert")
    owners = quarters.shape[1]
    core, x, y = lax.rem(me, 2), lax.rem(me // 2, 2), me // 4
    near, over_x, over_y = me + 1 - 2 * core, me + 2 - 4 * x, me + 4 - 8 * y
    barrier = pltpu.get_barrier_semaphore()
    for other in (near, over_x, over_y):
        pl.semaphore_signal(barrier, inc=1, device_id={"shard": other}, device_id_type=MESH)
    for d in range(1, owners):
        pl.semaphore_signal(
            barrier, inc=1, device_id={"expert": lax.rem(z + d, owners)}, device_id_type=MESH
        )
    pl.semaphore_wait(barrier, 3 + owners - 1)
    cols_a, cols_b = slice(0, SPLIT), slice(SPLIT, W_ALL)

    def rows(shard):
        return pl.ds(pl.multiple_of(shard * part, 16), part)

    def remote(src, dst, send_sem, recv_sem, to):
        made = pltpu.make_async_remote_copy(
            src_ref=src,
            dst_ref=dst,
            send_sem=send_sem,
            recv_sem=recv_sem,
            device_id=to,
            device_id_type=MESH,
        )
        made.start()
        return made

    def copy(n, src, dst, to):
        return remote(src, dst, send.at[n], recv.at[n], {"shard": to})

    def quarter(owner):
        return (
            pl.ds(pl.multiple_of((owner // 2) * (part // 2), 16), part // 2),
            pl.ds(pl.multiple_of(lax.rem(owner, 2) * SPLIT, 128), SPLIT),
        )

    def spread(l):
        made = []
        for d in range(1, owners):
            to = lax.rem(z + d, owners)
            made.append(
                remote(
                    mine.at[(l, *quarter(to))],
                    quarters.at[l, z],
                    z_send.at[l, 0, d - 1],
                    z_recv.at[l, 0, d - 1],
                    {"expert": to},
                )
            )
        quarters[l, z] = mine[(l, *quarter(z))]
        return made

    def gather(l, made):
        for one in made:
            one.wait_recv()
        total = quarters[l, 0].astype(f32)
        for owner in range(1, owners):
            total = total + quarters[l, owner].astype(f32)
        ready[(l, *quarter(z))] = total.astype(bf16)
        here = (l, *quarter(z))
        return [
            remote(
                ready.at[here],
                ready.at[here],
                z_send.at[l, 1, d - 1],
                z_recv.at[l, 1, d - 1],
                {"expert": lax.rem(z + d, owners)},
            )
            for d in range(1, owners)
        ]

    pairs = [{"shard": near}, {"shard": over_x}, {"shard": over_y}]
    pairs += [{"expert": z + 1 - 2 * lax.rem(z, 2)}, {"expert": z + 2 - 4 * (z // 2)}]
    mix_held[0] = mix_ref[...]

    def mix_start(n):
        return remote(mix_held.at[n], mix_got.at[n], mix_send.at[n], mix_recv.at[n], pairs[n])

    def mix_end(n, made):
        made.wait_recv()
        total = mix_held[n] + mix_got[n]
        if n + 1 < len(pairs):
            mix_held[n + 1] = total
        else:
            for l in range(LAYERS):
                mix_out[l] = total[l * 16 : l * 16 + labels, 0:labels]

    chips = [2 * (1 - y) + 1 - x, 2 * y + 1 - x, 2 * (1 - y) + x, 2 * y + x]
    first = [
        copy(n, g_ref.at[rows(2 * chip + 1 - core)], got_c.at[chip], near)
        for n, chip in enumerate(chips)
    ]
    mix = [mix_start(0)]
    mine[0, :, W_ALL:] = jnp.zeros((part, 2 * SPLIT - W_ALL), bf16)
    mine[1, :, W_ALL:] = jnp.zeros((part, 2 * SPLIT - W_ALL), bf16)
    mine[1, :, 0:W_ALL] = upper_ref[...]
    upper = spread(1)
    turn[...] = jnp.zeros_like(turn)

    def merge(n):
        chip = chips[n]
        first[n].wait_recv()
        own = g_ref[rows(2 * chip + core), :].astype(f32)
        sums[chip] = (own + got_c[chip].astype(f32)).astype(bf16)

    def total(chip, cols, got):
        return sums[chip, :, cols].astype(f32) + got[...].astype(f32)

    merge(0)
    a0 = copy(4, sums.at[chips[0], :, cols_a], got_a.at[1 - y], over_x)
    b0 = copy(5, sums.at[chips[0], :, cols_b], got_b.at[1 - x], over_y)
    merge(1)
    a1 = copy(6, sums.at[chips[1], :, cols_a], got_a.at[y], over_x)
    merge(2)
    b1 = copy(7, sums.at[chips[2], :, cols_b], got_b.at[x], over_y)
    merge(3)
    mix_end(0, mix[0])
    mix.append(mix_start(1))
    a0.wait_recv()
    half_a[...] = total(chips[2], cols_a, got_a.at[1 - y]).astype(bf16)
    a2 = copy(8, half_a, end_a, over_y)
    b0.wait_recv()
    half_b[...] = total(chips[1], cols_b, got_b.at[1 - x]).astype(bf16)
    b2 = copy(9, half_b, end_b, over_x)
    mix_end(1, mix[1])
    mix.append(mix_start(2))
    last_upper = gather(1, upper)
    a1.wait_recv()
    keep_a = total(chips[3], cols_a, got_a.at[y])
    a2.wait_recv()
    mine[0, :, cols_a] = (keep_a + end_a[...].astype(f32)).astype(bf16)
    b1.wait_recv()
    keep_b = total(chips[3], cols_b, got_b.at[x])
    b2.wait_recv()
    mine[0, :, cols_b] = (keep_b + end_b[...].astype(f32)).astype(bf16)
    lower = spread(0)
    mix_end(2, mix[2])
    mix.append(mix_start(3))
    for made in last_upper:
        made.wait_recv()
    write_dense(part, labels, 1, ready.at[1], outs[:6], turn)
    mix_end(3, mix[3])
    mix.append(mix_start(4))
    last_lower = gather(0, lower)
    mix_end(4, mix[4])
    for made in last_lower:
        made.wait_recv()
    write_dense(part, labels, 0, ready.at[0], outs[:6], turn)
    for made in first + [a0, b0, a1, b1, a2, b2] + mix + upper + lower + last_upper + last_lower:
        made.wait_send()


def finish_call(part, labels, grads, upper, mix):
    vmem = pl.BlockSpec(memory_space=pltpu.VMEM)
    rest = W_ALL - SPLIT
    owners = lax.axis_size("expert")
    outs = dense_shapes(part, labels) + [shape((LAYERS, labels, labels))]
    dma = pltpu.SemaphoreType.DMA
    return pl.pallas_call(
        functools.partial(cube_kernel, part, labels),
        out_shape=outs,
        in_specs=[vmem] * 3,
        out_specs=[vmem] * len(outs),
        scratch_shapes=[
            pltpu.VMEM((4, part, W_ALL), bf16),
            pltpu.VMEM((4, part, W_ALL), bf16),
            pltpu.VMEM((2, part, SPLIT), bf16),
            pltpu.VMEM((2, part, rest), bf16),
            pltpu.VMEM((part, SPLIT), bf16),
            pltpu.VMEM((part, rest), bf16),
            pltpu.VMEM((part, SPLIT), bf16),
            pltpu.VMEM((part, rest), bf16),
            pltpu.VMEM((2, part, 2 * SPLIT), bf16),
            pltpu.VMEM((2, owners, part // 2, SPLIT), bf16),
            pltpu.VMEM((2, part, 2 * SPLIT), bf16),
            pltpu.VMEM((5, 32, 128), f32),
            pltpu.VMEM((5, 32, 128), f32),
            pltpu.VMEM((128, 128), f32),
            dma((10,)),
            dma((10,)),
            dma((2, 2, owners - 1)),
            dma((2, 2, owners - 1)),
            dma((5,)),
            dma((5,)),
        ],
        compiler_params=pltpu.CompilerParams(
            vmem_limit_bytes=40 << 20, collective_id=4, has_side_effects=True
        ),
        cost_estimate=pl.CostEstimate(flops=70 * 10**9, bytes_accessed=10**7, transcendentals=0),
        name="dense_sums",
    )(grads, upper, mix)


EXCHANGE_IDS = {"forward": 0, "both": 1, "backward": 2}


def exchange_call(mode, pack, ex, args):
    rows, ff = ex.total, pack.ff
    forward, backward = mode in ("forward", "both"), mode in ("backward", "both")
    flat, wide = shape((rows, D), bf16), shape((rows, ff), bf16)
    packed = (pack.shards, pack.rows, 256)
    most = max(size for _, size in ex.ranges)
    vmem = pl.BlockSpec(memory_space=pltpu.VMEM)
    far = pl.BlockSpec(memory_space=pl.ANY)
    in_specs = [vmem] * len(args)
    in_specs[1] = far
    scratch = []
    if mode == "forward":
        outs = [flat, wide, wide]
    elif mode == "both":
        outs = [flat, flat, shape(packed, bf16)] + gating_outputs(True)
    else:
        in_specs[3] = in_specs[4] = far
        outs = [flat, shape(packed, bf16)] + gating_outputs(False)
    out_specs = [vmem] * len(outs)
    if mode == "forward":
        out_specs[1] = out_specs[2] = far
        scratch += [pltpu.VMEM((rows, ff), bf16)] * 2
    else:
        in_specs[-12:] = [far] * 12
        out_specs[2 if mode == "both" else 1] = far
    if forward:
        scratch += [pltpu.VMEM((rows, D), bf16), pltpu.VMEM((most, D), f32)]
    if backward:
        scratch += [pltpu.VMEM((rows, D), bf16)] * 2
        scratch += [pltpu.VMEM((rows, ff), bf16)] * 3
        scratch += [pltpu.VMEM((D, rows), bf16), pltpu.VMEM((most, D), f32)]
        scratch += [pltpu.VMEM(a.shape, a.dtype) for a in args[-12:]]
    scratch.append(pltpu.VMEM(packed, bf16))
    scratch += [pltpu.SemaphoreType.DMA((2, ex.experts - 1))] * 2
    scratch += [pltpu.SemaphoreType.DMA((2, 2, ex.experts - 1))] * 2
    scratch.append(pltpu.SemaphoreType.DMA((16,)))
    work = 6 * rows * D * ff * (1 if mode == "forward" else 2 if mode == "backward" else 3)
    return pl.pallas_call(
        functools.partial(exchange_kernel, mode, pack, ex),
        out_shape=outs,
        in_specs=in_specs,
        out_specs=out_specs,
        scratch_shapes=scratch,
        compiler_params=pltpu.CompilerParams(
            vmem_limit_bytes=62 << 20, collective_id=EXCHANGE_IDS[mode], has_side_effects=True
        ),
        cost_estimate=pl.CostEstimate(
            flops=10**9 if mode == "backward" else work + 40 * 10**9,
            bytes_accessed=6 * D * ff,
            transcendentals=0,
        ),
        name="experts_" + mode,
    )(*args)


def expert_outputs_kernel(pack, traffic, first_ref, second_ref, gate_ref, up_ref, down_ref):
    for l, ref in enumerate((first_ref, second_ref)):
        for n, out in enumerate((gate_ref, up_ref)):
            for j in range(pack.chunks):
                at = (n * pack.chunks + j) * pack.padded
                out[l, :, j * 256 : (j + 1) * 256] = ref[at : at + pack.part, :].astype(f32)
        for c in range(D // 256):
            at = pack.down + c * pack.own
            down_ref[l, :, c * 256 : (c + 1) * 256] = ref[at : at + pack.own, :].astype(f32)


def expert_outputs(pack, grads):
    wide = shape((LAYERS, pack.part, pack.ff))
    outs = [wide, wide, shape((LAYERS, pack.own, D))]
    body = functools.partial(expert_outputs_kernel, pack)
    return whole_call(body, "expert_outputs", outs, [], grads, 10**6)


def write_dense(part, labels, l, ref, outs, turn):
    proj_ref, out_ref, gain_ref, router_ref, vec_ref, const_ref = outs
    for c in range(3):
        proj_ref[l, c] = ref[:, c * D : (c + 1) * D].astype(f32)
    out_ref[l] = ref[:, W_OUT:W_SMALL].astype(f32)
    small = ref[:, W_SMALL:W_ALL].astype(f32)
    router_ref[l] = small[:, 0:labels]
    for c in range(2):
        const_ref[l, c] = small[:, S_CONST + 2 * c : S_CONST + 2 * c + 2]
    turn[0:part, :] = small
    rows = turn[...].T
    gain_ref[l] = rows[S_GAIN : S_GAIN + 2, 0:part]
    vec_ref[l] = rows[S_VEC : S_VEC + 2, 0:part]


def dense_outputs_kernel(part, labels, traffic, first_ref, second_ref, *refs):
    outs, turn = refs[:6], refs[6]
    turn[...] = jnp.zeros_like(turn)
    for l, ref in enumerate((first_ref, second_ref)):
        write_dense(part, labels, l, ref, outs, turn)


def dense_shapes(part, labels):
    return [
        shape((LAYERS, 3, part, D)),
        shape((LAYERS, part, D)),
        shape((LAYERS, 2, part)),
        shape((LAYERS, part, labels)),
        shape((LAYERS, 2, part)),
        shape((LAYERS, 2, part, 2)),
    ]


def dense_outputs(part, labels, grads):
    body = functools.partial(dense_outputs_kernel, part, labels)
    outs = dense_shapes(part, labels)
    return whole_call(body, "dense_outputs", outs, [pltpu.VMEM((128, 128), f32)], grads, 10**6)


def on_device(
    hidden_in,
    prior_logits,
    project_weight,
    output_weight,
    norm_gain,
    router_weight,
    mixing_weight,
    const_vector,
    const_weight,
    gate_weight,
    up_weight,
    down_weight,
    routes,
    priority,
    leaf_parent,
    cotangent,
):
    experts = lax.axis_size("expert")
    total_experts = experts + 4
    tokens = hidden_in.shape[0]
    capacity = 9 * tokens * TOP // (8 * total_experts)
    slots = -(-capacity // 16) * 16
    part = project_weight.shape[2]

    def pad_cols(a, width):
        return jnp.pad(a, [(0, 0)] * (a.ndim - 1) + [(0, width - a.shape[-1])])

    dense = []
    experts_w = []
    pack = Packing(lax.axis_size("shard"), part, gate_weight.shape[3])
    for l in range(LAYERS):
        small = jnp.concatenate(
            [
                pad_cols(router_weight[l], S_CONST),
                const_weight[l, 0],
                const_weight[l, 1],
                jnp.zeros((part, S_GAIN - S_CONST - 4), bf16),
                norm_gain[l].T,
                const_vector[l].T,
            ],
            axis=1,
        )
        packed = jnp.concatenate(
            [project_weight[l, c] for c in range(3)] + [output_weight[l], pad_cols(small, 128)],
            axis=1,
        )
        dense.append(lax.all_gather(packed, "shard", axis=0, tiled=True))
        mine = pack.pack(gate_weight[l, 0], up_weight[l, 0], down_weight[l, 0])
        experts_w.append(lax.all_gather(mine, "shard", axis=0, tiled=False))

    ranking = priority[0]
    earlier = (ranking[None, :] < ranking[:, None]).astype(bf16)
    labels = jnp.arange(total_experts, dtype=jnp.int32)
    hits = jnp.sum((routes[:, :, :, None] == labels).astype(f32), axis=2)
    chosen_rows = [jnp.pad(hits[l].T, [(0, 16 - total_experts), (0, 0)]) for l in range(LAYERS)]
    loaded = jnp.concatenate([hits[l, :, :experts] for l in range(LAYERS)], axis=1)
    loaded_half = loaded.astype(bf16)
    rank_col = dot(earlier, loaded_half)
    rank_row = lax.dot_general(
        loaded_half, earlier, (((0,), (1,)), ((), ())), preferred_element_type=f32
    )
    slot_col_all = jnp.where((loaded > 0) & (rank_col < capacity), rank_col, -1.0)
    slot_row_all = jnp.where((loaded.T > 0) & (rank_row < capacity), rank_row, -1.0)
    slot_col = [slot_col_all[:, l * experts : (l + 1) * experts] for l in range(LAYERS)]
    slot_row = [
        jnp.pad(
            slot_row_all[l * experts : (l + 1) * experts],
            [(0, 8 - experts), (0, 0)],
            constant_values=-1.0,
        )
        for l in range(LAYERS)
    ]
    visible = tree_visible(leaf_parent[0])
    bias = jnp.where(visible, 0.0, masked_fill)
    bias_t = jnp.where(visible.T, 0.0, masked_fill)
    mixes = [
        jnp.pad(mixing_weight[l], [(0, 16 - total_experts), (0, 16 - total_experts)])
        for l in range(LAYERS)
    ]
    z_rows = jnp.pad(prior_logits.T, [(0, 16 - total_experts), (0, 0)])

    ex = Exchange(experts, slots)
    saved = []
    front = [hidden_in]
    x_now = hidden_in
    for l in range(LAYERS):
        last = l == LAYERS - 1
        args = front + [dense[l], bias, z_rows, mixes[l].T, chosen_rows[l], slot_row[l]]
        if last:
            args.append(cotangent)
        outs = list(forward_call(l == 0, last, experts, slots, args))
        if l > 0:
            x_now = outs.pop(0)
        n1, qkv, att, lse, middle, n2, info, gcol, gpack, send, small = outs[:11]
        keep = dict(
            x=x_now, n1=n1, qkv=qkv, att=att, lse=lse, middle=middle, n2=n2, info=info,
            gcol=gcol, gpack=gpack, z=z_rows, small=small,
        )
        keep["received"] = dispatch_call(ex, send)
        if last:
            gating = [
                cotangent, n2, outs[11], slot_row[l], info, chosen_rows[l], gcol, small, z_rows,
                mixes[l], middle, slot_col[l],
            ]
            done = exchange_call(
                "both", pack, ex, [keep["received"], experts_w[l], outs[12]] + gating
            )
            keep["y"], keep["gin"], keep["dw"] = done[:3]
            keep["gating"] = done[3:]
        else:
            keep["y"], keep["gate"], keep["up"] = exchange_call(
                "forward", pack, ex, [keep["received"], experts_w[l]]
            )
        front = [middle, n2, keep["y"], gcol, slot_col[l], small]
        z_rows = info[0:16]
        saved.append(keep)

    gx = cotangent
    gz = None
    dense_grads = [None] * LAYERS
    mix_grads = [None] * LAYERS
    expert_grads = [None] * LAYERS
    hidden_out = None
    for l in range(LAYERS - 1, -1, -1):
        last = l == LAYERS - 1
        keep = saved[l]
        if not last:
            gating = [
                gx, keep["n2"], keep["y"], keep["gxs"], slot_row[l], keep["info"], chosen_rows[l],
                keep["gcol"], keep["small"], keep["z"], mixes[l], gz,
            ]
            done = exchange_call(
                "backward", pack, ex,
                [keep["received"], experts_w[l], keep["gy"], keep["gate"], keep["up"]] + gating,
            )
            keep["gin"], keep["dw"] = done[:2]
            keep["gating"] = done[2:]
        gn2, gsm, mix_grads[l], gz = keep["gating"][:4]
        if last:
            hidden_out = keep["gating"][4]
        d_experts, gn2 = lax.optimization_barrier((keep["dw"], gn2))
        if not last:
            gn2, expert_grads[l + 1] = lax.optimization_barrier((gn2, expert_grads[l + 1]))
        expert_grads[l] = lax.psum_scatter(d_experts, "shard", scatter_dimension=0, tiled=False)
        args = [
            gx, gn2, keep["gin"], slot_col[l], keep["middle"], keep["att"], dense[l], keep["qkv"],
            keep["n1"], keep["x"], bias_t, keep["lse"], gsm,
        ]
        if l > 0:
            args += [slot_row[l - 1], saved[l - 1]["gpack"]]
        outs = backward_call(l == 0, experts, slots, args)
        gx, d_dense = outs[:2]
        if l > 0:
            saved[l - 1]["gxs"], saved[l - 1]["gy"] = outs[2:4]
        if l > 0:
            dense_grads[l] = lax.psum_scatter(d_dense, "shard", scatter_dimension=0, tiled=True)

    if pack.shards == 8 and experts == 4:
        mix = jnp.pad(jnp.concatenate(mix_grads), [(0, 0), (0, 112)])
        dense_outs = finish_call(part, total_experts, d_dense, dense_grads[1], mix)
        mixing_grad = dense_outs[6]
    else:
        dense_grads[0] = lax.psum_scatter(d_dense, "shard", scatter_dimension=0, tiled=True)
        both_dense = lax.psum(jnp.stack(dense_grads), "expert")
        mixing_grad = lax.psum(jnp.stack(mix_grads), ("expert", "shard"))
        mixing_grad = mixing_grad[:, 0:total_experts, 0:total_experts]
        dense_outs = dense_outputs(part, total_experts, [both_dense[l] for l in range(LAYERS)])
    project_grad, output_grad, gain_grad, router_grad, vector_grad, const_grad = dense_outs[:6]
    gate_grad, up_grad, down_grad = expert_outputs(pack, expert_grads)
    return (
        hidden_out,
        gx,
        gz[0:total_experts].T,
        project_grad,
        output_grad,
        gain_grad,
        router_grad,
        mixing_grad,
        vector_grad,
        const_grad,
        gate_grad[:, None],
        up_grad[:, None],
        down_grad[:, None],
    )


def solution(mesh):
    both = ("expert", "shard")
    in_specs = (
        P(both, None),
        P(both, None),
        P(None, None, "shard", None),
        P(None, "shard", None),
        P(None, None, "shard"),
        P(None, "shard", None),
        P(),
        P(None, None, "shard"),
        P(None, None, "shard", None),
        P(None, "expert", "shard", None),
        P(None, "expert", "shard", None),
        P(None, "expert", "shard", None),
        P(None, both, None),
        P(both, None),
        P(both, None),
        P(both, None),
    )
    out_specs = (
        P(both, None),
        P(both, None),
        P(both, None),
        P(None, None, "shard", None),
        P(None, "shard", None),
        P(None, None, "shard"),
        P(None, "shard", None),
        P(),
        P(None, None, "shard"),
        P(None, None, "shard", None),
        P(None, "expert", "shard", None),
        P(None, "expert", "shard", None),
        P(None, "expert", "shard", None),
    )
    return jax.shard_map(
        on_device, mesh=mesh, in_specs=in_specs, out_specs=out_specs, check_vma=False
    )
```

```python
import functools

import jax
import jax.numpy as jnp
from jax import lax
from jax.experimental import pallas as pl
from jax.experimental.pallas import tpu as pltpu
from jax.sharding import PartitionSpec as P

D = 768
H = 12
HD = 64
TOP = 2
LAYERS = 2
TRUNK = 320
BRANCH = 64
LEAF = 32
TREE = 832

W_OUT = 3 * D
W_SMALL = 4 * D
W_ALL = 4 * D + 128
S_CONST = 16
S_GAIN = 24
S_VEC = 26

epsilon = 1e-06
masked_fill = -1e30
f32 = jnp.float32
bf16 = jnp.bfloat16
BLOCKS = 2
VMEM = 56 << 20


def dot(a, b):
    return jnp.dot(a, b, preferred_element_type=f32)


def dot_nt(a, b):
    return lax.dot_general(a, b, (((1,), (1,)), ((), ())), preferred_element_type=f32)


def dot_tn(a, b):
    return lax.dot_general(a, b, (((0,), (0,)), ((), ())), preferred_element_type=f32)


def split_bf16(v):
    high = v.astype(bf16)
    return high, (v - high.astype(f32)).astype(bf16)


def inv_rms(v):
    return lax.rsqrt(jnp.mean(v * v, axis=1, keepdims=True) + epsilon)


def tree_visible(parents):
    position = jnp.arange(TREE, dtype=jnp.int32)
    offset = position - TRUNK
    segment = jnp.where(
        position < TRUNK,
        0,
        jnp.where(offset < 4 * BRANCH, 1 + offset // BRANCH, 5 + (offset - 4 * BRANCH) // LEAF),
    )
    leaf_hits = (segment[:, None] - 5 == jnp.arange(8, dtype=jnp.int32)[None, :]).astype(jnp.int32)
    upper = jnp.where(segment >= 5, 1 + jnp.sum(leaf_hits * parents[None, :], axis=1), 0)
    key_segment = segment[None, :]
    causal = position[None, :] <= position[:, None]
    return causal & (
        (key_segment == segment[:, None]) | (key_segment == 0) | (key_segment == upper[:, None])
    )


def one_hot(slot_row, e, slots):
    row = lax.broadcasted_iota(jnp.int32, (slots, slot_row.shape[1]), 0).astype(f32)
    return jnp.where(row == slot_row[e : e + 1, :], 1.0, 0.0).astype(bf16)


def one_hot_col(slot_col, e, slots, scale=None):
    lane = lax.broadcasted_iota(jnp.int32, (slot_col.shape[0], slots), 1).astype(f32)
    value = 1.0 if scale is None else scale
    return jnp.where(lane == slot_col[:, e : e + 1], value, 0.0).astype(bf16)


def combine_rows(rows, middle_ref, n2_ref, y_ref, gcol_ref, slotc_ref, vectors, experts, slots):
    gcol = gcol_ref[rows, :]
    slot = slotc_ref[rows, :]
    total = middle_ref[rows, :] + gcol[:, 16:17] * n2_ref[rows, :].astype(f32)
    for c in range(2):
        total = total + gcol[:, 17 + c : 18 + c] * vectors[c : c + 1, :]
    for e in range(experts):
        weight = one_hot_col(slot, e, slots, gcol[:, e : e + 1])
        total = total + dot(weight, y_ref[e * slots : (e + 1) * slots, :])
    return total


def all_one_hot(slot_row, experts, slots):
    return jnp.concatenate([one_hot(slot_row, e, slots) for e in range(experts)], axis=0)


def send_grads(hot, gx, gpack, gxs_ref, gy_ref, experts, slots):
    got = dot(hot, gx)
    gates = dot(hot, gpack)
    gxs_ref[...] = got.astype(bf16)
    for e in range(experts):
        rows = slice(e * slots, (e + 1) * slots)
        gate = gates[rows, e : e + 1] + gates[rows, 64 + e : 65 + e]
        gy_ref[rows, :] = (got[rows, :] * gate).astype(bf16)


def row_blocks(tokens):
    size = tokens // BLOCKS
    return size, lambda i: pl.ds(pl.multiple_of(i * size, 16), size)


def causal_spans(tokens):
    edges = [0, 256, 512, tokens]
    return list(zip(edges[:-1], edges[1:]))


def forward_kernel(first, last, experts, slots, traffic, *refs):
    refs = list(refs)
    if first:
        x_in = refs.pop(0)
    else:
        mid_prev, n2_prev, y_ref, gcol_prev, slotc_prev, w_prev = [refs.pop(0) for _ in range(6)]
    w_ref, bias_ref, z_ref, mixt_ref, chosen_ref, slotr_ref = [refs.pop(0) for _ in range(6)]
    if last:
        cot_ref = refs.pop(0)
    if not first:
        x_out = refs.pop(0)
    n1_ref, qkv_ref, att_ref, lse_ref, mid_ref, n2_ref, info_ref, gcol_ref, gpack_ref, send_ref = [
        refs.pop(0) for _ in range(10)
    ]
    small_out = refs.pop(0)
    small_out[...] = w_ref[:, W_SMALL:]
    if last:
        gxs_ref, gy_ref = refs.pop(0), refs.pop(0)
    lse_cols, turn = refs
    tokens = n1_ref.shape[0]
    size, block = row_blocks(tokens)
    small = w_ref[:, W_SMALL:].astype(f32).T
    gain0 = small[S_GAIN : S_GAIN + 1, :]
    gain1 = small[S_GAIN + 1 : S_GAIN + 2, :]
    if not first:
        vectors_prev = w_prev[...].astype(f32).T[S_VEC : S_VEC + 2, :]

    def project(i, carry):
        rows = block(i)
        if first:
            x = x_in[rows, :].astype(f32)
        else:
            x = combine_rows(
                rows, mid_prev, n2_prev, y_ref, gcol_prev, slotc_prev, vectors_prev, experts, slots
            )
            x_out[rows, :] = x
        n1 = (x * inv_rms(x) * gain0).astype(bf16)
        n1_ref[rows, :] = n1
        for c in range(3):
            qkv_ref[rows, c * D : (c + 1) * D] = dot(n1, w_ref[:, c * D : (c + 1) * D]).astype(bf16)
        return carry

    lax.fori_loop(0, BLOCKS, project, 0)
    if not first:
        traffic.flush(x_out)
    traffic.flush(n1_ref)
    traffic.flush(qkv_ref)
    traffic.need(bias_ref)
    lane = lax.broadcasted_iota(jnp.int32, (1, 128), 1)
    low_f = jnp.where(lane < HD, 1.0, 0.0)
    low = low_f.astype(bf16)
    high = (1.0 - low_f).astype(bf16)
    lse_cols[...] = jnp.zeros_like(lse_cols)

    def pair(p, carry):
        k = qkv_ref[:, pl.ds(pl.multiple_of(D + p * 128, 128), 128)]
        v = qkv_ref[:, pl.ds(pl.multiple_of(2 * D + p * 128, 128), 128)]
        va = v * low + high
        vb = v * high + low
        here = pl.ds(pl.multiple_of(p * 128, 128), 128)
        spans = causal_spans(tokens)
        scores = []
        for start, stop in spans:
            q = qkv_ref[start:stop, here] * bf16(HD**-0.5)
            scores.append(
                [dot_nt(q * mask, k[:stop]) + bias_ref[start:stop, :stop] for mask in (low, high)]
            )
        for (start, stop), pairs in zip(spans, scores):
            peaks = [jnp.max(one, axis=1, keepdims=True) for one in pairs]
            expos = [jnp.exp(one - peak).astype(bf16) for one, peak in zip(pairs, peaks)]
            outs = [
                (dot(expo, value[:stop]), peak)
                for expo, value, peak in zip(expos, (va, vb), peaks)
            ]
            (oa, ma), (ob, mb) = outs
            numer = jnp.where(lane < HD, oa, ob)
            denom = pltpu.roll(jnp.where(lane < HD, ob, oa), HD, 1)
            att_ref[start:stop, here] = (numer / denom).astype(bf16)
            la = ma + jnp.log(oa[:, HD : HD + 1])
            lb = mb + jnp.log(ob[:, 0:1])
            old = lse_cols[start:stop, :]
            lse_cols[start:stop, :] = jnp.where(
                lane == 2 * p, la, jnp.where(lane == 2 * p + 1, lb, old)
            )
        return carry

    lax.fori_loop(0, H // 2, pair, 0)
    traffic.flush(att_ref)
    lse_ref[...] = lse_cols[...].T[0:16, :]

    def finish(i, carry):
        rows = block(i)
        if first:
            x = x_in[rows, :].astype(f32)
        else:
            x = x_out[rows, :]
        middle = x + dot(att_ref[rows, :], w_ref[:, W_OUT:W_SMALL])
        mid_ref[rows, :] = middle
        n2_ref[rows, :] = (middle * inv_rms(middle) * gain1).astype(bf16)
        return carry

    lax.fori_loop(0, BLOCKS, finish, 0)
    traffic.flush(mid_ref)
    traffic.flush(n2_ref)
    n2 = n2_ref[...]
    scores = dot_nt(small[0:32, :].astype(bf16), n2)
    logits = scores[0:16, :]
    z = z_ref[...]
    mixt = mixt_ref[...]
    for i in range(experts + 4):
        logits = logits + mixt[:, i : i + 1] * z[i : i + 1, :]
    row = lax.broadcasted_iota(jnp.int32, (16, tokens), 0)
    valid = row < experts + 4
    peak = jnp.max(jnp.where(valid, logits, masked_fill), axis=0, keepdims=True)
    expo = jnp.where(valid, jnp.exp(jnp.minimum(logits - peak, 0.0)), 0.0)
    prob = expo / jnp.sum(expo, axis=0, keepdims=True)
    gates = prob * chosen_ref[...]
    info_ref[0:16, :] = logits
    info_ref[16:32, :] = prob
    turn[...] = jnp.zeros_like(turn)
    turn[0:16, 0:tokens] = gates
    own = gates[experts + 1 : experts + 2, :]
    alphas = []
    for c in range(2):
        l0 = scores[S_CONST + 2 * c : S_CONST + 2 * c + 1, :]
        l1 = scores[S_CONST + 2 * c + 1 : S_CONST + 2 * c + 2, :]
        a0 = jax.nn.sigmoid(l0 - l1)
        a1 = jax.nn.sigmoid(l1 - l0)
        alphas += [a0, a1]
        share = gates[experts + 2 + c : experts + 3 + c, :]
        own = own + share * a0
        turn[17 + c : 18 + c, 0:tokens] = share * a1
    turn[16:17, 0:tokens] = own
    zero_row = jnp.zeros((4, tokens), f32)
    info_ref[32:40, :] = jnp.concatenate(alphas + [zero_row], axis=0)
    gcol = turn[...].T[0:tokens, :]
    gcol_ref[...] = gcol
    upper, lower = split_bf16(jnp.where(lane < 16, gcol, 0.0))
    gpack = upper + pltpu.roll(lower.astype(f32), 64, 1).astype(bf16)
    gpack_ref[...] = gpack
    hot = all_one_hot(slotr_ref[...], experts, slots)
    send_ref[...] = dot(hot, n2).astype(bf16)
    if last:
        traffic.need(cot_ref)
        send_grads(hot, cot_ref[...], gpack, gxs_ref, gy_ref, experts, slots)


def shape(dims, dtype=f32):
    return jax.ShapeDtypeStruct(tuple(dims), dtype)


class Traffic:
    def __init__(self):
        self.fetches, self.sinks, self.flushes = {}, {}, []

    def fetch(self, src, buffer, sem):
        copy = pltpu.make_async_copy(src, buffer, sem)
        copy.start()
        self.fetches[id(buffer)] = copy

    def need(self, *buffers):
        for buffer in buffers:
            copy = self.fetches.pop(id(buffer), None)
            if copy is not None:
                copy.wait()

    def sink(self, buffer, dst, sems):
        self.sinks[id(buffer)] = [dst, sems, 0]

    def flush(self, buffer, part=None):
        entry = self.sinks.get(id(buffer))
        if entry is None:
            return
        dst, sems, used = entry
        entry[2] += 1
        src, dst = (buffer, dst) if part is None else (buffer.at[part], dst.at[part])
        copy = pltpu.make_async_copy(src, dst, sems.at[used])
        copy.start()
        self.flushes.append(copy)

    def finish(self):
        for copy in self.flushes:
            copy.wait()


FLUSHES = 3


def whole_call(body, name, outs, scratch, args, flops, late=(), early=()):
    moved = sum(a.size * a.dtype.itemsize for a in args) + sum(
        o.size * o.dtype.itemsize for o in outs
    )
    late, early = sorted(late), sorted(early)

    def kernel(*refs):
        ins, rest = list(refs[: len(args)]), refs[len(args) :]
        results, rest = list(rest[: len(outs)]), rest[len(outs) :]
        own, rest = rest[: len(scratch)], rest[len(scratch) :]
        traffic = Traffic()
        fetch_sems, flush_sems = rest[len(late) + len(early) :]
        for n, at in enumerate(late):
            traffic.fetch(ins[at], rest[n], fetch_sems.at[n])
            ins[at] = rest[n]
        for n, at in enumerate(early):
            buffer = rest[len(late) + n]
            traffic.sink(buffer, results[at], flush_sems.at[n])
            results[at] = buffer
        body(traffic, *ins, *results, *own)
        traffic.finish()

    near, far = pl.BlockSpec(memory_space=pltpu.VMEM), pl.BlockSpec(memory_space=pl.ANY)
    buffers = [pltpu.VMEM(args[at].shape, args[at].dtype) for at in late]
    buffers += [pltpu.VMEM(outs[at].shape, outs[at].dtype) for at in early]
    buffers.append(pltpu.SemaphoreType.DMA((max(len(late), 1),)))
    buffers.append(pltpu.SemaphoreType.DMA((max(len(early), 1), FLUSHES)))
    return pl.pallas_call(
        kernel,
        out_shape=outs,
        in_specs=[far if n in late else near for n in range(len(args))],
        out_specs=[far if n in early else near for n in range(len(outs))],
        scratch_shapes=list(scratch) + buffers,
        compiler_params=pltpu.CompilerParams(vmem_limit_bytes=VMEM),
        cost_estimate=pl.CostEstimate(flops=flops, bytes_accessed=moved, transcendentals=0),
        name=name,
    )(*args)


def forward_call(first, last, experts, slots, args):
    tokens = TREE
    sent = experts * slots
    outs = [] if first else [shape((tokens, D))]
    outs += [
        shape((tokens, D), bf16),
        shape((tokens, 3 * D), bf16),
        shape((tokens, D), bf16),
        shape((16, tokens)),
        shape((tokens, D)),
        shape((tokens, D), bf16),
        shape((40, tokens)),
        shape((tokens, 128)),
        shape((tokens, 128), bf16),
        shape((sent, D), bf16),
        shape((D, 128), bf16),
    ]
    if last:
        outs += [shape((sent, D), bf16), shape((sent, D), bf16)]
    padded = -(-tokens // 128) * 128
    scratch = [pltpu.VMEM((tokens, 128), f32), pltpu.VMEM((128, padded), f32)]
    body = functools.partial(forward_kernel, first, last, experts, slots)
    inputs, results = (1, 0) if first else (6, 1)
    late = [inputs + 1] + ([inputs + 6] if last else [])
    early = ([] if first else [0]) + [results + n for n in (0, 1, 2, 4, 5)]
    return whole_call(body, "block_forward", outs, scratch, args, 20 * 10**9, late, early)


def gating_kernel(last, experts, slots, *refs):
    refs = list(refs)
    gx_ref, n2_ref, y_ref, gxs_ref, slotr_ref, info_ref, chosen_ref, gcol_ref, small_ref = [
        refs.pop(0) for _ in range(9)
    ]
    z_ref, mix_ref = refs.pop(0), refs.pop(0)
    if last:
        mid_ref, slotc_ref = refs.pop(0), refs.pop(0)
    else:
        gz_ref = refs.pop(0)
    gn2_ref, gsm_ref, gmix_ref, gprev_ref = [refs.pop(0) for _ in range(4)]
    if last:
        out_ref = refs.pop(0)
    tokens = n2_ref.shape[0]
    size, block = row_blocks(tokens)
    small = small_ref[...].astype(f32).T
    small_half = small[0:32, :].astype(bf16)
    vectors = small[S_VEC : S_VEC + 2, :]
    slot_row = slotr_ref[...]
    ones = jnp.ones((16, D), bf16)
    row = lax.broadcasted_iota(jnp.int32, (16, slots), 0)
    scattered = jnp.zeros((16, tokens), f32)
    for e in range(experts):
        rows = slice(e * slots, (e + 1) * slots)
        inner = y_ref[rows, :].astype(f32) * gxs_ref[rows, :].astype(f32)
        upper, lower = split_bf16(inner)
        sums = dot_nt(ones, upper) + dot_nt(ones, lower)
        upper, lower = split_bf16(sums)
        lhs = jnp.where(row == e, upper.astype(f32), 0.0) + jnp.where(
            row == 8 + e, lower.astype(f32), 0.0
        )
        scattered = scattered + dot(lhs.astype(bf16), one_hot(slot_row, e, slots))
    gx = gx_ref[...].astype(f32)
    gx_half = gx.astype(bf16)
    n2 = n2_ref[...]
    upper, lower = split_bf16(gx * n2.astype(f32))
    gx_n2 = (dot_nt(ones, upper) + dot_nt(ones, lower))[0:1, :]
    gx_small = dot_nt(small_half, gx_half)
    prob = info_ref[16:32, :]
    chosen = chosen_ref[...]
    gates = prob * chosen
    trow = lax.broadcasted_iota(jnp.int32, (16, tokens), 0)
    gp = jnp.concatenate([scattered[0:8, :] + scattered[8:16, :], jnp.zeros((8, tokens), f32)], 0)
    gp = jnp.where(trow == experts + 1, gx_n2, jnp.where(trow < experts, gp, 0.0))
    crow = lax.broadcasted_iota(jnp.int32, (8, tokens), 0)
    glog = jnp.zeros((8, tokens), f32)
    coefs = jnp.zeros((8, tokens), f32)
    for c in range(2):
        a0 = info_ref[32 + 2 * c : 33 + 2 * c, :]
        a1 = info_ref[33 + 2 * c : 34 + 2 * c, :]
        gx_v = gx_small[S_VEC + c : S_VEC + c + 1, :]
        share = gates[experts + 2 + c : experts + 3 + c, :]
        gp = jnp.where(trow == experts + 2 + c, a0 * gx_n2 + a1 * gx_v, gp)
        gl = share * (gx_n2 - gx_v) * a0 * a1
        glog = jnp.where(crow == 2 * c, gl, jnp.where(crow == 2 * c + 1, -gl, glog))
        coefs = jnp.where(crow == c, share * a1, coefs)
    gp = gp * chosen
    gz = prob * (gp - jnp.sum(prob * gp, axis=0, keepdims=True))
    if not last:
        gz = gz + gz_ref[...]
    z = z_ref[...]
    gmix_ref[...] = lax.dot_general(
        z, gz, (((1,), (1,)), ((), ())), precision=lax.Precision.HIGHEST, preferred_element_type=f32
    )
    mix = mix_ref[...]
    gprev = jnp.zeros((16, tokens), f32)
    for o in range(experts + 4):
        gprev = gprev + mix[:, o : o + 1] * gz[o : o + 1, :]
    gprev_ref[...] = gprev
    allg = jnp.concatenate([gz, glog, jnp.zeros((8, tokens), f32)], axis=0)
    upper, lower = split_bf16(allg)
    gsm = dot(upper, n2) + dot(lower, n2)
    cu, cl = split_bf16(jnp.concatenate([coefs, jnp.zeros((8, tokens), f32)], axis=0))
    gvec = dot(cu, gx_half) + dot(cl, gx_half)
    gsm_ref[0:24, :] = gsm[0:24, :]
    gsm_ref[24:32, :] = jnp.concatenate(
        [jnp.zeros((2, D), f32), gvec[0:2, :], jnp.zeros((4, D), f32)], axis=0
    )
    both = jnp.concatenate([upper, lower], axis=0)
    twice = jnp.concatenate([small_half, small_half], axis=0)
    gn2_ref[...] = dot_tn(both, twice)

    def add(i, carry):
        rows = block(i)
        gn2_ref[rows, :] = gn2_ref[rows, :] + gcol_ref[rows, 16:17] * gx_ref[rows, :].astype(f32)
        if last:
            out_ref[rows, :] = combine_rows(
                rows, mid_ref, n2_ref, y_ref, gcol_ref, slotc_ref, vectors, experts, slots
            ).astype(bf16)
        return carry

    lax.fori_loop(0, BLOCKS, add, 0)


def gating_outputs(last):
    tokens = TREE
    outs = [shape((tokens, D)), shape((32, D)), shape((16, 16)), shape((16, tokens))]
    if last:
        outs += [shape((tokens, D), bf16)]
    return outs


def backward_kernel(first, experts, slots, traffic, *refs):
    refs = list(refs)
    gx_ref, gn2p_ref, gn2e_ref, slotc_ref, mid_ref, att_ref, w_ref, qkv_ref, n1_ref, x_ref = [
        refs.pop(0) for _ in range(10)
    ]
    biast_ref, lse_ref, gsm_ref = [refs.pop(0) for _ in range(3)]
    if not first:
        slotr_ref, gpack_ref = refs.pop(0), refs.pop(0)
    gout_ref, dw_ref = refs.pop(0), refs.pop(0)
    if not first:
        gxs_ref, gy_ref = refs.pop(0), refs.pop(0)
    gatt, go, gqkv, turn = refs
    tokens = n1_ref.shape[0]
    size, block = row_blocks(tokens)
    small = w_ref[:, W_SMALL:].astype(f32).T
    gain0 = small[S_GAIN : S_GAIN + 1, :]
    gain1 = small[S_GAIN + 1 : S_GAIN + 2, :]

    def enter(i, total):
        rows = block(i)
        gn2 = gn2p_ref[rows, :]
        slot = slotc_ref[rows, :]
        for e in range(experts):
            gn2 = gn2 + dot(one_hot_col(slot, e, slots), gn2e_ref[e * slots : (e + 1) * slots, :])
        middle = mid_ref[rows, :]
        r = inv_rms(middle)
        scaled = gain1 * gn2
        inner = jnp.mean(middle * scaled, axis=1, keepdims=True)
        gmid = gx_ref[rows, :].astype(f32) + r * scaled - middle * (r * r * r * inner)
        gout_ref[rows, :] = gmid
        half = gmid.astype(bf16)
        gatt[rows, :] = half
        go[rows, :] = dot_nt(half, w_ref[:, W_OUT:W_SMALL]).astype(bf16)
        return total + jnp.sum(gn2 * middle * r, axis=0, keepdims=True)

    ggain1 = lax.fori_loop(0, BLOCKS, enter, jnp.zeros((1, D), f32))
    traffic.need(att_ref)
    lane = lax.broadcasted_iota(jnp.int32, (1, 128), 1)
    low_f = jnp.where(lane < HD, 1.0, 0.0)
    low = low_f.astype(bf16)
    high = (1.0 - low_f).astype(bf16)
    scale = HD**-0.5

    def out_grad(p, carry):
        here = pl.ds(pl.multiple_of(p * 128, 128), 128)
        dw_ref[here, W_OUT:W_SMALL] = dot_tn(att_ref[:, here], gatt[...]).astype(bf16)
        return carry

    lax.fori_loop(0, D // 128, out_grad, 0)
    traffic.flush(dw_ref, (slice(None), slice(W_OUT, W_SMALL)))
    traffic.need(qkv_ref, biast_ref, lse_ref)
    spans = causal_spans(tokens)

    def pair(p, carry):
        here = pl.ds(pl.multiple_of(p * 128, 128), 128)
        lanes_k = pl.ds(pl.multiple_of(D + p * 128, 128), 128)
        lanes_v = pl.ds(pl.multiple_of(2 * D + p * 128, 128), 128)
        q = qkv_ref[:, here] * bf16(scale)
        k = qkv_ref[:, lanes_k]
        v = qkv_ref[:, lanes_v]
        g = go[:, here]
        turn[0:tokens, :] = g.astype(f32) * att_ref[:, here].astype(f32)
        inner = turn[...].T[:, 0:tokens]
        turn[0:tokens, :] = k.astype(f32)
        kt = turn[...].T[:, 0:tokens].astype(bf16)
        gk = [0.0] * len(spans)
        gv = [0.0] * len(spans)
        masks = (low, high)
        qs = [q * mask for mask in masks]
        gs = [g * mask for mask in masks]
        dsums = [
            jnp.sum(inner[h * HD : (h + 1) * HD, :], axis=0, keepdims=True) for h in range(2)
        ]
        lses = [lse_ref[pl.ds(2 * p + h, 1), :] for h in range(2)]
        parts = [[], []]
        for n, (start, stop) in enumerate(spans):
            st = [
                dot_nt(k[start:stop], qs[h][start:]) + biast_ref[start:stop, start:]
                for h in range(2)
            ]
            gpt = [dot_nt(v[start:stop], gs[h][start:]) for h in range(2)]
            pt = [jnp.exp(st[h] - lses[h][:, start:]) for h in range(2)]
            gst = [(pt[h] * (gpt[h] - dsums[h][:, start:])).astype(bf16) for h in range(2)]
            for h in range(2):
                gv[n] = gv[n] + dot(pt[h].astype(bf16), gs[h][start:])
                gk[n] = gk[n] + dot(gst[h], qs[h][start:])
                parts[h].append(dot(kt[h * HD : (h + 1) * HD, start:stop], gst[h]))
        gq_t = []
        for h in range(2):
            cols = []
            for n, (start, stop) in enumerate(spans):
                piece = 0.0
                for m in range(n + 1):
                    origin = spans[m][0]
                    piece = piece + parts[h][m][:, start - origin : stop - origin]
                cols.append(piece)
            gq_t.append(jnp.concatenate(cols, axis=1))
        turn_t = jnp.concatenate(gq_t, axis=0) * scale
        pad = turn.shape[0] - tokens
        turn_t = jnp.concatenate([turn_t, jnp.zeros((128, pad), f32)], axis=1)
        gqkv[:, here] = turn_t.T[0:tokens, :].astype(bf16)
        for n, (start, stop) in enumerate(spans):
            gqkv[start:stop, lanes_k] = gk[n].astype(bf16)
            gqkv[start:stop, lanes_v] = gv[n].astype(bf16)
        return carry

    turn[...] = jnp.zeros_like(turn)
    lax.fori_loop(0, H // 2, pair, 0)
    traffic.need(n1_ref)

    def in_grad(p, carry):
        here = pl.ds(pl.multiple_of(p * 128, 128), 128)
        dw_ref[here, 0:W_OUT] = dot_tn(n1_ref[:, here], gqkv[...]).astype(bf16)
        return carry

    lax.fori_loop(0, D // 128, in_grad, 0)
    traffic.flush(dw_ref, (slice(None), slice(0, W_OUT)))
    traffic.need(x_ref)

    def leave(i, total):
        rows = block(i)
        gn1 = dot_nt(gqkv[rows, :], w_ref[:, 0:W_OUT])
        x = x_ref[rows, :].astype(f32)
        r = inv_rms(x)
        scaled = gain0 * gn1
        inner = jnp.mean(x * scaled, axis=1, keepdims=True)
        gx = gout_ref[rows, :] + r * scaled - x * (r * r * r * inner)
        gout_ref[rows, :] = gx
        gatt[rows, :] = gx.astype(bf16)
        return total + jnp.sum(gn1 * x * r, axis=0, keepdims=True)

    ggain0 = lax.fori_loop(0, BLOCKS, leave, jnp.zeros((1, D), f32))
    rows = jnp.concatenate(
        [gsm_ref[0:24, :], ggain0, ggain1, gsm_ref[26:32, :], jnp.zeros((96, D), f32)], axis=0
    )
    dw_ref[:, W_SMALL:] = rows.T.astype(bf16)
    traffic.flush(dw_ref, (slice(None), slice(W_SMALL, W_ALL)))
    traffic.flush(gout_ref)
    if not first:
        hot = all_one_hot(slotr_ref[...], experts, slots)
        send_grads(hot, gatt[...], gpack_ref[...], gxs_ref, gy_ref, experts, slots)


def backward_call(first, experts, slots, args):
    tokens = TREE
    sent = experts * slots
    outs = [shape((tokens, D)), shape((D, W_ALL), bf16)]
    if not first:
        outs += [shape((sent, D), bf16), shape((sent, D), bf16)]
    padded = -(-tokens // 128) * 128
    scratch = [
        pltpu.VMEM((tokens, D), bf16),
        pltpu.VMEM((tokens, D), bf16),
        pltpu.VMEM((tokens, 3 * D), bf16),
        pltpu.VMEM((padded, 128), f32),
    ]
    body = functools.partial(backward_kernel, first, experts, slots)
    return whole_call(
        body, "block_backward", outs, scratch, args, 40 * 10**9, (5, 7, 8, 9, 10, 11), (0, 1)
    )


class Packing:
    def __init__(self, shards, part, ff):
        self.shards, self.part, self.ff = shards, part, ff
        self.padded = -(-part // 16) * 16
        self.chunks = ff // 256
        self.own = ff // shards
        self.down = 2 * self.chunks * self.padded
        self.rows = self.down + (D // 256) * self.own

    def pack(self, gate, up, down):
        pieces = []
        for wide in (gate, up):
            cut = wide.reshape(self.part, self.chunks, 256).transpose(1, 0, 2)
            cut = jnp.pad(cut, [(0, 0), (0, self.padded - self.part), (0, 0)])
            pieces.append(cut.reshape(self.chunks * self.padded, 256))
        pieces.append(
            down.reshape(self.own, D // 256, 256).transpose(1, 0, 2).reshape(-1, 256)
        )
        return jnp.concatenate(pieces, axis=0)

    def wide_part(self, ref, n, j):
        at = pl.multiple_of((n * self.chunks + j) * self.padded, 16)
        return ref[:, pl.ds(at, self.padded), :][:, : self.part, :].reshape(D, 256)

    def tall_part(self, ref, j):
        group = 256 // self.own
        here = pl.ds(j * group, group)
        pieces = []
        for c in range(D // 256):
            at = self.down + c * self.own
            pieces.append(ref[here, at : at + self.own, :].reshape(256, 256))
        return jnp.concatenate(pieces, axis=1)

    def put_wide(self, ref, n, j, grad):
        at = pl.multiple_of((n * self.chunks + j) * self.padded, 16)
        ref[:, pl.ds(at, self.part), :] = grad.reshape(self.shards, self.part, 256)

    def put_tall(self, ref, j, grad):
        group = 256 // self.own
        for c in range(D // 256):
            at = self.down + c * self.own
            ref[pl.ds(j * group, group), at : at + self.own, :] = grad[
                :, c * 256 : (c + 1) * 256
            ].reshape(group, self.own, 256)


class Exchange:
    def __init__(self, experts, slots):
        self.experts, self.slots = experts, slots
        half = -(-slots // 32) * 16
        quarter = -(-half // 32) * 16
        edges = (0, quarter, half, slots)
        self.waves = tuple((low, high - low) for low, high in zip(edges[:-1], edges[1:]))
        self.ranges = [(0, slots)]
        for _, size in self.waves:
            start = self.ranges[-1][0] + self.ranges[-1][1]
            self.ranges.append((start, (experts - 1) * size))
        self.total = experts * slots

    def span(self, group):
        start = self.ranges[1 + group[0]][0]
        return start, sum(self.ranges[1 + wave][1] for wave in group)

    def held(self, wave, d):
        size = self.waves[wave][1]
        return pl.ds(self.ranges[1 + wave][0] + (d - 1) * size, size)

    def slot(self, device, wave):
        offset, size = self.waves[wave]
        return pl.ds(pl.multiple_of(device * self.slots + offset, 16), size)


MESH = pl.DeviceIdType.MESH


def greet(experts):
    me = lax.axis_index("expert")
    barrier = pltpu.get_barrier_semaphore()
    for d in range(1, experts):
        pl.semaphore_signal(
            barrier, inc=1, device_id={"expert": lax.rem(me + d, experts)}, device_id_type=MESH
        )
    pl.semaphore_wait(barrier, experts - 1)


def out_copies(ex, wave, src, dst, sends, recvs):
    me = lax.axis_index("expert")
    copies = []
    for d in range(1, ex.experts):
        to = lax.rem(me + d, ex.experts)
        copies.append(
            pltpu.make_async_remote_copy(
                src_ref=src.at[ex.slot(to, wave)],
                dst_ref=dst.at[ex.held(wave, d)],
                send_sem=sends.at[wave, d - 1],
                recv_sem=recvs.at[wave, d - 1],
                device_id={"expert": to},
                device_id_type=MESH,
            )
        )
    return copies


def back_copies(ex, wave, n, src, dst, sends, recvs):
    me = lax.axis_index("expert")
    copies = []
    for d in range(1, ex.experts):
        copies.append(
            pltpu.make_async_remote_copy(
                src_ref=src.at[ex.held(wave, d)],
                dst_ref=dst.at[ex.slot(me, wave)],
                send_sem=sends.at[n, wave, d - 1],
                recv_sem=recvs.at[n, wave, d - 1],
                device_id={"expert": lax.rem(me + ex.experts - d, ex.experts)},
                device_id_type=MESH,
            )
        )
    return copies


def own_slots(ex):
    me = lax.axis_index("expert")
    return pl.ds(pl.multiple_of(me * ex.slots, 16), ex.slots)


def dispatch_kernel(ex, send, recv, sends, recvs, local):
    own = pltpu.make_async_copy(send.at[own_slots(ex)], recv.at[pl.ds(0, ex.slots)], local)
    own.start()
    greet(ex.experts)
    copies = []
    for wave in range(len(ex.waves)):
        copies += out_copies(ex, wave, send, recv, sends, recvs)
    for copy in copies:
        copy.start()
    for copy in copies:
        copy.wait()
    own.wait()


def dispatch_call(ex, rows):
    far = pl.BlockSpec(memory_space=pl.ANY)
    return pl.pallas_call(
        functools.partial(dispatch_kernel, ex),
        out_shape=shape((ex.total, D), bf16),
        in_specs=[far],
        out_specs=far,
        scratch_shapes=[pltpu.SemaphoreType.DMA((len(ex.waves), ex.experts - 1))] * 2
        + [pltpu.SemaphoreType.DMA],
        compiler_params=pltpu.CompilerParams(
            vmem_limit_bytes=60 << 20, collective_id=3, has_side_effects=True
        ),
        cost_estimate=pl.CostEstimate(flops=35 * 10**9, bytes_accessed=10**6, transcendentals=0),
        name="dispatch",
    )(rows)


def exchange_kernel(mode, pack, ex, *refs):
    refs = list(refs)
    forward, backward = mode in ("forward", "both"), mode in ("backward", "both")
    recv_n = refs.pop(0)
    w_hbm = refs.pop(0)
    if backward:
        send_g = refs.pop(0)
        if mode == "backward":
            gate_hbm, up_hbm = refs.pop(0), refs.pop(0)
        gating_far = [refs.pop(0) for _ in range(12)]
    if forward:
        back_y = refs.pop(0)
    if mode == "forward":
        gates_far, ups_far, gates, ups = [refs.pop(0) for _ in range(4)]
    else:
        back_g, dw_far = refs.pop(0), refs.pop(0)
        gating_outs = [refs.pop(0) for _ in range(5 if mode == "both" else 4)]
    if forward:
        out_y, acc_y = refs.pop(0), refs.pop(0)
    if backward:
        recv_g, out_g, hids, gates, ups, rows_t, acc_g = [refs.pop(0) for _ in range(7)]
        gating = [refs.pop(0) for _ in range(12)]
    w = refs.pop(0)
    sends, recvs, backs, gots, local = refs
    traffic = Traffic()
    if mode == "forward":
        traffic.sink(gates, gates_far, local.at[4:8])
        traffic.sink(ups, ups_far, local.at[8:12])

    loads = [pltpu.make_async_copy(w_hbm, w, local.at[0])]
    if mode == "backward":
        loads.append(pltpu.make_async_copy(gate_hbm, gates, local.at[1]))
        loads.append(pltpu.make_async_copy(up_hbm, ups, local.at[2]))
    if mode == "backward":
        for n, (far, near) in enumerate(zip(gating_far, gating)):
            traffic.fetch(far, near, local.at[4 + n])
    for copy in loads:
        copy.start()
    if mode == "both":
        for n, (far, near) in enumerate(zip(gating_far, gating)):
            traffic.fetch(far, near, local.at[4 + n])
    greet(ex.experts)

    def work(start, size):
        rows = slice(start, start + size)
        part = slice(0, size)
        if forward:
            acc_y[part, :] = jnp.zeros((size, D), f32)
        if backward:
            acc_g[part, :] = jnp.zeros((size, D), f32)

        def chunk(j, carry):
            lanes = pl.ds(pl.multiple_of(j * 256, 256), 256)
            gate_w, up_w = pack.wide_part(w, 0, j), pack.wide_part(w, 1, j)
            down_w = pack.tall_part(w, j)
            if forward:
                r = recv_n[rows, :]
                gate, up = dot(r, gate_w), dot(r, up_w)
                if mode == "forward":
                    gates[rows, lanes] = gate.astype(bf16)
                    ups[rows, lanes] = up.astype(bf16)
            else:
                gate, up = gates[rows, lanes].astype(f32), ups[rows, lanes].astype(f32)
            s = jax.nn.sigmoid(gate)
            act = gate * s
            hid = (act * up).astype(bf16)
            if forward:
                acc_y[part, :] = acc_y[part, :] + dot(hid, down_w)
            if backward:
                hids[rows, lanes] = hid
                ghid = dot_nt(recv_g[rows, :], down_w)
                guv = (ghid * act).astype(bf16)
                ggu = (ghid * up * (s * (1.0 + gate * (1.0 - s)))).astype(bf16)
                gates[rows, lanes] = ggu
                ups[rows, lanes] = guv
                acc_g[part, :] = acc_g[part, :] + dot_nt(ggu, gate_w) + dot_nt(guv, up_w)
            return carry

        lax.fori_loop(0, pack.chunks, chunk, 0)
        if mode == "forward":
            here = pl.ds(start, size)
            traffic.flush(gates, here)
            traffic.flush(ups, here)
        if forward:
            out_y[rows, :] = acc_y[part, :].astype(bf16)
        if backward:
            out_g[rows, :] = acc_g[part, :].astype(bf16)

    def send_back(group):
        for wave in group:
            if forward:
                ys.extend(back_copies(ex, wave, 0, out_y, back_y, backs, gots))
                for copy in ys[1 - ex.experts :]:
                    copy.start()
        for wave in group:
            if backward:
                gs.extend(back_copies(ex, wave, 1, out_g, back_g, backs, gots))
                for copy in gs[1 - ex.experts :]:
                    copy.start()

    ys, gs = [], []
    groups = ((0,), (1,), (2,)) if mode == "forward" else ((0, 1), (2,))
    if backward:
        arrivals = []
        for group in groups:
            arrivals.append([])
            for wave in group:
                arrivals[-1] += out_copies(ex, wave, send_g, recv_g, sends, recvs)
        for copy in arrivals[0]:
            copy.start()
        recv_g[0 : ex.slots, :] = send_g[own_slots(ex), :]
        if mode == "backward":
            traffic.need(*gating)
            gating_kernel(False, ex.experts, ex.slots, *gating, *gating_outs)
    for copy in loads:
        copy.wait()
    if backward:
        work(*ex.ranges[0])
        for copy in arrivals[0]:
            copy.wait_send()
        for copy in arrivals[1]:
            copy.start()
        for copy in arrivals[0]:
            copy.wait_recv()
    for n, group in enumerate(groups):
        if backward and n > 0:
            for copy in arrivals[n]:
                copy.wait()
        work(*ex.span(group))
        send_back(group)
    if mode == "forward":
        work(*ex.ranges[0])
    if forward:
        back_y[own_slots(ex), :] = out_y[0 : ex.slots, :]
    if backward:
        back_g[own_slots(ex), :] = out_g[0 : ex.slots, :]
        rows_t[...] = recv_n[...].T
        dw = w
        if pack.padded != pack.part:
            dw[...] = jnp.zeros_like(dw)

        def weights(j, carry):
            lanes = pl.ds(pl.multiple_of(j * 256, 256), 256)
            pack.put_wide(dw, 0, j, dot(rows_t[...], gates[:, lanes]).astype(bf16))
            pack.put_wide(dw, 1, j, dot(rows_t[...], ups[:, lanes]).astype(bf16))
            pack.put_tall(dw, j, dot_tn(hids[:, lanes], recv_g[...]).astype(bf16))
            return carry

        lax.fori_loop(0, pack.chunks, weights, 0)
        leaving = pltpu.make_async_copy(dw, dw_far, local.at[3])
        leaving.start()
    for copy in ys:
        copy.wait()
    if mode == "both":
        traffic.need(*gating)
        gating_kernel(True, ex.experts, ex.slots, *gating[:2], back_y, *gating[2:], *gating_outs)
    for copy in gs:
        copy.wait()
    if backward:
        leaving.wait()
    traffic.finish()


SPLIT = 13 * 128


def cube_kernel(part, labels, g_ref, upper_ref, mix_ref, ready, mix_out, own, *refs):
    got_c, sums, got_a, got_b, half_a, half_b, end_a, end_b, mine, quarters, mix_held, mix_got = refs[:12]
    send, recv, z_send, z_recv, mix_send, mix_recv, own_sem = refs[12:]
    me = lax.axis_index("shard")
    z = lax.axis_index("expert")
    owners = quarters.shape[1]
    core, x, y = lax.rem(me, 2), lax.rem(me // 2, 2), me // 4
    near, over_x, over_y = me + 1 - 2 * core, me + 2 - 4 * x, me + 4 - 8 * y
    chips = [2 * (1 - y) + 1 - x, 2 * y + 1 - x, 2 * (1 - y) + x, 2 * y + x]

    def rows(shard):
        return pl.ds(pl.multiple_of(shard * part, 16), part)

    loads = [
        pltpu.make_async_copy(g_ref.at[rows(2 * chip + core)], own.at[n], own_sem.at[n])
        for n, chip in enumerate(chips)
    ]
    for load in loads:
        load.start()
    barrier = pltpu.get_barrier_semaphore()
    for other in (near, over_x, over_y):
        pl.semaphore_signal(barrier, inc=1, device_id={"shard": other}, device_id_type=MESH)
    for d in range(1, owners):
        pl.semaphore_signal(
            barrier, inc=1, device_id={"expert": lax.rem(z + d, owners)}, device_id_type=MESH
        )
    pl.semaphore_wait(barrier, 3 + owners - 1)
    cols_a, cols_b = slice(0, SPLIT), slice(SPLIT, W_ALL)

    def remote(src, dst, send_sem, recv_sem, to):
        made = pltpu.make_async_remote_copy(
            src_ref=src,
            dst_ref=dst,
            send_sem=send_sem,
            recv_sem=recv_sem,
            device_id=to,
            device_id_type=MESH,
        )
        made.start()
        return made

    def copy(n, src, dst, to):
        return remote(src, dst, send.at[n], recv.at[n], {"shard": to})

    def quarter(owner):
        return (
            pl.ds(pl.multiple_of((owner // 2) * (part // 2), 16), part // 2),
            pl.ds(pl.multiple_of(lax.rem(owner, 2) * SPLIT, 128), SPLIT),
        )

    def spread(l):
        made = []
        for d in range(1, owners):
            to = lax.rem(z + d, owners)
            made.append(
                remote(
                    mine.at[(l, *quarter(to))],
                    quarters.at[l, z],
                    z_send.at[l, 0, d - 1],
                    z_recv.at[l, 0, d - 1],
                    {"expert": to},
                )
            )
        quarters[l, z] = mine[(l, *quarter(z))]
        return made

    def gather(l, made):
        for one in made:
            one.wait_recv()
        total = quarters[l, 0].astype(f32)
        for owner in range(1, owners):
            total = total + quarters[l, owner].astype(f32)
        ready[(l, *quarter(z))] = total.astype(bf16)
        here = (l, *quarter(z))
        return [
            remote(
                ready.at[here],
                ready.at[here],
                z_send.at[l, 1, d - 1],
                z_recv.at[l, 1, d - 1],
                {"expert": lax.rem(z + d, owners)},
            )
            for d in range(1, owners)
        ]

    pairs = [{"shard": near}, {"shard": over_x}, {"shard": over_y}]
    pairs += [{"expert": z + 1 - 2 * lax.rem(z, 2)}, {"expert": z + 2 - 4 * (z // 2)}]
    mix_held[0] = mix_ref[...]

    def mix_start(n):
        return remote(mix_held.at[n], mix_got.at[n], mix_send.at[n], mix_recv.at[n], pairs[n])

    def mix_end(n, made):
        made.wait_recv()
        total = mix_held[n] + mix_got[n]
        if n + 1 < len(pairs):
            mix_held[n + 1] = total
        else:
            for l in range(LAYERS):
                mix_out[l] = total[l * 16 : l * 16 + labels, 0:labels]

    first = [
        copy(n, g_ref.at[rows(2 * chip + 1 - core)], got_c.at[chip], near)
        for n, chip in enumerate(chips)
    ]
    mix = [mix_start(0)]
    mine[0, :, W_ALL:] = jnp.zeros((part, 2 * SPLIT - W_ALL), bf16)
    mine[1, :, W_ALL:] = jnp.zeros((part, 2 * SPLIT - W_ALL), bf16)
    mine[1, :, 0:W_ALL] = upper_ref[...]
    upper = spread(1)

    def merge(n):
        chip = chips[n]
        loads[n].wait()
        first[n].wait_recv()
        sums[chip] = (own[n].astype(f32) + got_c[chip].astype(f32)).astype(bf16)

    def total(chip, cols, got):
        return sums[chip, :, cols].astype(f32) + got[...].astype(f32)

    merge(0)
    a0 = copy(4, sums.at[chips[0], :, cols_a], got_a.at[1 - y], over_x)
    b0 = copy(5, sums.at[chips[0], :, cols_b], got_b.at[1 - x], over_y)
    merge(1)
    a1 = copy(6, sums.at[chips[1], :, cols_a], got_a.at[y], over_x)
    merge(2)
    b1 = copy(7, sums.at[chips[2], :, cols_b], got_b.at[x], over_y)
    merge(3)
    mix_end(0, mix[0])
    mix.append(mix_start(1))
    a0.wait_recv()
    half_a[...] = total(chips[2], cols_a, got_a.at[1 - y]).astype(bf16)
    a2 = copy(8, half_a, end_a, over_y)
    b0.wait_recv()
    half_b[...] = total(chips[1], cols_b, got_b.at[1 - x]).astype(bf16)
    b2 = copy(9, half_b, end_b, over_x)
    mix_end(1, mix[1])
    mix.append(mix_start(2))
    last_upper = gather(1, upper)
    a1.wait_recv()
    keep_a = total(chips[3], cols_a, got_a.at[y])
    a2.wait_recv()
    mine[0, :, cols_a] = (keep_a + end_a[...].astype(f32)).astype(bf16)
    b1.wait_recv()
    keep_b = total(chips[3], cols_b, got_b.at[x])
    b2.wait_recv()
    mine[0, :, cols_b] = (keep_b + end_b[...].astype(f32)).astype(bf16)
    lower = spread(0)
    mix_end(2, mix[2])
    mix.append(mix_start(3))
    for made in last_upper:
        made.wait_recv()
    mix_end(3, mix[3])
    mix.append(mix_start(4))
    last_lower = gather(0, lower)
    mix_end(4, mix[4])
    for made in last_lower:
        made.wait_recv()
    for made in first + [a0, b0, a1, b1, a2, b2] + mix + upper + lower + last_upper + last_lower:
        made.wait_send()


def finish_call(part, labels, grads, upper, mix):
    vmem = pl.BlockSpec(memory_space=pltpu.VMEM)
    rest = W_ALL - SPLIT
    owners = lax.axis_size("expert")
    outs = [shape((2, part, 2 * SPLIT), bf16), shape((LAYERS, labels, labels))]
    dma = pltpu.SemaphoreType.DMA
    return pl.pallas_call(
        functools.partial(cube_kernel, part, labels),
        out_shape=outs,
        in_specs=[pl.BlockSpec(memory_space=pl.ANY), vmem, vmem],
        out_specs=[vmem] * len(outs),
        scratch_shapes=[
            pltpu.VMEM((4, part, W_ALL), bf16),
            pltpu.VMEM((4, part, W_ALL), bf16),
            pltpu.VMEM((4, part, W_ALL), bf16),
            pltpu.VMEM((2, part, SPLIT), bf16),
            pltpu.VMEM((2, part, rest), bf16),
            pltpu.VMEM((part, SPLIT), bf16),
            pltpu.VMEM((part, rest), bf16),
            pltpu.VMEM((part, SPLIT), bf16),
            pltpu.VMEM((part, rest), bf16),
            pltpu.VMEM((2, part, 2 * SPLIT), bf16),
            pltpu.VMEM((2, owners, part // 2, SPLIT), bf16),
            pltpu.VMEM((5, 32, 128), f32),
            pltpu.VMEM((5, 32, 128), f32),
            dma((10,)),
            dma((10,)),
            dma((2, 2, owners - 1)),
            dma((2, 2, owners - 1)),
            dma((5,)),
            dma((5,)),
            dma((4,)),
        ],
        compiler_params=pltpu.CompilerParams(
            vmem_limit_bytes=60 << 20, collective_id=4, has_side_effects=True
        ),
        cost_estimate=pl.CostEstimate(flops=70 * 10**9, bytes_accessed=10**7, transcendentals=0),
        name="dense_sums",
    )(grads, upper, mix)


EXCHANGE_IDS = {"forward": 0, "both": 1, "backward": 2}


def exchange_call(mode, pack, ex, args):
    rows, ff = ex.total, pack.ff
    forward, backward = mode in ("forward", "both"), mode in ("backward", "both")
    flat, wide = shape((rows, D), bf16), shape((rows, ff), bf16)
    packed = (pack.shards, pack.rows, 256)
    most = max(ex.slots, ex.span((0, 1))[1], ex.span((2,))[1])
    vmem = pl.BlockSpec(memory_space=pltpu.VMEM)
    far = pl.BlockSpec(memory_space=pl.ANY)
    in_specs = [vmem] * len(args)
    in_specs[1] = far
    scratch = []
    if mode == "forward":
        outs = [flat, wide, wide]
    elif mode == "both":
        outs = [flat, flat, shape(packed, bf16)] + gating_outputs(True)
    else:
        in_specs[3] = in_specs[4] = far
        outs = [flat, shape(packed, bf16)] + gating_outputs(False)
    out_specs = [vmem] * len(outs)
    if mode == "forward":
        out_specs[1] = out_specs[2] = far
        scratch += [pltpu.VMEM((rows, ff), bf16)] * 2
    else:
        in_specs[-12:] = [far] * 12
        out_specs[2 if mode == "both" else 1] = far
    if forward:
        scratch += [pltpu.VMEM((rows, D), bf16), pltpu.VMEM((most, D), f32)]
    if backward:
        scratch += [pltpu.VMEM((rows, D), bf16)] * 2
        scratch += [pltpu.VMEM((rows, ff), bf16)] * 3
        scratch += [pltpu.VMEM((D, rows), bf16), pltpu.VMEM((most, D), f32)]
        scratch += [pltpu.VMEM(a.shape, a.dtype) for a in args[-12:]]
    scratch.append(pltpu.VMEM(packed, bf16))
    count = len(ex.waves)
    scratch += [pltpu.SemaphoreType.DMA((count, ex.experts - 1))] * 2
    scratch += [pltpu.SemaphoreType.DMA((2, count, ex.experts - 1))] * 2
    scratch.append(pltpu.SemaphoreType.DMA((16,)))
    work = 6 * rows * D * ff * (1 if mode == "forward" else 2 if mode == "backward" else 3)
    return pl.pallas_call(
        functools.partial(exchange_kernel, mode, pack, ex),
        out_shape=outs,
        in_specs=in_specs,
        out_specs=out_specs,
        scratch_shapes=scratch,
        compiler_params=pltpu.CompilerParams(
            vmem_limit_bytes=62 << 20, collective_id=EXCHANGE_IDS[mode], has_side_effects=True
        ),
        cost_estimate=pl.CostEstimate(
            flops=10**9 if mode == "backward" else work + 40 * 10**9,
            bytes_accessed=6 * D * ff,
            transcendentals=0,
        ),
        name="experts_" + mode,
    )(*args)


def write_dense(part, labels, l, ref, outs, turn):
    proj_ref, out_ref, gain_ref, router_ref, vec_ref, const_ref = outs
    for c in range(3):
        proj_ref[l, c] = ref[:, c * D : (c + 1) * D].astype(f32)
    out_ref[l] = ref[:, W_OUT:W_SMALL].astype(f32)
    small = ref[:, W_SMALL:W_ALL].astype(f32)
    turn[0:part, :] = small
    rows = turn[...].T
    router_ref[l] = rows[0:labels, 0:part]
    for c in range(2):
        const_ref[l, c] = rows[S_CONST + 2 * c : S_CONST + 2 * c + 2, 0:part]
    gain_ref[l] = rows[S_GAIN : S_GAIN + 2, 0:part]
    vec_ref[l] = rows[S_VEC : S_VEC + 2, 0:part]


def outputs_kernel(pack, labels, traffic, low_ref, high_ref, dense_ref, hidden_ref, *refs):
    gate_ref, up_ref, down_ref = refs[:3]
    outs, hidden_out, turn = refs[3:9], refs[9], refs[10]
    turn[...] = jnp.zeros_like(turn)
    for l, ref in enumerate((low_ref, high_ref)):
        for n, out in enumerate((gate_ref, up_ref)):
            for j in range(pack.chunks):
                at = (n * pack.chunks + j) * pack.padded
                out[l, :, j * 256 : (j + 1) * 256] = ref[at : at + pack.part, :].astype(f32)
        for c in range(D // 256):
            at = pack.down + c * pack.own
            down_ref[l, :, c * 256 : (c + 1) * 256] = ref[at : at + pack.own, :].astype(f32)
        for out in (gate_ref, up_ref, down_ref):
            traffic.flush(out, l)
        write_dense(pack.part, labels, l, dense_ref.at[l], outs, turn)
        for out in outs[:2]:
            traffic.flush(out, l)
    traffic.need(hidden_ref)
    hidden_out[...] = hidden_ref[...]
    traffic.flush(hidden_out)


def dense_shapes(part, labels):
    return [
        shape((LAYERS, 3, part, D)),
        shape((LAYERS, part, D)),
        shape((LAYERS, 2, part)),
        shape((LAYERS, labels, part)),
        shape((LAYERS, 2, part)),
        shape((LAYERS, 2, 2, part)),
    ]


def outputs_call(pack, labels, grads, dense, hidden):
    wide = shape((LAYERS, pack.part, pack.ff))
    outs = [wide, wide, shape((LAYERS, pack.own, D))] + dense_shapes(pack.part, labels)
    outs.append(shape(hidden.shape, hidden.dtype))
    body = functools.partial(outputs_kernel, pack, labels)
    turn = [pltpu.VMEM((128, 128), f32)]
    return whole_call(body, "outputs", outs, turn, grads + [dense, hidden], 10**6, (3,), (0, 1, 2, 3, 4, 9))


def on_device(
    hidden_in,
    prior_logits,
    project_weight,
    output_weight,
    norm_gain,
    router_weight,
    mixing_weight,
    const_vector,
    const_weight,
    gate_weight,
    up_weight,
    down_weight,
    routes,
    priority,
    leaf_parent,
    cotangent,
):
    experts = lax.axis_size("expert")
    total_experts = experts + 4
    tokens = hidden_in.shape[0]
    capacity = 9 * tokens * TOP // (8 * total_experts)
    slots = -(-capacity // 16) * 16
    part = project_weight.shape[2]

    def pad_cols(a, width):
        return jnp.pad(a, [(0, 0)] * (a.ndim - 1) + [(0, width - a.shape[-1])])

    dense = []
    experts_w = []
    pack = Packing(lax.axis_size("shard"), part, gate_weight.shape[3])
    for l in range(LAYERS):
        small = jnp.concatenate(
            [
                pad_cols(router_weight[l], S_CONST),
                const_weight[l, 0],
                const_weight[l, 1],
                jnp.zeros((part, S_GAIN - S_CONST - 4), bf16),
                norm_gain[l].T,
                const_vector[l].T,
            ],
            axis=1,
        )
        packed = jnp.concatenate(
            [project_weight[l, c] for c in range(3)] + [output_weight[l], pad_cols(small, 128)],
            axis=1,
        )
        dense.append(lax.all_gather(packed, "shard", axis=0, tiled=True))
        mine = pack.pack(gate_weight[l, 0], up_weight[l, 0], down_weight[l, 0])
        experts_w.append(lax.all_gather(mine, "shard", axis=0, tiled=False))

    ranking = priority[0]
    earlier = (ranking[None, :] < ranking[:, None]).astype(bf16)
    labels = jnp.arange(total_experts, dtype=jnp.int32)
    hits = jnp.sum((routes[:, :, :, None] == labels).astype(f32), axis=2)
    chosen_rows = [jnp.pad(hits[l].T, [(0, 16 - total_experts), (0, 0)]) for l in range(LAYERS)]
    loaded = jnp.concatenate([hits[l, :, :experts] for l in range(LAYERS)], axis=1)
    loaded_half = loaded.astype(bf16)
    rank_row = lax.dot_general(
        loaded_half, earlier, (((0,), (1,)), ((), ())), preferred_element_type=f32
    )
    slot_row_all = jnp.where((loaded.T > 0) & (rank_row < capacity), rank_row, -1.0)
    slot_col = []
    for l in range(LAYERS):
        rank_col = dot(earlier, hits[l, :, :experts].astype(bf16))
        slot_col.append(
            jnp.where((hits[l, :, :experts] > 0) & (rank_col < capacity), rank_col, -1.0)
        )
    slot_row = [
        jnp.pad(
            slot_row_all[l * experts : (l + 1) * experts],
            [(0, 8 - experts), (0, 0)],
            constant_values=-1.0,
        )
        for l in range(LAYERS)
    ]
    visible = tree_visible(leaf_parent[0])
    bias = jnp.where(visible, 0.0, masked_fill)
    bias_t = jnp.where(visible.T, 0.0, masked_fill)
    mixes = [
        jnp.pad(mixing_weight[l], [(0, 16 - total_experts), (0, 16 - total_experts)])
        for l in range(LAYERS)
    ]
    z_rows = jnp.pad(prior_logits.T, [(0, 16 - total_experts), (0, 0)])

    ex = Exchange(experts, slots)
    saved = []
    front = [hidden_in]
    x_now = hidden_in
    for l in range(LAYERS):
        last = l == LAYERS - 1
        args = front + [dense[l], bias, z_rows, mixes[l].T, chosen_rows[l], slot_row[l]]
        if last:
            args.append(cotangent)
        outs = list(forward_call(l == 0, last, experts, slots, args))
        if l > 0:
            x_now = outs.pop(0)
        n1, qkv, att, lse, middle, n2, info, gcol, gpack, send, small = outs[:11]
        keep = dict(
            x=x_now, n1=n1, qkv=qkv, att=att, lse=lse, middle=middle, n2=n2, info=info,
            gcol=gcol, gpack=gpack, z=z_rows, small=small,
        )
        keep["received"] = dispatch_call(ex, send)
        if last:
            gating = [
                cotangent, n2, outs[11], slot_row[l], info, chosen_rows[l], gcol, small, z_rows,
                mixes[l], middle, slot_col[l],
            ]
            done = exchange_call(
                "both", pack, ex, [keep["received"], experts_w[l], outs[12]] + gating
            )
            keep["y"], keep["gin"], keep["dw"] = done[:3]
            keep["gating"] = done[3:]
        else:
            keep["y"], keep["gate"], keep["up"] = exchange_call(
                "forward", pack, ex, [keep["received"], experts_w[l]]
            )
        front = [middle, n2, keep["y"], gcol, slot_col[l], small]
        z_rows = info[0:16]
        saved.append(keep)

    gx = cotangent
    gz = None
    dense_grads = [None] * LAYERS
    mix_grads = [None] * LAYERS
    expert_grads = [None] * LAYERS
    hidden_out = None
    for l in range(LAYERS - 1, -1, -1):
        last = l == LAYERS - 1
        keep = saved[l]
        if not last:
            gating = [
                gx, keep["n2"], keep["y"], keep["gxs"], slot_row[l], keep["info"], chosen_rows[l],
                keep["gcol"], keep["small"], keep["z"], mixes[l], gz,
            ]
            done = exchange_call(
                "backward", pack, ex,
                [keep["received"], experts_w[l], keep["gy"], keep["gate"], keep["up"]] + gating,
            )
            keep["gin"], keep["dw"] = done[:2]
            keep["gating"] = done[2:]
        gn2, gsm, mix_grads[l], gz = keep["gating"][:4]
        if last:
            hidden_out = keep["gating"][4]
        d_experts, gn2 = lax.optimization_barrier((keep["dw"], gn2))
        if not last:
            gn2, expert_grads[l + 1] = lax.optimization_barrier((gn2, expert_grads[l + 1]))
        expert_grads[l] = lax.psum_scatter(d_experts, "shard", scatter_dimension=0, tiled=False)
        args = [
            gx, gn2, keep["gin"], slot_col[l], keep["middle"], keep["att"], dense[l], keep["qkv"],
            keep["n1"], keep["x"], bias_t, keep["lse"], gsm,
        ]
        if l > 0:
            args += [slot_row[l - 1], saved[l - 1]["gpack"]]
        outs = backward_call(l == 0, experts, slots, args)
        gx, d_dense = outs[:2]
        if l > 0:
            saved[l - 1]["gxs"], saved[l - 1]["gy"] = outs[2:4]
        if l > 0:
            dense_grads[l] = lax.psum_scatter(d_dense, "shard", scatter_dimension=0, tiled=True)

    if pack.shards == 8 and experts == 4:
        mix = jnp.pad(jnp.concatenate(mix_grads), [(0, 0), (0, 112)])
        dense_sums, mixing_grad = finish_call(part, total_experts, d_dense, dense_grads[1], mix)
    else:
        dense_grads[0] = lax.psum_scatter(d_dense, "shard", scatter_dimension=0, tiled=True)
        dense_sums = lax.psum(jnp.stack(dense_grads), "expert")
        mixing_grad = lax.psum(jnp.stack(mix_grads), ("expert", "shard"))
        mixing_grad = mixing_grad[:, 0:total_experts, 0:total_experts]
    made = outputs_call(pack, total_experts, expert_grads, dense_sums, hidden_out)
    gate_grad, up_grad, down_grad, project_grad, output_grad = made[:5]
    gain_grad, router_grad, vector_grad, const_grad, hidden_out = made[5:]
    return (
        hidden_out,
        gx,
        gz[0:total_experts].T,
        project_grad,
        output_grad,
        gain_grad,
        router_grad.transpose(0, 2, 1),
        mixing_grad,
        vector_grad,
        const_grad.transpose(0, 1, 3, 2),
        gate_grad[:, None],
        up_grad[:, None],
        down_grad[:, None],
    )


def solution(mesh):
    both = ("expert", "shard")
    in_specs = (
        P(both, None),
        P(both, None),
        P(None, None, "shard", None),
        P(None, "shard", None),
        P(None, None, "shard"),
        P(None, "shard", None),
        P(),
        P(None, None, "shard"),
        P(None, None, "shard", None),
        P(None, "expert", "shard", None),
        P(None, "expert", "shard", None),
        P(None, "expert", "shard", None),
        P(None, both, None),
        P(both, None),
        P(both, None),
        P(both, None),
    )
    out_specs = (
        P(both, None),
        P(both, None),
        P(both, None),
        P(None, None, "shard", None),
        P(None, "shard", None),
        P(None, None, "shard"),
        P(None, "shard", None),
        P(),
        P(None, None, "shard"),
        P(None, None, "shard", None),
        P(None, "expert", "shard", None),
        P(None, "expert", "shard", None),
        P(None, "expert", "shard", None),
    )
    return jax.shard_map(
        on_device, mesh=mesh, in_specs=in_specs, out_specs=out_specs, check_vma=False
    )
```

```python
import functools

import jax
import jax.numpy as jnp
from jax import lax
from jax.experimental import pallas as pl
from jax.experimental.pallas import tpu as pltpu
from jax.sharding import PartitionSpec as P

D = 768
H = 12
HD = 64
TOP = 2
LAYERS = 2
TRUNK = 320
BRANCH = 64
LEAF = 32
TREE = 832

W_OUT = 3 * D
W_SMALL = 4 * D
W_ALL = 4 * D + 128
S_CONST = 16
S_GAIN = 24
S_VEC = 26

epsilon = 1e-06
masked_fill = -1e30
f32 = jnp.float32
bf16 = jnp.bfloat16
BLOCKS = 2
VMEM = 56 << 20


def dot(a, b):
    return jnp.dot(a, b, preferred_element_type=f32)


def dot_nt(a, b):
    return lax.dot_general(a, b, (((1,), (1,)), ((), ())), preferred_element_type=f32)


def dot_tn(a, b):
    return lax.dot_general(a, b, (((0,), (0,)), ((), ())), preferred_element_type=f32)


def split_bf16(v):
    high = v.astype(bf16)
    return high, (v - high.astype(f32)).astype(bf16)


def inv_rms(v):
    return lax.rsqrt(jnp.mean(v * v, axis=1, keepdims=True) + epsilon)


def tree_visible(parents):
    position = jnp.arange(TREE, dtype=jnp.int32)
    offset = position - TRUNK
    segment = jnp.where(
        position < TRUNK,
        0,
        jnp.where(offset < 4 * BRANCH, 1 + offset // BRANCH, 5 + (offset - 4 * BRANCH) // LEAF),
    )
    leaf_hits = (segment[:, None] - 5 == jnp.arange(8, dtype=jnp.int32)[None, :]).astype(jnp.int32)
    upper = jnp.where(segment >= 5, 1 + jnp.sum(leaf_hits * parents[None, :], axis=1), 0)
    key_segment = segment[None, :]
    causal = position[None, :] <= position[:, None]
    return causal & (
        (key_segment == segment[:, None]) | (key_segment == 0) | (key_segment == upper[:, None])
    )


def one_hot(slot_row, e, slots):
    row = lax.broadcasted_iota(jnp.int32, (slots, slot_row.shape[1]), 0).astype(f32)
    return jnp.where(row == slot_row[e : e + 1, :], 1.0, 0.0).astype(bf16)


def one_hot_col(slot_col, e, slots, scale=None):
    lane = lax.broadcasted_iota(jnp.int32, (slot_col.shape[0], slots), 1).astype(f32)
    value = 1.0 if scale is None else scale
    return jnp.where(lane == slot_col[:, e : e + 1], value, 0.0).astype(bf16)


def combine_rows(rows, middle_ref, n2_ref, y_ref, gcol_ref, slotc_ref, vectors, experts, slots):
    gcol = gcol_ref[rows, :]
    slot = slotc_ref[rows, :]
    total = middle_ref[rows, :] + gcol[:, 16:17] * n2_ref[rows, :].astype(f32)
    for c in range(2):
        total = total + gcol[:, 17 + c : 18 + c] * vectors[c : c + 1, :]
    for e in range(experts):
        weight = one_hot_col(slot, e, slots, gcol[:, e : e + 1])
        total = total + dot(weight, y_ref[e * slots : (e + 1) * slots, :])
    return total


def all_one_hot(slot_row, experts, slots):
    return jnp.concatenate([one_hot(slot_row, e, slots) for e in range(experts)], axis=0)


def send_grads(hot, gx, gpack, gxs_ref, gy_ref, experts, slots):
    got = dot(hot, gx)
    gates = dot(hot, gpack)
    if gxs_ref is not None:
        gxs_ref[...] = got.astype(bf16)
    for e in range(experts):
        rows = slice(e * slots, (e + 1) * slots)
        gate = gates[rows, e : e + 1] + gates[rows, 64 + e : 65 + e]
        gy_ref[rows, :] = (got[rows, :] * gate).astype(bf16)


def row_blocks(tokens):
    size = tokens // BLOCKS
    return size, lambda i: pl.ds(pl.multiple_of(i * size, 16), size)


def causal_spans(tokens):
    edges = [0, 256, 512, tokens]
    return list(zip(edges[:-1], edges[1:]))


def forward_kernel(first, last, experts, slots, traffic, *refs):
    refs = list(refs)
    if first:
        x_in = refs.pop(0)
    else:
        mid_prev, n2_prev, y_ref, gcol_prev, slotc_prev, w_prev = [refs.pop(0) for _ in range(6)]
    w_ref, bias_ref, z_ref, mixt_ref, chosen_ref, slotr_ref = [refs.pop(0) for _ in range(6)]
    if last:
        cot_ref = refs.pop(0)
    if not first:
        x_out = refs.pop(0)
    n1_ref, qkv_ref, att_ref, lse_ref, mid_ref, n2_ref, info_ref, gcol_ref, gpack_ref, send_ref = [
        refs.pop(0) for _ in range(10)
    ]
    small_out = refs.pop(0)
    small_out[...] = w_ref[:, W_SMALL:]
    if last:
        gy_ref = refs.pop(0)
    lse_cols, turn = refs
    tokens = n1_ref.shape[0]
    size, block = row_blocks(tokens)
    small = w_ref[:, W_SMALL:].astype(f32).T
    gain0 = small[S_GAIN : S_GAIN + 1, :]
    gain1 = small[S_GAIN + 1 : S_GAIN + 2, :]
    if not first:
        vectors_prev = w_prev[...].astype(f32).T[S_VEC : S_VEC + 2, :]

    def project(i, carry):
        rows = block(i)
        if first:
            x = x_in[rows, :].astype(f32)
        else:
            x = combine_rows(
                rows, mid_prev, n2_prev, y_ref, gcol_prev, slotc_prev, vectors_prev, experts, slots
            )
            x_out[rows, :] = x
        n1 = (x * inv_rms(x) * gain0).astype(bf16)
        n1_ref[rows, :] = n1
        for c in range(3):
            qkv_ref[rows, c * D : (c + 1) * D] = dot(n1, w_ref[:, c * D : (c + 1) * D]).astype(bf16)
        return carry

    lax.fori_loop(0, BLOCKS, project, 0)
    if not first:
        traffic.flush(x_out)
    traffic.flush(n1_ref)
    traffic.flush(qkv_ref)
    traffic.need(bias_ref)
    lane = lax.broadcasted_iota(jnp.int32, (1, 128), 1)
    low_f = jnp.where(lane < HD, 1.0, 0.0)
    low = low_f.astype(bf16)
    high = (1.0 - low_f).astype(bf16)
    lse_cols[...] = jnp.zeros_like(lse_cols)

    def pair(p, carry):
        k = qkv_ref[:, pl.ds(pl.multiple_of(D + p * 128, 128), 128)]
        v = qkv_ref[:, pl.ds(pl.multiple_of(2 * D + p * 128, 128), 128)]
        va = v * low + high
        vb = v * high + low
        here = pl.ds(pl.multiple_of(p * 128, 128), 128)
        spans = causal_spans(tokens)
        scores = []
        for start, stop in spans:
            q = qkv_ref[start:stop, here] * bf16(HD**-0.5)
            scores.append(
                [dot_nt(q * mask, k[:stop]) + bias_ref[start:stop, :stop] for mask in (low, high)]
            )
        for (start, stop), pairs in zip(spans, scores):
            peaks = [jnp.max(one, axis=1, keepdims=True) for one in pairs]
            expos = [jnp.exp(one - peak).astype(bf16) for one, peak in zip(pairs, peaks)]
            outs = [
                (dot(expo, value[:stop]), peak)
                for expo, value, peak in zip(expos, (va, vb), peaks)
            ]
            (oa, ma), (ob, mb) = outs
            numer = jnp.where(lane < HD, oa, ob)
            denom = pltpu.roll(jnp.where(lane < HD, ob, oa), HD, 1)
            att_ref[start:stop, here] = (numer / denom).astype(bf16)
            la = ma + jnp.log(oa[:, HD : HD + 1])
            lb = mb + jnp.log(ob[:, 0:1])
            old = lse_cols[start:stop, :]
            lse_cols[start:stop, :] = jnp.where(
                lane == 2 * p, la, jnp.where(lane == 2 * p + 1, lb, old)
            )
        return carry

    lax.fori_loop(0, H // 2, pair, 0)
    traffic.flush(att_ref)
    lse_ref[...] = lse_cols[...].T[0:16, :]

    def finish(i, carry):
        rows = block(i)
        if first:
            x = x_in[rows, :].astype(f32)
        else:
            x = x_out[rows, :]
        middle = x + dot(att_ref[rows, :], w_ref[:, W_OUT:W_SMALL])
        mid_ref[rows, :] = middle
        n2_ref[rows, :] = (middle * inv_rms(middle) * gain1).astype(bf16)
        return carry

    lax.fori_loop(0, BLOCKS, finish, 0)
    traffic.flush(mid_ref)
    traffic.flush(n2_ref)
    n2 = n2_ref[...]
    scores = dot_nt(small[0:32, :].astype(bf16), n2)
    logits = scores[0:16, :]
    z = z_ref[...]
    mixt = mixt_ref[...]
    for i in range(experts + 4):
        logits = logits + mixt[:, i : i + 1] * z[i : i + 1, :]
    row = lax.broadcasted_iota(jnp.int32, (16, tokens), 0)
    valid = row < experts + 4
    peak = jnp.max(jnp.where(valid, logits, masked_fill), axis=0, keepdims=True)
    expo = jnp.where(valid, jnp.exp(jnp.minimum(logits - peak, 0.0)), 0.0)
    prob = expo / jnp.sum(expo, axis=0, keepdims=True)
    gates = prob * chosen_ref[...]
    info_ref[0:16, :] = logits
    info_ref[16:32, :] = prob
    turn[...] = jnp.zeros_like(turn)
    turn[0:16, 0:tokens] = gates
    own = gates[experts + 1 : experts + 2, :]
    alphas = []
    for c in range(2):
        l0 = scores[S_CONST + 2 * c : S_CONST + 2 * c + 1, :]
        l1 = scores[S_CONST + 2 * c + 1 : S_CONST + 2 * c + 2, :]
        a0 = jax.nn.sigmoid(l0 - l1)
        a1 = jax.nn.sigmoid(l1 - l0)
        alphas += [a0, a1]
        share = gates[experts + 2 + c : experts + 3 + c, :]
        own = own + share * a0
        turn[17 + c : 18 + c, 0:tokens] = share * a1
    turn[16:17, 0:tokens] = own
    zero_row = jnp.zeros((4, tokens), f32)
    info_ref[32:40, :] = jnp.concatenate(alphas + [zero_row], axis=0)
    gcol = turn[...].T[0:tokens, :]
    gcol_ref[...] = gcol
    upper, lower = split_bf16(jnp.where(lane < 16, gcol, 0.0))
    gpack = upper + pltpu.roll(lower.astype(f32), 64, 1).astype(bf16)
    gpack_ref[...] = gpack
    hot = all_one_hot(slotr_ref[...], experts, slots)
    send_ref[...] = dot(hot, n2).astype(bf16)
    if last:
        traffic.need(cot_ref)
        send_grads(hot, cot_ref[...], gpack, None, gy_ref, experts, slots)


def shape(dims, dtype=f32):
    return jax.ShapeDtypeStruct(tuple(dims), dtype)


class Traffic:
    def __init__(self):
        self.fetches, self.sinks, self.flushes = {}, {}, []

    def fetch(self, src, buffer, sem):
        copy = pltpu.make_async_copy(src, buffer, sem)
        copy.start()
        self.fetches[id(buffer)] = copy

    def need(self, *buffers):
        for buffer in buffers:
            copy = self.fetches.pop(id(buffer), None)
            if copy is not None:
                copy.wait()

    def sink(self, buffer, dst, sems):
        self.sinks[id(buffer)] = [dst, sems, 0]

    def flush(self, buffer, part=None):
        entry = self.sinks.get(id(buffer))
        if entry is None:
            return
        dst, sems, used = entry
        entry[2] += 1
        src, dst = (buffer, dst) if part is None else (buffer.at[part], dst.at[part])
        copy = pltpu.make_async_copy(src, dst, sems.at[used])
        copy.start()
        self.flushes.append(copy)

    def finish(self):
        for copy in self.flushes:
            copy.wait()


FLUSHES = 3


def whole_call(body, name, outs, scratch, args, flops, late=(), early=(), raw=(), collective=None):
    moved = sum(a.size * a.dtype.itemsize for a in args) + sum(
        o.size * o.dtype.itemsize for o in outs
    )
    late, early = sorted(late), sorted(early)

    def kernel(*refs):
        ins, rest = list(refs[: len(args)]), refs[len(args) :]
        results, rest = list(rest[: len(outs)]), rest[len(outs) :]
        own, rest = rest[: len(scratch)], rest[len(scratch) :]
        traffic = Traffic()
        fetch_sems, flush_sems = rest[len(late) + len(early) :]
        for n, at in enumerate(late):
            traffic.fetch(ins[at], rest[n], fetch_sems.at[n])
            ins[at] = rest[n]
        for n, at in enumerate(early):
            buffer = rest[len(late) + n]
            traffic.sink(buffer, results[at], flush_sems.at[n])
            results[at] = buffer
        body(traffic, *ins, *results, *own)
        traffic.finish()

    near, far = pl.BlockSpec(memory_space=pltpu.VMEM), pl.BlockSpec(memory_space=pl.ANY)
    buffers = [pltpu.VMEM(args[at].shape, args[at].dtype) for at in late]
    buffers += [pltpu.VMEM(outs[at].shape, outs[at].dtype) for at in early]
    buffers.append(pltpu.SemaphoreType.DMA((max(len(late), 1),)))
    buffers.append(pltpu.SemaphoreType.DMA((max(len(early), 1), FLUSHES)))
    return pl.pallas_call(
        kernel,
        out_shape=outs,
        in_specs=[far if n in late or n in raw else near for n in range(len(args))],
        out_specs=[far if n in early else near for n in range(len(outs))],
        scratch_shapes=list(scratch) + buffers,
        compiler_params=pltpu.CompilerParams(
            vmem_limit_bytes=VMEM,
            collective_id=collective,
            has_side_effects=collective is not None,
        ),
        cost_estimate=pl.CostEstimate(flops=flops, bytes_accessed=moved, transcendentals=0),
        name=name,
    )(*args)


def forward_call(first, last, experts, slots, args):
    tokens = TREE
    sent = experts * slots
    outs = [] if first else [shape((tokens, D))]
    outs += [
        shape((tokens, D), bf16),
        shape((tokens, 3 * D), bf16),
        shape((tokens, D), bf16),
        shape((16, tokens)),
        shape((tokens, D)),
        shape((tokens, D), bf16),
        shape((40, tokens)),
        shape((tokens, 128)),
        shape((tokens, 128), bf16),
        shape((sent, D), bf16),
        shape((D, 128), bf16),
    ]
    if last:
        outs += [shape((sent, D), bf16)]
    padded = -(-tokens // 128) * 128
    scratch = [pltpu.VMEM((tokens, 128), f32), pltpu.VMEM((128, padded), f32)]
    body = functools.partial(forward_kernel, first, last, experts, slots)
    inputs, results = (1, 0) if first else (6, 1)
    late = [inputs + 1] + ([inputs + 6] if last else [])
    early = ([] if first else [0]) + [results + n for n in (0, 1, 2, 4, 5)]
    return whole_call(body, "block_forward", outs, scratch, args, 20 * 10**9, late, early)


def row_dots(a, b):
    ones = jnp.ones((16, D), bf16)
    upper, lower = split_bf16(a.astype(f32) * b.astype(f32))
    return (dot_nt(ones, upper) + dot_nt(ones, lower))[0:8, :]


def gating_kernel(last, experts, slots, *refs):
    refs = list(refs)
    gx_ref, n2_ref = refs.pop(0), refs.pop(0)
    if last:
        dots_ref = refs.pop(0)
    else:
        y_ref, gxs_ref = refs.pop(0), refs.pop(0)
    slotr_ref, info_ref, chosen_ref, gcol_ref, small_ref, z_ref, mix_ref = [
        refs.pop(0) for _ in range(7)
    ]
    if not last:
        gz_ref = refs.pop(0)
    gn2_ref, gsm_ref, gmix_ref, gprev_ref = refs
    tokens = n2_ref.shape[0]
    size, block = row_blocks(tokens)
    small = small_ref[...].astype(f32).T
    small_half = small[0:32, :].astype(bf16)
    slot_row = slotr_ref[...]
    ones = jnp.ones((16, D), bf16)
    row = lax.broadcasted_iota(jnp.int32, (16, slots), 0)
    scattered = jnp.zeros((16, tokens), f32)
    for e in range(experts):
        if last:
            half = Exchange(experts, slots).half
            sums = jnp.concatenate(
                [dots_ref[0, e, 0:1, 0:half], dots_ref[1, e, 0:1, 0 : slots - half]], axis=1
            )
        else:
            rows = slice(e * slots, (e + 1) * slots)
            sums = row_dots(y_ref[rows, :], gxs_ref[rows, :])[0:1, :]
        upper, lower = split_bf16(sums)
        lhs = jnp.where(row == e, upper.astype(f32), 0.0) + jnp.where(
            row == 8 + e, lower.astype(f32), 0.0
        )
        scattered = scattered + dot(lhs.astype(bf16), one_hot(slot_row, e, slots))
    gx = gx_ref[...].astype(f32)
    gx_half = gx.astype(bf16)
    n2 = n2_ref[...]
    upper, lower = split_bf16(gx * n2.astype(f32))
    gx_n2 = (dot_nt(ones, upper) + dot_nt(ones, lower))[0:1, :]
    gx_small = dot_nt(small_half, gx_half)
    prob = info_ref[16:32, :]
    chosen = chosen_ref[...]
    gates = prob * chosen
    trow = lax.broadcasted_iota(jnp.int32, (16, tokens), 0)
    gp = jnp.concatenate([scattered[0:8, :] + scattered[8:16, :], jnp.zeros((8, tokens), f32)], 0)
    weighted = gp if last else prob * gp
    weighted = jnp.where(trow < experts, weighted, 0.0) * chosen
    gp = jnp.where(trow == experts + 1, gx_n2, 0.0)
    crow = lax.broadcasted_iota(jnp.int32, (8, tokens), 0)
    glog = jnp.zeros((8, tokens), f32)
    coefs = jnp.zeros((8, tokens), f32)
    for c in range(2):
        a0 = info_ref[32 + 2 * c : 33 + 2 * c, :]
        a1 = info_ref[33 + 2 * c : 34 + 2 * c, :]
        gx_v = gx_small[S_VEC + c : S_VEC + c + 1, :]
        share = gates[experts + 2 + c : experts + 3 + c, :]
        gp = jnp.where(trow == experts + 2 + c, a0 * gx_n2 + a1 * gx_v, gp)
        gl = share * (gx_n2 - gx_v) * a0 * a1
        glog = jnp.where(crow == 2 * c, gl, jnp.where(crow == 2 * c + 1, -gl, glog))
        coefs = jnp.where(crow == c, share * a1, coefs)
    weighted = weighted + prob * gp * chosen
    gz = weighted - prob * jnp.sum(weighted, axis=0, keepdims=True)
    if not last:
        gz = gz + gz_ref[...]
    z = z_ref[...]
    gmix_ref[...] = lax.dot_general(
        z, gz, (((1,), (1,)), ((), ())), precision=lax.Precision.HIGHEST, preferred_element_type=f32
    )
    mix = mix_ref[...]
    gprev = jnp.zeros((16, tokens), f32)
    for o in range(experts + 4):
        gprev = gprev + mix[:, o : o + 1] * gz[o : o + 1, :]
    gprev_ref[...] = gprev
    allg = jnp.concatenate([gz, glog, jnp.zeros((8, tokens), f32)], axis=0)
    upper, lower = split_bf16(allg)
    gsm = dot(upper, n2) + dot(lower, n2)
    cu, cl = split_bf16(jnp.concatenate([coefs, jnp.zeros((8, tokens), f32)], axis=0))
    gvec = dot(cu, gx_half) + dot(cl, gx_half)
    gsm_ref[0:24, :] = gsm[0:24, :]
    gsm_ref[24:32, :] = jnp.concatenate(
        [jnp.zeros((2, D), f32), gvec[0:2, :], jnp.zeros((4, D), f32)], axis=0
    )
    both = jnp.concatenate([upper, lower], axis=0)
    twice = jnp.concatenate([small_half, small_half], axis=0)
    gn2_ref[...] = dot_tn(both, twice)

    def add(i, carry):
        rows = block(i)
        gn2_ref[rows, :] = gn2_ref[rows, :] + gcol_ref[rows, 16:17] * gx_ref[rows, :].astype(f32)
        return carry

    lax.fori_loop(0, BLOCKS, add, 0)


def gating_outputs():
    tokens = TREE
    return [shape((tokens, D)), shape((32, D)), shape((16, 16)), shape((16, tokens))]


def backward_kernel(first, experts, slots, traffic, *refs):
    refs = list(refs)
    gx_ref, gn2p_ref, gn2e_ref, slotc_ref, mid_ref, att_ref, w_ref, qkv_ref, n1_ref, x_ref = [
        refs.pop(0) for _ in range(10)
    ]
    biast_ref, lse_ref, gsm_ref = [refs.pop(0) for _ in range(3)]
    if not first:
        slotr_ref, gpack_ref = refs.pop(0), refs.pop(0)
        y_held, n2_ref, gcol_ref = refs.pop(0), refs.pop(0), refs.pop(0)
    gout_ref, dw_ref = refs.pop(0), refs.pop(0)
    if not first:
        gxs_ref, gy_ref, hidden_out = refs.pop(0), refs.pop(0), refs.pop(0)
    gatt, go, gqkv, turn = refs[:4]
    if not first:
        y_home, y_sends, y_recvs, y_local = refs[4:]
        ex = Exchange(experts, slots)
        own = pltpu.make_async_copy(
            y_held.at[pl.ds(0, slots)], y_home.at[own_slots(ex)], y_local
        )
        own.start()
        greet(experts)
        returning = []
        for wave in range(len(ex.waves)):
            returning += back_copies(ex, wave, 0, y_held, y_home, y_sends, y_recvs)
        for copy in returning:
            copy.start()
    tokens = n1_ref.shape[0]
    size, block = row_blocks(tokens)
    small = w_ref[:, W_SMALL:].astype(f32).T
    gain0 = small[S_GAIN : S_GAIN + 1, :]
    gain1 = small[S_GAIN + 1 : S_GAIN + 2, :]

    def enter(i, total):
        rows = block(i)
        gn2 = gn2p_ref[rows, :]
        slot = slotc_ref[rows, :]
        for e in range(experts):
            gn2 = gn2 + dot(one_hot_col(slot, e, slots), gn2e_ref[e * slots : (e + 1) * slots, :])
        middle = mid_ref[rows, :]
        r = inv_rms(middle)
        scaled = gain1 * gn2
        inner = jnp.mean(middle * scaled, axis=1, keepdims=True)
        gmid = gx_ref[rows, :].astype(f32) + r * scaled - middle * (r * r * r * inner)
        gout_ref[rows, :] = gmid
        half = gmid.astype(bf16)
        gatt[rows, :] = half
        go[rows, :] = dot_nt(half, w_ref[:, W_OUT:W_SMALL]).astype(bf16)
        return total + jnp.sum(gn2 * middle * r, axis=0, keepdims=True)

    ggain1 = lax.fori_loop(0, BLOCKS, enter, jnp.zeros((1, D), f32))
    traffic.need(att_ref)
    lane = lax.broadcasted_iota(jnp.int32, (1, 128), 1)
    low_f = jnp.where(lane < HD, 1.0, 0.0)
    low = low_f.astype(bf16)
    high = (1.0 - low_f).astype(bf16)
    scale = HD**-0.5

    def out_grad(p, carry):
        here = pl.ds(pl.multiple_of(p * 128, 128), 128)
        dw_ref[here, W_OUT:W_SMALL] = dot_tn(att_ref[:, here], gatt[...]).astype(bf16)
        return carry

    lax.fori_loop(0, D // 128, out_grad, 0)
    traffic.flush(dw_ref, (slice(None), slice(W_OUT, W_SMALL)))
    traffic.need(qkv_ref, biast_ref, lse_ref)
    spans = causal_spans(tokens)

    def pair(p, carry):
        here = pl.ds(pl.multiple_of(p * 128, 128), 128)
        lanes_k = pl.ds(pl.multiple_of(D + p * 128, 128), 128)
        lanes_v = pl.ds(pl.multiple_of(2 * D + p * 128, 128), 128)
        q = qkv_ref[:, here] * bf16(scale)
        k = qkv_ref[:, lanes_k]
        v = qkv_ref[:, lanes_v]
        g = go[:, here]
        turn[0:tokens, :] = g.astype(f32) * att_ref[:, here].astype(f32)
        inner = turn[...].T[:, 0:tokens]
        turn[0:tokens, :] = k.astype(f32)
        kt = turn[...].T[:, 0:tokens].astype(bf16)
        gk = [0.0] * len(spans)
        gv = [0.0] * len(spans)
        masks = (low, high)
        qs = [q * mask for mask in masks]
        gs = [g * mask for mask in masks]
        dsums = [
            jnp.sum(inner[h * HD : (h + 1) * HD, :], axis=0, keepdims=True) for h in range(2)
        ]
        lses = [lse_ref[pl.ds(2 * p + h, 1), :] for h in range(2)]
        parts = [[], []]
        for n, (start, stop) in enumerate(spans):
            st = [
                dot_nt(k[start:stop], qs[h][start:]) + biast_ref[start:stop, start:]
                for h in range(2)
            ]
            gpt = [dot_nt(v[start:stop], gs[h][start:]) for h in range(2)]
            pt = [jnp.exp(st[h] - lses[h][:, start:]) for h in range(2)]
            gst = [(pt[h] * (gpt[h] - dsums[h][:, start:])).astype(bf16) for h in range(2)]
            for h in range(2):
                gv[n] = gv[n] + dot(pt[h].astype(bf16), gs[h][start:])
                gk[n] = gk[n] + dot(gst[h], qs[h][start:])
                parts[h].append(dot(kt[h * HD : (h + 1) * HD, start:stop], gst[h]))
        gq_t = []
        for h in range(2):
            cols = []
            for n, (start, stop) in enumerate(spans):
                piece = 0.0
                for m in range(n + 1):
                    origin = spans[m][0]
                    piece = piece + parts[h][m][:, start - origin : stop - origin]
                cols.append(piece)
            gq_t.append(jnp.concatenate(cols, axis=1))
        turn_t = jnp.concatenate(gq_t, axis=0) * scale
        pad = turn.shape[0] - tokens
        turn_t = jnp.concatenate([turn_t, jnp.zeros((128, pad), f32)], axis=1)
        gqkv[:, here] = turn_t.T[0:tokens, :].astype(bf16)
        for n, (start, stop) in enumerate(spans):
            gqkv[start:stop, lanes_k] = gk[n].astype(bf16)
            gqkv[start:stop, lanes_v] = gv[n].astype(bf16)
        return carry

    turn[...] = jnp.zeros_like(turn)
    lax.fori_loop(0, H // 2, pair, 0)
    traffic.need(n1_ref)

    def in_grad(p, carry):
        here = pl.ds(pl.multiple_of(p * 128, 128), 128)
        dw_ref[here, 0:W_OUT] = dot_tn(n1_ref[:, here], gqkv[...]).astype(bf16)
        return carry

    lax.fori_loop(0, D // 128, in_grad, 0)
    traffic.flush(dw_ref, (slice(None), slice(0, W_OUT)))
    traffic.need(x_ref)

    def leave(i, total):
        rows = block(i)
        gn1 = dot_nt(gqkv[rows, :], w_ref[:, 0:W_OUT])
        x = x_ref[rows, :].astype(f32)
        r = inv_rms(x)
        scaled = gain0 * gn1
        inner = jnp.mean(x * scaled, axis=1, keepdims=True)
        gx = gout_ref[rows, :] + r * scaled - x * (r * r * r * inner)
        gout_ref[rows, :] = gx
        gatt[rows, :] = gx.astype(bf16)
        return total + jnp.sum(gn1 * x * r, axis=0, keepdims=True)

    ggain0 = lax.fori_loop(0, BLOCKS, leave, jnp.zeros((1, D), f32))
    rows = jnp.concatenate(
        [gsm_ref[0:24, :], ggain0, ggain1, gsm_ref[26:32, :], jnp.zeros((96, D), f32)], axis=0
    )
    dw_ref[:, W_SMALL:] = rows.T.astype(bf16)
    traffic.flush(dw_ref, (slice(None), slice(W_SMALL, W_ALL)))
    traffic.flush(gout_ref)
    if not first:
        hot = all_one_hot(slotr_ref[...], experts, slots)
        send_grads(hot, gatt[...], gpack_ref[...], gxs_ref, gy_ref, experts, slots)
        own.wait()
        for copy in returning:
            copy.wait()
        traffic.need(n2_ref, gcol_ref)
        vectors = small[S_VEC : S_VEC + 2, :]

        def home(i, carry):
            rows = block(i)
            hidden_out[rows, :] = combine_rows(
                rows, mid_ref, n2_ref, y_home, gcol_ref, slotc_ref, vectors, experts, slots
            ).astype(bf16)
            return carry

        lax.fori_loop(0, BLOCKS, home, 0)


def backward_call(first, experts, slots, args):
    tokens = TREE
    sent = experts * slots
    outs = [shape((tokens, D)), shape((D, W_ALL), bf16)]
    if not first:
        outs += [shape((sent, D), bf16)] * 2 + [shape((tokens, D), bf16)]
    padded = -(-tokens // 128) * 128
    scratch = [
        pltpu.VMEM((tokens, D), bf16),
        pltpu.VMEM((tokens, D), bf16),
        pltpu.VMEM((tokens, 3 * D), bf16),
        pltpu.VMEM((padded, 128), f32),
    ]
    body = functools.partial(backward_kernel, first, experts, slots)
    late = (5, 7, 8, 9, 10, 11)
    if first:
        return whole_call(body, "block_backward", outs, scratch, args, 40 * 10**9, late, (0, 1))
    count = len(Exchange(experts, slots).waves)
    scratch.append(pltpu.VMEM((sent, D), bf16))
    scratch += [pltpu.SemaphoreType.DMA((1, count, experts - 1))] * 2
    scratch.append(pltpu.SemaphoreType.DMA)
    late += (16, 17)
    return whole_call(
        body, "block_backward", outs, scratch, args, 40 * 10**9, late, (0, 1), (15,), 5
    )


class Packing:
    def __init__(self, shards, part, ff):
        self.shards, self.part, self.ff = shards, part, ff
        self.padded = -(-part // 16) * 16
        self.chunks = ff // 256
        self.own = ff // shards
        self.down = 2 * self.chunks * self.padded
        self.rows = self.down + (D // 256) * self.own

    def pack(self, gate, up, down):
        pieces = []
        for wide in (gate, up):
            cut = wide.reshape(self.part, self.chunks, 256).transpose(1, 0, 2)
            cut = jnp.pad(cut, [(0, 0), (0, self.padded - self.part), (0, 0)])
            pieces.append(cut.reshape(self.chunks * self.padded, 256))
        pieces.append(
            down.reshape(self.own, D // 256, 256).transpose(1, 0, 2).reshape(-1, 256)
        )
        return jnp.concatenate(pieces, axis=0)

    def wide_part(self, ref, n, j):
        at = pl.multiple_of((n * self.chunks + j) * self.padded, 16)
        return ref[:, pl.ds(at, self.padded), :][:, : self.part, :].reshape(D, 256)

    def tall_part(self, ref, j):
        group = 256 // self.own
        here = pl.ds(j * group, group)
        pieces = []
        for c in range(D // 256):
            at = self.down + c * self.own
            pieces.append(ref[here, at : at + self.own, :].reshape(256, 256))
        return jnp.concatenate(pieces, axis=1)

    def put_wide(self, ref, n, j, grad):
        at = pl.multiple_of((n * self.chunks + j) * self.padded, 16)
        ref[:, pl.ds(at, self.part), :] = grad.reshape(self.shards, self.part, 256)

    def put_tall(self, ref, j, grad):
        group = 256 // self.own
        for c in range(D // 256):
            at = self.down + c * self.own
            ref[pl.ds(j * group, group), at : at + self.own, :] = grad[
                :, c * 256 : (c + 1) * 256
            ].reshape(group, self.own, 256)


class Exchange:
    def __init__(self, experts, slots):
        self.experts, self.slots = experts, slots
        half = -(-slots // 32) * 16
        quarter = -(-half // 32) * 16
        self.half = half
        edges = (0, quarter, half, slots)
        self.waves = tuple((low, high - low) for low, high in zip(edges[:-1], edges[1:]))
        self.ranges = [(0, slots)]
        for _, size in self.waves:
            start = self.ranges[-1][0] + self.ranges[-1][1]
            self.ranges.append((start, (experts - 1) * size))
        self.total = experts * slots

    def span(self, group):
        start = self.ranges[1 + group[0]][0]
        return start, sum(self.ranges[1 + wave][1] for wave in group)

    def held(self, wave, d):
        size = self.waves[wave][1]
        return pl.ds(self.ranges[1 + wave][0] + (d - 1) * size, size)

    def slot(self, device, wave):
        offset, size = self.waves[wave]
        return pl.ds(pl.multiple_of(device * self.slots + offset, 16), size)


MESH = pl.DeviceIdType.MESH


def greet(experts):
    me = lax.axis_index("expert")
    barrier = pltpu.get_barrier_semaphore()
    for d in range(1, experts):
        pl.semaphore_signal(
            barrier, inc=1, device_id={"expert": lax.rem(me + d, experts)}, device_id_type=MESH
        )
    pl.semaphore_wait(barrier, experts - 1)


def out_copies(ex, wave, src, dst, sends, recvs):
    me = lax.axis_index("expert")
    copies = []
    for d in range(1, ex.experts):
        to = lax.rem(me + d, ex.experts)
        copies.append(
            pltpu.make_async_remote_copy(
                src_ref=src.at[ex.slot(to, wave)],
                dst_ref=dst.at[ex.held(wave, d)],
                send_sem=sends.at[wave, d - 1],
                recv_sem=recvs.at[wave, d - 1],
                device_id={"expert": to},
                device_id_type=MESH,
            )
        )
    return copies


def back_copies(ex, wave, n, src, dst, sends, recvs):
    me = lax.axis_index("expert")
    copies = []
    for d in range(1, ex.experts):
        copies.append(
            pltpu.make_async_remote_copy(
                src_ref=src.at[ex.held(wave, d)],
                dst_ref=dst.at[ex.slot(me, wave)],
                send_sem=sends.at[n, wave, d - 1],
                recv_sem=recvs.at[n, wave, d - 1],
                device_id={"expert": lax.rem(me + ex.experts - d, ex.experts)},
                device_id_type=MESH,
            )
        )
    return copies


def own_slots(ex):
    me = lax.axis_index("expert")
    return pl.ds(pl.multiple_of(me * ex.slots, 16), ex.slots)


def dispatch_kernel(ex, send, recv, sends, recvs, local):
    own = pltpu.make_async_copy(send.at[own_slots(ex)], recv.at[pl.ds(0, ex.slots)], local)
    own.start()
    greet(ex.experts)
    copies = []
    for wave in range(len(ex.waves)):
        copies += out_copies(ex, wave, send, recv, sends, recvs)
    for copy in copies:
        copy.start()
    for copy in copies:
        copy.wait()
    own.wait()


def dispatch_call(ex, rows):
    far = pl.BlockSpec(memory_space=pl.ANY)
    return pl.pallas_call(
        functools.partial(dispatch_kernel, ex),
        out_shape=shape((ex.total, D), bf16),
        in_specs=[far],
        out_specs=far,
        scratch_shapes=[pltpu.SemaphoreType.DMA((len(ex.waves), ex.experts - 1))] * 2
        + [pltpu.SemaphoreType.DMA],
        compiler_params=pltpu.CompilerParams(
            vmem_limit_bytes=60 << 20, collective_id=3, has_side_effects=True
        ),
        cost_estimate=pl.CostEstimate(flops=35 * 10**9, bytes_accessed=10**6, transcendentals=0),
        name="dispatch",
    )(rows)


def exchange_kernel(mode, pack, ex, *refs):
    refs = list(refs)
    forward, backward = mode in ("forward", "both"), mode in ("backward", "both")
    recv_n = refs.pop(0)
    w_hbm = refs.pop(0)
    if backward:
        send_g = refs.pop(0)
        if mode == "backward":
            gate_hbm, up_hbm = refs.pop(0), refs.pop(0)
        inputs = 9 if mode == "both" else 12
        gating_far = [refs.pop(0) for _ in range(inputs)]
    if mode == "forward":
        back_y = refs.pop(0)
    if mode == "both":
        out_y = refs.pop(0)
    if mode == "forward":
        gates_far, ups_far, gates, ups = [refs.pop(0) for _ in range(4)]
    else:
        back_g, dw_far = refs.pop(0), refs.pop(0)
        gating_outs = [refs.pop(0) for _ in range(4)]
    if mode == "forward":
        out_y = refs.pop(0)
    if forward:
        acc_y = refs.pop(0)
    if backward:
        recv_g, out_g, hids, gates, ups, rows_t, acc_g = [refs.pop(0) for _ in range(7)]
        gating = [refs.pop(0) for _ in range(inputs)]
    if mode == "both":
        dots_out, dots, dots_send, dots_recv = [refs.pop(0) for _ in range(4)]
    w = refs.pop(0)
    sends, recvs, backs, gots, local = refs
    traffic = Traffic()
    if mode == "forward":
        traffic.sink(gates, gates_far, local.at[4:8])
        traffic.sink(ups, ups_far, local.at[8:12])

    loads = [pltpu.make_async_copy(w_hbm, w, local.at[0])]
    if mode == "backward":
        loads.append(pltpu.make_async_copy(gate_hbm, gates, local.at[1]))
        loads.append(pltpu.make_async_copy(up_hbm, ups, local.at[2]))
    if mode == "backward":
        for n, (far, near) in enumerate(zip(gating_far, gating)):
            traffic.fetch(far, near, local.at[4 + n])
    for copy in loads:
        copy.start()
    if mode == "both":
        for n, (far, near) in enumerate(zip(gating_far, gating)):
            traffic.fetch(far, near, local.at[4 + n])
    greet(ex.experts)

    def work(start, size):
        rows = slice(start, start + size)
        part = slice(0, size)
        if forward:
            acc_y[part, :] = jnp.zeros((size, D), f32)
        if backward:
            acc_g[part, :] = jnp.zeros((size, D), f32)

        def chunk(j, carry):
            lanes = pl.ds(pl.multiple_of(j * 256, 256), 256)
            gate_w, up_w = pack.wide_part(w, 0, j), pack.wide_part(w, 1, j)
            down_w = pack.tall_part(w, j)
            if forward:
                r = recv_n[rows, :]
                gate, up = dot(r, gate_w), dot(r, up_w)
                if mode == "forward":
                    gates[rows, lanes] = gate.astype(bf16)
                    ups[rows, lanes] = up.astype(bf16)
            else:
                gate, up = gates[rows, lanes].astype(f32), ups[rows, lanes].astype(f32)
            s = jax.nn.sigmoid(gate)
            act = gate * s
            hid = (act * up).astype(bf16)
            if forward:
                acc_y[part, :] = acc_y[part, :] + dot(hid, down_w)
            if backward:
                hids[rows, lanes] = hid
                ghid = dot_nt(recv_g[rows, :], down_w)
                guv = (ghid * act).astype(bf16)
                ggu = (ghid * up * (s * (1.0 + gate * (1.0 - s)))).astype(bf16)
                gates[rows, lanes] = ggu
                ups[rows, lanes] = guv
                acc_g[part, :] = acc_g[part, :] + dot_nt(ggu, gate_w) + dot_nt(guv, up_w)
            return carry

        lax.fori_loop(0, pack.chunks, chunk, 0)
        if mode == "forward":
            here = pl.ds(start, size)
            traffic.flush(gates, here)
            traffic.flush(ups, here)
        if forward:
            out_y[rows, :] = acc_y[part, :].astype(bf16)
        if backward:
            out_g[rows, :] = acc_g[part, :].astype(bf16)

    def send_dots(n, group):
        me = lax.axis_index("expert")
        for d in range(1, ex.experts):
            pieces = []
            for wave in group:
                here = ex.held(wave, d)
                pieces.append(row_dots(out_y[here, :], recv_g[here, :]))
            size = sum(ex.waves[wave][1] for wave in group)
            if size < 128:
                pieces.append(jnp.zeros((8, 128 - size), f32))
            dots_out[n, d - 1] = jnp.concatenate(pieces, axis=1)
            copy = pltpu.make_async_remote_copy(
                src_ref=dots_out.at[n, d - 1],
                dst_ref=dots.at[n, me],
                send_sem=dots_send.at[n, d - 1],
                recv_sem=dots_recv.at[n, d - 1],
                device_id={"expert": lax.rem(me + ex.experts - d, ex.experts)},
                device_id_type=MESH,
            )
            copy.start()
            dot_copies.append(copy)

    def send_back(group):
        for wave in group:
            if mode == "forward":
                ys.extend(back_copies(ex, wave, 0, out_y, back_y, backs, gots))
                for copy in ys[1 - ex.experts :]:
                    copy.start()
        for wave in group:
            if backward:
                gs.extend(back_copies(ex, wave, 1, out_g, back_g, backs, gots))
                for copy in gs[1 - ex.experts :]:
                    copy.start()

    ys, gs, dot_copies = [], [], []
    groups = ((0,), (1,), (2,)) if mode == "forward" else ((0, 1), (2,))
    if backward:
        arrivals = []
        for group in groups:
            arrivals.append([])
            for wave in group:
                arrivals[-1] += out_copies(ex, wave, send_g, recv_g, sends, recvs)
        for copy in arrivals[0]:
            copy.start()
        recv_g[0 : ex.slots, :] = send_g[own_slots(ex), :]
        if mode == "backward":
            traffic.need(*gating)
            gating_kernel(False, ex.experts, ex.slots, *gating, *gating_outs)
    for copy in loads:
        copy.wait()
    if backward:
        work(*ex.ranges[0])
        if mode == "both":
            own_dots = row_dots(out_y[0 : ex.slots, :], recv_g[0 : ex.slots, :])
            me = lax.axis_index("expert")
            dots[0, me, :, 0 : ex.half] = own_dots[:, 0 : ex.half]
            dots[1, me, :, 0 : ex.slots - ex.half] = own_dots[:, ex.half :]
        for copy in arrivals[0]:
            copy.wait_send()
        for copy in arrivals[1]:
            copy.start()
        for copy in arrivals[0]:
            copy.wait_recv()
    for n, group in enumerate(groups):
        if backward and n > 0:
            for copy in arrivals[n]:
                copy.wait()
        work(*ex.span(group))
        if mode == "both":
            send_dots(n, group)
        send_back(group)
    if mode == "forward":
        work(*ex.ranges[0])
        back_y[own_slots(ex), :] = out_y[0 : ex.slots, :]
    if backward:
        back_g[own_slots(ex), :] = out_g[0 : ex.slots, :]
        rows_t[...] = recv_n[...].T
        dw = w
        if pack.padded != pack.part:
            dw[...] = jnp.zeros_like(dw)

        def weights(j, carry):
            lanes = pl.ds(pl.multiple_of(j * 256, 256), 256)
            pack.put_wide(dw, 0, j, dot(rows_t[...], gates[:, lanes]).astype(bf16))
            pack.put_wide(dw, 1, j, dot(rows_t[...], ups[:, lanes]).astype(bf16))
            pack.put_tall(dw, j, dot_tn(hids[:, lanes], recv_g[...]).astype(bf16))
            return carry

        lax.fori_loop(0, pack.chunks, weights, 0)
        leaving = pltpu.make_async_copy(dw, dw_far, local.at[3])
        leaving.start()
    for copy in ys + dot_copies:
        copy.wait()
    if mode == "both":
        traffic.need(*gating)
        gating_kernel(True, ex.experts, ex.slots, *gating[:2], dots, *gating[2:], *gating_outs)
    for copy in gs:
        copy.wait()
    if backward:
        leaving.wait()
    traffic.finish()


SPLIT = 13 * 128


def cube_kernel(part, labels, g_ref, upper_ref, mix_ref, ready, mix_out, own, *refs):
    got_c, sums, got_a, got_b, half_a, half_b, end_a, end_b, mine, quarters, mix_held, mix_got = refs[:12]
    send, recv, z_send, z_recv, mix_send, mix_recv, own_sem = refs[12:]
    me = lax.axis_index("shard")
    z = lax.axis_index("expert")
    owners = quarters.shape[1]
    core, x, y = lax.rem(me, 2), lax.rem(me // 2, 2), me // 4
    near, over_x, over_y = me + 1 - 2 * core, me + 2 - 4 * x, me + 4 - 8 * y
    chips = [2 * (1 - y) + 1 - x, 2 * y + 1 - x, 2 * (1 - y) + x, 2 * y + x]

    def rows(shard):
        return pl.ds(pl.multiple_of(shard * part, 16), part)

    loads = [
        pltpu.make_async_copy(g_ref.at[rows(2 * chip + core)], own.at[n], own_sem.at[n])
        for n, chip in enumerate(chips)
    ]
    for load in loads:
        load.start()
    barrier = pltpu.get_barrier_semaphore()
    for other in (near, over_x, over_y):
        pl.semaphore_signal(barrier, inc=1, device_id={"shard": other}, device_id_type=MESH)
    for d in range(1, owners):
        pl.semaphore_signal(
            barrier, inc=1, device_id={"expert": lax.rem(z + d, owners)}, device_id_type=MESH
        )
    pl.semaphore_wait(barrier, 3 + owners - 1)
    cols_a, cols_b = slice(0, SPLIT), slice(SPLIT, W_ALL)

    def remote(src, dst, send_sem, recv_sem, to):
        made = pltpu.make_async_remote_copy(
            src_ref=src,
            dst_ref=dst,
            send_sem=send_sem,
            recv_sem=recv_sem,
            device_id=to,
            device_id_type=MESH,
        )
        made.start()
        return made

    def copy(n, src, dst, to):
        return remote(src, dst, send.at[n], recv.at[n], {"shard": to})

    def quarter(owner):
        return (
            pl.ds(pl.multiple_of((owner // 2) * (part // 2), 16), part // 2),
            pl.ds(pl.multiple_of(lax.rem(owner, 2) * SPLIT, 128), SPLIT),
        )

    def spread(l):
        made = []
        for d in range(1, owners):
            to = lax.rem(z + d, owners)
            made.append(
                remote(
                    mine.at[(l, *quarter(to))],
                    quarters.at[l, z],
                    z_send.at[l, 0, d - 1],
                    z_recv.at[l, 0, d - 1],
                    {"expert": to},
                )
            )
        quarters[l, z] = mine[(l, *quarter(z))]
        return made

    def gather(l, made):
        for one in made:
            one.wait_recv()
        total = quarters[l, 0].astype(f32)
        for owner in range(1, owners):
            total = total + quarters[l, owner].astype(f32)
        ready[(l, *quarter(z))] = total.astype(bf16)
        here = (l, *quarter(z))
        return [
            remote(
                ready.at[here],
                ready.at[here],
                z_send.at[l, 1, d - 1],
                z_recv.at[l, 1, d - 1],
                {"expert": lax.rem(z + d, owners)},
            )
            for d in range(1, owners)
        ]

    pairs = [{"shard": near}, {"shard": over_x}, {"shard": over_y}]
    pairs += [{"expert": z + 1 - 2 * lax.rem(z, 2)}, {"expert": z + 2 - 4 * (z // 2)}]
    mix_held[0] = mix_ref[...]

    def mix_start(n):
        return remote(mix_held.at[n], mix_got.at[n], mix_send.at[n], mix_recv.at[n], pairs[n])

    def mix_end(n, made):
        made.wait_recv()
        total = mix_held[n] + mix_got[n]
        if n + 1 < len(pairs):
            mix_held[n + 1] = total
        else:
            for l in range(LAYERS):
                mix_out[l] = total[l * 16 : l * 16 + labels, 0:labels]

    first = [
        copy(n, g_ref.at[rows(2 * chip + 1 - core)], got_c.at[chip], near)
        for n, chip in enumerate(chips)
    ]
    mix = [mix_start(0)]
    mine[0, :, W_ALL:] = jnp.zeros((part, 2 * SPLIT - W_ALL), bf16)
    mine[1, :, W_ALL:] = jnp.zeros((part, 2 * SPLIT - W_ALL), bf16)
    mine[1, :, 0:W_ALL] = upper_ref[...]
    upper = spread(1)

    def merge(n):
        chip = chips[n]
        loads[n].wait()
        first[n].wait_recv()
        sums[chip] = (own[n].astype(f32) + got_c[chip].astype(f32)).astype(bf16)

    def total(chip, cols, got):
        return sums[chip, :, cols].astype(f32) + got[...].astype(f32)

    merge(0)
    a0 = copy(4, sums.at[chips[0], :, cols_a], got_a.at[1 - y], over_x)
    b0 = copy(5, sums.at[chips[0], :, cols_b], got_b.at[1 - x], over_y)
    merge(1)
    a1 = copy(6, sums.at[chips[1], :, cols_a], got_a.at[y], over_x)
    merge(2)
    b1 = copy(7, sums.at[chips[2], :, cols_b], got_b.at[x], over_y)
    merge(3)
    mix_end(0, mix[0])
    mix.append(mix_start(1))
    a0.wait_recv()
    half_a[...] = total(chips[2], cols_a, got_a.at[1 - y]).astype(bf16)
    a2 = copy(8, half_a, end_a, over_y)
    b0.wait_recv()
    half_b[...] = total(chips[1], cols_b, got_b.at[1 - x]).astype(bf16)
    b2 = copy(9, half_b, end_b, over_x)
    mix_end(1, mix[1])
    mix.append(mix_start(2))
    last_upper = gather(1, upper)
    a1.wait_recv()
    keep_a = total(chips[3], cols_a, got_a.at[y])
    a2.wait_recv()
    mine[0, :, cols_a] = (keep_a + end_a[...].astype(f32)).astype(bf16)
    b1.wait_recv()
    keep_b = total(chips[3], cols_b, got_b.at[x])
    b2.wait_recv()
    mine[0, :, cols_b] = (keep_b + end_b[...].astype(f32)).astype(bf16)
    lower = spread(0)
    mix_end(2, mix[2])
    mix.append(mix_start(3))
    for made in last_upper:
        made.wait_recv()
    mix_end(3, mix[3])
    mix.append(mix_start(4))
    last_lower = gather(0, lower)
    mix_end(4, mix[4])
    for made in last_lower:
        made.wait_recv()
    for made in first + [a0, b0, a1, b1, a2, b2] + mix + upper + lower + last_upper + last_lower:
        made.wait_send()


def finish_call(part, labels, grads, upper, mix):
    vmem = pl.BlockSpec(memory_space=pltpu.VMEM)
    rest = W_ALL - SPLIT
    owners = lax.axis_size("expert")
    outs = [shape((2, part, 2 * SPLIT), bf16), shape((LAYERS, labels, labels))]
    dma = pltpu.SemaphoreType.DMA
    return pl.pallas_call(
        functools.partial(cube_kernel, part, labels),
        out_shape=outs,
        in_specs=[pl.BlockSpec(memory_space=pl.ANY), vmem, vmem],
        out_specs=[vmem] * len(outs),
        scratch_shapes=[
            pltpu.VMEM((4, part, W_ALL), bf16),
            pltpu.VMEM((4, part, W_ALL), bf16),
            pltpu.VMEM((4, part, W_ALL), bf16),
            pltpu.VMEM((2, part, SPLIT), bf16),
            pltpu.VMEM((2, part, rest), bf16),
            pltpu.VMEM((part, SPLIT), bf16),
            pltpu.VMEM((part, rest), bf16),
            pltpu.VMEM((part, SPLIT), bf16),
            pltpu.VMEM((part, rest), bf16),
            pltpu.VMEM((2, part, 2 * SPLIT), bf16),
            pltpu.VMEM((2, owners, part // 2, SPLIT), bf16),
            pltpu.VMEM((5, 32, 128), f32),
            pltpu.VMEM((5, 32, 128), f32),
            dma((10,)),
            dma((10,)),
            dma((2, 2, owners - 1)),
            dma((2, 2, owners - 1)),
            dma((5,)),
            dma((5,)),
            dma((4,)),
        ],
        compiler_params=pltpu.CompilerParams(
            vmem_limit_bytes=60 << 20, collective_id=4, has_side_effects=True
        ),
        cost_estimate=pl.CostEstimate(flops=70 * 10**9, bytes_accessed=10**7, transcendentals=0),
        name="dense_sums",
    )(grads, upper, mix)


EXCHANGE_IDS = {"forward": 0, "both": 1, "backward": 2}


def exchange_call(mode, pack, ex, args):
    rows, ff = ex.total, pack.ff
    forward, backward = mode in ("forward", "both"), mode in ("backward", "both")
    flat, wide = shape((rows, D), bf16), shape((rows, ff), bf16)
    packed = (pack.shards, pack.rows, 256)
    most = max(ex.slots, ex.span((0, 1))[1], ex.span((2,))[1])
    vmem = pl.BlockSpec(memory_space=pltpu.VMEM)
    far = pl.BlockSpec(memory_space=pl.ANY)
    in_specs = [vmem] * len(args)
    in_specs[1] = far
    scratch = []
    if mode == "forward":
        outs = [flat, wide, wide]
    elif mode == "both":
        outs = [flat, flat, shape(packed, bf16)] + gating_outputs()
    else:
        in_specs[3] = in_specs[4] = far
        outs = [flat, shape(packed, bf16)] + gating_outputs()
    out_specs = [vmem] * len(outs)
    if mode == "forward":
        out_specs[1] = out_specs[2] = far
        scratch += [pltpu.VMEM((rows, ff), bf16)] * 2
    else:
        inputs = 9 if mode == "both" else 12
        in_specs[-inputs:] = [far] * inputs
        out_specs[2 if mode == "both" else 1] = far
    if mode == "forward":
        scratch.append(pltpu.VMEM((rows, D), bf16))
    if forward:
        scratch.append(pltpu.VMEM((most, D), f32))
    if backward:
        scratch += [pltpu.VMEM((rows, D), bf16)] * 2
        scratch += [pltpu.VMEM((rows, ff), bf16)] * 3
        scratch += [pltpu.VMEM((D, rows), bf16), pltpu.VMEM((most, D), f32)]
        scratch += [pltpu.VMEM(a.shape, a.dtype) for a in args[-inputs:]]
    if mode == "both":
        scratch.append(pltpu.VMEM((2, ex.experts - 1, 8, 128), f32))
        scratch.append(pltpu.VMEM((2, ex.experts, 8, 128), f32))
        scratch += [pltpu.SemaphoreType.DMA((2, ex.experts - 1))] * 2
    scratch.append(pltpu.VMEM(packed, bf16))
    count = len(ex.waves)
    scratch += [pltpu.SemaphoreType.DMA((count, ex.experts - 1))] * 2
    scratch += [pltpu.SemaphoreType.DMA((2, count, ex.experts - 1))] * 2
    scratch.append(pltpu.SemaphoreType.DMA((16,)))
    work = 6 * rows * D * ff * (1 if mode == "forward" else 2 if mode == "backward" else 3)
    return pl.pallas_call(
        functools.partial(exchange_kernel, mode, pack, ex),
        out_shape=outs,
        in_specs=in_specs,
        out_specs=out_specs,
        scratch_shapes=scratch,
        compiler_params=pltpu.CompilerParams(
            vmem_limit_bytes=62 << 20, collective_id=EXCHANGE_IDS[mode], has_side_effects=True
        ),
        cost_estimate=pl.CostEstimate(
            flops=10**9 if mode == "backward" else work + 40 * 10**9,
            bytes_accessed=6 * D * ff,
            transcendentals=0,
        ),
        name="experts_" + mode,
    )(*args)


def write_dense(part, labels, l, ref, outs, turn):
    proj_ref, out_ref, gain_ref, router_ref, vec_ref, const_ref = outs
    for c in range(3):
        proj_ref[l, c] = ref[:, c * D : (c + 1) * D].astype(f32)
    out_ref[l] = ref[:, W_OUT:W_SMALL].astype(f32)
    small = ref[:, W_SMALL:W_ALL].astype(f32)
    turn[0:part, :] = small
    rows = turn[...].T
    router_ref[l] = rows[0:labels, 0:part]
    for c in range(2):
        const_ref[l, c] = rows[S_CONST + 2 * c : S_CONST + 2 * c + 2, 0:part]
    gain_ref[l] = rows[S_GAIN : S_GAIN + 2, 0:part]
    vec_ref[l] = rows[S_VEC : S_VEC + 2, 0:part]


def outputs_kernel(pack, labels, traffic, low_ref, high_ref, dense_ref, hidden_ref, *refs):
    gate_ref, up_ref, down_ref = refs[:3]
    outs, hidden_out, turn = refs[3:9], refs[9], refs[10]
    turn[...] = jnp.zeros_like(turn)
    for l, ref in enumerate((low_ref, high_ref)):
        for n, out in enumerate((gate_ref, up_ref)):
            for j in range(pack.chunks):
                at = (n * pack.chunks + j) * pack.padded
                out[l, :, j * 256 : (j + 1) * 256] = ref[at : at + pack.part, :].astype(f32)
        for c in range(D // 256):
            at = pack.down + c * pack.own
            down_ref[l, :, c * 256 : (c + 1) * 256] = ref[at : at + pack.own, :].astype(f32)
        for out in (gate_ref, up_ref, down_ref):
            traffic.flush(out, l)
        write_dense(pack.part, labels, l, dense_ref.at[l], outs, turn)
        for out in outs[:2]:
            traffic.flush(out, l)
    traffic.need(hidden_ref)
    hidden_out[...] = hidden_ref[...]
    traffic.flush(hidden_out)


def dense_shapes(part, labels):
    return [
        shape((LAYERS, 3, part, D)),
        shape((LAYERS, part, D)),
        shape((LAYERS, 2, part)),
        shape((LAYERS, labels, part)),
        shape((LAYERS, 2, part)),
        shape((LAYERS, 2, 2, part)),
    ]


def outputs_call(pack, labels, grads, dense, hidden):
    wide = shape((LAYERS, pack.part, pack.ff))
    outs = [wide, wide, shape((LAYERS, pack.own, D))] + dense_shapes(pack.part, labels)
    outs.append(shape(hidden.shape, hidden.dtype))
    body = functools.partial(outputs_kernel, pack, labels)
    turn = [pltpu.VMEM((128, 128), f32)]
    return whole_call(body, "outputs", outs, turn, grads + [dense, hidden], 10**6, (3,), (0, 1, 2, 3, 4, 9))


def on_device(
    hidden_in,
    prior_logits,
    project_weight,
    output_weight,
    norm_gain,
    router_weight,
    mixing_weight,
    const_vector,
    const_weight,
    gate_weight,
    up_weight,
    down_weight,
    routes,
    priority,
    leaf_parent,
    cotangent,
):
    experts = lax.axis_size("expert")
    total_experts = experts + 4
    tokens = hidden_in.shape[0]
    capacity = 9 * tokens * TOP // (8 * total_experts)
    slots = -(-capacity // 16) * 16
    part = project_weight.shape[2]

    def pad_cols(a, width):
        return jnp.pad(a, [(0, 0)] * (a.ndim - 1) + [(0, width - a.shape[-1])])

    dense = []
    experts_w = []
    pack = Packing(lax.axis_size("shard"), part, gate_weight.shape[3])
    for l in range(LAYERS):
        small = jnp.concatenate(
            [
                pad_cols(router_weight[l], S_CONST),
                const_weight[l, 0],
                const_weight[l, 1],
                jnp.zeros((part, S_GAIN - S_CONST - 4), bf16),
                norm_gain[l].T,
                const_vector[l].T,
            ],
            axis=1,
        )
        packed = jnp.concatenate(
            [project_weight[l, c] for c in range(3)] + [output_weight[l], pad_cols(small, 128)],
            axis=1,
        )
        dense.append(lax.all_gather(packed, "shard", axis=0, tiled=True))
        mine = pack.pack(gate_weight[l, 0], up_weight[l, 0], down_weight[l, 0])
        experts_w.append(lax.all_gather(mine, "shard", axis=0, tiled=False))

    ranking = priority[0]
    earlier = (ranking[None, :] < ranking[:, None]).astype(bf16)
    labels = jnp.arange(total_experts, dtype=jnp.int32)
    hits = jnp.sum((routes[:, :, :, None] == labels).astype(f32), axis=2)
    chosen_rows = [jnp.pad(hits[l].T, [(0, 16 - total_experts), (0, 0)]) for l in range(LAYERS)]
    loaded = jnp.concatenate([hits[l, :, :experts] for l in range(LAYERS)], axis=1)
    loaded_half = loaded.astype(bf16)
    rank_row = lax.dot_general(
        loaded_half, earlier, (((0,), (1,)), ((), ())), preferred_element_type=f32
    )
    slot_row_all = jnp.where((loaded.T > 0) & (rank_row < capacity), rank_row, -1.0)
    slot_col = []
    for l in range(LAYERS):
        rank_col = dot(earlier, hits[l, :, :experts].astype(bf16))
        slot_col.append(
            jnp.where((hits[l, :, :experts] > 0) & (rank_col < capacity), rank_col, -1.0)
        )
    slot_row = [
        jnp.pad(
            slot_row_all[l * experts : (l + 1) * experts],
            [(0, 8 - experts), (0, 0)],
            constant_values=-1.0,
        )
        for l in range(LAYERS)
    ]
    visible = tree_visible(leaf_parent[0])
    bias = jnp.where(visible, 0.0, masked_fill)
    bias_t = jnp.where(visible.T, 0.0, masked_fill)
    mixes = [
        jnp.pad(mixing_weight[l], [(0, 16 - total_experts), (0, 16 - total_experts)])
        for l in range(LAYERS)
    ]
    z_rows = jnp.pad(prior_logits.T, [(0, 16 - total_experts), (0, 0)])

    ex = Exchange(experts, slots)
    saved = []
    front = [hidden_in]
    x_now = hidden_in
    for l in range(LAYERS):
        last = l == LAYERS - 1
        args = front + [dense[l], bias, z_rows, mixes[l].T, chosen_rows[l], slot_row[l]]
        if last:
            args.append(cotangent)
        outs = list(forward_call(l == 0, last, experts, slots, args))
        if l > 0:
            x_now = outs.pop(0)
        n1, qkv, att, lse, middle, n2, info, gcol, gpack, send, small = outs[:11]
        keep = dict(
            x=x_now, n1=n1, qkv=qkv, att=att, lse=lse, middle=middle, n2=n2, info=info,
            gcol=gcol, gpack=gpack, z=z_rows, small=small,
        )
        keep["received"] = dispatch_call(ex, send)
        if last:
            gating = [
                cotangent, n2, slot_row[l], info, chosen_rows[l], gcol, small, z_rows, mixes[l],
            ]
            done = exchange_call(
                "both", pack, ex, [keep["received"], experts_w[l], outs[11]] + gating
            )
            y_held, keep["gin"], keep["dw"] = done[:3]
            keep["gating"] = done[3:]
        else:
            keep["y"], keep["gate"], keep["up"] = exchange_call(
                "forward", pack, ex, [keep["received"], experts_w[l]]
            )
            front = [middle, n2, keep["y"], gcol, slot_col[l], small]
        z_rows = info[0:16]
        saved.append(keep)

    gx = cotangent
    gz = None
    dense_grads = [None] * LAYERS
    mix_grads = [None] * LAYERS
    expert_grads = [None] * LAYERS
    hidden_out = None
    for l in range(LAYERS - 1, -1, -1):
        last = l == LAYERS - 1
        keep = saved[l]
        if not last:
            gating = [
                gx, keep["n2"], keep["y"], keep["gxs"], slot_row[l], keep["info"], chosen_rows[l],
                keep["gcol"], keep["small"], keep["z"], mixes[l], gz,
            ]
            done = exchange_call(
                "backward", pack, ex,
                [keep["received"], experts_w[l], keep["gy"], keep["gate"], keep["up"]] + gating,
            )
            keep["gin"], keep["dw"] = done[:2]
            keep["gating"] = done[2:]
        gn2, gsm, mix_grads[l], gz = keep["gating"][:4]
        d_experts, gn2 = lax.optimization_barrier((keep["dw"], gn2))
        if not last:
            gn2, expert_grads[l + 1] = lax.optimization_barrier((gn2, expert_grads[l + 1]))
        expert_grads[l] = lax.psum_scatter(d_experts, "shard", scatter_dimension=0, tiled=False)
        args = [
            gx, gn2, keep["gin"], slot_col[l], keep["middle"], keep["att"], dense[l], keep["qkv"],
            keep["n1"], keep["x"], bias_t, keep["lse"], gsm,
        ]
        if l > 0:
            args += [slot_row[l - 1], saved[l - 1]["gpack"], y_held, keep["n2"], keep["gcol"]]
        outs = backward_call(l == 0, experts, slots, args)
        gx, d_dense = outs[:2]
        if l > 0:
            saved[l - 1]["gxs"], saved[l - 1]["gy"], hidden_out = outs[2:5]
        if l > 0:
            dense_grads[l] = lax.psum_scatter(d_dense, "shard", scatter_dimension=0, tiled=True)

    if pack.shards == 8 and experts == 4:
        mix = jnp.pad(jnp.concatenate(mix_grads), [(0, 0), (0, 112)])
        dense_sums, mixing_grad = finish_call(part, total_experts, d_dense, dense_grads[1], mix)
    else:
        dense_grads[0] = lax.psum_scatter(d_dense, "shard", scatter_dimension=0, tiled=True)
        dense_sums = lax.psum(jnp.stack(dense_grads), "expert")
        mixing_grad = lax.psum(jnp.stack(mix_grads), ("expert", "shard"))
        mixing_grad = mixing_grad[:, 0:total_experts, 0:total_experts]
    made = outputs_call(pack, total_experts, expert_grads, dense_sums, hidden_out)
    gate_grad, up_grad, down_grad, project_grad, output_grad = made[:5]
    gain_grad, router_grad, vector_grad, const_grad, hidden_out = made[5:]
    return (
        hidden_out,
        gx,
        gz[0:total_experts].T,
        project_grad,
        output_grad,
        gain_grad,
        router_grad.transpose(0, 2, 1),
        mixing_grad,
        vector_grad,
        const_grad.transpose(0, 1, 3, 2),
        gate_grad[:, None],
        up_grad[:, None],
        down_grad[:, None],
    )


def solution(mesh):
    both = ("expert", "shard")
    in_specs = (
        P(both, None),
        P(both, None),
        P(None, None, "shard", None),
        P(None, "shard", None),
        P(None, None, "shard"),
        P(None, "shard", None),
        P(),
        P(None, None, "shard"),
        P(None, None, "shard", None),
        P(None, "expert", "shard", None),
        P(None, "expert", "shard", None),
        P(None, "expert", "shard", None),
        P(None, both, None),
        P(both, None),
        P(both, None),
        P(both, None),
    )
    out_specs = (
        P(both, None),
        P(both, None),
        P(both, None),
        P(None, None, "shard", None),
        P(None, "shard", None),
        P(None, None, "shard"),
        P(None, "shard", None),
        P(),
        P(None, None, "shard"),
        P(None, None, "shard", None),
        P(None, "expert", "shard", None),
        P(None, "expert", "shard", None),
        P(None, "expert", "shard", None),
    )
    return jax.shard_map(
        on_device, mesh=mesh, in_specs=in_specs, out_specs=out_specs, check_vma=False
    )
```

```python
import functools

import jax
import jax.numpy as jnp
from jax import lax
from jax.experimental import pallas as pl
from jax.experimental.pallas import tpu as pltpu
from jax.sharding import PartitionSpec as P

D = 768
H = 12
HD = 64
TOP = 2
LAYERS = 2
TRUNK = 320
BRANCH = 64
LEAF = 32
TREE = 832

W_OUT = 3 * D
W_SMALL = 4 * D
W_ALL = 4 * D + 128
S_CONST = 16
S_GAIN = 24
S_VEC = 26

epsilon = 1e-06
masked_fill = -1e30
f32 = jnp.float32
bf16 = jnp.bfloat16
BLOCKS = 2
VMEM = 56 << 20


def dot(a, b):
    return jnp.dot(a, b, preferred_element_type=f32)


def dot_nt(a, b):
    return lax.dot_general(a, b, (((1,), (1,)), ((), ())), preferred_element_type=f32)


def dot_tn(a, b):
    return lax.dot_general(a, b, (((0,), (0,)), ((), ())), preferred_element_type=f32)


def split_bf16(v):
    high = v.astype(bf16)
    return high, (v - high.astype(f32)).astype(bf16)


def inv_rms(v):
    return lax.rsqrt(jnp.mean(v * v, axis=1, keepdims=True) + epsilon)


def tree_visible(parents):
    position = jnp.arange(TREE, dtype=jnp.int32)
    offset = position - TRUNK
    segment = jnp.where(
        position < TRUNK,
        0,
        jnp.where(offset < 4 * BRANCH, 1 + offset // BRANCH, 5 + (offset - 4 * BRANCH) // LEAF),
    )
    leaf_hits = (segment[:, None] - 5 == jnp.arange(8, dtype=jnp.int32)[None, :]).astype(jnp.int32)
    upper = jnp.where(segment >= 5, 1 + jnp.sum(leaf_hits * parents[None, :], axis=1), 0)
    key_segment = segment[None, :]
    causal = position[None, :] <= position[:, None]
    return causal & (
        (key_segment == segment[:, None]) | (key_segment == 0) | (key_segment == upper[:, None])
    )


def one_hot(slot_row, e, slots):
    row = lax.broadcasted_iota(jnp.int32, (slots, slot_row.shape[1]), 0).astype(f32)
    return jnp.where(row == slot_row[e : e + 1, :], 1.0, 0.0).astype(bf16)


def one_hot_col(slot_col, e, slots, scale=None):
    lane = lax.broadcasted_iota(jnp.int32, (slot_col.shape[0], slots), 1).astype(f32)
    value = 1.0 if scale is None else scale
    return jnp.where(lane == slot_col[:, e : e + 1], value, 0.0).astype(bf16)


def combine_rows(rows, middle_ref, n2_ref, y_ref, gcol_ref, slotc_ref, vectors, experts, slots):
    gcol = gcol_ref[rows, :]
    slot = slotc_ref[rows, :]
    total = middle_ref[rows, :] + gcol[:, 16:17] * n2_ref[rows, :].astype(f32)
    for c in range(2):
        total = total + gcol[:, 17 + c : 18 + c] * vectors[c : c + 1, :]
    for e in range(experts):
        weight = one_hot_col(slot, e, slots, gcol[:, e : e + 1])
        total = total + dot(weight, y_ref[e * slots : (e + 1) * slots, :])
    return total


def all_one_hot(slot_row, experts, slots):
    return jnp.concatenate([one_hot(slot_row, e, slots) for e in range(experts)], axis=0)


def send_grads(hot, gx, gpack, gxs_ref, gy_ref, experts, slots):
    got = dot(hot, gx)
    gates = dot(hot, gpack)
    if gxs_ref is not None:
        gxs_ref[...] = got.astype(bf16)
    for e in range(experts):
        rows = slice(e * slots, (e + 1) * slots)
        gate = gates[rows, e : e + 1] + gates[rows, 64 + e : 65 + e]
        gy_ref[rows, :] = (got[rows, :] * gate).astype(bf16)


def row_blocks(tokens):
    size = tokens // BLOCKS
    return size, lambda i: pl.ds(pl.multiple_of(i * size, 16), size)


def causal_spans(tokens):
    edges = [0, 256, 512, tokens]
    return list(zip(edges[:-1], edges[1:]))


def forward_kernel(first, last, experts, slots, traffic, *refs):
    refs = list(refs)
    if first:
        x_in = refs.pop(0)
    else:
        mid_prev, n2_prev, y_ref, gcol_prev, slotc_prev, w_prev = [refs.pop(0) for _ in range(6)]
    w_ref, bias_ref, z_ref, mixt_ref, chosen_ref, slotr_ref = [refs.pop(0) for _ in range(6)]
    if last:
        cot_ref = refs.pop(0)
    if not first:
        x_out = refs.pop(0)
    n1_ref, qkv_ref, att_ref, lse_ref, mid_ref, n2_ref, info_ref, gcol_ref, gpack_ref, send_ref = [
        refs.pop(0) for _ in range(10)
    ]
    small_out, z_out = refs.pop(0), refs.pop(0)
    small_out[...] = w_ref[:, W_SMALL:]
    if last:
        gy_ref = refs.pop(0)
    lse_cols, turn = refs
    tokens = n1_ref.shape[0]
    size, block = row_blocks(tokens)
    small = w_ref[:, W_SMALL:].astype(f32).T
    gain0 = small[S_GAIN : S_GAIN + 1, :]
    gain1 = small[S_GAIN + 1 : S_GAIN + 2, :]
    if not first:
        vectors_prev = w_prev[...].astype(f32).T[S_VEC : S_VEC + 2, :]

    def project(i, carry):
        rows = block(i)
        if first:
            x = x_in[rows, :].astype(f32)
        else:
            x = combine_rows(
                rows, mid_prev, n2_prev, y_ref, gcol_prev, slotc_prev, vectors_prev, experts, slots
            )
            x_out[rows, :] = x
        n1 = (x * inv_rms(x) * gain0).astype(bf16)
        n1_ref[rows, :] = n1
        for c in range(3):
            qkv_ref[rows, c * D : (c + 1) * D] = dot(n1, w_ref[:, c * D : (c + 1) * D]).astype(bf16)
        return carry

    lax.fori_loop(0, BLOCKS, project, 0)
    if not first:
        traffic.flush(x_out)
    traffic.flush(n1_ref)
    traffic.flush(qkv_ref)
    traffic.need(bias_ref)
    lane = lax.broadcasted_iota(jnp.int32, (1, 128), 1)
    low_f = jnp.where(lane < HD, 1.0, 0.0)
    low = low_f.astype(bf16)
    high = (1.0 - low_f).astype(bf16)
    lse_cols[...] = jnp.zeros_like(lse_cols)

    def pair(p, carry):
        k = qkv_ref[:, pl.ds(pl.multiple_of(D + p * 128, 128), 128)]
        v = qkv_ref[:, pl.ds(pl.multiple_of(2 * D + p * 128, 128), 128)]
        va = v * low + high
        vb = v * high + low
        here = pl.ds(pl.multiple_of(p * 128, 128), 128)
        spans = causal_spans(tokens)
        scores = []
        for start, stop in spans:
            q = qkv_ref[start:stop, here] * bf16(HD**-0.5)
            scores.append(
                [dot_nt(q * mask, k[:stop]) + bias_ref[start:stop, :stop] for mask in (low, high)]
            )
        for (start, stop), pairs in zip(spans, scores):
            peaks = [jnp.max(one, axis=1, keepdims=True) for one in pairs]
            expos = [jnp.exp(one - peak).astype(bf16) for one, peak in zip(pairs, peaks)]
            outs = [
                (dot(expo, value[:stop]), peak)
                for expo, value, peak in zip(expos, (va, vb), peaks)
            ]
            (oa, ma), (ob, mb) = outs
            numer = jnp.where(lane < HD, oa, ob)
            denom = pltpu.roll(jnp.where(lane < HD, ob, oa), HD, 1)
            att_ref[start:stop, here] = (numer / denom).astype(bf16)
            la = ma + jnp.log(oa[:, HD : HD + 1])
            lb = mb + jnp.log(ob[:, 0:1])
            old = lse_cols[start:stop, :]
            lse_cols[start:stop, :] = jnp.where(
                lane == 2 * p, la, jnp.where(lane == 2 * p + 1, lb, old)
            )
        return carry

    lax.fori_loop(0, H // 2, pair, 0)
    traffic.flush(att_ref)
    lse_ref[...] = lse_cols[...].T[0:16, :]

    def finish(i, carry):
        rows = block(i)
        if first:
            x = x_in[rows, :].astype(f32)
        else:
            x = x_out[rows, :]
        middle = x + dot(att_ref[rows, :], w_ref[:, W_OUT:W_SMALL])
        mid_ref[rows, :] = middle
        n2_ref[rows, :] = (middle * inv_rms(middle) * gain1).astype(bf16)
        return carry

    lax.fori_loop(0, BLOCKS, finish, 0)
    traffic.flush(mid_ref)
    traffic.flush(n2_ref)
    n2 = n2_ref[...]
    scores = dot_nt(small[0:32, :].astype(bf16), n2)
    logits = scores[0:16, :]
    z = z_ref[...]
    mixt = mixt_ref[...]
    for i in range(experts + 4):
        logits = logits + mixt[:, i : i + 1] * z[i : i + 1, :]
    row = lax.broadcasted_iota(jnp.int32, (16, tokens), 0)
    valid = row < experts + 4
    peak = jnp.max(jnp.where(valid, logits, masked_fill), axis=0, keepdims=True)
    expo = jnp.where(valid, jnp.exp(jnp.minimum(logits - peak, 0.0)), 0.0)
    prob = expo / jnp.sum(expo, axis=0, keepdims=True)
    gates = prob * chosen_ref[...]
    info_ref[0:16, :] = logits
    z_out[...] = logits
    info_ref[16:32, :] = prob
    turn[...] = jnp.zeros_like(turn)
    turn[0:16, 0:tokens] = gates
    own = gates[experts + 1 : experts + 2, :]
    alphas = []
    for c in range(2):
        l0 = scores[S_CONST + 2 * c : S_CONST + 2 * c + 1, :]
        l1 = scores[S_CONST + 2 * c + 1 : S_CONST + 2 * c + 2, :]
        a0 = jax.nn.sigmoid(l0 - l1)
        a1 = jax.nn.sigmoid(l1 - l0)
        alphas += [a0, a1]
        share = gates[experts + 2 + c : experts + 3 + c, :]
        own = own + share * a0
        turn[17 + c : 18 + c, 0:tokens] = share * a1
    turn[16:17, 0:tokens] = own
    zero_row = jnp.zeros((4, tokens), f32)
    info_ref[32:40, :] = jnp.concatenate(alphas + [zero_row], axis=0)
    gcol = turn[...].T[0:tokens, :]
    gcol_ref[...] = gcol
    upper, lower = split_bf16(jnp.where(lane < 16, gcol, 0.0))
    gpack = upper + pltpu.roll(lower.astype(f32), 64, 1).astype(bf16)
    gpack_ref[...] = gpack
    hot = all_one_hot(slotr_ref[...], experts, slots)
    send_ref[...] = dot(hot, n2).astype(bf16)
    if last:
        traffic.need(cot_ref)
        send_grads(hot, cot_ref[...], gpack, None, gy_ref, experts, slots)


def shape(dims, dtype=f32):
    return jax.ShapeDtypeStruct(tuple(dims), dtype)


class Traffic:
    def __init__(self):
        self.fetches, self.sinks, self.flushes = {}, {}, []

    def fetch(self, src, buffer, sem):
        copy = pltpu.make_async_copy(src, buffer, sem)
        copy.start()
        self.fetches[id(buffer)] = copy

    def need(self, *buffers):
        for buffer in buffers:
            copy = self.fetches.pop(id(buffer), None)
            if copy is not None:
                copy.wait()

    def sink(self, buffer, dst, sems):
        self.sinks[id(buffer)] = [dst, sems, 0]

    def flush(self, buffer, part=None):
        entry = self.sinks.get(id(buffer))
        if entry is None:
            return
        dst, sems, used = entry
        entry[2] += 1
        src, dst = (buffer, dst) if part is None else (buffer.at[part], dst.at[part])
        copy = pltpu.make_async_copy(src, dst, sems.at[used])
        copy.start()
        self.flushes.append(copy)

    def finish(self):
        for copy in self.flushes:
            copy.wait()


FLUSHES = 3


def whole_call(body, name, outs, scratch, args, flops, late=(), early=(), raw=(), collective=None):
    moved = sum(a.size * a.dtype.itemsize for a in args) + sum(
        o.size * o.dtype.itemsize for o in outs
    )
    late, early = sorted(late), sorted(early)

    def kernel(*refs):
        ins, rest = list(refs[: len(args)]), refs[len(args) :]
        results, rest = list(rest[: len(outs)]), rest[len(outs) :]
        own, rest = rest[: len(scratch)], rest[len(scratch) :]
        traffic = Traffic()
        fetch_sems, flush_sems = rest[len(late) + len(early) :]
        for n, at in enumerate(late):
            traffic.fetch(ins[at], rest[n], fetch_sems.at[n])
            ins[at] = rest[n]
        for n, at in enumerate(early):
            buffer = rest[len(late) + n]
            traffic.sink(buffer, results[at], flush_sems.at[n])
            results[at] = buffer
        body(traffic, *ins, *results, *own)
        traffic.finish()

    near, far = pl.BlockSpec(memory_space=pltpu.VMEM), pl.BlockSpec(memory_space=pl.ANY)
    buffers = [pltpu.VMEM(args[at].shape, args[at].dtype) for at in late]
    buffers += [pltpu.VMEM(outs[at].shape, outs[at].dtype) for at in early]
    buffers.append(pltpu.SemaphoreType.DMA((max(len(late), 1),)))
    buffers.append(pltpu.SemaphoreType.DMA((max(len(early), 1), FLUSHES)))
    return pl.pallas_call(
        kernel,
        out_shape=outs,
        in_specs=[far if n in late or n in raw else near for n in range(len(args))],
        out_specs=[far if n in early else near for n in range(len(outs))],
        scratch_shapes=list(scratch) + buffers,
        compiler_params=pltpu.CompilerParams(
            vmem_limit_bytes=VMEM,
            collective_id=collective,
            has_side_effects=collective is not None,
        ),
        cost_estimate=pl.CostEstimate(flops=flops, bytes_accessed=moved, transcendentals=0),
        name=name,
    )(*args)


def forward_call(first, last, experts, slots, args):
    tokens = TREE
    sent = experts * slots
    outs = [] if first else [shape((tokens, D))]
    outs += [
        shape((tokens, D), bf16),
        shape((tokens, 3 * D), bf16),
        shape((tokens, D), bf16),
        shape((16, tokens)),
        shape((tokens, D)),
        shape((tokens, D), bf16),
        shape((40, tokens)),
        shape((tokens, 128)),
        shape((tokens, 128), bf16),
        shape((sent, D), bf16),
        shape((D, 128), bf16),
        shape((16, tokens)),
    ]
    if last:
        outs += [shape((sent, D), bf16)]
    padded = -(-tokens // 128) * 128
    scratch = [pltpu.VMEM((tokens, 128), f32), pltpu.VMEM((128, padded), f32)]
    body = functools.partial(forward_kernel, first, last, experts, slots)
    inputs, results = (1, 0) if first else (6, 1)
    late = [inputs + 1] + ([inputs + 6] if last else [])
    early = ([] if first else [0]) + [results + n for n in (0, 1, 2, 4, 5)]
    return whole_call(body, "block_forward", outs, scratch, args, 20 * 10**9, late, early)


def row_dots(a, b):
    ones = jnp.ones((16, D), bf16)
    upper, lower = split_bf16(a.astype(f32) * b.astype(f32))
    return (dot_nt(ones, upper) + dot_nt(ones, lower))[0:8, :]


def gating_kernel(last, experts, slots, *refs):
    refs = list(refs)
    gx_ref, n2_ref = refs.pop(0), refs.pop(0)
    if last:
        dots_ref = refs.pop(0)
    else:
        y_ref, gxs_ref = refs.pop(0), refs.pop(0)
    slotr_ref, info_ref, chosen_ref, gcol_ref, small_ref, z_ref, mix_ref = [
        refs.pop(0) for _ in range(7)
    ]
    if not last:
        gz_ref = refs.pop(0)
    gn2_ref, gsm_ref, gmix_ref, gprev_ref = refs
    tokens = n2_ref.shape[0]
    size, block = row_blocks(tokens)
    small = small_ref[...].astype(f32).T
    small_half = small[0:32, :].astype(bf16)
    slot_row = slotr_ref[...]
    ones = jnp.ones((16, D), bf16)
    row = lax.broadcasted_iota(jnp.int32, (16, slots), 0)
    scattered = jnp.zeros((16, tokens), f32)
    for e in range(experts):
        if last:
            half = Exchange(experts, slots).half
            sums = jnp.concatenate(
                [dots_ref[0, e, 0:1, 0:half], dots_ref[1, e, 0:1, 0 : slots - half]], axis=1
            )
        else:
            rows = slice(e * slots, (e + 1) * slots)
            sums = row_dots(y_ref[rows, :], gxs_ref[rows, :])[0:1, :]
        upper, lower = split_bf16(sums)
        lhs = jnp.where(row == e, upper.astype(f32), 0.0) + jnp.where(
            row == 8 + e, lower.astype(f32), 0.0
        )
        scattered = scattered + dot(lhs.astype(bf16), one_hot(slot_row, e, slots))
    gx = gx_ref[...].astype(f32)
    gx_half = gx.astype(bf16)
    n2 = n2_ref[...]
    upper, lower = split_bf16(gx * n2.astype(f32))
    gx_n2 = (dot_nt(ones, upper) + dot_nt(ones, lower))[0:1, :]
    gx_small = dot_nt(small_half, gx_half)
    prob = info_ref[16:32, :]
    chosen = chosen_ref[...]
    gates = prob * chosen
    trow = lax.broadcasted_iota(jnp.int32, (16, tokens), 0)
    gp = jnp.concatenate([scattered[0:8, :] + scattered[8:16, :], jnp.zeros((8, tokens), f32)], 0)
    weighted = gp if last else prob * gp
    weighted = jnp.where(trow < experts, weighted, 0.0) * chosen
    gp = jnp.where(trow == experts + 1, gx_n2, 0.0)
    crow = lax.broadcasted_iota(jnp.int32, (8, tokens), 0)
    glog = jnp.zeros((8, tokens), f32)
    coefs = jnp.zeros((8, tokens), f32)
    for c in range(2):
        a0 = info_ref[32 + 2 * c : 33 + 2 * c, :]
        a1 = info_ref[33 + 2 * c : 34 + 2 * c, :]
        gx_v = gx_small[S_VEC + c : S_VEC + c + 1, :]
        share = gates[experts + 2 + c : experts + 3 + c, :]
        gp = jnp.where(trow == experts + 2 + c, a0 * gx_n2 + a1 * gx_v, gp)
        gl = share * (gx_n2 - gx_v) * a0 * a1
        glog = jnp.where(crow == 2 * c, gl, jnp.where(crow == 2 * c + 1, -gl, glog))
        coefs = jnp.where(crow == c, share * a1, coefs)
    weighted = weighted + prob * gp * chosen
    gz = weighted - prob * jnp.sum(weighted, axis=0, keepdims=True)
    if not last:
        gz = gz + gz_ref[...]
    z = z_ref[...]
    gmix_ref[...] = lax.dot_general(
        z, gz, (((1,), (1,)), ((), ())), precision=lax.Precision.HIGHEST, preferred_element_type=f32
    )
    mix = mix_ref[...]
    gprev = jnp.zeros((16, tokens), f32)
    for o in range(experts + 4):
        gprev = gprev + mix[:, o : o + 1] * gz[o : o + 1, :]
    gprev_ref[...] = gprev
    allg = jnp.concatenate([gz, glog, jnp.zeros((8, tokens), f32)], axis=0)
    upper, lower = split_bf16(allg)
    gsm = dot(upper, n2) + dot(lower, n2)
    cu, cl = split_bf16(jnp.concatenate([coefs, jnp.zeros((8, tokens), f32)], axis=0))
    gvec = dot(cu, gx_half) + dot(cl, gx_half)
    gsm_ref[0:24, :] = gsm[0:24, :]
    gsm_ref[24:32, :] = jnp.concatenate(
        [jnp.zeros((2, D), f32), gvec[0:2, :], jnp.zeros((4, D), f32)], axis=0
    )
    both = jnp.concatenate([upper, lower], axis=0)
    twice = jnp.concatenate([small_half, small_half], axis=0)
    gn2_ref[...] = dot_tn(both, twice)

    def add(i, carry):
        rows = block(i)
        gn2_ref[rows, :] = gn2_ref[rows, :] + gcol_ref[rows, 16:17] * gx_ref[rows, :].astype(f32)
        return carry

    lax.fori_loop(0, BLOCKS, add, 0)


def gating_outputs():
    tokens = TREE
    return [shape((tokens, D)), shape((32, D)), shape((16, 16)), shape((16, tokens))]


def backward_kernel(first, experts, slots, traffic, *refs):
    refs = list(refs)
    gx_ref, gn2p_ref, gn2e_ref, slotc_ref, mid_ref, att_ref, w_ref, qkv_ref, n1_ref, x_ref = [
        refs.pop(0) for _ in range(10)
    ]
    biast_ref, lse_ref, gsm_ref = [refs.pop(0) for _ in range(3)]
    if not first:
        slotr_ref, gpack_ref = refs.pop(0), refs.pop(0)
        y_held, n2_ref, gcol_ref = refs.pop(0), refs.pop(0), refs.pop(0)
    gout_ref, dw_ref = refs.pop(0), refs.pop(0)
    if not first:
        gxs_ref, gy_ref, hidden_out = refs.pop(0), refs.pop(0), refs.pop(0)
    gatt, go, gqkv, turn = refs[:4]
    if not first:
        y_home, y_sends, y_recvs, y_local = refs[4:]
        ex = Exchange(experts, slots)
        own = pltpu.make_async_copy(
            y_held.at[pl.ds(0, slots)], y_home.at[own_slots(ex)], y_local
        )
        own.start()
        greet(experts)
        returning = []
        for wave in range(len(ex.waves)):
            returning += back_copies(ex, wave, 0, y_held, y_home, y_sends, y_recvs)
        for copy in returning:
            copy.start()
    tokens = n1_ref.shape[0]
    size, block = row_blocks(tokens)
    small = w_ref[:, W_SMALL:].astype(f32).T
    gain0 = small[S_GAIN : S_GAIN + 1, :]
    gain1 = small[S_GAIN + 1 : S_GAIN + 2, :]

    def enter(i, total):
        rows = block(i)
        gn2 = gn2p_ref[rows, :]
        slot = slotc_ref[rows, :]
        for e in range(experts):
            gn2 = gn2 + dot(one_hot_col(slot, e, slots), gn2e_ref[e * slots : (e + 1) * slots, :])
        middle = mid_ref[rows, :]
        r = inv_rms(middle)
        scaled = gain1 * gn2
        inner = jnp.mean(middle * scaled, axis=1, keepdims=True)
        gmid = gx_ref[rows, :].astype(f32) + r * scaled - middle * (r * r * r * inner)
        gout_ref[rows, :] = gmid
        half = gmid.astype(bf16)
        gatt[rows, :] = half
        go[rows, :] = dot_nt(half, w_ref[:, W_OUT:W_SMALL]).astype(bf16)
        return total + jnp.sum(gn2 * middle * r, axis=0, keepdims=True)

    ggain1 = lax.fori_loop(0, BLOCKS, enter, jnp.zeros((1, D), f32))
    traffic.need(att_ref)
    lane = lax.broadcasted_iota(jnp.int32, (1, 128), 1)
    low_f = jnp.where(lane < HD, 1.0, 0.0)
    low = low_f.astype(bf16)
    high = (1.0 - low_f).astype(bf16)
    scale = HD**-0.5

    def out_grad(p, carry):
        here = pl.ds(pl.multiple_of(p * 128, 128), 128)
        dw_ref[here, W_OUT:W_SMALL] = dot_tn(att_ref[:, here], gatt[...]).astype(bf16)
        return carry

    lax.fori_loop(0, D // 128, out_grad, 0)
    traffic.flush(dw_ref, (slice(None), slice(W_OUT, W_SMALL)))
    traffic.need(qkv_ref, biast_ref, lse_ref)
    spans = causal_spans(tokens)

    def pair(p, carry):
        here = pl.ds(pl.multiple_of(p * 128, 128), 128)
        lanes_k = pl.ds(pl.multiple_of(D + p * 128, 128), 128)
        lanes_v = pl.ds(pl.multiple_of(2 * D + p * 128, 128), 128)
        q = qkv_ref[:, here] * bf16(scale)
        k = qkv_ref[:, lanes_k]
        v = qkv_ref[:, lanes_v]
        g = go[:, here]
        turn[0:tokens, :] = g.astype(f32) * att_ref[:, here].astype(f32)
        inner = turn[...].T[:, 0:tokens]
        turn[0:tokens, :] = k.astype(f32)
        kt = turn[...].T[:, 0:tokens].astype(bf16)
        gk = [0.0] * len(spans)
        gv = [0.0] * len(spans)
        masks = (low, high)
        qs = [q * mask for mask in masks]
        gs = [g * mask for mask in masks]
        dsums = [
            jnp.sum(inner[h * HD : (h + 1) * HD, :], axis=0, keepdims=True) for h in range(2)
        ]
        lses = [lse_ref[pl.ds(2 * p + h, 1), :] for h in range(2)]
        parts = [[], []]
        for n, (start, stop) in enumerate(spans):
            st = [
                dot_nt(k[start:stop], qs[h][start:]) + biast_ref[start:stop, start:]
                for h in range(2)
            ]
            gpt = [dot_nt(v[start:stop], gs[h][start:]) for h in range(2)]
            pt = [jnp.exp(st[h] - lses[h][:, start:]) for h in range(2)]
            gst = [(pt[h] * (gpt[h] - dsums[h][:, start:])).astype(bf16) for h in range(2)]
            for h in range(2):
                gv[n] = gv[n] + dot(pt[h].astype(bf16), gs[h][start:])
                gk[n] = gk[n] + dot(gst[h], qs[h][start:])
                parts[h].append(dot(kt[h * HD : (h + 1) * HD, start:stop], gst[h]))
        gq_t = []
        for h in range(2):
            cols = []
            for n, (start, stop) in enumerate(spans):
                piece = 0.0
                for m in range(n + 1):
                    origin = spans[m][0]
                    piece = piece + parts[h][m][:, start - origin : stop - origin]
                cols.append(piece)
            gq_t.append(jnp.concatenate(cols, axis=1))
        turn_t = jnp.concatenate(gq_t, axis=0) * scale
        pad = turn.shape[0] - tokens
        turn_t = jnp.concatenate([turn_t, jnp.zeros((128, pad), f32)], axis=1)
        gqkv[:, here] = turn_t.T[0:tokens, :].astype(bf16)
        for n, (start, stop) in enumerate(spans):
            gqkv[start:stop, lanes_k] = gk[n].astype(bf16)
            gqkv[start:stop, lanes_v] = gv[n].astype(bf16)
        return carry

    turn[...] = jnp.zeros_like(turn)
    lax.fori_loop(0, H // 2, pair, 0)
    traffic.need(n1_ref)

    def in_grad(p, carry):
        here = pl.ds(pl.multiple_of(p * 128, 128), 128)
        dw_ref[here, 0:W_OUT] = dot_tn(n1_ref[:, here], gqkv[...]).astype(bf16)
        return carry

    lax.fori_loop(0, D // 128, in_grad, 0)
    traffic.flush(dw_ref, (slice(None), slice(0, W_OUT)))
    traffic.need(x_ref)

    def leave(i, total):
        rows = block(i)
        gn1 = dot_nt(gqkv[rows, :], w_ref[:, 0:W_OUT])
        x = x_ref[rows, :].astype(f32)
        r = inv_rms(x)
        scaled = gain0 * gn1
        inner = jnp.mean(x * scaled, axis=1, keepdims=True)
        gx = gout_ref[rows, :] + r * scaled - x * (r * r * r * inner)
        gout_ref[rows, :] = gx
        gatt[rows, :] = gx.astype(bf16)
        return total + jnp.sum(gn1 * x * r, axis=0, keepdims=True)

    ggain0 = lax.fori_loop(0, BLOCKS, leave, jnp.zeros((1, D), f32))
    rows = jnp.concatenate(
        [gsm_ref[0:24, :], ggain0, ggain1, gsm_ref[26:32, :], jnp.zeros((96, D), f32)], axis=0
    )
    dw_ref[:, W_SMALL:] = rows.T.astype(bf16)
    traffic.flush(dw_ref, (slice(None), slice(W_SMALL, W_ALL)))
    traffic.flush(gout_ref)
    if not first:
        hot = all_one_hot(slotr_ref[...], experts, slots)
        send_grads(hot, gatt[...], gpack_ref[...], gxs_ref, gy_ref, experts, slots)
        own.wait()
        for copy in returning:
            copy.wait()
        traffic.need(n2_ref, gcol_ref)
        vectors = small[S_VEC : S_VEC + 2, :]

        def home(i, carry):
            rows = block(i)
            hidden_out[rows, :] = combine_rows(
                rows, mid_ref, n2_ref, y_home, gcol_ref, slotc_ref, vectors, experts, slots
            ).astype(bf16)
            return carry

        lax.fori_loop(0, BLOCKS, home, 0)


def backward_call(first, experts, slots, args):
    tokens = TREE
    sent = experts * slots
    outs = [shape((tokens, D)), shape((D, W_ALL), bf16)]
    if not first:
        outs += [shape((sent, D), bf16)] * 2 + [shape((tokens, D), bf16)]
    padded = -(-tokens // 128) * 128
    scratch = [
        pltpu.VMEM((tokens, D), bf16),
        pltpu.VMEM((tokens, D), bf16),
        pltpu.VMEM((tokens, 3 * D), bf16),
        pltpu.VMEM((padded, 128), f32),
    ]
    body = functools.partial(backward_kernel, first, experts, slots)
    late = (5, 7, 8, 9, 10, 11)
    if first:
        return whole_call(body, "block_backward", outs, scratch, args, 40 * 10**9, late, (0, 1))
    count = len(Exchange(experts, slots).waves)
    scratch.append(pltpu.VMEM((sent, D), bf16))
    scratch += [pltpu.SemaphoreType.DMA((1, count, experts - 1))] * 2
    scratch.append(pltpu.SemaphoreType.DMA)
    late += (16, 17)
    return whole_call(
        body, "block_backward", outs, scratch, args, 40 * 10**9, late, (0, 1), (15,), 5
    )


class Packing:
    def __init__(self, shards, part, ff):
        self.shards, self.part, self.ff = shards, part, ff
        self.padded = -(-part // 16) * 16
        self.chunks = ff // 256
        self.own = ff // shards
        self.down = 2 * self.chunks * self.padded
        self.rows = self.down + (D // 256) * self.own

    def pack(self, gate, up, down):
        pieces = []
        for wide in (gate, up):
            cut = wide.reshape(self.part, self.chunks, 256).transpose(1, 0, 2)
            cut = jnp.pad(cut, [(0, 0), (0, self.padded - self.part), (0, 0)])
            pieces.append(cut.reshape(self.chunks * self.padded, 256))
        pieces.append(
            down.reshape(self.own, D // 256, 256).transpose(1, 0, 2).reshape(-1, 256)
        )
        return jnp.concatenate(pieces, axis=0)

    def wide_part(self, ref, n, j):
        at = pl.multiple_of((n * self.chunks + j) * self.padded, 16)
        return ref[:, pl.ds(at, self.padded), :][:, : self.part, :].reshape(D, 256)

    def tall_part(self, ref, j):
        group = 256 // self.own
        here = pl.ds(j * group, group)
        pieces = []
        for c in range(D // 256):
            at = self.down + c * self.own
            pieces.append(ref[here, at : at + self.own, :].reshape(256, 256))
        return jnp.concatenate(pieces, axis=1)

    def put_wide(self, ref, n, j, grad):
        at = pl.multiple_of((n * self.chunks + j) * self.padded, 16)
        ref[:, pl.ds(at, self.part), :] = grad.reshape(self.shards, self.part, 256)

    def put_tall(self, ref, j, grad):
        group = 256 // self.own
        for c in range(D // 256):
            at = self.down + c * self.own
            ref[pl.ds(j * group, group), at : at + self.own, :] = grad[
                :, c * 256 : (c + 1) * 256
            ].reshape(group, self.own, 256)


class Exchange:
    def __init__(self, experts, slots):
        self.experts, self.slots = experts, slots
        half = -(-slots // 32) * 16
        quarter = -(-half // 32) * 16
        self.half = half
        edges = (0, quarter, half, slots)
        self.waves = tuple((low, high - low) for low, high in zip(edges[:-1], edges[1:]))
        self.ranges = [(0, slots)]
        for _, size in self.waves:
            start = self.ranges[-1][0] + self.ranges[-1][1]
            self.ranges.append((start, (experts - 1) * size))
        self.total = experts * slots

    def span(self, group):
        start = self.ranges[1 + group[0]][0]
        return start, sum(self.ranges[1 + wave][1] for wave in group)

    def held(self, wave, d):
        size = self.waves[wave][1]
        return pl.ds(self.ranges[1 + wave][0] + (d - 1) * size, size)

    def slot(self, device, wave):
        offset, size = self.waves[wave]
        return pl.ds(pl.multiple_of(device * self.slots + offset, 16), size)


MESH = pl.DeviceIdType.MESH


def greet(experts):
    me = lax.axis_index("expert")
    barrier = pltpu.get_barrier_semaphore()
    for d in range(1, experts):
        pl.semaphore_signal(
            barrier, inc=1, device_id={"expert": lax.rem(me + d, experts)}, device_id_type=MESH
        )
    pl.semaphore_wait(barrier, experts - 1)


def out_copies(ex, wave, src, dst, sends, recvs):
    me = lax.axis_index("expert")
    copies = []
    for d in range(1, ex.experts):
        to = lax.rem(me + d, ex.experts)
        copies.append(
            pltpu.make_async_remote_copy(
                src_ref=src.at[ex.slot(to, wave)],
                dst_ref=dst.at[ex.held(wave, d)],
                send_sem=sends.at[wave, d - 1],
                recv_sem=recvs.at[wave, d - 1],
                device_id={"expert": to},
                device_id_type=MESH,
            )
        )
    return copies


def back_copies(ex, wave, n, src, dst, sends, recvs):
    me = lax.axis_index("expert")
    copies = []
    for d in range(1, ex.experts):
        copies.append(
            pltpu.make_async_remote_copy(
                src_ref=src.at[ex.held(wave, d)],
                dst_ref=dst.at[ex.slot(me, wave)],
                send_sem=sends.at[n, wave, d - 1],
                recv_sem=recvs.at[n, wave, d - 1],
                device_id={"expert": lax.rem(me + ex.experts - d, ex.experts)},
                device_id_type=MESH,
            )
        )
    return copies


def own_slots(ex):
    me = lax.axis_index("expert")
    return pl.ds(pl.multiple_of(me * ex.slots, 16), ex.slots)


def dispatch_kernel(ex, send, recv, sends, recvs, local):
    own = pltpu.make_async_copy(send.at[own_slots(ex)], recv.at[pl.ds(0, ex.slots)], local)
    own.start()
    greet(ex.experts)
    copies = []
    for wave in range(len(ex.waves)):
        copies += out_copies(ex, wave, send, recv, sends, recvs)
    for copy in copies:
        copy.start()
    for copy in copies:
        copy.wait()
    own.wait()


def dispatch_call(ex, rows):
    far = pl.BlockSpec(memory_space=pl.ANY)
    return pl.pallas_call(
        functools.partial(dispatch_kernel, ex),
        out_shape=shape((ex.total, D), bf16),
        in_specs=[far],
        out_specs=far,
        scratch_shapes=[pltpu.SemaphoreType.DMA((len(ex.waves), ex.experts - 1))] * 2
        + [pltpu.SemaphoreType.DMA],
        compiler_params=pltpu.CompilerParams(
            vmem_limit_bytes=60 << 20, collective_id=3, has_side_effects=True
        ),
        cost_estimate=pl.CostEstimate(flops=35 * 10**9, bytes_accessed=10**6, transcendentals=0),
        name="dispatch",
    )(rows)


def exchange_kernel(mode, pack, ex, *refs):
    refs = list(refs)
    forward, backward = mode in ("forward", "both"), mode in ("backward", "both")
    recv_n = refs.pop(0)
    w_hbm = refs.pop(0)
    if backward:
        send_g = refs.pop(0)
        if mode == "backward":
            gate_hbm, up_hbm = refs.pop(0), refs.pop(0)
        inputs = 9 if mode == "both" else 12
        gating_far = [refs.pop(0) for _ in range(inputs)]
    if mode == "forward":
        back_y = refs.pop(0)
    if mode == "both":
        out_y = refs.pop(0)
    if mode == "forward":
        gates_far, ups_far, gates, ups = [refs.pop(0) for _ in range(4)]
    else:
        back_g, dw_far = refs.pop(0), refs.pop(0)
        gating_outs = [refs.pop(0) for _ in range(4)]
    if mode == "forward":
        out_y = refs.pop(0)
    if forward:
        acc_y = refs.pop(0)
    if backward:
        recv_g, out_g, hids, gates, ups, rows_t, acc_g = [refs.pop(0) for _ in range(7)]
        gating = [refs.pop(0) for _ in range(inputs)]
    if mode == "both":
        dots_out, dots, dots_send, dots_recv = [refs.pop(0) for _ in range(4)]
    w = refs.pop(0)
    sends, recvs, backs, gots, local = refs
    traffic = Traffic()
    if mode == "forward":
        traffic.sink(gates, gates_far, local.at[4:8])
        traffic.sink(ups, ups_far, local.at[8:12])

    loads = [pltpu.make_async_copy(w_hbm, w, local.at[0])]
    if mode == "backward":
        loads.append(pltpu.make_async_copy(gate_hbm, gates, local.at[1]))
        loads.append(pltpu.make_async_copy(up_hbm, ups, local.at[2]))
    if mode == "backward":
        for n, (far, near) in enumerate(zip(gating_far, gating)):
            traffic.fetch(far, near, local.at[4 + n])
    for copy in loads:
        copy.start()
    if mode == "both":
        for n, (far, near) in enumerate(zip(gating_far, gating)):
            traffic.fetch(far, near, local.at[4 + n])
    greet(ex.experts)

    def work(start, size):
        rows = slice(start, start + size)
        part = slice(0, size)
        if forward:
            acc_y[part, :] = jnp.zeros((size, D), f32)
        if backward:
            acc_g[part, :] = jnp.zeros((size, D), f32)

        def chunk(j, carry):
            lanes = pl.ds(pl.multiple_of(j * 256, 256), 256)
            gate_w, up_w = pack.wide_part(w, 0, j), pack.wide_part(w, 1, j)
            down_w = pack.tall_part(w, j)
            if forward:
                r = recv_n[rows, :]
                gate, up = dot(r, gate_w), dot(r, up_w)
                if mode == "forward":
                    gates[rows, lanes] = gate.astype(bf16)
                    ups[rows, lanes] = up.astype(bf16)
            else:
                gate, up = gates[rows, lanes].astype(f32), ups[rows, lanes].astype(f32)
            s = jax.nn.sigmoid(gate)
            act = gate * s
            hid = (act * up).astype(bf16)
            if forward:
                acc_y[part, :] = acc_y[part, :] + dot(hid, down_w)
            if backward:
                hids[rows, lanes] = hid
                ghid = dot_nt(recv_g[rows, :], down_w)
                guv = (ghid * act).astype(bf16)
                ggu = (ghid * up * (s * (1.0 + gate * (1.0 - s)))).astype(bf16)
                gates[rows, lanes] = ggu
                ups[rows, lanes] = guv
                acc_g[part, :] = acc_g[part, :] + dot_nt(ggu, gate_w) + dot_nt(guv, up_w)
            return carry

        lax.fori_loop(0, pack.chunks, chunk, 0)
        if mode == "forward":
            here = pl.ds(start, size)
            traffic.flush(gates, here)
            traffic.flush(ups, here)
        if forward:
            out_y[rows, :] = acc_y[part, :].astype(bf16)
        if backward:
            out_g[rows, :] = acc_g[part, :].astype(bf16)

    def send_dots(n, group):
        me = lax.axis_index("expert")
        for d in range(1, ex.experts):
            pieces = []
            for wave in group:
                here = ex.held(wave, d)
                pieces.append(row_dots(out_y[here, :], recv_g[here, :]))
            size = sum(ex.waves[wave][1] for wave in group)
            if size < 128:
                pieces.append(jnp.zeros((8, 128 - size), f32))
            dots_out[n, d - 1] = jnp.concatenate(pieces, axis=1)
            copy = pltpu.make_async_remote_copy(
                src_ref=dots_out.at[n, d - 1],
                dst_ref=dots.at[n, me],
                send_sem=dots_send.at[n, d - 1],
                recv_sem=dots_recv.at[n, d - 1],
                device_id={"expert": lax.rem(me + ex.experts - d, ex.experts)},
                device_id_type=MESH,
            )
            copy.start()
            dot_copies.append(copy)

    def send_back(group):
        for wave in group:
            if mode == "forward":
                ys.extend(back_copies(ex, wave, 0, out_y, back_y, backs, gots))
                for copy in ys[1 - ex.experts :]:
                    copy.start()
        for wave in group:
            if backward:
                gs.extend(back_copies(ex, wave, 1, out_g, back_g, backs, gots))
                for copy in gs[1 - ex.experts :]:
                    copy.start()

    ys, gs, dot_copies = [], [], []
    groups = ((0,), (1,), (2,)) if mode == "forward" else ((0, 1), (2,))
    if backward:
        arrivals = []
        for group in groups:
            arrivals.append([])
            for wave in group:
                arrivals[-1] += out_copies(ex, wave, send_g, recv_g, sends, recvs)
        for copy in arrivals[0]:
            copy.start()
        recv_g[0 : ex.slots, :] = send_g[own_slots(ex), :]
        if mode == "backward":
            traffic.need(*gating)
            gating_kernel(False, ex.experts, ex.slots, *gating, *gating_outs)
    for copy in loads:
        copy.wait()
    if backward:
        work(*ex.ranges[0])
        if mode == "both":
            own_dots = row_dots(out_y[0 : ex.slots, :], recv_g[0 : ex.slots, :])
            me = lax.axis_index("expert")
            dots[0, me, :, 0 : ex.half] = own_dots[:, 0 : ex.half]
            dots[1, me, :, 0 : ex.slots - ex.half] = own_dots[:, ex.half :]
        for copy in arrivals[0]:
            copy.wait_send()
        for copy in arrivals[1]:
            copy.start()
        for copy in arrivals[0]:
            copy.wait_recv()
    for n, group in enumerate(groups):
        if backward and n > 0:
            for copy in arrivals[n]:
                copy.wait()
        work(*ex.span(group))
        if mode == "both":
            send_dots(n, group)
        send_back(group)
    if mode == "forward":
        work(*ex.ranges[0])
        back_y[own_slots(ex), :] = out_y[0 : ex.slots, :]
    if backward:
        back_g[own_slots(ex), :] = out_g[0 : ex.slots, :]
        rows_t[...] = recv_n[...].T
        dw = w
        if pack.padded != pack.part:
            dw[...] = jnp.zeros_like(dw)

        def weights(j, carry):
            lanes = pl.ds(pl.multiple_of(j * 256, 256), 256)
            pack.put_wide(dw, 0, j, dot(rows_t[...], gates[:, lanes]).astype(bf16))
            pack.put_wide(dw, 1, j, dot(rows_t[...], ups[:, lanes]).astype(bf16))
            pack.put_tall(dw, j, dot_tn(hids[:, lanes], recv_g[...]).astype(bf16))
            return carry

        lax.fori_loop(0, pack.chunks, weights, 0)
        leaving = pltpu.make_async_copy(dw, dw_far, local.at[3])
        leaving.start()
    for copy in ys + dot_copies:
        copy.wait()
    if mode == "both":
        traffic.need(*gating)
        gating_kernel(True, ex.experts, ex.slots, *gating[:2], dots, *gating[2:], *gating_outs)
    for copy in gs:
        copy.wait()
    if backward:
        leaving.wait()
    traffic.finish()


SPLIT = 13 * 128
QUARTER = 7 * 128


def cube_kernel(part, labels, g_ref, upper_ref, mix_ref, ready, mix_out, own, *refs):
    got_c, sums, got_a, got_b, half_a, half_b, end_a, end_b, mine, quarters, mix_held, mix_got = refs[:12]
    send, recv, z_send, z_recv, mix_send, mix_recv, own_sem = refs[12:]
    me = lax.axis_index("shard")
    z = lax.axis_index("expert")
    owners = quarters.shape[1]
    core, x, y = lax.rem(me, 2), lax.rem(me // 2, 2), me // 4
    near, over_x, over_y = me + 1 - 2 * core, me + 2 - 4 * x, me + 4 - 8 * y
    chips = [2 * (1 - y) + 1 - x, 2 * y + 1 - x, 2 * (1 - y) + x, 2 * y + x]

    def rows(shard):
        return pl.ds(pl.multiple_of(shard * part, 16), part)

    loads = [
        pltpu.make_async_copy(g_ref.at[rows(2 * chip + core)], own.at[n], own_sem.at[n])
        for n, chip in enumerate(chips)
    ]
    for load in loads:
        load.start()
    barrier = pltpu.get_barrier_semaphore()
    for other in (near, over_x, over_y):
        pl.semaphore_signal(barrier, inc=1, device_id={"shard": other}, device_id_type=MESH)
    for d in range(1, owners):
        pl.semaphore_signal(
            barrier, inc=1, device_id={"expert": lax.rem(z + d, owners)}, device_id_type=MESH
        )
    pl.semaphore_wait(barrier, 3 + owners - 1)
    cols_a, cols_b = slice(0, SPLIT), slice(SPLIT, W_ALL)

    def remote(src, dst, send_sem, recv_sem, to):
        made = pltpu.make_async_remote_copy(
            src_ref=src,
            dst_ref=dst,
            send_sem=send_sem,
            recv_sem=recv_sem,
            device_id=to,
            device_id_type=MESH,
        )
        made.start()
        return made

    def copy(n, src, dst, to):
        return remote(src, dst, send.at[n], recv.at[n], {"shard": to})

    half = part // 2
    jobs = ((1, 0, part), (0, 0, half), (0, half, half))

    def quarter(job, owner):
        l, start, size = jobs[job]
        return l, pl.ds(start, size), pl.ds(pl.multiple_of(owner * QUARTER, 128), QUARTER)

    def spread(job):
        made = []
        held = pl.ds(0, jobs[job][2])
        for d in range(1, owners):
            to = lax.rem(z + d, owners)
            made.append(
                remote(
                    mine.at[quarter(job, to)],
                    quarters.at[job, z, held],
                    z_send.at[job, 0, d - 1],
                    z_recv.at[job, 0, d - 1],
                    {"expert": to},
                )
            )
        quarters[job, z, held] = mine[quarter(job, z)]
        return made

    def gather(job, made):
        for one in made:
            one.wait_recv()
        held = pl.ds(0, jobs[job][2])
        total = quarters[job, 0, held].astype(f32)
        for owner in range(1, owners):
            total = total + quarters[job, owner, held].astype(f32)
        here = quarter(job, z)
        ready[here] = total.astype(bf16)
        return [
            remote(
                ready.at[here],
                ready.at[here],
                z_send.at[job, 1, d - 1],
                z_recv.at[job, 1, d - 1],
                {"expert": lax.rem(z + d, owners)},
            )
            for d in range(1, owners)
        ]

    pairs = [{"shard": near}, {"shard": over_x}, {"shard": over_y}]
    pairs += [{"expert": z + 1 - 2 * lax.rem(z, 2)}, {"expert": z + 2 - 4 * (z // 2)}]
    mix_held[0] = mix_ref[...]

    def mix_start(n):
        return remote(mix_held.at[n], mix_got.at[n], mix_send.at[n], mix_recv.at[n], pairs[n])

    def mix_end(n, made):
        made.wait_recv()
        total = mix_held[n] + mix_got[n]
        if n + 1 < len(pairs):
            mix_held[n + 1] = total
        else:
            for l in range(LAYERS):
                mix_out[l] = total[l * 16 : l * 16 + labels, 0:labels]

    def begin(h):
        shift = h * half
        return [
            copy(
                10 * h + n,
                g_ref.at[pl.ds(pl.multiple_of((2 * chip + 1 - core) * part + shift, 16), half)],
                got_c.at[chip, pl.ds(shift, half)],
                near,
            )
            for n, chip in enumerate(chips)
        ]

    def cross(h, first):
        hs = pl.ds(h * half, half)

        def merge(n):
            if h == 0:
                loads[n].wait()
            first[n].wait_recv()
            chip = chips[n]
            value = own[n, hs, :].astype(f32) + got_c[chip, hs, :].astype(f32)
            sums[chip, hs, :] = value.astype(bf16)

        merge(0)
        a0 = copy(10 * h + 4, sums.at[chips[0], hs, cols_a], got_a.at[1 - y, hs], over_x)
        b0 = copy(10 * h + 5, sums.at[chips[0], hs, cols_b], got_b.at[1 - x, hs], over_y)
        merge(1)
        a1 = copy(10 * h + 6, sums.at[chips[1], hs, cols_a], got_a.at[y, hs], over_x)
        merge(2)
        b1 = copy(10 * h + 7, sums.at[chips[2], hs, cols_b], got_b.at[x, hs], over_y)
        merge(3)
        return a0, b0, a1, b1

    def turn_over(h, crossed):
        hs = pl.ds(h * half, half)
        a0, b0 = crossed[:2]
        a0.wait_recv()
        value = sums[chips[2], hs, cols_a].astype(f32) + got_a[1 - y, hs, :].astype(f32)
        half_a[hs, :] = value.astype(bf16)
        a2 = copy(10 * h + 8, half_a.at[hs], end_a.at[hs], over_y)
        b0.wait_recv()
        value = sums[chips[1], hs, cols_b].astype(f32) + got_b[1 - x, hs, :].astype(f32)
        half_b[hs, :] = value.astype(bf16)
        b2 = copy(10 * h + 9, half_b.at[hs], end_b.at[hs], over_x)
        return a2, b2

    def end(h, crossed, turned):
        hs = pl.ds(h * half, half)
        parts = (
            (cols_a, crossed[2], turned[0], got_a.at[y], end_a),
            (cols_b, crossed[3], turned[1], got_b.at[x], end_b),
        )
        for cols, one, two, got, last in parts:
            one.wait_recv()
            value = sums[chips[3], hs, cols].astype(f32) + got[hs, :].astype(f32)
            two.wait_recv()
            mine[0, hs, cols] = (value + last[hs, :].astype(f32)).astype(bf16)
        return spread(1 + h)

    first = [begin(0), begin(1)]
    mix = [mix_start(0)]
    for l in range(2):
        mine[l, :, W_ALL:] = jnp.zeros((part, 4 * QUARTER - W_ALL), bf16)
    mine[1, :, 0:W_ALL] = upper_ref[...]
    upper = spread(0)
    crossed = [cross(0, first[0])]
    mix_end(0, mix[0])
    mix.append(mix_start(1))
    crossed.append(cross(1, first[1]))
    turned = [turn_over(0, crossed[0])]
    mix_end(1, mix[1])
    mix.append(mix_start(2))
    upper_back = gather(0, upper)
    turned.append(turn_over(1, crossed[1]))
    lower = [end(0, crossed[0], turned[0])]
    mix_end(2, mix[2])
    mix.append(mix_start(3))
    lower.append(end(1, crossed[1], turned[1]))
    lower_back = gather(1, lower[0])
    mix_end(3, mix[3])
    mix.append(mix_start(4))
    lower_back += gather(2, lower[1])
    mix_end(4, mix[4])
    for made in upper_back + lower_back:
        made.wait_recv()
    started = mix + upper + upper_back + lower_back
    for h in range(2):
        started += first[h] + list(crossed[h]) + list(turned[h]) + lower[h]
    for made in started:
        made.wait_send()


def finish_call(part, labels, grads, upper, mix):
    vmem = pl.BlockSpec(memory_space=pltpu.VMEM)
    rest = W_ALL - SPLIT
    owners = lax.axis_size("expert")
    outs = [shape((2, part, 4 * QUARTER), bf16), shape((LAYERS, labels, labels))]
    dma = pltpu.SemaphoreType.DMA
    return pl.pallas_call(
        functools.partial(cube_kernel, part, labels),
        out_shape=outs,
        in_specs=[pl.BlockSpec(memory_space=pl.ANY), vmem, vmem],
        out_specs=[vmem] * len(outs),
        scratch_shapes=[
            pltpu.VMEM((4, part, W_ALL), bf16),
            pltpu.VMEM((4, part, W_ALL), bf16),
            pltpu.VMEM((4, part, W_ALL), bf16),
            pltpu.VMEM((2, part, SPLIT), bf16),
            pltpu.VMEM((2, part, rest), bf16),
            pltpu.VMEM((part, SPLIT), bf16),
            pltpu.VMEM((part, rest), bf16),
            pltpu.VMEM((part, SPLIT), bf16),
            pltpu.VMEM((part, rest), bf16),
            pltpu.VMEM((2, part, 4 * QUARTER), bf16),
            pltpu.VMEM((3, owners, part, QUARTER), bf16),
            pltpu.VMEM((5, 32, 128), f32),
            pltpu.VMEM((5, 32, 128), f32),
            dma((20,)),
            dma((20,)),
            dma((3, 2, owners - 1)),
            dma((3, 2, owners - 1)),
            dma((5,)),
            dma((5,)),
            dma((4,)),
        ],
        compiler_params=pltpu.CompilerParams(
            vmem_limit_bytes=60 << 20, collective_id=4, has_side_effects=True
        ),
        cost_estimate=pl.CostEstimate(flops=70 * 10**9, bytes_accessed=10**7, transcendentals=0),
        name="dense_sums",
    )(grads, upper, mix)


EXCHANGE_IDS = {"forward": 0, "both": 1, "backward": 2}


def exchange_call(mode, pack, ex, args):
    rows, ff = ex.total, pack.ff
    forward, backward = mode in ("forward", "both"), mode in ("backward", "both")
    flat, wide = shape((rows, D), bf16), shape((rows, ff), bf16)
    packed = (pack.shards, pack.rows, 256)
    most = max(ex.slots, ex.span((0, 1))[1], ex.span((2,))[1])
    vmem = pl.BlockSpec(memory_space=pltpu.VMEM)
    far = pl.BlockSpec(memory_space=pl.ANY)
    in_specs = [vmem] * len(args)
    in_specs[1] = far
    scratch = []
    if mode == "forward":
        outs = [flat, wide, wide]
    elif mode == "both":
        outs = [flat, flat, shape(packed, bf16)] + gating_outputs()
    else:
        in_specs[3] = in_specs[4] = far
        outs = [flat, shape(packed, bf16)] + gating_outputs()
    out_specs = [vmem] * len(outs)
    if mode == "forward":
        out_specs[1] = out_specs[2] = far
        scratch += [pltpu.VMEM((rows, ff), bf16)] * 2
    else:
        inputs = 9 if mode == "both" else 12
        in_specs[-inputs:] = [far] * inputs
        out_specs[2 if mode == "both" else 1] = far
    if mode == "forward":
        scratch.append(pltpu.VMEM((rows, D), bf16))
    if forward:
        scratch.append(pltpu.VMEM((most, D), f32))
    if backward:
        scratch += [pltpu.VMEM((rows, D), bf16)] * 2
        scratch += [pltpu.VMEM((rows, ff), bf16)] * 3
        scratch += [pltpu.VMEM((D, rows), bf16), pltpu.VMEM((most, D), f32)]
        scratch += [pltpu.VMEM(a.shape, a.dtype) for a in args[-inputs:]]
    if mode == "both":
        scratch.append(pltpu.VMEM((2, ex.experts - 1, 8, 128), f32))
        scratch.append(pltpu.VMEM((2, ex.experts, 8, 128), f32))
        scratch += [pltpu.SemaphoreType.DMA((2, ex.experts - 1))] * 2
    scratch.append(pltpu.VMEM(packed, bf16))
    count = len(ex.waves)
    scratch += [pltpu.SemaphoreType.DMA((count, ex.experts - 1))] * 2
    scratch += [pltpu.SemaphoreType.DMA((2, count, ex.experts - 1))] * 2
    scratch.append(pltpu.SemaphoreType.DMA((16,)))
    work = 6 * rows * D * ff * (1 if mode == "forward" else 2 if mode == "backward" else 3)
    return pl.pallas_call(
        functools.partial(exchange_kernel, mode, pack, ex),
        out_shape=outs,
        in_specs=in_specs,
        out_specs=out_specs,
        scratch_shapes=scratch,
        compiler_params=pltpu.CompilerParams(
            vmem_limit_bytes=62 << 20, collective_id=EXCHANGE_IDS[mode], has_side_effects=True
        ),
        cost_estimate=pl.CostEstimate(
            flops=10**9 if mode == "backward" else work + 40 * 10**9,
            bytes_accessed=6 * D * ff,
            transcendentals=0,
        ),
        name="experts_" + mode,
    )(*args)


def write_dense(part, labels, l, ref, outs, turn):
    proj_ref, out_ref, gain_ref, router_ref, vec_ref, const_ref = outs
    for c in range(3):
        proj_ref[l, c] = ref[:, c * D : (c + 1) * D].astype(f32)
    out_ref[l] = ref[:, W_OUT:W_SMALL].astype(f32)
    small = ref[:, W_SMALL:W_ALL].astype(f32)
    turn[0:part, :] = small
    rows = turn[...].T
    router_ref[l] = rows[0:labels, 0:part]
    for c in range(2):
        const_ref[l, c] = rows[S_CONST + 2 * c : S_CONST + 2 * c + 2, 0:part]
    gain_ref[l] = rows[S_GAIN : S_GAIN + 2, 0:part]
    vec_ref[l] = rows[S_VEC : S_VEC + 2, 0:part]


def outputs_kernel(pack, labels, traffic, low_ref, high_ref, dense_ref, hidden_ref, *refs):
    gate_ref, up_ref, down_ref = refs[:3]
    outs, hidden_out, turn = refs[3:9], refs[9], refs[10]
    turn[...] = jnp.zeros_like(turn)
    for l, ref in enumerate((low_ref, high_ref)):
        for n, out in enumerate((gate_ref, up_ref)):
            for j in range(pack.chunks):
                at = (n * pack.chunks + j) * pack.padded
                out[l, :, j * 256 : (j + 1) * 256] = ref[at : at + pack.part, :].astype(f32)
        for c in range(D // 256):
            at = pack.down + c * pack.own
            down_ref[l, :, c * 256 : (c + 1) * 256] = ref[at : at + pack.own, :].astype(f32)
        for out in (gate_ref, up_ref, down_ref):
            traffic.flush(out, l)
        write_dense(pack.part, labels, l, dense_ref.at[l], outs, turn)
        for out in outs[:2]:
            traffic.flush(out, l)
    traffic.need(hidden_ref)
    hidden_out[...] = hidden_ref[...]
    traffic.flush(hidden_out)


def dense_shapes(part, labels):
    return [
        shape((LAYERS, 3, part, D)),
        shape((LAYERS, part, D)),
        shape((LAYERS, 2, part)),
        shape((LAYERS, labels, part)),
        shape((LAYERS, 2, part)),
        shape((LAYERS, 2, 2, part)),
    ]


def outputs_call(pack, labels, grads, dense, hidden):
    wide = shape((LAYERS, pack.part, pack.ff))
    outs = [wide, wide, shape((LAYERS, pack.own, D))] + dense_shapes(pack.part, labels)
    outs.append(shape(hidden.shape, hidden.dtype))
    body = functools.partial(outputs_kernel, pack, labels)
    turn = [pltpu.VMEM((128, 128), f32)]
    return whole_call(body, "outputs", outs, turn, grads + [dense, hidden], 10**6, (3,), (0, 1, 2, 3, 4, 9))


def pack_kernel(traffic, proj_ref, out_ref, small_ref, *packed):
    for l, ref in enumerate(packed):
        for c in range(3):
            ref[:, c * D : (c + 1) * D] = proj_ref[l, c]
        ref[:, W_OUT:W_SMALL] = out_ref[l]
        ref[:, W_SMALL:] = small_ref[l]


def pack_call(project, output, small):
    outs = [shape((project.shape[2], W_ALL), bf16)] * LAYERS
    return whole_call(pack_kernel, "pack", outs, [], [project, output, small], 10**6)


def on_device(
    hidden_in,
    prior_logits,
    project_weight,
    output_weight,
    norm_gain,
    router_weight,
    mixing_weight,
    const_vector,
    const_weight,
    gate_weight,
    up_weight,
    down_weight,
    routes,
    priority,
    leaf_parent,
    cotangent,
):
    experts = lax.axis_size("expert")
    total_experts = experts + 4
    tokens = hidden_in.shape[0]
    capacity = 9 * tokens * TOP // (8 * total_experts)
    slots = -(-capacity // 16) * 16
    part = project_weight.shape[2]

    def pad_cols(a, width):
        return jnp.pad(a, [(0, 0)] * (a.ndim - 1) + [(0, width - a.shape[-1])])

    dense = []
    experts_w = []
    pack = Packing(lax.axis_size("shard"), part, gate_weight.shape[3])
    small = jnp.concatenate(
        [
            pad_cols(router_weight, S_CONST),
            const_weight[:, 0],
            const_weight[:, 1],
            jnp.zeros((LAYERS, part, S_GAIN - S_CONST - 4), bf16),
            norm_gain.transpose(0, 2, 1),
            const_vector.transpose(0, 2, 1),
        ],
        axis=2,
    )
    packed = pack_call(project_weight, output_weight, pad_cols(small, 128))
    for l in range(LAYERS):
        dense.append(lax.all_gather(packed[l], "shard", axis=0, tiled=True))
        mine = pack.pack(gate_weight[l, 0], up_weight[l, 0], down_weight[l, 0])
        experts_w.append(lax.all_gather(mine, "shard", axis=0, tiled=False))

    ranking = priority[0]
    earlier = (ranking[None, :] < ranking[:, None]).astype(bf16)
    labels = jnp.arange(total_experts, dtype=jnp.int32)
    hits = jnp.sum((routes[:, :, :, None] == labels).astype(f32), axis=2)
    chosen_rows = [jnp.pad(hits[l].T, [(0, 16 - total_experts), (0, 0)]) for l in range(LAYERS)]
    loaded = jnp.concatenate([hits[l, :, :experts] for l in range(LAYERS)], axis=1)
    loaded_half = loaded.astype(bf16)
    rank_row = lax.dot_general(
        loaded_half, earlier, (((0,), (1,)), ((), ())), preferred_element_type=f32
    )
    slot_row_all = jnp.where((loaded.T > 0) & (rank_row < capacity), rank_row, -1.0)
    slot_col = []
    for l in range(LAYERS):
        rank_col = dot(earlier, hits[l, :, :experts].astype(bf16))
        slot_col.append(
            jnp.where((hits[l, :, :experts] > 0) & (rank_col < capacity), rank_col, -1.0)
        )
    slot_row = [
        jnp.pad(
            slot_row_all[l * experts : (l + 1) * experts],
            [(0, 8 - experts), (0, 0)],
            constant_values=-1.0,
        )
        for l in range(LAYERS)
    ]
    visible = tree_visible(leaf_parent[0])
    bias = jnp.where(visible, 0.0, masked_fill)
    bias_t = jnp.where(visible.T, 0.0, masked_fill)
    mixes = [
        jnp.pad(mixing_weight[l], [(0, 16 - total_experts), (0, 16 - total_experts)])
        for l in range(LAYERS)
    ]
    z_rows = jnp.pad(prior_logits.T, [(0, 16 - total_experts), (0, 0)])

    plan = (bias, bias_t, slot_col, slot_row, chosen_rows, mixes, z_rows)
    bias, bias_t, slot_col, slot_row, chosen_rows, mixes, z_rows = lax.optimization_barrier(plan)
    ex = Exchange(experts, slots)
    saved = []
    front = [hidden_in]
    x_now = hidden_in
    for l in range(LAYERS):
        last = l == LAYERS - 1
        args = front + [dense[l], bias, z_rows, mixes[l].T, chosen_rows[l], slot_row[l]]
        if last:
            args.append(cotangent)
        outs = list(forward_call(l == 0, last, experts, slots, args))
        if l > 0:
            x_now = outs.pop(0)
        n1, qkv, att, lse, middle, n2, info, gcol, gpack, send, small, z_next = outs[:12]
        keep = dict(
            x=x_now, n1=n1, qkv=qkv, att=att, lse=lse, middle=middle, n2=n2, info=info,
            gcol=gcol, gpack=gpack, z=z_rows, small=small,
        )
        keep["received"] = dispatch_call(ex, send)
        if last:
            gating = [
                cotangent, n2, slot_row[l], info, chosen_rows[l], gcol, small, z_rows, mixes[l],
            ]
            done = exchange_call(
                "both", pack, ex, [keep["received"], experts_w[l], outs[12]] + gating
            )
            y_held, keep["gin"], keep["dw"] = done[:3]
            keep["gating"] = done[3:]
        else:
            keep["y"], keep["gate"], keep["up"] = exchange_call(
                "forward", pack, ex, [keep["received"], experts_w[l]]
            )
            front = [middle, n2, keep["y"], gcol, slot_col[l], small]
        z_rows = z_next
        saved.append(keep)

    gx = cotangent
    gz = None
    dense_grads = [None] * LAYERS
    mix_grads = [None] * LAYERS
    expert_grads = [None] * LAYERS
    hidden_out = None
    for l in range(LAYERS - 1, -1, -1):
        last = l == LAYERS - 1
        keep = saved[l]
        if not last:
            gating = [
                gx, keep["n2"], keep["y"], keep["gxs"], slot_row[l], keep["info"], chosen_rows[l],
                keep["gcol"], keep["small"], keep["z"], mixes[l], gz,
            ]
            done = exchange_call(
                "backward", pack, ex,
                [keep["received"], experts_w[l], keep["gy"], keep["gate"], keep["up"]] + gating,
            )
            keep["gin"], keep["dw"] = done[:2]
            keep["gating"] = done[2:]
        gn2, gsm, mix_grads[l], gz = keep["gating"][:4]
        d_experts, gn2 = lax.optimization_barrier((keep["dw"], gn2))
        if not last:
            gn2, expert_grads[l + 1] = lax.optimization_barrier((gn2, expert_grads[l + 1]))
        expert_grads[l] = lax.psum_scatter(d_experts, "shard", scatter_dimension=0, tiled=False)
        args = [
            gx, gn2, keep["gin"], slot_col[l], keep["middle"], keep["att"], dense[l], keep["qkv"],
            keep["n1"], keep["x"], bias_t, keep["lse"], gsm,
        ]
        if l > 0:
            args += [slot_row[l - 1], saved[l - 1]["gpack"], y_held, keep["n2"], keep["gcol"]]
        outs = backward_call(l == 0, experts, slots, args)
        gx, d_dense = outs[:2]
        if l > 0:
            saved[l - 1]["gxs"], saved[l - 1]["gy"], hidden_out = outs[2:5]
        if l > 0:
            dense_grads[l] = lax.psum_scatter(d_dense, "shard", scatter_dimension=0, tiled=True)

    if pack.shards == 8 and experts == 4:
        mix = jnp.pad(jnp.concatenate(mix_grads), [(0, 0), (0, 112)])
        dense_sums, mixing_grad = finish_call(part, total_experts, d_dense, dense_grads[1], mix)
    else:
        dense_grads[0] = lax.psum_scatter(d_dense, "shard", scatter_dimension=0, tiled=True)
        dense_sums = lax.psum(jnp.stack(dense_grads), "expert")
        mixing_grad = lax.psum(jnp.stack(mix_grads), ("expert", "shard"))
        mixing_grad = mixing_grad[:, 0:total_experts, 0:total_experts]
    made = outputs_call(pack, total_experts, expert_grads, dense_sums, hidden_out)
    gate_grad, up_grad, down_grad, project_grad, output_grad = made[:5]
    gain_grad, router_grad, vector_grad, const_grad, hidden_out = made[5:]
    return (
        hidden_out,
        gx,
        gz[0:total_experts].T,
        project_grad,
        output_grad,
        gain_grad,
        router_grad.transpose(0, 2, 1),
        mixing_grad,
        vector_grad,
        const_grad.transpose(0, 1, 3, 2),
        gate_grad[:, None],
        up_grad[:, None],
        down_grad[:, None],
    )


def solution(mesh):
    both = ("expert", "shard")
    in_specs = (
        P(both, None),
        P(both, None),
        P(None, None, "shard", None),
        P(None, "shard", None),
        P(None, None, "shard"),
        P(None, "shard", None),
        P(),
        P(None, None, "shard"),
        P(None, None, "shard", None),
        P(None, "expert", "shard", None),
        P(None, "expert", "shard", None),
        P(None, "expert", "shard", None),
        P(None, both, None),
        P(both, None),
        P(both, None),
        P(both, None),
    )
    out_specs = (
        P(both, None),
        P(both, None),
        P(both, None),
        P(None, None, "shard", None),
        P(None, "shard", None),
        P(None, None, "shard"),
        P(None, "shard", None),
        P(),
        P(None, None, "shard"),
        P(None, None, "shard", None),
        P(None, "expert", "shard", None),
        P(None, "expert", "shard", None),
        P(None, "expert", "shard", None),
    )
    return jax.shard_map(
        on_device, mesh=mesh, in_specs=in_specs, out_specs=out_specs, check_vma=False
    )
```

```python
import functools

import jax
import jax.numpy as jnp
from jax import lax
from jax.experimental import pallas as pl
from jax.experimental.pallas import tpu as pltpu
from jax.sharding import PartitionSpec as P

D = 768
H = 12
HD = 64
TOP = 2
LAYERS = 2
TRUNK = 320
BRANCH = 64
LEAF = 32
TREE = 832

W_OUT = 3 * D
W_SMALL = 4 * D
W_ALL = 4 * D + 128
S_CONST = 16
S_GAIN = 24
S_VEC = 26

epsilon = 1e-06
masked_fill = -1e30
f32 = jnp.float32
bf16 = jnp.bfloat16
BLOCKS = 2
VMEM = 56 << 20


def dot(a, b):
    return jnp.dot(a, b, preferred_element_type=f32)


def dot_nt(a, b):
    return lax.dot_general(a, b, (((1,), (1,)), ((), ())), preferred_element_type=f32)


def dot_tn(a, b):
    return lax.dot_general(a, b, (((0,), (0,)), ((), ())), preferred_element_type=f32)


def split_bf16(v):
    high = v.astype(bf16)
    return high, (v - high.astype(f32)).astype(bf16)


def inv_rms(v):
    return lax.rsqrt(jnp.mean(v * v, axis=1, keepdims=True) + epsilon)


def tree_visible(parents):
    position = jnp.arange(TREE, dtype=jnp.int32)
    offset = position - TRUNK
    segment = jnp.where(
        position < TRUNK,
        0,
        jnp.where(offset < 4 * BRANCH, 1 + offset // BRANCH, 5 + (offset - 4 * BRANCH) // LEAF),
    )
    leaf_hits = (segment[:, None] - 5 == jnp.arange(8, dtype=jnp.int32)[None, :]).astype(jnp.int32)
    upper = jnp.where(segment >= 5, 1 + jnp.sum(leaf_hits * parents[None, :], axis=1), 0)
    key_segment = segment[None, :]
    causal = position[None, :] <= position[:, None]
    return causal & (
        (key_segment == segment[:, None]) | (key_segment == 0) | (key_segment == upper[:, None])
    )


def one_hot(slot_row, e, slots):
    row = lax.broadcasted_iota(jnp.int32, (slots, slot_row.shape[1]), 0).astype(f32)
    return jnp.where(row == slot_row[e : e + 1, :], 1.0, 0.0).astype(bf16)


def one_hot_col(slot_col, e, slots, scale=None):
    lane = lax.broadcasted_iota(jnp.int32, (slot_col.shape[0], slots), 1).astype(f32)
    value = 1.0 if scale is None else scale
    return jnp.where(lane == slot_col[:, e : e + 1], value, 0.0).astype(bf16)


def combine_rows(rows, middle_ref, n2_ref, y_ref, gcol_ref, slotc_ref, vectors, experts, slots):
    gcol = gcol_ref[rows, :]
    slot = slotc_ref[rows, :]
    total = middle_ref[rows, :] + gcol[:, 16:17] * n2_ref[rows, :].astype(f32)
    for c in range(2):
        total = total + gcol[:, 17 + c : 18 + c] * vectors[c : c + 1, :]
    for e in range(experts):
        weight = one_hot_col(slot, e, slots, gcol[:, e : e + 1])
        total = total + dot(weight, y_ref[e * slots : (e + 1) * slots, :])
    return total


def all_one_hot(slot_row, experts, slots):
    return jnp.concatenate([one_hot(slot_row, e, slots) for e in range(experts)], axis=0)


def send_grads(hot, gx, gpack, gxs_ref, gy_ref, experts, slots):
    got = dot(hot, gx)
    gates = dot(hot, gpack)
    if gxs_ref is not None:
        gxs_ref[...] = got.astype(bf16)
    for e in range(experts):
        rows = slice(e * slots, (e + 1) * slots)
        gate = gates[rows, e : e + 1] + gates[rows, 64 + e : 65 + e]
        gy_ref[rows, :] = (got[rows, :] * gate).astype(bf16)


def row_blocks(tokens):
    size = tokens // BLOCKS
    return size, lambda i: pl.ds(pl.multiple_of(i * size, 16), size)


def causal_spans(tokens):
    edges = [0, 256, 512, tokens]
    return list(zip(edges[:-1], edges[1:]))


def forward_kernel(first, last, experts, slots, traffic, *refs):
    refs = list(refs)
    if first:
        x_in = refs.pop(0)
    else:
        mid_prev, n2_prev, y_ref, gcol_prev, slotc_prev, w_prev = [refs.pop(0) for _ in range(6)]
    w_ref, bias_ref, z_ref, mixt_ref, chosen_ref, slotr_ref = [refs.pop(0) for _ in range(6)]
    if last:
        cot_ref = refs.pop(0)
    if not first:
        x_out = refs.pop(0)
    n1_ref, qkv_ref, att_ref, lse_ref, mid_ref, n2_ref, info_ref, gcol_ref, gpack_ref, send_ref = [
        refs.pop(0) for _ in range(10)
    ]
    small_out, z_out = refs.pop(0), refs.pop(0)
    small_out[...] = w_ref[:, W_SMALL:]
    if last:
        gy_ref = refs.pop(0)
    lse_cols, turn = refs
    tokens = n1_ref.shape[0]
    size, block = row_blocks(tokens)
    small = w_ref[:, W_SMALL:].astype(f32).T
    gain0 = small[S_GAIN : S_GAIN + 1, :]
    gain1 = small[S_GAIN + 1 : S_GAIN + 2, :]
    if not first:
        vectors_prev = w_prev[...].astype(f32).T[S_VEC : S_VEC + 2, :]

    def project(i, carry):
        rows = block(i)
        if first:
            x = x_in[rows, :].astype(f32)
        else:
            x = combine_rows(
                rows, mid_prev, n2_prev, y_ref, gcol_prev, slotc_prev, vectors_prev, experts, slots
            )
            x_out[rows, :] = x
        n1 = (x * inv_rms(x) * gain0).astype(bf16)
        n1_ref[rows, :] = n1
        for c in range(3):
            qkv_ref[rows, c * D : (c + 1) * D] = dot(n1, w_ref[:, c * D : (c + 1) * D]).astype(bf16)
        return carry

    lax.fori_loop(0, BLOCKS, project, 0)
    if not first:
        traffic.flush(x_out)
    traffic.flush(n1_ref)
    traffic.flush(qkv_ref)
    traffic.need(bias_ref)
    lane = lax.broadcasted_iota(jnp.int32, (1, 128), 1)
    low_f = jnp.where(lane < HD, 1.0, 0.0)
    low = low_f.astype(bf16)
    high = (1.0 - low_f).astype(bf16)
    lse_cols[...] = jnp.zeros_like(lse_cols)

    def pair(p, carry):
        k = qkv_ref[:, pl.ds(pl.multiple_of(D + p * 128, 128), 128)]
        v = qkv_ref[:, pl.ds(pl.multiple_of(2 * D + p * 128, 128), 128)]
        va = v * low + high
        vb = v * high + low
        here = pl.ds(pl.multiple_of(p * 128, 128), 128)
        spans = causal_spans(tokens)
        scores = []
        for start, stop in spans:
            q = qkv_ref[start:stop, here] * bf16(HD**-0.5)
            scores.append(
                [dot_nt(q * mask, k[:stop]) + bias_ref[start:stop, :stop] for mask in (low, high)]
            )
        for (start, stop), pairs in zip(spans, scores):
            peaks = [jnp.max(one, axis=1, keepdims=True) for one in pairs]
            expos = [jnp.exp(one - peak).astype(bf16) for one, peak in zip(pairs, peaks)]
            outs = [
                (dot(expo, value[:stop]), peak)
                for expo, value, peak in zip(expos, (va, vb), peaks)
            ]
            (oa, ma), (ob, mb) = outs
            numer = jnp.where(lane < HD, oa, ob)
            denom = pltpu.roll(jnp.where(lane < HD, ob, oa), HD, 1)
            att_ref[start:stop, here] = (numer / denom).astype(bf16)
            la = ma + jnp.log(oa[:, HD : HD + 1])
            lb = mb + jnp.log(ob[:, 0:1])
            old = lse_cols[start:stop, :]
            lse_cols[start:stop, :] = jnp.where(
                lane == 2 * p, la, jnp.where(lane == 2 * p + 1, lb, old)
            )
        return carry

    lax.fori_loop(0, H // 2, pair, 0)
    traffic.flush(att_ref)
    lse_ref[...] = lse_cols[...].T[0:16, :]

    def finish(i, carry):
        rows = block(i)
        if first:
            x = x_in[rows, :].astype(f32)
        else:
            x = x_out[rows, :]
        middle = x + dot(att_ref[rows, :], w_ref[:, W_OUT:W_SMALL])
        mid_ref[rows, :] = middle
        n2_ref[rows, :] = (middle * inv_rms(middle) * gain1).astype(bf16)
        return carry

    lax.fori_loop(0, BLOCKS, finish, 0)
    traffic.flush(mid_ref)
    traffic.flush(n2_ref)
    n2 = n2_ref[...]
    scores = dot_nt(small[0:32, :].astype(bf16), n2)
    logits = scores[0:16, :]
    z = z_ref[...]
    mixt = mixt_ref[...]
    for i in range(experts + 4):
        logits = logits + mixt[:, i : i + 1] * z[i : i + 1, :]
    row = lax.broadcasted_iota(jnp.int32, (16, tokens), 0)
    valid = row < experts + 4
    peak = jnp.max(jnp.where(valid, logits, masked_fill), axis=0, keepdims=True)
    expo = jnp.where(valid, jnp.exp(jnp.minimum(logits - peak, 0.0)), 0.0)
    prob = expo / jnp.sum(expo, axis=0, keepdims=True)
    gates = prob * chosen_ref[...]
    info_ref[0:16, :] = logits
    z_out[...] = logits
    info_ref[16:32, :] = prob
    turn[...] = jnp.zeros_like(turn)
    turn[0:16, 0:tokens] = gates
    own = gates[experts + 1 : experts + 2, :]
    alphas = []
    for c in range(2):
        l0 = scores[S_CONST + 2 * c : S_CONST + 2 * c + 1, :]
        l1 = scores[S_CONST + 2 * c + 1 : S_CONST + 2 * c + 2, :]
        a0 = jax.nn.sigmoid(l0 - l1)
        a1 = jax.nn.sigmoid(l1 - l0)
        alphas += [a0, a1]
        share = gates[experts + 2 + c : experts + 3 + c, :]
        own = own + share * a0
        turn[17 + c : 18 + c, 0:tokens] = share * a1
    turn[16:17, 0:tokens] = own
    zero_row = jnp.zeros((4, tokens), f32)
    info_ref[32:40, :] = jnp.concatenate(alphas + [zero_row], axis=0)
    gcol = turn[...].T[0:tokens, :]
    gcol_ref[...] = gcol
    upper, lower = split_bf16(jnp.where(lane < 16, gcol, 0.0))
    gpack = upper + pltpu.roll(lower.astype(f32), 64, 1).astype(bf16)
    gpack_ref[...] = gpack
    hot = all_one_hot(slotr_ref[...], experts, slots)
    send_ref[...] = dot(hot, n2).astype(bf16)
    if last:
        traffic.need(cot_ref)
        send_grads(hot, cot_ref[...], gpack, None, gy_ref, experts, slots)


def shape(dims, dtype=f32):
    return jax.ShapeDtypeStruct(tuple(dims), dtype)


class Traffic:
    def __init__(self):
        self.fetches, self.sinks, self.flushes = {}, {}, []

    def fetch(self, src, buffer, sem):
        copy = pltpu.make_async_copy(src, buffer, sem)
        copy.start()
        self.fetches[id(buffer)] = copy

    def need(self, *buffers):
        for buffer in buffers:
            copy = self.fetches.pop(id(buffer), None)
            if copy is not None:
                copy.wait()

    def sink(self, buffer, dst, sems):
        self.sinks[id(buffer)] = [dst, sems, 0]

    def flush(self, buffer, part=None):
        entry = self.sinks.get(id(buffer))
        if entry is None:
            return
        dst, sems, used = entry
        entry[2] += 1
        src, dst = (buffer, dst) if part is None else (buffer.at[part], dst.at[part])
        copy = pltpu.make_async_copy(src, dst, sems.at[used])
        copy.start()
        self.flushes.append(copy)

    def finish(self):
        for copy in self.flushes:
            copy.wait()


FLUSHES = 3


def whole_call(body, name, outs, scratch, args, flops, late=(), early=(), raw=(), collective=None):
    moved = sum(a.size * a.dtype.itemsize for a in args) + sum(
        o.size * o.dtype.itemsize for o in outs
    )
    late, early = sorted(late), sorted(early)

    def kernel(*refs):
        ins, rest = list(refs[: len(args)]), refs[len(args) :]
        results, rest = list(rest[: len(outs)]), rest[len(outs) :]
        own, rest = rest[: len(scratch)], rest[len(scratch) :]
        traffic = Traffic()
        fetch_sems, flush_sems = rest[len(late) + len(early) :]
        for n, at in enumerate(late):
            traffic.fetch(ins[at], rest[n], fetch_sems.at[n])
            ins[at] = rest[n]
        for n, at in enumerate(early):
            buffer = rest[len(late) + n]
            traffic.sink(buffer, results[at], flush_sems.at[n])
            results[at] = buffer
        body(traffic, *ins, *results, *own)
        traffic.finish()

    near, far = pl.BlockSpec(memory_space=pltpu.VMEM), pl.BlockSpec(memory_space=pl.ANY)
    buffers = [pltpu.VMEM(args[at].shape, args[at].dtype) for at in late]
    buffers += [pltpu.VMEM(outs[at].shape, outs[at].dtype) for at in early]
    buffers.append(pltpu.SemaphoreType.DMA((max(len(late), 1),)))
    buffers.append(pltpu.SemaphoreType.DMA((max(len(early), 1), FLUSHES)))
    return pl.pallas_call(
        kernel,
        out_shape=outs,
        in_specs=[far if n in late or n in raw else near for n in range(len(args))],
        out_specs=[far if n in early else near for n in range(len(outs))],
        scratch_shapes=list(scratch) + buffers,
        compiler_params=pltpu.CompilerParams(
            vmem_limit_bytes=VMEM,
            collective_id=collective,
            has_side_effects=collective is not None,
        ),
        cost_estimate=pl.CostEstimate(flops=flops, bytes_accessed=moved, transcendentals=0),
        name=name,
    )(*args)


def forward_call(first, last, experts, slots, args):
    tokens = TREE
    sent = experts * slots
    outs = [] if first else [shape((tokens, D))]
    outs += [
        shape((tokens, D), bf16),
        shape((tokens, 3 * D), bf16),
        shape((tokens, D), bf16),
        shape((16, tokens)),
        shape((tokens, D)),
        shape((tokens, D), bf16),
        shape((40, tokens)),
        shape((tokens, 128)),
        shape((tokens, 128), bf16),
        shape((sent, D), bf16),
        shape((D, 128), bf16),
        shape((16, tokens)),
    ]
    if last:
        outs += [shape((sent, D), bf16)]
    padded = -(-tokens // 128) * 128
    scratch = [pltpu.VMEM((tokens, 128), f32), pltpu.VMEM((128, padded), f32)]
    body = functools.partial(forward_kernel, first, last, experts, slots)
    inputs, results = (1, 0) if first else (6, 1)
    late = [inputs + 1] + ([inputs + 6] if last else [])
    early = ([] if first else [0]) + [results + n for n in (0, 1, 2, 4, 5)]
    return whole_call(body, "block_forward", outs, scratch, args, 20 * 10**9, late, early)


def row_dots(a, b):
    ones = jnp.ones((16, D), bf16)
    upper, lower = split_bf16(a.astype(f32) * b.astype(f32))
    return (dot_nt(ones, upper) + dot_nt(ones, lower))[0:8, :]


def gating_kernel(last, experts, slots, *refs):
    refs = list(refs)
    gx_ref, n2_ref = refs.pop(0), refs.pop(0)
    if last:
        dots_ref = refs.pop(0)
    else:
        y_ref, gxs_ref = refs.pop(0), refs.pop(0)
    slotr_ref, info_ref, chosen_ref, gcol_ref, small_ref, z_ref, mix_ref = [
        refs.pop(0) for _ in range(7)
    ]
    if not last:
        gz_ref = refs.pop(0)
    gn2_ref, gsm_ref, gmix_ref, gprev_ref = refs
    tokens = n2_ref.shape[0]
    size, block = row_blocks(tokens)
    small = small_ref[...].astype(f32).T
    small_half = small[0:32, :].astype(bf16)
    slot_row = slotr_ref[...]
    ones = jnp.ones((16, D), bf16)
    row = lax.broadcasted_iota(jnp.int32, (16, slots), 0)
    scattered = jnp.zeros((16, tokens), f32)
    for e in range(experts):
        if last:
            half = Exchange(experts, slots).half
            sums = jnp.concatenate(
                [dots_ref[0, e, 0:1, 0:half], dots_ref[1, e, 0:1, 0 : slots - half]], axis=1
            )
        else:
            rows = slice(e * slots, (e + 1) * slots)
            sums = row_dots(y_ref[rows, :], gxs_ref[rows, :])[0:1, :]
        upper, lower = split_bf16(sums)
        lhs = jnp.where(row == e, upper.astype(f32), 0.0) + jnp.where(
            row == 8 + e, lower.astype(f32), 0.0
        )
        scattered = scattered + dot(lhs.astype(bf16), one_hot(slot_row, e, slots))
    gx = gx_ref[...].astype(f32)
    gx_half = gx.astype(bf16)
    n2 = n2_ref[...]
    upper, lower = split_bf16(gx * n2.astype(f32))
    gx_n2 = (dot_nt(ones, upper) + dot_nt(ones, lower))[0:1, :]
    gx_small = dot_nt(small_half, gx_half)
    prob = info_ref[16:32, :]
    chosen = chosen_ref[...]
    gates = prob * chosen
    trow = lax.broadcasted_iota(jnp.int32, (16, tokens), 0)
    gp = jnp.concatenate([scattered[0:8, :] + scattered[8:16, :], jnp.zeros((8, tokens), f32)], 0)
    weighted = gp if last else prob * gp
    weighted = jnp.where(trow < experts, weighted, 0.0) * chosen
    gp = jnp.where(trow == experts + 1, gx_n2, 0.0)
    crow = lax.broadcasted_iota(jnp.int32, (8, tokens), 0)
    glog = jnp.zeros((8, tokens), f32)
    coefs = jnp.zeros((8, tokens), f32)
    for c in range(2):
        a0 = info_ref[32 + 2 * c : 33 + 2 * c, :]
        a1 = info_ref[33 + 2 * c : 34 + 2 * c, :]
        gx_v = gx_small[S_VEC + c : S_VEC + c + 1, :]
        share = gates[experts + 2 + c : experts + 3 + c, :]
        gp = jnp.where(trow == experts + 2 + c, a0 * gx_n2 + a1 * gx_v, gp)
        gl = share * (gx_n2 - gx_v) * a0 * a1
        glog = jnp.where(crow == 2 * c, gl, jnp.where(crow == 2 * c + 1, -gl, glog))
        coefs = jnp.where(crow == c, share * a1, coefs)
    weighted = weighted + prob * gp * chosen
    gz = weighted - prob * jnp.sum(weighted, axis=0, keepdims=True)
    if not last:
        gz = gz + gz_ref[...]
    z = z_ref[...]
    gmix_ref[...] = lax.dot_general(
        z, gz, (((1,), (1,)), ((), ())), precision=lax.Precision.HIGHEST, preferred_element_type=f32
    )
    mix = mix_ref[...]
    gprev = jnp.zeros((16, tokens), f32)
    for o in range(experts + 4):
        gprev = gprev + mix[:, o : o + 1] * gz[o : o + 1, :]
    gprev_ref[...] = gprev
    allg = jnp.concatenate([gz, glog, jnp.zeros((8, tokens), f32)], axis=0)
    upper, lower = split_bf16(allg)
    gsm = dot(upper, n2) + dot(lower, n2)
    cu, cl = split_bf16(jnp.concatenate([coefs, jnp.zeros((8, tokens), f32)], axis=0))
    gvec = dot(cu, gx_half) + dot(cl, gx_half)
    gsm_ref[0:24, :] = gsm[0:24, :]
    gsm_ref[24:32, :] = jnp.concatenate(
        [jnp.zeros((2, D), f32), gvec[0:2, :], jnp.zeros((4, D), f32)], axis=0
    )
    both = jnp.concatenate([upper, lower], axis=0)
    twice = jnp.concatenate([small_half, small_half], axis=0)
    gn2_ref[...] = dot_tn(both, twice)

    def add(i, carry):
        rows = block(i)
        gn2_ref[rows, :] = gn2_ref[rows, :] + gcol_ref[rows, 16:17] * gx_ref[rows, :].astype(f32)
        return carry

    lax.fori_loop(0, BLOCKS, add, 0)


def gating_outputs():
    tokens = TREE
    return [shape((tokens, D)), shape((32, D)), shape((16, 16)), shape((16, tokens))]


def backward_kernel(first, experts, slots, traffic, *refs):
    refs = list(refs)
    gx_ref, gn2p_ref, gn2e_ref, slotc_ref, mid_ref, att_ref, w_ref, qkv_ref, n1_ref, x_ref = [
        refs.pop(0) for _ in range(10)
    ]
    biast_ref, lse_ref, gsm_ref = [refs.pop(0) for _ in range(3)]
    if not first:
        slotr_ref, gpack_ref = refs.pop(0), refs.pop(0)
        y_held, n2_ref, gcol_ref = refs.pop(0), refs.pop(0), refs.pop(0)
    gout_ref, dw_ref = refs.pop(0), refs.pop(0)
    if not first:
        gxs_ref, gy_ref, hidden_out = refs.pop(0), refs.pop(0), refs.pop(0)
    gatt, go, gqkv, turn = refs[:4]
    if not first:
        y_home, y_sends, y_recvs, y_local = refs[4:]
        ex = Exchange(experts, slots)
        own = pltpu.make_async_copy(
            y_held.at[pl.ds(0, slots)], y_home.at[own_slots(ex)], y_local
        )
        own.start()
        greet(experts)
        returning = []
        for wave in range(len(ex.waves)):
            returning += back_copies(ex, wave, 0, y_held, y_home, y_sends, y_recvs)
        for copy in returning:
            copy.start()
    tokens = n1_ref.shape[0]
    size, block = row_blocks(tokens)
    small = w_ref[:, W_SMALL:].astype(f32).T
    gain0 = small[S_GAIN : S_GAIN + 1, :]
    gain1 = small[S_GAIN + 1 : S_GAIN + 2, :]

    def enter(i, total):
        rows = block(i)
        gn2 = gn2p_ref[rows, :]
        slot = slotc_ref[rows, :]
        for e in range(experts):
            gn2 = gn2 + dot(one_hot_col(slot, e, slots), gn2e_ref[e * slots : (e + 1) * slots, :])
        middle = mid_ref[rows, :]
        r = inv_rms(middle)
        scaled = gain1 * gn2
        inner = jnp.mean(middle * scaled, axis=1, keepdims=True)
        gmid = gx_ref[rows, :].astype(f32) + r * scaled - middle * (r * r * r * inner)
        gout_ref[rows, :] = gmid
        half = gmid.astype(bf16)
        gatt[rows, :] = half
        go[rows, :] = dot_nt(half, w_ref[:, W_OUT:W_SMALL]).astype(bf16)
        return total + jnp.sum(gn2 * middle * r, axis=0, keepdims=True)

    ggain1 = lax.fori_loop(0, BLOCKS, enter, jnp.zeros((1, D), f32))
    traffic.need(att_ref)
    lane = lax.broadcasted_iota(jnp.int32, (1, 128), 1)
    low_f = jnp.where(lane < HD, 1.0, 0.0)
    low = low_f.astype(bf16)
    high = (1.0 - low_f).astype(bf16)
    scale = HD**-0.5

    def out_grad(p, carry):
        here = pl.ds(pl.multiple_of(p * 128, 128), 128)
        dw_ref[here, W_OUT:W_SMALL] = dot_tn(att_ref[:, here], gatt[...]).astype(bf16)
        return carry

    lax.fori_loop(0, D // 128, out_grad, 0)
    traffic.flush(dw_ref, (slice(None), slice(W_OUT, W_SMALL)))
    traffic.need(qkv_ref, biast_ref, lse_ref)
    spans = causal_spans(tokens)

    def pair(p, carry):
        here = pl.ds(pl.multiple_of(p * 128, 128), 128)
        lanes_k = pl.ds(pl.multiple_of(D + p * 128, 128), 128)
        lanes_v = pl.ds(pl.multiple_of(2 * D + p * 128, 128), 128)
        q = qkv_ref[:, here] * bf16(scale)
        k = qkv_ref[:, lanes_k]
        v = qkv_ref[:, lanes_v]
        g = go[:, here]
        turn[0:tokens, :] = g.astype(f32) * att_ref[:, here].astype(f32)
        inner = turn[...].T[:, 0:tokens]
        turn[0:tokens, :] = k.astype(f32)
        kt = turn[...].T[:, 0:tokens].astype(bf16)
        gk = [0.0] * len(spans)
        gv = [0.0] * len(spans)
        masks = (low, high)
        qs = [q * mask for mask in masks]
        gs = [g * mask for mask in masks]
        dsums = [
            jnp.sum(inner[h * HD : (h + 1) * HD, :], axis=0, keepdims=True) for h in range(2)
        ]
        lses = [lse_ref[pl.ds(2 * p + h, 1), :] for h in range(2)]
        parts = [[], []]
        for n, (start, stop) in enumerate(spans):
            st = [
                dot_nt(k[start:stop], qs[h][start:]) + biast_ref[start:stop, start:]
                for h in range(2)
            ]
            gpt = [dot_nt(v[start:stop], gs[h][start:]) for h in range(2)]
            pt = [jnp.exp(st[h] - lses[h][:, start:]) for h in range(2)]
            gst = [(pt[h] * (gpt[h] - dsums[h][:, start:])).astype(bf16) for h in range(2)]
            for h in range(2):
                gv[n] = gv[n] + dot(pt[h].astype(bf16), gs[h][start:])
                gk[n] = gk[n] + dot(gst[h], qs[h][start:])
                parts[h].append(dot(kt[h * HD : (h + 1) * HD, start:stop], gst[h]))
        gq_t = []
        for h in range(2):
            cols = []
            for n, (start, stop) in enumerate(spans):
                piece = 0.0
                for m in range(n + 1):
                    origin = spans[m][0]
                    piece = piece + parts[h][m][:, start - origin : stop - origin]
                cols.append(piece)
            gq_t.append(jnp.concatenate(cols, axis=1))
        turn_t = jnp.concatenate(gq_t, axis=0) * scale
        pad = turn.shape[0] - tokens
        turn_t = jnp.concatenate([turn_t, jnp.zeros((128, pad), f32)], axis=1)
        gqkv[:, here] = turn_t.T[0:tokens, :].astype(bf16)
        for n, (start, stop) in enumerate(spans):
            gqkv[start:stop, lanes_k] = gk[n].astype(bf16)
            gqkv[start:stop, lanes_v] = gv[n].astype(bf16)
        return carry

    turn[...] = jnp.zeros_like(turn)
    lax.fori_loop(0, H // 2, pair, 0)
    traffic.need(n1_ref)

    def in_grad(p, carry):
        here = pl.ds(pl.multiple_of(p * 128, 128), 128)
        dw_ref[here, 0:W_OUT] = dot_tn(n1_ref[:, here], gqkv[...]).astype(bf16)
        return carry

    lax.fori_loop(0, D // 128, in_grad, 0)
    traffic.flush(dw_ref, (slice(None), slice(0, W_OUT)))
    traffic.need(x_ref)

    def leave(i, total):
        rows = block(i)
        gn1 = dot_nt(gqkv[rows, :], w_ref[:, 0:W_OUT])
        x = x_ref[rows, :].astype(f32)
        r = inv_rms(x)
        scaled = gain0 * gn1
        inner = jnp.mean(x * scaled, axis=1, keepdims=True)
        gx = gout_ref[rows, :] + r * scaled - x * (r * r * r * inner)
        gout_ref[rows, :] = gx
        gatt[rows, :] = gx.astype(bf16)
        return total + jnp.sum(gn1 * x * r, axis=0, keepdims=True)

    ggain0 = lax.fori_loop(0, BLOCKS, leave, jnp.zeros((1, D), f32))
    rows = jnp.concatenate(
        [gsm_ref[0:24, :], ggain0, ggain1, gsm_ref[26:32, :], jnp.zeros((96, D), f32)], axis=0
    )
    dw_ref[:, W_SMALL:] = rows.T.astype(bf16)
    traffic.flush(dw_ref, (slice(None), slice(W_SMALL, W_ALL)))
    traffic.flush(gout_ref)
    if not first:
        hot = all_one_hot(slotr_ref[...], experts, slots)
        send_grads(hot, gatt[...], gpack_ref[...], gxs_ref, gy_ref, experts, slots)
        own.wait()
        for copy in returning:
            copy.wait()
        traffic.need(n2_ref, gcol_ref)
        vectors = small[S_VEC : S_VEC + 2, :]

        def home(i, carry):
            rows = block(i)
            hidden_out[rows, :] = combine_rows(
                rows, mid_ref, n2_ref, y_home, gcol_ref, slotc_ref, vectors, experts, slots
            ).astype(bf16)
            return carry

        lax.fori_loop(0, BLOCKS, home, 0)


def backward_call(first, experts, slots, args):
    tokens = TREE
    sent = experts * slots
    outs = [shape((tokens, D)), shape((D, W_ALL), bf16)]
    if not first:
        outs += [shape((sent, D), bf16)] * 2 + [shape((tokens, D), bf16)]
    padded = -(-tokens // 128) * 128
    scratch = [
        pltpu.VMEM((tokens, D), bf16),
        pltpu.VMEM((tokens, D), bf16),
        pltpu.VMEM((tokens, 3 * D), bf16),
        pltpu.VMEM((padded, 128), f32),
    ]
    body = functools.partial(backward_kernel, first, experts, slots)
    late = (5, 7, 8, 9, 10, 11)
    if first:
        return whole_call(body, "block_backward", outs, scratch, args, 40 * 10**9, late, (0, 1))
    count = len(Exchange(experts, slots).waves)
    scratch.append(pltpu.VMEM((sent, D), bf16))
    scratch += [pltpu.SemaphoreType.DMA((1, count, experts - 1))] * 2
    scratch.append(pltpu.SemaphoreType.DMA)
    late += (16, 17)
    return whole_call(
        body, "block_backward", outs, scratch, args, 40 * 10**9, late, (0, 1), (15,), 5
    )


class Packing:
    def __init__(self, shards, part, ff):
        self.shards, self.part, self.ff = shards, part, ff
        self.padded = -(-part // 16) * 16
        self.chunks = ff // 256
        self.own = ff // shards
        self.down = 2 * self.chunks * self.padded
        self.rows = self.down + (D // 256) * self.own

    def pack(self, gate, up, down):
        pieces = []
        for wide in (gate, up):
            cut = wide.reshape(self.part, self.chunks, 256).transpose(1, 0, 2)
            cut = jnp.pad(cut, [(0, 0), (0, self.padded - self.part), (0, 0)])
            pieces.append(cut.reshape(self.chunks * self.padded, 256))
        pieces.append(
            down.reshape(self.own, D // 256, 256).transpose(1, 0, 2).reshape(-1, 256)
        )
        return jnp.concatenate(pieces, axis=0)

    def wide_part(self, ref, n, j):
        at = pl.multiple_of((n * self.chunks + j) * self.padded, 16)
        return ref[:, pl.ds(at, self.padded), :][:, : self.part, :].reshape(D, 256)

    def tall_part(self, ref, j):
        group = 256 // self.own
        here = pl.ds(j * group, group)
        pieces = []
        for c in range(D // 256):
            at = self.down + c * self.own
            pieces.append(ref[here, at : at + self.own, :].reshape(256, 256))
        return jnp.concatenate(pieces, axis=1)

    def put_wide(self, ref, n, j, grad):
        at = pl.multiple_of((n * self.chunks + j) * self.padded, 16)
        ref[:, pl.ds(at, self.part), :] = grad.reshape(self.shards, self.part, 256)

    def put_tall(self, ref, j, grad):
        group = 256 // self.own
        for c in range(D // 256):
            at = self.down + c * self.own
            ref[pl.ds(j * group, group), at : at + self.own, :] = grad[
                :, c * 256 : (c + 1) * 256
            ].reshape(group, self.own, 256)


class Exchange:
    def __init__(self, experts, slots):
        self.experts, self.slots = experts, slots
        half = -(-slots // 32) * 16
        quarter = -(-half // 32) * 16
        self.half = half
        edges = (0, quarter, half, slots)
        self.waves = tuple((low, high - low) for low, high in zip(edges[:-1], edges[1:]))
        self.ranges = [(0, slots)]
        for _, size in self.waves:
            start = self.ranges[-1][0] + self.ranges[-1][1]
            self.ranges.append((start, (experts - 1) * size))
        self.total = experts * slots

    def span(self, group):
        start = self.ranges[1 + group[0]][0]
        return start, sum(self.ranges[1 + wave][1] for wave in group)

    def held(self, wave, d):
        size = self.waves[wave][1]
        return pl.ds(self.ranges[1 + wave][0] + (d - 1) * size, size)

    def slot(self, device, wave):
        offset, size = self.waves[wave]
        return pl.ds(pl.multiple_of(device * self.slots + offset, 16), size)


MESH = pl.DeviceIdType.MESH


def greet(experts):
    me = lax.axis_index("expert")
    barrier = pltpu.get_barrier_semaphore()
    for d in range(1, experts):
        pl.semaphore_signal(
            barrier, inc=1, device_id={"expert": lax.rem(me + d, experts)}, device_id_type=MESH
        )
    pl.semaphore_wait(barrier, experts - 1)


def out_copies(ex, wave, src, dst, sends, recvs):
    me = lax.axis_index("expert")
    copies = []
    for d in range(1, ex.experts):
        to = lax.rem(me + d, ex.experts)
        copies.append(
            pltpu.make_async_remote_copy(
                src_ref=src.at[ex.slot(to, wave)],
                dst_ref=dst.at[ex.held(wave, d)],
                send_sem=sends.at[wave, d - 1],
                recv_sem=recvs.at[wave, d - 1],
                device_id={"expert": to},
                device_id_type=MESH,
            )
        )
    return copies


def back_copies(ex, wave, n, src, dst, sends, recvs):
    me = lax.axis_index("expert")
    copies = []
    for d in range(1, ex.experts):
        copies.append(
            pltpu.make_async_remote_copy(
                src_ref=src.at[ex.held(wave, d)],
                dst_ref=dst.at[ex.slot(me, wave)],
                send_sem=sends.at[n, wave, d - 1],
                recv_sem=recvs.at[n, wave, d - 1],
                device_id={"expert": lax.rem(me + ex.experts - d, ex.experts)},
                device_id_type=MESH,
            )
        )
    return copies


def own_slots(ex):
    me = lax.axis_index("expert")
    return pl.ds(pl.multiple_of(me * ex.slots, 16), ex.slots)


def dispatch_kernel(ex, send, recv, sends, recvs, local):
    own = pltpu.make_async_copy(send.at[own_slots(ex)], recv.at[pl.ds(0, ex.slots)], local)
    own.start()
    greet(ex.experts)
    copies = []
    for wave in range(len(ex.waves)):
        copies += out_copies(ex, wave, send, recv, sends, recvs)
    for copy in copies:
        copy.start()
    for copy in copies:
        copy.wait()
    own.wait()


def dispatch_call(ex, rows):
    far = pl.BlockSpec(memory_space=pl.ANY)
    return pl.pallas_call(
        functools.partial(dispatch_kernel, ex),
        out_shape=shape((ex.total, D), bf16),
        in_specs=[far],
        out_specs=far,
        scratch_shapes=[pltpu.SemaphoreType.DMA((len(ex.waves), ex.experts - 1))] * 2
        + [pltpu.SemaphoreType.DMA],
        compiler_params=pltpu.CompilerParams(
            vmem_limit_bytes=60 << 20, collective_id=3, has_side_effects=True
        ),
        cost_estimate=pl.CostEstimate(flops=35 * 10**9, bytes_accessed=10**6, transcendentals=0),
        name="dispatch",
    )(rows)


def exchange_kernel(mode, pack, ex, *refs):
    refs = list(refs)
    forward, backward = mode in ("forward", "both"), mode in ("backward", "both")
    recv_n = refs.pop(0)
    w_hbm = refs.pop(0)
    if backward:
        send_g = refs.pop(0)
        if mode == "backward":
            gate_hbm, up_hbm = refs.pop(0), refs.pop(0)
        inputs = 9 if mode == "both" else 12
        gating_far = [refs.pop(0) for _ in range(inputs)]
    if mode == "forward":
        back_y = refs.pop(0)
    if mode == "both":
        out_y = refs.pop(0)
    if mode == "forward":
        gates_far, ups_far, gates, ups = [refs.pop(0) for _ in range(4)]
    else:
        back_g, dw_far = refs.pop(0), refs.pop(0)
        gating_outs = [refs.pop(0) for _ in range(4)]
    if mode == "forward":
        out_y = refs.pop(0)
    if forward:
        acc_y = refs.pop(0)
    if backward:
        recv_g, out_g, hids, gates, ups, rows_t, acc_g = [refs.pop(0) for _ in range(7)]
        gating = [refs.pop(0) for _ in range(inputs)]
    if mode == "both":
        dots_out, dots, dots_send, dots_recv = [refs.pop(0) for _ in range(4)]
    w = refs.pop(0)
    sends, recvs, backs, gots, local = refs
    traffic = Traffic()
    if mode == "forward":
        traffic.sink(gates, gates_far, local.at[4:8])
        traffic.sink(ups, ups_far, local.at[8:12])

    loads = [pltpu.make_async_copy(w_hbm, w, local.at[0])]
    if mode == "backward":
        loads.append(pltpu.make_async_copy(gate_hbm, gates, local.at[1]))
        loads.append(pltpu.make_async_copy(up_hbm, ups, local.at[2]))
    if mode == "backward":
        for n, (far, near) in enumerate(zip(gating_far, gating)):
            traffic.fetch(far, near, local.at[4 + n])
    for copy in loads:
        copy.start()
    if mode == "both":
        for n, (far, near) in enumerate(zip(gating_far, gating)):
            traffic.fetch(far, near, local.at[4 + n])
    greet(ex.experts)

    def work(start, size):
        rows = slice(start, start + size)
        part = slice(0, size)
        if forward:
            acc_y[part, :] = jnp.zeros((size, D), f32)
        if backward:
            acc_g[part, :] = jnp.zeros((size, D), f32)

        def chunk(j, carry):
            lanes = pl.ds(pl.multiple_of(j * 256, 256), 256)
            gate_w, up_w = pack.wide_part(w, 0, j), pack.wide_part(w, 1, j)
            down_w = pack.tall_part(w, j)
            if forward:
                r = recv_n[rows, :]
                gate, up = dot(r, gate_w), dot(r, up_w)
                if mode == "forward":
                    gates[rows, lanes] = gate.astype(bf16)
                    ups[rows, lanes] = up.astype(bf16)
            else:
                gate, up = gates[rows, lanes].astype(f32), ups[rows, lanes].astype(f32)
            s = jax.nn.sigmoid(gate)
            act = gate * s
            hid = (act * up).astype(bf16)
            if forward:
                acc_y[part, :] = acc_y[part, :] + dot(hid, down_w)
            if backward:
                hids[rows, lanes] = hid
                ghid = dot_nt(recv_g[rows, :], down_w)
                guv = (ghid * act).astype(bf16)
                ggu = (ghid * up * (s * (1.0 + gate * (1.0 - s)))).astype(bf16)
                gates[rows, lanes] = ggu
                ups[rows, lanes] = guv
                acc_g[part, :] = acc_g[part, :] + dot_nt(ggu, gate_w) + dot_nt(guv, up_w)
            return carry

        lax.fori_loop(0, pack.chunks, chunk, 0)
        if mode == "forward":
            here = pl.ds(start, size)
            traffic.flush(gates, here)
            traffic.flush(ups, here)
        if forward:
            out_y[rows, :] = acc_y[part, :].astype(bf16)
        if backward:
            out_g[rows, :] = acc_g[part, :].astype(bf16)

    def send_dots(n, group):
        me = lax.axis_index("expert")
        for d in range(1, ex.experts):
            pieces = []
            for wave in group:
                here = ex.held(wave, d)
                pieces.append(row_dots(out_y[here, :], recv_g[here, :]))
            size = sum(ex.waves[wave][1] for wave in group)
            if size < 128:
                pieces.append(jnp.zeros((8, 128 - size), f32))
            dots_out[n, d - 1] = jnp.concatenate(pieces, axis=1)
            copy = pltpu.make_async_remote_copy(
                src_ref=dots_out.at[n, d - 1],
                dst_ref=dots.at[n, me],
                send_sem=dots_send.at[n, d - 1],
                recv_sem=dots_recv.at[n, d - 1],
                device_id={"expert": lax.rem(me + ex.experts - d, ex.experts)},
                device_id_type=MESH,
            )
            copy.start()
            dot_copies.append(copy)

    def send_back(group):
        for wave in group:
            if mode == "forward":
                ys.extend(back_copies(ex, wave, 0, out_y, back_y, backs, gots))
                for copy in ys[1 - ex.experts :]:
                    copy.start()
        for wave in group:
            if backward:
                gs.extend(back_copies(ex, wave, 1, out_g, back_g, backs, gots))
                for copy in gs[1 - ex.experts :]:
                    copy.start()

    ys, gs, dot_copies = [], [], []
    groups = ((0,), (1,), (2,)) if mode == "forward" else ((0, 1), (2,))
    if backward:
        arrivals = []
        for group in groups:
            arrivals.append([])
            for wave in group:
                arrivals[-1] += out_copies(ex, wave, send_g, recv_g, sends, recvs)
        for copy in arrivals[0]:
            copy.start()
        recv_g[0 : ex.slots, :] = send_g[own_slots(ex), :]
        if mode == "backward":
            traffic.need(*gating)
            gating_kernel(False, ex.experts, ex.slots, *gating, *gating_outs)
            for copy in arrivals[1]:
                copy.start()
    for copy in loads:
        copy.wait()
    if backward:
        work(*ex.ranges[0])
        if mode == "both":
            own_dots = row_dots(out_y[0 : ex.slots, :], recv_g[0 : ex.slots, :])
            me = lax.axis_index("expert")
            dots[0, me, :, 0 : ex.half] = own_dots[:, 0 : ex.half]
            dots[1, me, :, 0 : ex.slots - ex.half] = own_dots[:, ex.half :]
        for copy in arrivals[0]:
            copy.wait_send()
        if mode == "both":
            for copy in arrivals[1]:
                copy.start()
        for copy in arrivals[0]:
            copy.wait_recv()
    for n, group in enumerate(groups):
        if backward and n > 0:
            for copy in arrivals[n]:
                copy.wait()
        work(*ex.span(group))
        if mode == "both":
            send_dots(n, group)
        send_back(group)
    if mode == "forward":
        work(*ex.ranges[0])
        back_y[own_slots(ex), :] = out_y[0 : ex.slots, :]
    if backward:
        back_g[own_slots(ex), :] = out_g[0 : ex.slots, :]
        rows_t[...] = recv_n[...].T
        dw = w
        if pack.padded != pack.part:
            dw[...] = jnp.zeros_like(dw)

        def weights(j, carry):
            lanes = pl.ds(pl.multiple_of(j * 256, 256), 256)
            pack.put_wide(dw, 0, j, dot(rows_t[...], gates[:, lanes]).astype(bf16))
            pack.put_wide(dw, 1, j, dot(rows_t[...], ups[:, lanes]).astype(bf16))
            pack.put_tall(dw, j, dot_tn(hids[:, lanes], recv_g[...]).astype(bf16))
            return carry

        lax.fori_loop(0, pack.chunks, weights, 0)
        leaving = pltpu.make_async_copy(dw, dw_far, local.at[3])
        leaving.start()
    for copy in ys + dot_copies:
        copy.wait()
    if mode == "both":
        traffic.need(*gating)
        gating_kernel(True, ex.experts, ex.slots, *gating[:2], dots, *gating[2:], *gating_outs)
    for copy in gs:
        copy.wait()
    if backward:
        leaving.wait()
    traffic.finish()


SPLIT = 13 * 128
QUARTER = 7 * 128


def cube_kernel(part, labels, g_ref, upper_ref, mix_ref, ready, mix_out, own, *refs):
    got_c, sums, got_a, got_b, half_a, half_b, end_a, end_b, mine, quarters, mix_held, mix_got = refs[:12]
    send, recv, z_send, z_recv, mix_send, mix_recv, own_sem = refs[12:]
    me = lax.axis_index("shard")
    z = lax.axis_index("expert")
    owners = quarters.shape[1]
    core, x, y = lax.rem(me, 2), lax.rem(me // 2, 2), me // 4
    near, over_x, over_y = me + 1 - 2 * core, me + 2 - 4 * x, me + 4 - 8 * y
    chips = [2 * (1 - y) + 1 - x, 2 * y + 1 - x, 2 * (1 - y) + x, 2 * y + x]

    def rows(shard):
        return pl.ds(pl.multiple_of(shard * part, 16), part)

    loads = [
        pltpu.make_async_copy(g_ref.at[rows(2 * chip + core)], own.at[n], own_sem.at[n])
        for n, chip in enumerate(chips)
    ]
    for load in loads:
        load.start()
    barrier = pltpu.get_barrier_semaphore()
    for other in (near, over_x, over_y):
        pl.semaphore_signal(barrier, inc=1, device_id={"shard": other}, device_id_type=MESH)
    for d in range(1, owners):
        pl.semaphore_signal(
            barrier, inc=1, device_id={"expert": lax.rem(z + d, owners)}, device_id_type=MESH
        )
    pl.semaphore_wait(barrier, 3 + owners - 1)
    cols_a, cols_b = slice(0, SPLIT), slice(SPLIT, W_ALL)

    def remote(src, dst, send_sem, recv_sem, to):
        made = pltpu.make_async_remote_copy(
            src_ref=src,
            dst_ref=dst,
            send_sem=send_sem,
            recv_sem=recv_sem,
            device_id=to,
            device_id_type=MESH,
        )
        made.start()
        return made

    def copy(n, src, dst, to):
        return remote(src, dst, send.at[n], recv.at[n], {"shard": to})

    half = part // 2
    jobs = ((1, 0, part), (0, 0, half), (0, half, half))

    def quarter(job, owner):
        l, start, size = jobs[job]
        return l, pl.ds(start, size), pl.ds(pl.multiple_of(owner * QUARTER, 128), QUARTER)

    def spread(job):
        made = []
        held = pl.ds(0, jobs[job][2])
        for d in range(1, owners):
            to = lax.rem(z + d, owners)
            made.append(
                remote(
                    mine.at[quarter(job, to)],
                    quarters.at[job, z, held],
                    z_send.at[job, 0, d - 1],
                    z_recv.at[job, 0, d - 1],
                    {"expert": to},
                )
            )
        quarters[job, z, held] = mine[quarter(job, z)]
        return made

    def gather(job, made):
        for one in made:
            one.wait_recv()
        held = pl.ds(0, jobs[job][2])
        total = quarters[job, 0, held].astype(f32)
        for owner in range(1, owners):
            total = total + quarters[job, owner, held].astype(f32)
        here = quarter(job, z)
        ready[here] = total.astype(bf16)
        return [
            remote(
                ready.at[here],
                ready.at[here],
                z_send.at[job, 1, d - 1],
                z_recv.at[job, 1, d - 1],
                {"expert": lax.rem(z + d, owners)},
            )
            for d in range(1, owners)
        ]

    pairs = [{"shard": near}, {"shard": over_x}, {"shard": over_y}]
    pairs += [{"expert": z + 1 - 2 * lax.rem(z, 2)}, {"expert": z + 2 - 4 * (z // 2)}]
    mix_held[0] = mix_ref[...]

    def mix_start(n):
        return remote(mix_held.at[n], mix_got.at[n], mix_send.at[n], mix_recv.at[n], pairs[n])

    def mix_end(n, made):
        made.wait_recv()
        total = mix_held[n] + mix_got[n]
        if n + 1 < len(pairs):
            mix_held[n + 1] = total
        else:
            for l in range(LAYERS):
                mix_out[l] = total[l * 16 : l * 16 + labels, 0:labels]

    def begin(h):
        shift = h * half
        return [
            copy(
                10 * h + n,
                g_ref.at[pl.ds(pl.multiple_of((2 * chip + 1 - core) * part + shift, 16), half)],
                got_c.at[chip, pl.ds(shift, half)],
                near,
            )
            for n, chip in enumerate(chips)
        ]

    def cross(h, first):
        hs = pl.ds(h * half, half)

        def merge(n):
            if h == 0:
                loads[n].wait()
            first[n].wait_recv()
            chip = chips[n]
            value = own[n, hs, :].astype(f32) + got_c[chip, hs, :].astype(f32)
            sums[chip, hs, :] = value.astype(bf16)

        merge(0)
        a0 = copy(10 * h + 4, sums.at[chips[0], hs, cols_a], got_a.at[1 - y, hs], over_x)
        b0 = copy(10 * h + 5, sums.at[chips[0], hs, cols_b], got_b.at[1 - x, hs], over_y)
        merge(1)
        a1 = copy(10 * h + 6, sums.at[chips[1], hs, cols_a], got_a.at[y, hs], over_x)
        merge(2)
        b1 = copy(10 * h + 7, sums.at[chips[2], hs, cols_b], got_b.at[x, hs], over_y)
        merge(3)
        return a0, b0, a1, b1

    def turn_over(h, crossed):
        hs = pl.ds(h * half, half)
        a0, b0 = crossed[:2]
        a0.wait_recv()
        value = sums[chips[2], hs, cols_a].astype(f32) + got_a[1 - y, hs, :].astype(f32)
        half_a[hs, :] = value.astype(bf16)
        a2 = copy(10 * h + 8, half_a.at[hs], end_a.at[hs], over_y)
        b0.wait_recv()
        value = sums[chips[1], hs, cols_b].astype(f32) + got_b[1 - x, hs, :].astype(f32)
        half_b[hs, :] = value.astype(bf16)
        b2 = copy(10 * h + 9, half_b.at[hs], end_b.at[hs], over_x)
        return a2, b2

    def end(h, crossed, turned):
        hs = pl.ds(h * half, half)
        parts = (
            (cols_a, crossed[2], turned[0], got_a.at[y], end_a),
            (cols_b, crossed[3], turned[1], got_b.at[x], end_b),
        )
        for cols, one, two, got, last in parts:
            one.wait_recv()
            value = sums[chips[3], hs, cols].astype(f32) + got[hs, :].astype(f32)
            two.wait_recv()
            mine[0, hs, cols] = (value + last[hs, :].astype(f32)).astype(bf16)
        return spread(1 + h)

    first = [begin(0), begin(1)]
    mix = [mix_start(0)]
    for l in range(2):
        mine[l, :, W_ALL:] = jnp.zeros((part, 4 * QUARTER - W_ALL), bf16)
    mine[1, :, 0:W_ALL] = upper_ref[...]
    upper = spread(0)
    crossed = [cross(0, first[0])]
    mix_end(0, mix[0])
    mix.append(mix_start(1))
    crossed.append(cross(1, first[1]))
    turned = [turn_over(0, crossed[0])]
    mix_end(1, mix[1])
    mix.append(mix_start(2))
    upper_back = gather(0, upper)
    turned.append(turn_over(1, crossed[1]))
    lower = [end(0, crossed[0], turned[0])]
    mix_end(2, mix[2])
    mix.append(mix_start(3))
    lower.append(end(1, crossed[1], turned[1]))
    lower_back = gather(1, lower[0])
    mix_end(3, mix[3])
    mix.append(mix_start(4))
    lower_back += gather(2, lower[1])
    mix_end(4, mix[4])
    for made in upper_back + lower_back:
        made.wait_recv()
    started = mix + upper + upper_back + lower_back
    for h in range(2):
        started += first[h] + list(crossed[h]) + list(turned[h]) + lower[h]
    for made in started:
        made.wait_send()


def finish_call(part, labels, grads, upper, mix):
    vmem = pl.BlockSpec(memory_space=pltpu.VMEM)
    rest = W_ALL - SPLIT
    owners = lax.axis_size("expert")
    outs = [shape((2, part, 4 * QUARTER), bf16), shape((LAYERS, labels, labels))]
    dma = pltpu.SemaphoreType.DMA
    return pl.pallas_call(
        functools.partial(cube_kernel, part, labels),
        out_shape=outs,
        in_specs=[pl.BlockSpec(memory_space=pl.ANY), vmem, vmem],
        out_specs=[vmem] * len(outs),
        scratch_shapes=[
            pltpu.VMEM((4, part, W_ALL), bf16),
            pltpu.VMEM((4, part, W_ALL), bf16),
            pltpu.VMEM((4, part, W_ALL), bf16),
            pltpu.VMEM((2, part, SPLIT), bf16),
            pltpu.VMEM((2, part, rest), bf16),
            pltpu.VMEM((part, SPLIT), bf16),
            pltpu.VMEM((part, rest), bf16),
            pltpu.VMEM((part, SPLIT), bf16),
            pltpu.VMEM((part, rest), bf16),
            pltpu.VMEM((2, part, 4 * QUARTER), bf16),
            pltpu.VMEM((3, owners, part, QUARTER), bf16),
            pltpu.VMEM((5, 32, 128), f32),
            pltpu.VMEM((5, 32, 128), f32),
            dma((20,)),
            dma((20,)),
            dma((3, 2, owners - 1)),
            dma((3, 2, owners - 1)),
            dma((5,)),
            dma((5,)),
            dma((4,)),
        ],
        compiler_params=pltpu.CompilerParams(
            vmem_limit_bytes=60 << 20, collective_id=4, has_side_effects=True
        ),
        cost_estimate=pl.CostEstimate(flops=70 * 10**9, bytes_accessed=10**7, transcendentals=0),
        name="dense_sums",
    )(grads, upper, mix)


EXCHANGE_IDS = {"forward": 0, "both": 1, "backward": 2}


def exchange_call(mode, pack, ex, args):
    rows, ff = ex.total, pack.ff
    forward, backward = mode in ("forward", "both"), mode in ("backward", "both")
    flat, wide = shape((rows, D), bf16), shape((rows, ff), bf16)
    packed = (pack.shards, pack.rows, 256)
    most = max(ex.slots, ex.span((0, 1))[1], ex.span((2,))[1])
    vmem = pl.BlockSpec(memory_space=pltpu.VMEM)
    far = pl.BlockSpec(memory_space=pl.ANY)
    in_specs = [vmem] * len(args)
    in_specs[1] = far
    scratch = []
    if mode == "forward":
        outs = [flat, wide, wide]
    elif mode == "both":
        outs = [flat, flat, shape(packed, bf16)] + gating_outputs()
    else:
        in_specs[3] = in_specs[4] = far
        outs = [flat, shape(packed, bf16)] + gating_outputs()
    out_specs = [vmem] * len(outs)
    if mode == "forward":
        out_specs[1] = out_specs[2] = far
        scratch += [pltpu.VMEM((rows, ff), bf16)] * 2
    else:
        inputs = 9 if mode == "both" else 12
        in_specs[-inputs:] = [far] * inputs
        out_specs[2 if mode == "both" else 1] = far
    if mode == "forward":
        scratch.append(pltpu.VMEM((rows, D), bf16))
    if forward:
        scratch.append(pltpu.VMEM((most, D), f32))
    if backward:
        scratch += [pltpu.VMEM((rows, D), bf16)] * 2
        scratch += [pltpu.VMEM((rows, ff), bf16)] * 3
        scratch += [pltpu.VMEM((D, rows), bf16), pltpu.VMEM((most, D), f32)]
        scratch += [pltpu.VMEM(a.shape, a.dtype) for a in args[-inputs:]]
    if mode == "both":
        scratch.append(pltpu.VMEM((2, ex.experts - 1, 8, 128), f32))
        scratch.append(pltpu.VMEM((2, ex.experts, 8, 128), f32))
        scratch += [pltpu.SemaphoreType.DMA((2, ex.experts - 1))] * 2
    scratch.append(pltpu.VMEM(packed, bf16))
    count = len(ex.waves)
    scratch += [pltpu.SemaphoreType.DMA((count, ex.experts - 1))] * 2
    scratch += [pltpu.SemaphoreType.DMA((2, count, ex.experts - 1))] * 2
    scratch.append(pltpu.SemaphoreType.DMA((16,)))
    work = 6 * rows * D * ff * (1 if mode == "forward" else 2 if mode == "backward" else 3)
    return pl.pallas_call(
        functools.partial(exchange_kernel, mode, pack, ex),
        out_shape=outs,
        in_specs=in_specs,
        out_specs=out_specs,
        scratch_shapes=scratch,
        compiler_params=pltpu.CompilerParams(
            vmem_limit_bytes=62 << 20, collective_id=EXCHANGE_IDS[mode], has_side_effects=True
        ),
        cost_estimate=pl.CostEstimate(
            flops=10**9 if mode == "backward" else work + 40 * 10**9,
            bytes_accessed=6 * D * ff,
            transcendentals=0,
        ),
        name="experts_" + mode,
    )(*args)


def write_dense(part, labels, l, ref, outs, turn):
    proj_ref, out_ref, gain_ref, router_ref, vec_ref, const_ref = outs
    for c in range(3):
        proj_ref[l, c] = ref[:, c * D : (c + 1) * D].astype(f32)
    out_ref[l] = ref[:, W_OUT:W_SMALL].astype(f32)
    small = ref[:, W_SMALL:W_ALL].astype(f32)
    turn[0:part, :] = small
    rows = turn[...].T
    router_ref[l] = rows[0:labels, 0:part]
    for c in range(2):
        const_ref[l, c] = rows[S_CONST + 2 * c : S_CONST + 2 * c + 2, 0:part]
    gain_ref[l] = rows[S_GAIN : S_GAIN + 2, 0:part]
    vec_ref[l] = rows[S_VEC : S_VEC + 2, 0:part]


def outputs_kernel(pack, labels, traffic, low_ref, high_ref, dense_ref, hidden_ref, *refs):
    gate_ref, up_ref, down_ref = refs[:3]
    outs, hidden_out, turn = refs[3:9], refs[9], refs[10]
    turn[...] = jnp.zeros_like(turn)
    for l, ref in enumerate((low_ref, high_ref)):
        for n, out in enumerate((gate_ref, up_ref)):
            for j in range(pack.chunks):
                at = (n * pack.chunks + j) * pack.padded
                out[l, :, j * 256 : (j + 1) * 256] = ref[at : at + pack.part, :].astype(f32)
        for c in range(D // 256):
            at = pack.down + c * pack.own
            down_ref[l, :, c * 256 : (c + 1) * 256] = ref[at : at + pack.own, :].astype(f32)
        for out in (gate_ref, up_ref, down_ref):
            traffic.flush(out, l)
        write_dense(pack.part, labels, l, dense_ref.at[l], outs, turn)
        for out in outs[:2]:
            traffic.flush(out, l)
    traffic.need(hidden_ref)
    hidden_out[...] = hidden_ref[...]
    traffic.flush(hidden_out)


def dense_shapes(part, labels):
    return [
        shape((LAYERS, 3, part, D)),
        shape((LAYERS, part, D)),
        shape((LAYERS, 2, part)),
        shape((LAYERS, labels, part)),
        shape((LAYERS, 2, part)),
        shape((LAYERS, 2, 2, part)),
    ]


def outputs_call(pack, labels, grads, dense, hidden):
    wide = shape((LAYERS, pack.part, pack.ff))
    outs = [wide, wide, shape((LAYERS, pack.own, D))] + dense_shapes(pack.part, labels)
    outs.append(shape(hidden.shape, hidden.dtype))
    body = functools.partial(outputs_kernel, pack, labels)
    turn = [pltpu.VMEM((128, 128), f32)]
    return whole_call(body, "outputs", outs, turn, grads + [dense, hidden], 10**6, (3,), (0, 1, 2, 3, 4, 9))


def pack_kernel(traffic, proj_ref, out_ref, small_ref, *packed):
    for l, ref in enumerate(packed):
        for c in range(3):
            ref[:, c * D : (c + 1) * D] = proj_ref[l, c]
        ref[:, W_OUT:W_SMALL] = out_ref[l]
        ref[:, W_SMALL:] = small_ref[l]


def pack_call(project, output, small):
    outs = [shape((project.shape[2], W_ALL), bf16)] * LAYERS
    return whole_call(pack_kernel, "pack", outs, [], [project, output, small], 10**6)


def on_device(
    hidden_in,
    prior_logits,
    project_weight,
    output_weight,
    norm_gain,
    router_weight,
    mixing_weight,
    const_vector,
    const_weight,
    gate_weight,
    up_weight,
    down_weight,
    routes,
    priority,
    leaf_parent,
    cotangent,
):
    experts = lax.axis_size("expert")
    total_experts = experts + 4
    tokens = hidden_in.shape[0]
    capacity = 9 * tokens * TOP // (8 * total_experts)
    slots = -(-capacity // 16) * 16
    part = project_weight.shape[2]

    def pad_cols(a, width):
        return jnp.pad(a, [(0, 0)] * (a.ndim - 1) + [(0, width - a.shape[-1])])

    dense = []
    experts_w = []
    pack = Packing(lax.axis_size("shard"), part, gate_weight.shape[3])
    small = jnp.concatenate(
        [
            pad_cols(router_weight, S_CONST),
            const_weight[:, 0],
            const_weight[:, 1],
            jnp.zeros((LAYERS, part, S_GAIN - S_CONST - 4), bf16),
            norm_gain.transpose(0, 2, 1),
            const_vector.transpose(0, 2, 1),
        ],
        axis=2,
    )
    packed = pack_call(project_weight, output_weight, pad_cols(small, 128))
    for l in range(LAYERS):
        dense.append(lax.all_gather(packed[l], "shard", axis=0, tiled=True))
        mine = pack.pack(gate_weight[l, 0], up_weight[l, 0], down_weight[l, 0])
        experts_w.append(lax.all_gather(mine, "shard", axis=0, tiled=False))

    ranking = priority[0]
    earlier = (ranking[None, :] < ranking[:, None]).astype(bf16)
    labels = jnp.arange(total_experts, dtype=jnp.int32)
    hits = jnp.sum((routes[:, :, :, None] == labels).astype(f32), axis=2)
    chosen_rows = [jnp.pad(hits[l].T, [(0, 16 - total_experts), (0, 0)]) for l in range(LAYERS)]
    loaded = jnp.concatenate([hits[l, :, :experts] for l in range(LAYERS)], axis=1)
    loaded_half = loaded.astype(bf16)
    rank_row = lax.dot_general(
        loaded_half, earlier, (((0,), (1,)), ((), ())), preferred_element_type=f32
    )
    slot_row_all = jnp.where((loaded.T > 0) & (rank_row < capacity), rank_row, -1.0)
    slot_col = []
    for l in range(LAYERS):
        rank_col = dot(earlier, hits[l, :, :experts].astype(bf16))
        slot_col.append(
            jnp.where((hits[l, :, :experts] > 0) & (rank_col < capacity), rank_col, -1.0)
        )
    slot_row = [
        jnp.pad(
            slot_row_all[l * experts : (l + 1) * experts],
            [(0, 8 - experts), (0, 0)],
            constant_values=-1.0,
        )
        for l in range(LAYERS)
    ]
    visible = tree_visible(leaf_parent[0])
    bias = jnp.where(visible, 0.0, masked_fill)
    bias_t = jnp.where(visible.T, 0.0, masked_fill)
    mixes = [
        jnp.pad(mixing_weight[l], [(0, 16 - total_experts), (0, 16 - total_experts)])
        for l in range(LAYERS)
    ]
    z_rows = jnp.pad(prior_logits.T, [(0, 16 - total_experts), (0, 0)])

    plan = (bias, bias_t, slot_col, slot_row, chosen_rows, mixes, z_rows)
    bias, bias_t, slot_col, slot_row, chosen_rows, mixes, z_rows = lax.optimization_barrier(plan)
    ex = Exchange(experts, slots)
    saved = []
    front = [hidden_in]
    x_now = hidden_in
    for l in range(LAYERS):
        last = l == LAYERS - 1
        args = front + [dense[l], bias, z_rows, mixes[l].T, chosen_rows[l], slot_row[l]]
        if last:
            args.append(cotangent)
        outs = list(forward_call(l == 0, last, experts, slots, args))
        if l > 0:
            x_now = outs.pop(0)
        n1, qkv, att, lse, middle, n2, info, gcol, gpack, send, small, z_next = outs[:12]
        keep = dict(
            x=x_now, n1=n1, qkv=qkv, att=att, lse=lse, middle=middle, n2=n2, info=info,
            gcol=gcol, gpack=gpack, z=z_rows, small=small,
        )
        keep["received"] = dispatch_call(ex, send)
        if last:
            gating = [
                cotangent, n2, slot_row[l], info, chosen_rows[l], gcol, small, z_rows, mixes[l],
            ]
            done = exchange_call(
                "both", pack, ex, [keep["received"], experts_w[l], outs[12]] + gating
            )
            y_held, keep["gin"], keep["dw"] = done[:3]
            keep["gating"] = done[3:]
        else:
            keep["y"], keep["gate"], keep["up"] = exchange_call(
                "forward", pack, ex, [keep["received"], experts_w[l]]
            )
            front = [middle, n2, keep["y"], gcol, slot_col[l], small]
        z_rows = z_next
        saved.append(keep)

    gx = cotangent
    gz = None
    dense_grads = [None] * LAYERS
    mix_grads = [None] * LAYERS
    expert_grads = [None] * LAYERS
    hidden_out = None
    for l in range(LAYERS - 1, -1, -1):
        last = l == LAYERS - 1
        keep = saved[l]
        if not last:
            gating = [
                gx, keep["n2"], keep["y"], keep["gxs"], slot_row[l], keep["info"], chosen_rows[l],
                keep["gcol"], keep["small"], keep["z"], mixes[l], gz,
            ]
            done = exchange_call(
                "backward", pack, ex,
                [keep["received"], experts_w[l], keep["gy"], keep["gate"], keep["up"]] + gating,
            )
            keep["gin"], keep["dw"] = done[:2]
            keep["gating"] = done[2:]
        gn2, gsm, mix_grads[l], gz = keep["gating"][:4]
        d_experts, gn2 = lax.optimization_barrier((keep["dw"], gn2))
        if not last:
            gn2, expert_grads[l + 1] = lax.optimization_barrier((gn2, expert_grads[l + 1]))
        expert_grads[l] = lax.psum_scatter(d_experts, "shard", scatter_dimension=0, tiled=False)
        args = [
            gx, gn2, keep["gin"], slot_col[l], keep["middle"], keep["att"], dense[l], keep["qkv"],
            keep["n1"], keep["x"], bias_t, keep["lse"], gsm,
        ]
        if l > 0:
            args += [slot_row[l - 1], saved[l - 1]["gpack"], y_held, keep["n2"], keep["gcol"]]
        outs = backward_call(l == 0, experts, slots, args)
        gx, d_dense = outs[:2]
        if l > 0:
            saved[l - 1]["gxs"], saved[l - 1]["gy"], hidden_out = outs[2:5]
        if l > 0:
            dense_grads[l] = lax.psum_scatter(d_dense, "shard", scatter_dimension=0, tiled=True)

    if pack.shards == 8 and experts == 4:
        mix = jnp.pad(jnp.concatenate(mix_grads), [(0, 0), (0, 112)])
        dense_sums, mixing_grad = finish_call(part, total_experts, d_dense, dense_grads[1], mix)
    else:
        dense_grads[0] = lax.psum_scatter(d_dense, "shard", scatter_dimension=0, tiled=True)
        dense_sums = lax.psum(jnp.stack(dense_grads), "expert")
        mixing_grad = lax.psum(jnp.stack(mix_grads), ("expert", "shard"))
        mixing_grad = mixing_grad[:, 0:total_experts, 0:total_experts]
    made = outputs_call(pack, total_experts, expert_grads, dense_sums, hidden_out)
    gate_grad, up_grad, down_grad, project_grad, output_grad = made[:5]
    gain_grad, router_grad, vector_grad, const_grad, hidden_out = made[5:]
    return (
        hidden_out,
        gx,
        gz[0:total_experts].T,
        project_grad,
        output_grad,
        gain_grad,
        router_grad.transpose(0, 2, 1),
        mixing_grad,
        vector_grad,
        const_grad.transpose(0, 1, 3, 2),
        gate_grad[:, None],
        up_grad[:, None],
        down_grad[:, None],
    )


def solution(mesh):
    both = ("expert", "shard")
    in_specs = (
        P(both, None),
        P(both, None),
        P(None, None, "shard", None),
        P(None, "shard", None),
        P(None, None, "shard"),
        P(None, "shard", None),
        P(),
        P(None, None, "shard"),
        P(None, None, "shard", None),
        P(None, "expert", "shard", None),
        P(None, "expert", "shard", None),
        P(None, "expert", "shard", None),
        P(None, both, None),
        P(both, None),
        P(both, None),
        P(both, None),
    )
    out_specs = (
        P(both, None),
        P(both, None),
        P(both, None),
        P(None, None, "shard", None),
        P(None, "shard", None),
        P(None, None, "shard"),
        P(None, "shard", None),
        P(),
        P(None, None, "shard"),
        P(None, None, "shard", None),
        P(None, "expert", "shard", None),
        P(None, "expert", "shard", None),
        P(None, "expert", "shard", None),
    )
    return jax.shard_map(
        on_device, mesh=mesh, in_specs=in_specs, out_specs=out_specs, check_vma=False
    )
```

```python
import functools

import jax
import jax.numpy as jnp
from jax import lax
from jax.experimental import pallas as pl
from jax.experimental.pallas import tpu as pltpu
from jax.sharding import PartitionSpec as P

D = 768
H = 12
HD = 64
TOP = 2
LAYERS = 2
TRUNK = 320
BRANCH = 64
LEAF = 32
TREE = 832

W_OUT = 3 * D
W_SMALL = 4 * D
W_ALL = 4 * D + 128
S_CONST = 16
S_GAIN = 24
S_VEC = 26

epsilon = 1e-06
masked_fill = -1e30
f32 = jnp.float32
bf16 = jnp.bfloat16
BLOCKS = 2
VMEM = 56 << 20


def dot(a, b):
    return jnp.dot(a, b, preferred_element_type=f32)


def dot_nt(a, b):
    return lax.dot_general(a, b, (((1,), (1,)), ((), ())), preferred_element_type=f32)


def dot_tn(a, b):
    return lax.dot_general(a, b, (((0,), (0,)), ((), ())), preferred_element_type=f32)


def split_bf16(v):
    high = v.astype(bf16)
    return high, (v - high.astype(f32)).astype(bf16)


def inv_rms(v):
    return lax.rsqrt(jnp.mean(v * v, axis=1, keepdims=True) + epsilon)


def tree_visible(parents):
    position = jnp.arange(TREE, dtype=jnp.int32)
    offset = position - TRUNK
    segment = jnp.where(
        position < TRUNK,
        0,
        jnp.where(offset < 4 * BRANCH, 1 + offset // BRANCH, 5 + (offset - 4 * BRANCH) // LEAF),
    )
    leaf_hits = (segment[:, None] - 5 == jnp.arange(8, dtype=jnp.int32)[None, :]).astype(jnp.int32)
    upper = jnp.where(segment >= 5, 1 + jnp.sum(leaf_hits * parents[None, :], axis=1), 0)
    key_segment = segment[None, :]
    causal = position[None, :] <= position[:, None]
    return causal & (
        (key_segment == segment[:, None]) | (key_segment == 0) | (key_segment == upper[:, None])
    )


def one_hot(slot_row, e, slots):
    row = lax.broadcasted_iota(jnp.int32, (slots, slot_row.shape[1]), 0).astype(f32)
    return jnp.where(row == slot_row[e : e + 1, :], 1.0, 0.0).astype(bf16)


def one_hot_col(slot_col, e, slots, scale=None):
    lane = lax.broadcasted_iota(jnp.int32, (slot_col.shape[0], slots), 1).astype(f32)
    value = 1.0 if scale is None else scale
    return jnp.where(lane == slot_col[:, e : e + 1], value, 0.0).astype(bf16)


def combine_rows(rows, middle_ref, n2_ref, y_ref, gcol_ref, slotc_ref, vectors, experts, slots):
    gcol = gcol_ref[rows, :]
    slot = slotc_ref[rows, :]
    total = middle_ref[rows, :] + gcol[:, 16:17] * n2_ref[rows, :].astype(f32)
    for c in range(2):
        total = total + gcol[:, 17 + c : 18 + c] * vectors[c : c + 1, :]
    for e in range(experts):
        weight = one_hot_col(slot, e, slots, gcol[:, e : e + 1])
        total = total + dot(weight, y_ref[e * slots : (e + 1) * slots, :])
    return total


def all_one_hot(slot_row, experts, slots):
    return jnp.concatenate([one_hot(slot_row, e, slots) for e in range(experts)], axis=0)


def send_grads(hot, gx, gpack, gxs_ref, gy_ref, experts, slots):
    got = dot(hot, gx)
    gates = dot(hot, gpack)
    if gxs_ref is not None:
        gxs_ref[...] = got.astype(bf16)
    for e in range(experts):
        rows = slice(e * slots, (e + 1) * slots)
        gate = gates[rows, e : e + 1] + gates[rows, 64 + e : 65 + e]
        gy_ref[rows, :] = (got[rows, :] * gate).astype(bf16)


def row_blocks(tokens):
    size = tokens // BLOCKS
    return size, lambda i: pl.ds(pl.multiple_of(i * size, 16), size)


def causal_spans(tokens):
    edges = [0, 256, 512, tokens]
    return list(zip(edges[:-1], edges[1:]))


def forward_kernel(first, last, experts, slots, traffic, *refs):
    refs = list(refs)
    if first:
        x_in = refs.pop(0)
    else:
        mid_prev, n2_prev, y_ref, gcol_prev, slotc_prev, w_prev = [refs.pop(0) for _ in range(6)]
    w_ref, bias_ref, z_ref, mixt_ref, chosen_ref, slotr_ref = [refs.pop(0) for _ in range(6)]
    if last:
        cot_ref = refs.pop(0)
    if not first:
        x_out = refs.pop(0)
    n1_ref, qkv_ref, att_ref, lse_ref, mid_ref, n2_ref, info_ref, gcol_ref, gpack_ref, send_ref = [
        refs.pop(0) for _ in range(10)
    ]
    small_out, z_out = refs.pop(0), refs.pop(0)
    small_out[...] = w_ref[:, W_SMALL:]
    if last:
        gy_ref = refs.pop(0)
    lse_cols, turn = refs
    tokens = n1_ref.shape[0]
    size, block = row_blocks(tokens)
    small = w_ref[:, W_SMALL:].astype(f32).T
    gain0 = small[S_GAIN : S_GAIN + 1, :]
    gain1 = small[S_GAIN + 1 : S_GAIN + 2, :]
    if not first:
        vectors_prev = w_prev[...].astype(f32).T[S_VEC : S_VEC + 2, :]

    def project(i, carry):
        rows = block(i)
        if first:
            x = x_in[rows, :].astype(f32)
        else:
            x = combine_rows(
                rows, mid_prev, n2_prev, y_ref, gcol_prev, slotc_prev, vectors_prev, experts, slots
            )
            x_out[rows, :] = x
        n1 = (x * inv_rms(x) * gain0).astype(bf16)
        n1_ref[rows, :] = n1
        for c in range(3):
            qkv_ref[rows, c * D : (c + 1) * D] = dot(n1, w_ref[:, c * D : (c + 1) * D]).astype(bf16)
        return carry

    lax.fori_loop(0, BLOCKS, project, 0)
    if not first:
        traffic.flush(x_out)
    traffic.flush(n1_ref)
    traffic.flush(qkv_ref)
    traffic.need(bias_ref)
    lane = lax.broadcasted_iota(jnp.int32, (1, 128), 1)
    low_f = jnp.where(lane < HD, 1.0, 0.0)
    low = low_f.astype(bf16)
    high = (1.0 - low_f).astype(bf16)
    lse_cols[...] = jnp.zeros_like(lse_cols)

    def pair(p, carry):
        k = qkv_ref[:, pl.ds(pl.multiple_of(D + p * 128, 128), 128)]
        v = qkv_ref[:, pl.ds(pl.multiple_of(2 * D + p * 128, 128), 128)]
        va = v * low + high
        vb = v * high + low
        here = pl.ds(pl.multiple_of(p * 128, 128), 128)
        spans = causal_spans(tokens)
        scores = []
        for start, stop in spans:
            q = qkv_ref[start:stop, here] * bf16(HD**-0.5)
            scores.append(
                [dot_nt(q * mask, k[:stop]) + bias_ref[start:stop, :stop] for mask in (low, high)]
            )
        for (start, stop), pairs in zip(spans, scores):
            peaks = [jnp.max(one, axis=1, keepdims=True) for one in pairs]
            expos = [jnp.exp(one - peak).astype(bf16) for one, peak in zip(pairs, peaks)]
            outs = [
                (dot(expo, value[:stop]), peak)
                for expo, value, peak in zip(expos, (va, vb), peaks)
            ]
            (oa, ma), (ob, mb) = outs
            numer = jnp.where(lane < HD, oa, ob)
            denom = pltpu.roll(jnp.where(lane < HD, ob, oa), HD, 1)
            att_ref[start:stop, here] = (numer / denom).astype(bf16)
            la = ma + jnp.log(oa[:, HD : HD + 1])
            lb = mb + jnp.log(ob[:, 0:1])
            old = lse_cols[start:stop, :]
            lse_cols[start:stop, :] = jnp.where(
                lane == 2 * p, la, jnp.where(lane == 2 * p + 1, lb, old)
            )
        return carry

    lax.fori_loop(0, H // 2, pair, 0)
    traffic.flush(att_ref)
    lse_ref[...] = lse_cols[...].T[0:16, :]

    def finish(i, carry):
        rows = block(i)
        if first:
            x = x_in[rows, :].astype(f32)
        else:
            x = x_out[rows, :]
        middle = x + dot(att_ref[rows, :], w_ref[:, W_OUT:W_SMALL])
        mid_ref[rows, :] = middle
        n2_ref[rows, :] = (middle * inv_rms(middle) * gain1).astype(bf16)
        return carry

    lax.fori_loop(0, BLOCKS, finish, 0)
    traffic.flush(mid_ref)
    traffic.flush(n2_ref)
    n2 = n2_ref[...]
    scores = dot_nt(small[0:32, :].astype(bf16), n2)
    logits = scores[0:16, :]
    z = z_ref[...]
    mixt = mixt_ref[...]
    for i in range(experts + 4):
        logits = logits + mixt[:, i : i + 1] * z[i : i + 1, :]
    row = lax.broadcasted_iota(jnp.int32, (16, tokens), 0)
    valid = row < experts + 4
    peak = jnp.max(jnp.where(valid, logits, masked_fill), axis=0, keepdims=True)
    expo = jnp.where(valid, jnp.exp(jnp.minimum(logits - peak, 0.0)), 0.0)
    prob = expo / jnp.sum(expo, axis=0, keepdims=True)
    gates = prob * chosen_ref[...]
    info_ref[0:16, :] = logits
    z_out[...] = logits
    info_ref[16:32, :] = prob
    turn[...] = jnp.zeros_like(turn)
    turn[0:16, 0:tokens] = gates
    own = gates[experts + 1 : experts + 2, :]
    alphas = []
    for c in range(2):
        l0 = scores[S_CONST + 2 * c : S_CONST + 2 * c + 1, :]
        l1 = scores[S_CONST + 2 * c + 1 : S_CONST + 2 * c + 2, :]
        a0 = jax.nn.sigmoid(l0 - l1)
        a1 = jax.nn.sigmoid(l1 - l0)
        alphas += [a0, a1]
        share = gates[experts + 2 + c : experts + 3 + c, :]
        own = own + share * a0
        turn[17 + c : 18 + c, 0:tokens] = share * a1
    turn[16:17, 0:tokens] = own
    zero_row = jnp.zeros((4, tokens), f32)
    info_ref[32:40, :] = jnp.concatenate(alphas + [zero_row], axis=0)
    gcol = turn[...].T[0:tokens, :]
    gcol_ref[...] = gcol
    upper, lower = split_bf16(jnp.where(lane < 16, gcol, 0.0))
    gpack = upper + pltpu.roll(lower.astype(f32), 64, 1).astype(bf16)
    gpack_ref[...] = gpack
    hot = all_one_hot(slotr_ref[...], experts, slots)
    send_ref[...] = dot(hot, n2).astype(bf16)
    if last:
        traffic.need(cot_ref)
        send_grads(hot, cot_ref[...], gpack, None, gy_ref, experts, slots)


def shape(dims, dtype=f32):
    return jax.ShapeDtypeStruct(tuple(dims), dtype)


class Traffic:
    def __init__(self):
        self.fetches, self.sinks, self.flushes = {}, {}, []

    def fetch(self, src, buffer, sem):
        copy = pltpu.make_async_copy(src, buffer, sem)
        copy.start()
        self.fetches[id(buffer)] = copy

    def need(self, *buffers):
        for buffer in buffers:
            copy = self.fetches.pop(id(buffer), None)
            if copy is not None:
                copy.wait()

    def sink(self, buffer, dst, sems):
        self.sinks[id(buffer)] = [dst, sems, 0]

    def flush(self, buffer, part=None):
        entry = self.sinks.get(id(buffer))
        if entry is None:
            return
        dst, sems, used = entry
        entry[2] += 1
        src, dst = (buffer, dst) if part is None else (buffer.at[part], dst.at[part])
        copy = pltpu.make_async_copy(src, dst, sems.at[used])
        copy.start()
        self.flushes.append(copy)

    def finish(self):
        for copy in self.flushes:
            copy.wait()


FLUSHES = 3


def whole_call(body, name, outs, scratch, args, flops, late=(), early=(), raw=(), collective=None):
    moved = sum(a.size * a.dtype.itemsize for a in args) + sum(
        o.size * o.dtype.itemsize for o in outs
    )
    late, early = sorted(late), sorted(early)

    def kernel(*refs):
        ins, rest = list(refs[: len(args)]), refs[len(args) :]
        results, rest = list(rest[: len(outs)]), rest[len(outs) :]
        own, rest = rest[: len(scratch)], rest[len(scratch) :]
        traffic = Traffic()
        fetch_sems, flush_sems = rest[len(late) + len(early) :]
        for n, at in enumerate(late):
            traffic.fetch(ins[at], rest[n], fetch_sems.at[n])
            ins[at] = rest[n]
        for n, at in enumerate(early):
            buffer = rest[len(late) + n]
            traffic.sink(buffer, results[at], flush_sems.at[n])
            results[at] = buffer
        body(traffic, *ins, *results, *own)
        traffic.finish()

    near, far = pl.BlockSpec(memory_space=pltpu.VMEM), pl.BlockSpec(memory_space=pl.ANY)
    buffers = [pltpu.VMEM(args[at].shape, args[at].dtype) for at in late]
    buffers += [pltpu.VMEM(outs[at].shape, outs[at].dtype) for at in early]
    buffers.append(pltpu.SemaphoreType.DMA((max(len(late), 1),)))
    buffers.append(pltpu.SemaphoreType.DMA((max(len(early), 1), FLUSHES)))
    return pl.pallas_call(
        kernel,
        out_shape=outs,
        in_specs=[far if n in late or n in raw else near for n in range(len(args))],
        out_specs=[far if n in early else near for n in range(len(outs))],
        scratch_shapes=list(scratch) + buffers,
        compiler_params=pltpu.CompilerParams(
            vmem_limit_bytes=VMEM,
            collective_id=collective,
            has_side_effects=collective is not None,
        ),
        cost_estimate=pl.CostEstimate(flops=flops, bytes_accessed=moved, transcendentals=0),
        name=name,
    )(*args)


def forward_call(first, last, experts, slots, args):
    tokens = TREE
    sent = experts * slots
    outs = [] if first else [shape((tokens, D))]
    outs += [
        shape((tokens, D), bf16),
        shape((tokens, 3 * D), bf16),
        shape((tokens, D), bf16),
        shape((16, tokens)),
        shape((tokens, D)),
        shape((tokens, D), bf16),
        shape((40, tokens)),
        shape((tokens, 128)),
        shape((tokens, 128), bf16),
        shape((sent, D), bf16),
        shape((D, 128), bf16),
        shape((16, tokens)),
    ]
    if last:
        outs += [shape((sent, D), bf16)]
    padded = -(-tokens // 128) * 128
    scratch = [pltpu.VMEM((tokens, 128), f32), pltpu.VMEM((128, padded), f32)]
    body = functools.partial(forward_kernel, first, last, experts, slots)
    inputs, results = (1, 0) if first else (6, 1)
    late = [inputs + 1] + ([inputs + 6] if last else [])
    early = ([] if first else [0]) + [results + n for n in (0, 1, 2, 4, 5)]
    return whole_call(body, "block_forward", outs, scratch, args, 20 * 10**9, late, early)


def row_dots(a, b):
    ones = jnp.ones((16, D), bf16)
    upper, lower = split_bf16(a.astype(f32) * b.astype(f32))
    return (dot_nt(ones, upper) + dot_nt(ones, lower))[0:8, :]


def gating_steps(last, experts, slots, *refs):
    refs = list(refs)
    gx_ref, n2_ref = refs.pop(0), refs.pop(0)
    if last:
        dots_ref = refs.pop(0)
    else:
        y_ref, gxs_ref = refs.pop(0), refs.pop(0)
    slotr_ref, info_ref, chosen_ref, gcol_ref, small_ref, z_ref, mix_ref = [
        refs.pop(0) for _ in range(7)
    ]
    if not last:
        gz_ref = refs.pop(0)
    gn2_ref, gsm_ref, gmix_ref, gprev_ref = refs
    tokens = n2_ref.shape[0]
    size, block = row_blocks(tokens)
    small = small_ref[...].astype(f32).T
    small_half = small[0:32, :].astype(bf16)
    ones = jnp.ones((16, D), bf16)
    gx = gx_ref[...].astype(f32)
    gx_half = gx.astype(bf16)
    n2 = n2_ref[...]
    upper, lower = split_bf16(gx * n2.astype(f32))
    gx_n2 = (dot_nt(ones, upper) + dot_nt(ones, lower))[0:1, :]
    gx_small = dot_nt(small_half, gx_half)
    prob = info_ref[16:32, :]
    chosen = chosen_ref[...]
    gates = prob * chosen
    trow = lax.broadcasted_iota(jnp.int32, (16, tokens), 0)
    gp = jnp.where(trow == experts + 1, gx_n2, 0.0)
    crow = lax.broadcasted_iota(jnp.int32, (8, tokens), 0)
    glog = jnp.zeros((8, tokens), f32)
    coefs = jnp.zeros((8, tokens), f32)
    for c in range(2):
        a0 = info_ref[32 + 2 * c : 33 + 2 * c, :]
        a1 = info_ref[33 + 2 * c : 34 + 2 * c, :]
        gx_v = gx_small[S_VEC + c : S_VEC + c + 1, :]
        share = gates[experts + 2 + c : experts + 3 + c, :]
        gp = jnp.where(trow == experts + 2 + c, a0 * gx_n2 + a1 * gx_v, gp)
        gl = share * (gx_n2 - gx_v) * a0 * a1
        glog = jnp.where(crow == 2 * c, gl, jnp.where(crow == 2 * c + 1, -gl, glog))
        coefs = jnp.where(crow == c, share * a1, coefs)
    cu, cl = split_bf16(jnp.concatenate([coefs, jnp.zeros((8, tokens), f32)], axis=0))
    gvec = dot(cu, gx_half) + dot(cl, gx_half)

    def add(i, carry):
        rows = block(i)
        gn2_ref[rows, :] = gcol_ref[rows, 16:17] * gx_ref[rows, :].astype(f32)
        return carry

    lax.fori_loop(0, BLOCKS, add, 0)

    yield
    slot_row = slotr_ref[...]
    row = lax.broadcasted_iota(jnp.int32, (16, slots), 0)
    scattered = jnp.zeros((16, tokens), f32)
    for e in range(experts):
        if last:
            half = Exchange(experts, slots).half
            sums = jnp.concatenate(
                [dots_ref[0, e, 0:1, 0:half], dots_ref[1, e, 0:1, 0 : slots - half]], axis=1
            )
        else:
            rows = slice(e * slots, (e + 1) * slots)
            sums = row_dots(y_ref[rows, :], gxs_ref[rows, :])[0:1, :]
        upper, lower = split_bf16(sums)
        lhs = jnp.where(row == e, upper.astype(f32), 0.0) + jnp.where(
            row == 8 + e, lower.astype(f32), 0.0
        )
        scattered = scattered + dot(lhs.astype(bf16), one_hot(slot_row, e, slots))
    dotted = jnp.concatenate([scattered[0:8, :] + scattered[8:16, :], jnp.zeros((8, tokens), f32)], 0)
    weighted = dotted if last else prob * dotted
    weighted = jnp.where(trow < experts, weighted, 0.0) * chosen
    weighted = weighted + prob * gp * chosen
    gz = weighted - prob * jnp.sum(weighted, axis=0, keepdims=True)
    if not last:
        gz = gz + gz_ref[...]
    z = z_ref[...]
    gmix_ref[...] = lax.dot_general(
        z, gz, (((1,), (1,)), ((), ())), precision=lax.Precision.HIGHEST, preferred_element_type=f32
    )
    mix = mix_ref[...]
    gprev = jnp.zeros((16, tokens), f32)
    for o in range(experts + 4):
        gprev = gprev + mix[:, o : o + 1] * gz[o : o + 1, :]
    gprev_ref[...] = gprev
    allg = jnp.concatenate([gz, glog, jnp.zeros((8, tokens), f32)], axis=0)
    upper, lower = split_bf16(allg)
    gsm = dot(upper, n2) + dot(lower, n2)
    gsm_ref[0:24, :] = gsm[0:24, :]
    gsm_ref[24:32, :] = jnp.concatenate(
        [jnp.zeros((2, D), f32), gvec[0:2, :], jnp.zeros((4, D), f32)], axis=0
    )
    both = jnp.concatenate([upper, lower], axis=0)
    twice = jnp.concatenate([small_half, small_half], axis=0)
    gn2_ref[...] = gn2_ref[...] + dot_tn(both, twice)


def gating_kernel(*args):
    for _ in gating_steps(*args):
        pass


def gating_outputs():
    tokens = TREE
    return [shape((tokens, D)), shape((32, D)), shape((16, 16)), shape((16, tokens))]


def backward_kernel(first, experts, slots, traffic, *refs):
    refs = list(refs)
    gx_ref, gn2p_ref, gn2e_ref, slotc_ref, mid_ref, att_ref, w_ref, qkv_ref, n1_ref, x_ref = [
        refs.pop(0) for _ in range(10)
    ]
    biast_ref, lse_ref, gsm_ref = [refs.pop(0) for _ in range(3)]
    if not first:
        slotr_ref, gpack_ref = refs.pop(0), refs.pop(0)
        y_held, n2_ref, gcol_ref = refs.pop(0), refs.pop(0), refs.pop(0)
    gout_ref, dw_ref = refs.pop(0), refs.pop(0)
    if not first:
        gxs_ref, gy_ref, hidden_out = refs.pop(0), refs.pop(0), refs.pop(0)
    gatt, go, gqkv, turn = refs[:4]
    if not first:
        y_home, y_sends, y_recvs, y_local = refs[4:]
        ex = Exchange(experts, slots)
        own = pltpu.make_async_copy(
            y_held.at[pl.ds(0, slots)], y_home.at[own_slots(ex)], y_local
        )
        own.start()
        greet(experts)
        returning = []
        for wave in range(len(ex.waves)):
            returning += back_copies(ex, wave, 0, y_held, y_home, y_sends, y_recvs)
        for copy in returning:
            copy.start()
    tokens = n1_ref.shape[0]
    size, block = row_blocks(tokens)
    small = w_ref[:, W_SMALL:].astype(f32).T
    gain0 = small[S_GAIN : S_GAIN + 1, :]
    gain1 = small[S_GAIN + 1 : S_GAIN + 2, :]

    def enter(i, total):
        rows = block(i)
        gn2 = gn2p_ref[rows, :]
        slot = slotc_ref[rows, :]
        for e in range(experts):
            gn2 = gn2 + dot(one_hot_col(slot, e, slots), gn2e_ref[e * slots : (e + 1) * slots, :])
        middle = mid_ref[rows, :]
        r = inv_rms(middle)
        scaled = gain1 * gn2
        inner = jnp.mean(middle * scaled, axis=1, keepdims=True)
        gmid = gx_ref[rows, :].astype(f32) + r * scaled - middle * (r * r * r * inner)
        gout_ref[rows, :] = gmid
        half = gmid.astype(bf16)
        gatt[rows, :] = half
        go[rows, :] = dot_nt(half, w_ref[:, W_OUT:W_SMALL]).astype(bf16)
        return total + jnp.sum(gn2 * middle * r, axis=0, keepdims=True)

    ggain1 = lax.fori_loop(0, BLOCKS, enter, jnp.zeros((1, D), f32))
    traffic.need(att_ref)
    lane = lax.broadcasted_iota(jnp.int32, (1, 128), 1)
    low_f = jnp.where(lane < HD, 1.0, 0.0)
    low = low_f.astype(bf16)
    high = (1.0 - low_f).astype(bf16)
    scale = HD**-0.5

    def out_grad(p, carry):
        here = pl.ds(pl.multiple_of(p * 128, 128), 128)
        dw_ref[here, W_OUT:W_SMALL] = dot_tn(att_ref[:, here], gatt[...]).astype(bf16)
        return carry

    lax.fori_loop(0, D // 128, out_grad, 0)
    traffic.flush(dw_ref, (slice(None), slice(W_OUT, W_SMALL)))
    traffic.need(qkv_ref, biast_ref, lse_ref)
    spans = causal_spans(tokens)

    def pair(p, carry):
        here = pl.ds(pl.multiple_of(p * 128, 128), 128)
        lanes_k = pl.ds(pl.multiple_of(D + p * 128, 128), 128)
        lanes_v = pl.ds(pl.multiple_of(2 * D + p * 128, 128), 128)
        q = qkv_ref[:, here] * bf16(scale)
        k = qkv_ref[:, lanes_k]
        v = qkv_ref[:, lanes_v]
        g = go[:, here]
        turn[0:tokens, :] = g.astype(f32) * att_ref[:, here].astype(f32)
        inner = turn[...].T[:, 0:tokens]
        turn[0:tokens, :] = k.astype(f32)
        kt = turn[...].T[:, 0:tokens].astype(bf16)
        gk = [0.0] * len(spans)
        gv = [0.0] * len(spans)
        masks = (low, high)
        qs = [q * mask for mask in masks]
        gs = [g * mask for mask in masks]
        dsums = [
            jnp.sum(inner[h * HD : (h + 1) * HD, :], axis=0, keepdims=True) for h in range(2)
        ]
        lses = [lse_ref[pl.ds(2 * p + h, 1), :] for h in range(2)]
        parts = [[], []]
        for n, (start, stop) in enumerate(spans):
            st = [
                dot_nt(k[start:stop], qs[h][start:]) + biast_ref[start:stop, start:]
                for h in range(2)
            ]
            gpt = [dot_nt(v[start:stop], gs[h][start:]) for h in range(2)]
            pt = [jnp.exp(st[h] - lses[h][:, start:]) for h in range(2)]
            gst = [(pt[h] * (gpt[h] - dsums[h][:, start:])).astype(bf16) for h in range(2)]
            for h in range(2):
                gv[n] = gv[n] + dot(pt[h].astype(bf16), gs[h][start:])
                gk[n] = gk[n] + dot(gst[h], qs[h][start:])
                parts[h].append(dot(kt[h * HD : (h + 1) * HD, start:stop], gst[h]))
        gq_t = []
        for h in range(2):
            cols = []
            for n, (start, stop) in enumerate(spans):
                piece = 0.0
                for m in range(n + 1):
                    origin = spans[m][0]
                    piece = piece + parts[h][m][:, start - origin : stop - origin]
                cols.append(piece)
            gq_t.append(jnp.concatenate(cols, axis=1))
        turn_t = jnp.concatenate(gq_t, axis=0) * scale
        pad = turn.shape[0] - tokens
        turn_t = jnp.concatenate([turn_t, jnp.zeros((128, pad), f32)], axis=1)
        gqkv[:, here] = turn_t.T[0:tokens, :].astype(bf16)
        for n, (start, stop) in enumerate(spans):
            gqkv[start:stop, lanes_k] = gk[n].astype(bf16)
            gqkv[start:stop, lanes_v] = gv[n].astype(bf16)
        return carry

    turn[...] = jnp.zeros_like(turn)
    lax.fori_loop(0, H // 2, pair, 0)
    traffic.need(n1_ref)

    def in_grad(p, carry):
        here = pl.ds(pl.multiple_of(p * 128, 128), 128)
        dw_ref[here, 0:W_OUT] = dot_tn(n1_ref[:, here], gqkv[...]).astype(bf16)
        return carry

    lax.fori_loop(0, D // 128, in_grad, 0)
    traffic.flush(dw_ref, (slice(None), slice(0, W_OUT)))
    traffic.need(x_ref)

    def leave(i, total):
        rows = block(i)
        gn1 = dot_nt(gqkv[rows, :], w_ref[:, 0:W_OUT])
        x = x_ref[rows, :].astype(f32)
        r = inv_rms(x)
        scaled = gain0 * gn1
        inner = jnp.mean(x * scaled, axis=1, keepdims=True)
        gx = gout_ref[rows, :] + r * scaled - x * (r * r * r * inner)
        gout_ref[rows, :] = gx
        gatt[rows, :] = gx.astype(bf16)
        return total + jnp.sum(gn1 * x * r, axis=0, keepdims=True)

    ggain0 = lax.fori_loop(0, BLOCKS, leave, jnp.zeros((1, D), f32))
    rows = jnp.concatenate(
        [gsm_ref[0:24, :], ggain0, ggain1, gsm_ref[26:32, :], jnp.zeros((96, D), f32)], axis=0
    )
    dw_ref[:, W_SMALL:] = rows.T.astype(bf16)
    traffic.flush(dw_ref, (slice(None), slice(W_SMALL, W_ALL)))
    traffic.flush(gout_ref)
    if not first:
        hot = all_one_hot(slotr_ref[...], experts, slots)
        send_grads(hot, gatt[...], gpack_ref[...], gxs_ref, gy_ref, experts, slots)
        own.wait()
        for copy in returning:
            copy.wait()
        traffic.need(n2_ref, gcol_ref)
        vectors = small[S_VEC : S_VEC + 2, :]

        def home(i, carry):
            rows = block(i)
            hidden_out[rows, :] = combine_rows(
                rows, mid_ref, n2_ref, y_home, gcol_ref, slotc_ref, vectors, experts, slots
            ).astype(bf16)
            return carry

        lax.fori_loop(0, BLOCKS, home, 0)


def backward_call(first, experts, slots, args):
    tokens = TREE
    sent = experts * slots
    outs = [shape((tokens, D)), shape((D, W_ALL), bf16)]
    if not first:
        outs += [shape((sent, D), bf16)] * 2 + [shape((tokens, D), bf16)]
    padded = -(-tokens // 128) * 128
    scratch = [
        pltpu.VMEM((tokens, D), bf16),
        pltpu.VMEM((tokens, D), bf16),
        pltpu.VMEM((tokens, 3 * D), bf16),
        pltpu.VMEM((padded, 128), f32),
    ]
    body = functools.partial(backward_kernel, first, experts, slots)
    late = (5, 7, 8, 9, 10, 11)
    if first:
        return whole_call(body, "block_backward", outs, scratch, args, 40 * 10**9, late, (0, 1))
    count = len(Exchange(experts, slots).waves)
    scratch.append(pltpu.VMEM((sent, D), bf16))
    scratch += [pltpu.SemaphoreType.DMA((1, count, experts - 1))] * 2
    scratch.append(pltpu.SemaphoreType.DMA)
    late += (16, 17)
    return whole_call(
        body, "block_backward", outs, scratch, args, 40 * 10**9, late, (0, 1), (15,), 5
    )


class Packing:
    def __init__(self, shards, part, ff):
        self.shards, self.part, self.ff = shards, part, ff
        self.padded = -(-part // 16) * 16
        self.chunks = ff // 256
        self.own = ff // shards
        self.down = 2 * self.chunks * self.padded
        self.rows = self.down + (D // 256) * self.own

    def pack(self, gate, up, down):
        pieces = []
        for wide in (gate, up):
            cut = wide.reshape(self.part, self.chunks, 256).transpose(1, 0, 2)
            cut = jnp.pad(cut, [(0, 0), (0, self.padded - self.part), (0, 0)])
            pieces.append(cut.reshape(self.chunks * self.padded, 256))
        pieces.append(
            down.reshape(self.own, D // 256, 256).transpose(1, 0, 2).reshape(-1, 256)
        )
        return jnp.concatenate(pieces, axis=0)

    def wide_part(self, ref, n, j):
        at = pl.multiple_of((n * self.chunks + j) * self.padded, 16)
        return ref[:, pl.ds(at, self.padded), :][:, : self.part, :].reshape(D, 256)

    def tall_part(self, ref, j):
        group = 256 // self.own
        here = pl.ds(j * group, group)
        pieces = []
        for c in range(D // 256):
            at = self.down + c * self.own
            pieces.append(ref[here, at : at + self.own, :].reshape(256, 256))
        return jnp.concatenate(pieces, axis=1)

    def put_wide(self, ref, n, j, grad):
        at = pl.multiple_of((n * self.chunks + j) * self.padded, 16)
        ref[:, pl.ds(at, self.part), :] = grad.reshape(self.shards, self.part, 256)

    def put_tall(self, ref, j, grad):
        group = 256 // self.own
        for c in range(D // 256):
            at = self.down + c * self.own
            ref[pl.ds(j * group, group), at : at + self.own, :] = grad[
                :, c * 256 : (c + 1) * 256
            ].reshape(group, self.own, 256)


class Exchange:
    def __init__(self, experts, slots):
        self.experts, self.slots = experts, slots
        half = -(-slots // 32) * 16
        quarter = -(-half // 32) * 16
        self.half = half
        edges = (0, quarter, half, slots)
        self.waves = tuple((low, high - low) for low, high in zip(edges[:-1], edges[1:]))
        self.ranges = [(0, slots)]
        for _, size in self.waves:
            start = self.ranges[-1][0] + self.ranges[-1][1]
            self.ranges.append((start, (experts - 1) * size))
        self.total = experts * slots

    def span(self, group):
        start = self.ranges[1 + group[0]][0]
        return start, sum(self.ranges[1 + wave][1] for wave in group)

    def held(self, wave, d):
        size = self.waves[wave][1]
        return pl.ds(self.ranges[1 + wave][0] + (d - 1) * size, size)

    def slot(self, device, wave):
        offset, size = self.waves[wave]
        return pl.ds(pl.multiple_of(device * self.slots + offset, 16), size)


MESH = pl.DeviceIdType.MESH


def greet(experts):
    me = lax.axis_index("expert")
    barrier = pltpu.get_barrier_semaphore()
    for d in range(1, experts):
        pl.semaphore_signal(
            barrier, inc=1, device_id={"expert": lax.rem(me + d, experts)}, device_id_type=MESH
        )
    pl.semaphore_wait(barrier, experts - 1)


def out_copies(ex, wave, src, dst, sends, recvs):
    me = lax.axis_index("expert")
    copies = []
    for d in range(1, ex.experts):
        to = lax.rem(me + d, ex.experts)
        copies.append(
            pltpu.make_async_remote_copy(
                src_ref=src.at[ex.slot(to, wave)],
                dst_ref=dst.at[ex.held(wave, d)],
                send_sem=sends.at[wave, d - 1],
                recv_sem=recvs.at[wave, d - 1],
                device_id={"expert": to},
                device_id_type=MESH,
            )
        )
    return copies


def back_copies(ex, wave, n, src, dst, sends, recvs):
    me = lax.axis_index("expert")
    copies = []
    for d in range(1, ex.experts):
        copies.append(
            pltpu.make_async_remote_copy(
                src_ref=src.at[ex.held(wave, d)],
                dst_ref=dst.at[ex.slot(me, wave)],
                send_sem=sends.at[n, wave, d - 1],
                recv_sem=recvs.at[n, wave, d - 1],
                device_id={"expert": lax.rem(me + ex.experts - d, ex.experts)},
                device_id_type=MESH,
            )
        )
    return copies


def own_slots(ex):
    me = lax.axis_index("expert")
    return pl.ds(pl.multiple_of(me * ex.slots, 16), ex.slots)


def dispatch_kernel(ex, send, recv, sends, recvs, local):
    own = pltpu.make_async_copy(send.at[own_slots(ex)], recv.at[pl.ds(0, ex.slots)], local)
    own.start()
    greet(ex.experts)
    copies = []
    for wave in range(len(ex.waves)):
        copies += out_copies(ex, wave, send, recv, sends, recvs)
    for copy in copies:
        copy.start()
    for copy in copies:
        copy.wait()
    own.wait()


def dispatch_call(ex, rows):
    far = pl.BlockSpec(memory_space=pl.ANY)
    return pl.pallas_call(
        functools.partial(dispatch_kernel, ex),
        out_shape=shape((ex.total, D), bf16),
        in_specs=[far],
        out_specs=far,
        scratch_shapes=[pltpu.SemaphoreType.DMA((len(ex.waves), ex.experts - 1))] * 2
        + [pltpu.SemaphoreType.DMA],
        compiler_params=pltpu.CompilerParams(
            vmem_limit_bytes=60 << 20, collective_id=3, has_side_effects=True
        ),
        cost_estimate=pl.CostEstimate(flops=35 * 10**9, bytes_accessed=10**6, transcendentals=0),
        name="dispatch",
    )(rows)


def exchange_kernel(mode, pack, ex, *refs):
    refs = list(refs)
    forward, backward = mode in ("forward", "both"), mode in ("backward", "both")
    recv_n = refs.pop(0)
    w_hbm = refs.pop(0)
    if backward:
        send_g = refs.pop(0)
        if mode == "backward":
            gate_hbm, up_hbm = refs.pop(0), refs.pop(0)
        inputs = 9 if mode == "both" else 12
        gating_far = [refs.pop(0) for _ in range(inputs)]
    if mode == "forward":
        back_y = refs.pop(0)
    if mode == "both":
        out_y = refs.pop(0)
    if mode == "forward":
        gates_far, ups_far, gates, ups = [refs.pop(0) for _ in range(4)]
    else:
        back_g, dw_far = refs.pop(0), refs.pop(0)
        gating_outs = [refs.pop(0) for _ in range(4)]
    if mode == "forward":
        out_y = refs.pop(0)
    if forward:
        acc_y = refs.pop(0)
    if backward:
        recv_g, out_g, hids, gates, ups, rows_t, acc_g = [refs.pop(0) for _ in range(7)]
        gating = [refs.pop(0) for _ in range(inputs)]
    if mode == "both":
        dots_out, dots, dots_send, dots_recv = [refs.pop(0) for _ in range(4)]
    w = refs.pop(0)
    sends, recvs, backs, gots, local = refs
    traffic = Traffic()
    if mode == "forward":
        traffic.sink(gates, gates_far, local.at[4:8])
        traffic.sink(ups, ups_far, local.at[8:12])

    loads = [pltpu.make_async_copy(w_hbm, w, local.at[0])]
    if mode == "backward":
        loads.append(pltpu.make_async_copy(gate_hbm, gates, local.at[1]))
        loads.append(pltpu.make_async_copy(up_hbm, ups, local.at[2]))
    if mode == "backward":
        for n, (far, near) in enumerate(zip(gating_far, gating)):
            traffic.fetch(far, near, local.at[4 + n])
    for copy in loads:
        copy.start()
    if mode == "both":
        for n, (far, near) in enumerate(zip(gating_far, gating)):
            traffic.fetch(far, near, local.at[4 + n])
    greet(ex.experts)

    def work(start, size):
        rows = slice(start, start + size)
        part = slice(0, size)
        if forward:
            acc_y[part, :] = jnp.zeros((size, D), f32)
        if backward:
            acc_g[part, :] = jnp.zeros((size, D), f32)

        def chunk(j, carry):
            lanes = pl.ds(pl.multiple_of(j * 256, 256), 256)
            gate_w, up_w = pack.wide_part(w, 0, j), pack.wide_part(w, 1, j)
            down_w = pack.tall_part(w, j)
            if forward:
                r = recv_n[rows, :]
                gate, up = dot(r, gate_w), dot(r, up_w)
                if mode == "forward":
                    gates[rows, lanes] = gate.astype(bf16)
                    ups[rows, lanes] = up.astype(bf16)
            else:
                gate, up = gates[rows, lanes].astype(f32), ups[rows, lanes].astype(f32)
            s = jax.nn.sigmoid(gate)
            act = gate * s
            hid = (act * up).astype(bf16)
            if forward:
                acc_y[part, :] = acc_y[part, :] + dot(hid, down_w)
            if backward:
                hids[rows, lanes] = hid
                ghid = dot_nt(recv_g[rows, :], down_w)
                guv = (ghid * act).astype(bf16)
                ggu = (ghid * up * (s * (1.0 + gate * (1.0 - s)))).astype(bf16)
                gates[rows, lanes] = ggu
                ups[rows, lanes] = guv
                acc_g[part, :] = acc_g[part, :] + dot_nt(ggu, gate_w) + dot_nt(guv, up_w)
            return carry

        lax.fori_loop(0, pack.chunks, chunk, 0)
        if mode == "forward":
            here = pl.ds(start, size)
            traffic.flush(gates, here)
            traffic.flush(ups, here)
        if forward:
            out_y[rows, :] = acc_y[part, :].astype(bf16)
        if backward:
            out_g[rows, :] = acc_g[part, :].astype(bf16)

    def send_dots(n, group):
        me = lax.axis_index("expert")
        for d in range(1, ex.experts):
            pieces = []
            for wave in group:
                here = ex.held(wave, d)
                pieces.append(row_dots(out_y[here, :], recv_g[here, :]))
            size = sum(ex.waves[wave][1] for wave in group)
            if size < 128:
                pieces.append(jnp.zeros((8, 128 - size), f32))
            dots_out[n, d - 1] = jnp.concatenate(pieces, axis=1)
            copy = pltpu.make_async_remote_copy(
                src_ref=dots_out.at[n, d - 1],
                dst_ref=dots.at[n, me],
                send_sem=dots_send.at[n, d - 1],
                recv_sem=dots_recv.at[n, d - 1],
                device_id={"expert": lax.rem(me + ex.experts - d, ex.experts)},
                device_id_type=MESH,
            )
            copy.start()
            dot_copies.append(copy)

    def send_back(group):
        for wave in group:
            if mode == "forward":
                ys.extend(back_copies(ex, wave, 0, out_y, back_y, backs, gots))
                for copy in ys[1 - ex.experts :]:
                    copy.start()
        for wave in group:
            if backward:
                gs.extend(back_copies(ex, wave, 1, out_g, back_g, backs, gots))
                for copy in gs[1 - ex.experts :]:
                    copy.start()

    ys, gs, dot_copies = [], [], []
    groups = ((0,), (1,), (2,)) if mode == "forward" else ((0, 1), (2,))
    if backward:
        arrivals = []
        for group in groups:
            arrivals.append([])
            for wave in group:
                arrivals[-1] += out_copies(ex, wave, send_g, recv_g, sends, recvs)
        for copy in arrivals[0]:
            copy.start()
        recv_g[0 : ex.slots, :] = send_g[own_slots(ex), :]
        if mode == "backward":
            traffic.need(*gating)
            gating_kernel(False, ex.experts, ex.slots, *gating, *gating_outs)
            for copy in arrivals[1]:
                copy.start()
    for copy in loads:
        copy.wait()
    if backward:
        work(*ex.ranges[0])
        if mode == "both":
            own_dots = row_dots(out_y[0 : ex.slots, :], recv_g[0 : ex.slots, :])
            me = lax.axis_index("expert")
            dots[0, me, :, 0 : ex.half] = own_dots[:, 0 : ex.half]
            dots[1, me, :, 0 : ex.slots - ex.half] = own_dots[:, ex.half :]
            traffic.need(*gating)
            steps = gating_steps(
                True, ex.experts, ex.slots, *gating[:2], dots, *gating[2:], *gating_outs
            )
            next(steps)
        for copy in arrivals[0]:
            copy.wait_send()
        if mode == "both":
            for copy in arrivals[1]:
                copy.start()
        for copy in arrivals[0]:
            copy.wait_recv()
    for n, group in enumerate(groups):
        if backward and n > 0:
            for copy in arrivals[n]:
                copy.wait()
        work(*ex.span(group))
        if mode == "both":
            send_dots(n, group)
        send_back(group)
    if mode == "forward":
        work(*ex.ranges[0])
        back_y[own_slots(ex), :] = out_y[0 : ex.slots, :]
    if backward:
        back_g[own_slots(ex), :] = out_g[0 : ex.slots, :]
        rows_t[...] = recv_n[...].T
        dw = w
        if pack.padded != pack.part:
            dw[...] = jnp.zeros_like(dw)

        def weights(j, carry):
            lanes = pl.ds(pl.multiple_of(j * 256, 256), 256)
            pack.put_wide(dw, 0, j, dot(rows_t[...], gates[:, lanes]).astype(bf16))
            pack.put_wide(dw, 1, j, dot(rows_t[...], ups[:, lanes]).astype(bf16))
            pack.put_tall(dw, j, dot_tn(hids[:, lanes], recv_g[...]).astype(bf16))
            return carry

        lax.fori_loop(0, pack.chunks, weights, 0)
        leaving = pltpu.make_async_copy(dw, dw_far, local.at[3])
        leaving.start()
    for copy in ys + dot_copies:
        copy.wait()
    if mode == "both":
        for _ in steps:
            pass
    for copy in gs:
        copy.wait()
    if backward:
        leaving.wait()
    traffic.finish()


SPLIT = 13 * 128
QUARTER = 7 * 128


def cube_kernel(part, labels, g_ref, upper_ref, mix_ref, ready, mix_out, own, *refs):
    got_c, sums, got_a, got_b, half_a, half_b, end_a, end_b, mine, quarters, mix_held, mix_got = refs[:12]
    send, recv, z_send, z_recv, mix_send, mix_recv, own_sem = refs[12:]
    me = lax.axis_index("shard")
    z = lax.axis_index("expert")
    owners = quarters.shape[1]
    core, x, y = lax.rem(me, 2), lax.rem(me // 2, 2), me // 4
    near, over_x, over_y = me + 1 - 2 * core, me + 2 - 4 * x, me + 4 - 8 * y
    chips = [2 * (1 - y) + 1 - x, 2 * y + 1 - x, 2 * (1 - y) + x, 2 * y + x]

    def rows(shard):
        return pl.ds(pl.multiple_of(shard * part, 16), part)

    loads = [
        pltpu.make_async_copy(g_ref.at[rows(2 * chip + core)], own.at[n], own_sem.at[n])
        for n, chip in enumerate(chips)
    ]
    for load in loads:
        load.start()
    barrier = pltpu.get_barrier_semaphore()
    for other in (near, over_x, over_y):
        pl.semaphore_signal(barrier, inc=1, device_id={"shard": other}, device_id_type=MESH)
    for d in range(1, owners):
        pl.semaphore_signal(
            barrier, inc=1, device_id={"expert": lax.rem(z + d, owners)}, device_id_type=MESH
        )
    pl.semaphore_wait(barrier, 3 + owners - 1)
    cols_a, cols_b = slice(0, SPLIT), slice(SPLIT, W_ALL)

    def remote(src, dst, send_sem, recv_sem, to):
        made = pltpu.make_async_remote_copy(
            src_ref=src,
            dst_ref=dst,
            send_sem=send_sem,
            recv_sem=recv_sem,
            device_id=to,
            device_id_type=MESH,
        )
        made.start()
        return made

    def copy(n, src, dst, to):
        return remote(src, dst, send.at[n], recv.at[n], {"shard": to})

    half = part // 2
    jobs = ((1, 0, part), (0, 0, half), (0, half, half))

    def quarter(job, owner):
        l, start, size = jobs[job]
        return l, pl.ds(start, size), pl.ds(pl.multiple_of(owner * QUARTER, 128), QUARTER)

    def spread(job):
        made = []
        held = pl.ds(0, jobs[job][2])
        for d in range(1, owners):
            to = lax.rem(z + d, owners)
            made.append(
                remote(
                    mine.at[quarter(job, to)],
                    quarters.at[job, z, held],
                    z_send.at[job, 0, d - 1],
                    z_recv.at[job, 0, d - 1],
                    {"expert": to},
                )
            )
        quarters[job, z, held] = mine[quarter(job, z)]
        return made

    def gather(job, made):
        for one in made:
            one.wait_recv()
        held = pl.ds(0, jobs[job][2])
        total = quarters[job, 0, held].astype(f32)
        for owner in range(1, owners):
            total = total + quarters[job, owner, held].astype(f32)
        here = quarter(job, z)
        ready[here] = total.astype(bf16)
        return [
            remote(
                ready.at[here],
                ready.at[here],
                z_send.at[job, 1, d - 1],
                z_recv.at[job, 1, d - 1],
                {"expert": lax.rem(z + d, owners)},
            )
            for d in range(1, owners)
        ]

    pairs = [{"shard": near}, {"shard": over_x}, {"shard": over_y}]
    pairs += [{"expert": z + 1 - 2 * lax.rem(z, 2)}, {"expert": z + 2 - 4 * (z // 2)}]
    mix_held[0] = mix_ref[...]

    def mix_start(n):
        return remote(mix_held.at[n], mix_got.at[n], mix_send.at[n], mix_recv.at[n], pairs[n])

    def mix_end(n, made):
        made.wait_recv()
        total = mix_held[n] + mix_got[n]
        if n + 1 < len(pairs):
            mix_held[n + 1] = total
        else:
            for l in range(LAYERS):
                mix_out[l] = total[l * 16 : l * 16 + labels, 0:labels]

    def begin(h):
        shift = h * half
        return [
            copy(
                10 * h + n,
                g_ref.at[pl.ds(pl.multiple_of((2 * chip + 1 - core) * part + shift, 16), half)],
                got_c.at[chip, pl.ds(shift, half)],
                near,
            )
            for n, chip in enumerate(chips)
        ]

    def cross(h, first):
        hs = pl.ds(h * half, half)

        def merge(n):
            if h == 0:
                loads[n].wait()
            first[n].wait_recv()
            chip = chips[n]
            value = own[n, hs, :].astype(f32) + got_c[chip, hs, :].astype(f32)
            sums[chip, hs, :] = value.astype(bf16)

        merge(0)
        a0 = copy(10 * h + 4, sums.at[chips[0], hs, cols_a], got_a.at[1 - y, hs], over_x)
        b0 = copy(10 * h + 5, sums.at[chips[0], hs, cols_b], got_b.at[1 - x, hs], over_y)
        merge(1)
        a1 = copy(10 * h + 6, sums.at[chips[1], hs, cols_a], got_a.at[y, hs], over_x)
        merge(2)
        b1 = copy(10 * h + 7, sums.at[chips[2], hs, cols_b], got_b.at[x, hs], over_y)
        merge(3)
        return a0, b0, a1, b1

    def turn_over(h, crossed):
        hs = pl.ds(h * half, half)
        a0, b0 = crossed[:2]
        a0.wait_recv()
        value = sums[chips[2], hs, cols_a].astype(f32) + got_a[1 - y, hs, :].astype(f32)
        half_a[hs, :] = value.astype(bf16)
        a2 = copy(10 * h + 8, half_a.at[hs], end_a.at[hs], over_y)
        b0.wait_recv()
        value = sums[chips[1], hs, cols_b].astype(f32) + got_b[1 - x, hs, :].astype(f32)
        half_b[hs, :] = value.astype(bf16)
        b2 = copy(10 * h + 9, half_b.at[hs], end_b.at[hs], over_x)
        return a2, b2

    def end(h, crossed, turned):
        hs = pl.ds(h * half, half)
        parts = (
            (cols_a, crossed[2], turned[0], got_a.at[y], end_a),
            (cols_b, crossed[3], turned[1], got_b.at[x], end_b),
        )
        for cols, one, two, got, last in parts:
            one.wait_recv()
            value = sums[chips[3], hs, cols].astype(f32) + got[hs, :].astype(f32)
            two.wait_recv()
            mine[0, hs, cols] = (value + last[hs, :].astype(f32)).astype(bf16)
        return spread(1 + h)

    first = [begin(0), begin(1)]
    mix = [mix_start(0)]
    for l in range(2):
        mine[l, :, W_ALL:] = jnp.zeros((part, 4 * QUARTER - W_ALL), bf16)
    mine[1, :, 0:W_ALL] = upper_ref[...]
    upper = spread(0)
    crossed = [cross(0, first[0])]
    mix_end(0, mix[0])
    mix.append(mix_start(1))
    crossed.append(cross(1, first[1]))
    turned = [turn_over(0, crossed[0])]
    mix_end(1, mix[1])
    mix.append(mix_start(2))
    upper_back = gather(0, upper)
    turned.append(turn_over(1, crossed[1]))
    lower = [end(0, crossed[0], turned[0])]
    mix_end(2, mix[2])
    mix.append(mix_start(3))
    lower.append(end(1, crossed[1], turned[1]))
    lower_back = gather(1, lower[0])
    mix_end(3, mix[3])
    mix.append(mix_start(4))
    lower_back += gather(2, lower[1])
    mix_end(4, mix[4])
    for made in upper_back + lower_back:
        made.wait_recv()
    started = mix + upper + upper_back + lower_back
    for h in range(2):
        started += first[h] + list(crossed[h]) + list(turned[h]) + lower[h]
    for made in started:
        made.wait_send()


def finish_call(part, labels, grads, upper, mix):
    vmem = pl.BlockSpec(memory_space=pltpu.VMEM)
    rest = W_ALL - SPLIT
    owners = lax.axis_size("expert")
    outs = [shape((2, part, 4 * QUARTER), bf16), shape((LAYERS, labels, labels))]
    dma = pltpu.SemaphoreType.DMA
    return pl.pallas_call(
        functools.partial(cube_kernel, part, labels),
        out_shape=outs,
        in_specs=[pl.BlockSpec(memory_space=pl.ANY), vmem, vmem],
        out_specs=[vmem] * len(outs),
        scratch_shapes=[
            pltpu.VMEM((4, part, W_ALL), bf16),
            pltpu.VMEM((4, part, W_ALL), bf16),
            pltpu.VMEM((4, part, W_ALL), bf16),
            pltpu.VMEM((2, part, SPLIT), bf16),
            pltpu.VMEM((2, part, rest), bf16),
            pltpu.VMEM((part, SPLIT), bf16),
            pltpu.VMEM((part, rest), bf16),
            pltpu.VMEM((part, SPLIT), bf16),
            pltpu.VMEM((part, rest), bf16),
            pltpu.VMEM((2, part, 4 * QUARTER), bf16),
            pltpu.VMEM((3, owners, part, QUARTER), bf16),
            pltpu.VMEM((5, 32, 128), f32),
            pltpu.VMEM((5, 32, 128), f32),
            dma((20,)),
            dma((20,)),
            dma((3, 2, owners - 1)),
            dma((3, 2, owners - 1)),
            dma((5,)),
            dma((5,)),
            dma((4,)),
        ],
        compiler_params=pltpu.CompilerParams(
            vmem_limit_bytes=60 << 20, collective_id=4, has_side_effects=True
        ),
        cost_estimate=pl.CostEstimate(flops=70 * 10**9, bytes_accessed=10**7, transcendentals=0),
        name="dense_sums",
    )(grads, upper, mix)


EXCHANGE_IDS = {"forward": 0, "both": 1, "backward": 2}


def exchange_call(mode, pack, ex, args):
    rows, ff = ex.total, pack.ff
    forward, backward = mode in ("forward", "both"), mode in ("backward", "both")
    flat, wide = shape((rows, D), bf16), shape((rows, ff), bf16)
    packed = (pack.shards, pack.rows, 256)
    most = max(ex.slots, ex.span((0, 1))[1], ex.span((2,))[1])
    vmem = pl.BlockSpec(memory_space=pltpu.VMEM)
    far = pl.BlockSpec(memory_space=pl.ANY)
    in_specs = [vmem] * len(args)
    in_specs[1] = far
    scratch = []
    if mode == "forward":
        outs = [flat, wide, wide]
    elif mode == "both":
        outs = [flat, flat, shape(packed, bf16)] + gating_outputs()
    else:
        in_specs[3] = in_specs[4] = far
        outs = [flat, shape(packed, bf16)] + gating_outputs()
    out_specs = [vmem] * len(outs)
    if mode == "forward":
        out_specs[1] = out_specs[2] = far
        scratch += [pltpu.VMEM((rows, ff), bf16)] * 2
    else:
        inputs = 9 if mode == "both" else 12
        in_specs[-inputs:] = [far] * inputs
        out_specs[2 if mode == "both" else 1] = far
    if mode == "forward":
        scratch.append(pltpu.VMEM((rows, D), bf16))
    if forward:
        scratch.append(pltpu.VMEM((most, D), f32))
    if backward:
        scratch += [pltpu.VMEM((rows, D), bf16)] * 2
        scratch += [pltpu.VMEM((rows, ff), bf16)] * 3
        scratch += [pltpu.VMEM((D, rows), bf16), pltpu.VMEM((most, D), f32)]
        scratch += [pltpu.VMEM(a.shape, a.dtype) for a in args[-inputs:]]
    if mode == "both":
        scratch.append(pltpu.VMEM((2, ex.experts - 1, 8, 128), f32))
        scratch.append(pltpu.VMEM((2, ex.experts, 8, 128), f32))
        scratch += [pltpu.SemaphoreType.DMA((2, ex.experts - 1))] * 2
    scratch.append(pltpu.VMEM(packed, bf16))
    count = len(ex.waves)
    scratch += [pltpu.SemaphoreType.DMA((count, ex.experts - 1))] * 2
    scratch += [pltpu.SemaphoreType.DMA((2, count, ex.experts - 1))] * 2
    scratch.append(pltpu.SemaphoreType.DMA((16,)))
    work = 6 * rows * D * ff * (1 if mode == "forward" else 2 if mode == "backward" else 3)
    return pl.pallas_call(
        functools.partial(exchange_kernel, mode, pack, ex),
        out_shape=outs,
        in_specs=in_specs,
        out_specs=out_specs,
        scratch_shapes=scratch,
        compiler_params=pltpu.CompilerParams(
            vmem_limit_bytes=62 << 20, collective_id=EXCHANGE_IDS[mode], has_side_effects=True
        ),
        cost_estimate=pl.CostEstimate(
            flops=10**9 if mode == "backward" else work + 40 * 10**9,
            bytes_accessed=6 * D * ff,
            transcendentals=0,
        ),
        name="experts_" + mode,
    )(*args)


def write_dense(part, labels, l, ref, outs, turn):
    proj_ref, out_ref, gain_ref, router_ref, vec_ref, const_ref = outs
    for c in range(3):
        proj_ref[l, c] = ref[:, c * D : (c + 1) * D].astype(f32)
    out_ref[l] = ref[:, W_OUT:W_SMALL].astype(f32)
    small = ref[:, W_SMALL:W_ALL].astype(f32)
    turn[0:part, :] = small
    rows = turn[...].T
    router_ref[l] = rows[0:labels, 0:part]
    for c in range(2):
        const_ref[l, c] = rows[S_CONST + 2 * c : S_CONST + 2 * c + 2, 0:part]
    gain_ref[l] = rows[S_GAIN : S_GAIN + 2, 0:part]
    vec_ref[l] = rows[S_VEC : S_VEC + 2, 0:part]


def outputs_kernel(pack, labels, traffic, low_ref, high_ref, dense_ref, hidden_ref, *refs):
    gate_ref, up_ref, down_ref = refs[:3]
    outs, hidden_out, turn = refs[3:9], refs[9], refs[10]
    turn[...] = jnp.zeros_like(turn)
    for l, ref in enumerate((low_ref, high_ref)):
        for n, out in enumerate((gate_ref, up_ref)):
            for j in range(pack.chunks):
                at = (n * pack.chunks + j) * pack.padded
                out[l, :, j * 256 : (j + 1) * 256] = ref[at : at + pack.part, :].astype(f32)
        for c in range(D // 256):
            at = pack.down + c * pack.own
            down_ref[l, :, c * 256 : (c + 1) * 256] = ref[at : at + pack.own, :].astype(f32)
        for out in (gate_ref, up_ref, down_ref):
            traffic.flush(out, l)
        write_dense(pack.part, labels, l, dense_ref.at[l], outs, turn)
        for out in outs[:2]:
            traffic.flush(out, l)
    traffic.need(hidden_ref)
    hidden_out[...] = hidden_ref[...]
    traffic.flush(hidden_out)


def dense_shapes(part, labels):
    return [
        shape((LAYERS, 3, part, D)),
        shape((LAYERS, part, D)),
        shape((LAYERS, 2, part)),
        shape((LAYERS, labels, part)),
        shape((LAYERS, 2, part)),
        shape((LAYERS, 2, 2, part)),
    ]


def outputs_call(pack, labels, grads, dense, hidden):
    wide = shape((LAYERS, pack.part, pack.ff))
    outs = [wide, wide, shape((LAYERS, pack.own, D))] + dense_shapes(pack.part, labels)
    outs.append(shape(hidden.shape, hidden.dtype))
    body = functools.partial(outputs_kernel, pack, labels)
    turn = [pltpu.VMEM((128, 128), f32)]
    return whole_call(body, "outputs", outs, turn, grads + [dense, hidden], 10**6, (3,), (0, 1, 2, 3, 4, 9))


def pack_kernel(traffic, proj_ref, out_ref, small_ref, *packed):
    for l, ref in enumerate(packed):
        for c in range(3):
            ref[:, c * D : (c + 1) * D] = proj_ref[l, c]
        ref[:, W_OUT:W_SMALL] = out_ref[l]
        ref[:, W_SMALL:] = small_ref[l]


def pack_call(project, output, small):
    outs = [shape((project.shape[2], W_ALL), bf16)] * LAYERS
    return whole_call(pack_kernel, "pack", outs, [], [project, output, small], 10**6)


def on_device(
    hidden_in,
    prior_logits,
    project_weight,
    output_weight,
    norm_gain,
    router_weight,
    mixing_weight,
    const_vector,
    const_weight,
    gate_weight,
    up_weight,
    down_weight,
    routes,
    priority,
    leaf_parent,
    cotangent,
):
    experts = lax.axis_size("expert")
    total_experts = experts + 4
    tokens = hidden_in.shape[0]
    capacity = 9 * tokens * TOP // (8 * total_experts)
    slots = -(-capacity // 16) * 16
    part = project_weight.shape[2]

    def pad_cols(a, width):
        return jnp.pad(a, [(0, 0)] * (a.ndim - 1) + [(0, width - a.shape[-1])])

    dense = []
    experts_w = []
    pack = Packing(lax.axis_size("shard"), part, gate_weight.shape[3])
    small = jnp.concatenate(
        [
            pad_cols(router_weight, S_CONST),
            const_weight[:, 0],
            const_weight[:, 1],
            jnp.zeros((LAYERS, part, S_GAIN - S_CONST - 4), bf16),
            norm_gain.transpose(0, 2, 1),
            const_vector.transpose(0, 2, 1),
        ],
        axis=2,
    )
    packed = pack_call(project_weight, output_weight, pad_cols(small, 128))
    for l in range(LAYERS):
        dense.append(lax.all_gather(packed[l], "shard", axis=0, tiled=True))
        mine = pack.pack(gate_weight[l, 0], up_weight[l, 0], down_weight[l, 0])
        experts_w.append(lax.all_gather(mine, "shard", axis=0, tiled=False))

    ranking = priority[0]
    earlier = (ranking[None, :] < ranking[:, None]).astype(bf16)
    labels = jnp.arange(total_experts, dtype=jnp.int32)
    hits = jnp.sum((routes[:, :, :, None] == labels).astype(f32), axis=2)
    chosen_rows = [jnp.pad(hits[l].T, [(0, 16 - total_experts), (0, 0)]) for l in range(LAYERS)]
    loaded = jnp.concatenate([hits[l, :, :experts] for l in range(LAYERS)], axis=1)
    loaded_half = loaded.astype(bf16)
    rank_row = lax.dot_general(
        loaded_half, earlier, (((0,), (1,)), ((), ())), preferred_element_type=f32
    )
    slot_row_all = jnp.where((loaded.T > 0) & (rank_row < capacity), rank_row, -1.0)
    slot_col = []
    for l in range(LAYERS):
        rank_col = dot(earlier, hits[l, :, :experts].astype(bf16))
        slot_col.append(
            jnp.where((hits[l, :, :experts] > 0) & (rank_col < capacity), rank_col, -1.0)
        )
    slot_row = [
        jnp.pad(
            slot_row_all[l * experts : (l + 1) * experts],
            [(0, 8 - experts), (0, 0)],
            constant_values=-1.0,
        )
        for l in range(LAYERS)
    ]
    visible = tree_visible(leaf_parent[0])
    bias = jnp.where(visible, 0.0, masked_fill)
    bias_t = jnp.where(visible.T, 0.0, masked_fill)
    mixes = [
        jnp.pad(mixing_weight[l], [(0, 16 - total_experts), (0, 16 - total_experts)])
        for l in range(LAYERS)
    ]
    z_rows = jnp.pad(prior_logits.T, [(0, 16 - total_experts), (0, 0)])

    plan = (bias, bias_t, slot_col, slot_row, chosen_rows, mixes, z_rows)
    bias, bias_t, slot_col, slot_row, chosen_rows, mixes, z_rows = lax.optimization_barrier(plan)
    ex = Exchange(experts, slots)
    saved = []
    front = [hidden_in]
    x_now = hidden_in
    for l in range(LAYERS):
        last = l == LAYERS - 1
        args = front + [dense[l], bias, z_rows, mixes[l].T, chosen_rows[l], slot_row[l]]
        if last:
            args.append(cotangent)
        outs = list(forward_call(l == 0, last, experts, slots, args))
        if l > 0:
            x_now = outs.pop(0)
        n1, qkv, att, lse, middle, n2, info, gcol, gpack, send, small, z_next = outs[:12]
        keep = dict(
            x=x_now, n1=n1, qkv=qkv, att=att, lse=lse, middle=middle, n2=n2, info=info,
            gcol=gcol, gpack=gpack, z=z_rows, small=small,
        )
        keep["received"] = dispatch_call(ex, send)
        if last:
            gating = [
                cotangent, n2, slot_row[l], info, chosen_rows[l], gcol, small, z_rows, mixes[l],
            ]
            done = exchange_call(
                "both", pack, ex, [keep["received"], experts_w[l], outs[12]] + gating
            )
            y_held, keep["gin"], keep["dw"] = done[:3]
            keep["gating"] = done[3:]
        else:
            keep["y"], keep["gate"], keep["up"] = exchange_call(
                "forward", pack, ex, [keep["received"], experts_w[l]]
            )
            front = [middle, n2, keep["y"], gcol, slot_col[l], small]
        z_rows = z_next
        saved.append(keep)

    gx = cotangent
    gz = None
    dense_grads = [None] * LAYERS
    mix_grads = [None] * LAYERS
    expert_grads = [None] * LAYERS
    hidden_out = None
    for l in range(LAYERS - 1, -1, -1):
        last = l == LAYERS - 1
        keep = saved[l]
        if not last:
            gating = [
                gx, keep["n2"], keep["y"], keep["gxs"], slot_row[l], keep["info"], chosen_rows[l],
                keep["gcol"], keep["small"], keep["z"], mixes[l], gz,
            ]
            done = exchange_call(
                "backward", pack, ex,
                [keep["received"], experts_w[l], keep["gy"], keep["gate"], keep["up"]] + gating,
            )
            keep["gin"], keep["dw"] = done[:2]
            keep["gating"] = done[2:]
        gn2, gsm, mix_grads[l], gz = keep["gating"][:4]
        d_experts, gn2 = lax.optimization_barrier((keep["dw"], gn2))
        if not last:
            gn2, expert_grads[l + 1] = lax.optimization_barrier((gn2, expert_grads[l + 1]))
        expert_grads[l] = lax.psum_scatter(d_experts, "shard", scatter_dimension=0, tiled=False)
        args = [
            gx, gn2, keep["gin"], slot_col[l], keep["middle"], keep["att"], dense[l], keep["qkv"],
            keep["n1"], keep["x"], bias_t, keep["lse"], gsm,
        ]
        if l > 0:
            args += [slot_row[l - 1], saved[l - 1]["gpack"], y_held, keep["n2"], keep["gcol"]]
        outs = backward_call(l == 0, experts, slots, args)
        gx, d_dense = outs[:2]
        if l > 0:
            saved[l - 1]["gxs"], saved[l - 1]["gy"], hidden_out = outs[2:5]
        if l > 0:
            dense_grads[l] = lax.psum_scatter(d_dense, "shard", scatter_dimension=0, tiled=True)

    if pack.shards == 8 and experts == 4:
        mix = jnp.pad(jnp.concatenate(mix_grads), [(0, 0), (0, 112)])
        dense_sums, mixing_grad = finish_call(part, total_experts, d_dense, dense_grads[1], mix)
    else:
        dense_grads[0] = lax.psum_scatter(d_dense, "shard", scatter_dimension=0, tiled=True)
        dense_sums = lax.psum(jnp.stack(dense_grads), "expert")
        mixing_grad = lax.psum(jnp.stack(mix_grads), ("expert", "shard"))
        mixing_grad = mixing_grad[:, 0:total_experts, 0:total_experts]
    made = outputs_call(pack, total_experts, expert_grads, dense_sums, hidden_out)
    gate_grad, up_grad, down_grad, project_grad, output_grad = made[:5]
    gain_grad, router_grad, vector_grad, const_grad, hidden_out = made[5:]
    return (
        hidden_out,
        gx,
        gz[0:total_experts].T,
        project_grad,
        output_grad,
        gain_grad,
        router_grad.transpose(0, 2, 1),
        mixing_grad,
        vector_grad,
        const_grad.transpose(0, 1, 3, 2),
        gate_grad[:, None],
        up_grad[:, None],
        down_grad[:, None],
    )


def solution(mesh):
    both = ("expert", "shard")
    in_specs = (
        P(both, None),
        P(both, None),
        P(None, None, "shard", None),
        P(None, "shard", None),
        P(None, None, "shard"),
        P(None, "shard", None),
        P(),
        P(None, None, "shard"),
        P(None, None, "shard", None),
        P(None, "expert", "shard", None),
        P(None, "expert", "shard", None),
        P(None, "expert", "shard", None),
        P(None, both, None),
        P(both, None),
        P(both, None),
        P(both, None),
    )
    out_specs = (
        P(both, None),
        P(both, None),
        P(both, None),
        P(None, None, "shard", None),
        P(None, "shard", None),
        P(None, None, "shard"),
        P(None, "shard", None),
        P(),
        P(None, None, "shard"),
        P(None, None, "shard", None),
        P(None, "expert", "shard", None),
        P(None, "expert", "shard", None),
        P(None, "expert", "shard", None),
    )
    return jax.shard_map(
        on_device, mesh=mesh, in_specs=in_specs, out_specs=out_specs, check_vma=False
    )
```
